32 devices in a mesh: batch: 8 (over z, y), tensor: 4 (over x, core).
Axes of the slice: x: 2, y: 2, z: 4, core: 2. Of those that a mesh axis runs over, the one named last changes fastest.
Arguments:
- tokens: bfloat16 [16384, 768], P(('batch', 'tensor')), may hold values from -6 to 6
- out_cotangent: bfloat16 [16384, 768], P(('batch', 'tensor')), may hold values from -6 to 6
- ln_gain: bfloat16 [768], replicated, may hold values from 0.25 to 1.75
- qkv_weight: bfloat16 [768, 2304], P(None, 'tensor'), may hold values from -0.21875 to 0.21875
- q_gain: bfloat16 [768], P('tensor'), may hold values from 0.099609375 to 1.8984375
- k_gain: bfloat16 [768], P('tensor'), may hold values from 0.099609375 to 1.8984375
- attn_out: bfloat16 [768, 768], P('tensor'), may hold values from -1.75 to 1.75
- mlp_in: bfloat16 [768, 3072], P(None, 'tensor'), may hold values from -0.21875 to 0.21875
- mlp_bias: bfloat16 [3072], P('tensor'), may hold values from -3 to 3
- mlp_out: bfloat16 [3072, 768], P('tensor'), may hold values from -0.109375 to 0.109375
- out_bias: bfloat16 [768], replicated, may hold values from -3 to 3
- image_len: int32 [80], replicated, may hold values from 0 to 1024, as said below
- image_group: int32 [80], replicated, may hold values from 0 to 7, as said below
Outputs:
- output: bfloat16 [16384, 768], P(('batch', 'tensor'))
- input_grad: bfloat16 [16384, 768], P(('batch', 'tensor'))
- ln_gain_grad: float32 [768], replicated
- qkv_grad: float32 [768, 2304], P(None, 'tensor')
- q_gain_grad: float32 [768], P('tensor')
- k_gain_grad: float32 [768], P('tensor')
- attn_out_grad: float32 [768, 768], P('tensor')
- mlp_in_grad: float32 [768, 3072], P(None, 'tensor')
- mlp_bias_grad: float32 [3072], P('tensor')
- mlp_out_grad: float32 [3072, 768], P('tensor')
- out_bias_grad: float32 [768], replicated
The draws below stay inside these ranges and needn't reach their ends.
Inputs may be any that keep to these rules, and one draw needn't show every extreme that they name: `image_len`: each entry is 0, 196 or 1024; every draw holds an image of 1024 tokens; the entries of one group never total more than 2048. `image_group`: each group index is named by exactly 10 entries.
All inputs are finite; a program needn't handle non-finite values.
Results may differ from the reference program's by a relative error of at most 0.015.
Values may be sent and summed in bfloat16 or wider, within the bound.
A program may use at most 128 MiB of HBM per device.

```python
import jax
import jax.numpy as jnp
from jax import lax

D = 768
HEADS = 12
DH = 64
FF = 3072
TOK_DEV = 512
SMALL_LEN = 196
BIG_LEN = 1024
CAP = 2048
IMG_GROUP = 10
IMAGES = 80
TOKENS = 16384
N_BATCH = 8
N_TENSOR = 4


def group_layout(key):
    forced = jax.random.randint(jax.random.fold_in(key, 11), (), 0, N_BATCH)
    coins = jax.random.randint(jax.random.fold_in(key, 12), (N_BATCH,), 0, 8)
    heavy = (coins == 0) | (jnp.arange(N_BATCH) == forced)
    slot_ids = jnp.arange(IMG_GROUP)[None, :]
    extra = (CAP - BIG_LEN) // SMALL_LEN
    heavy_len = jnp.where(slot_ids == 0, BIG_LEN, jnp.where(slot_ids <= extra, SMALL_LEN, 0))
    light_len = jnp.where(slot_ids < IMG_GROUP, SMALL_LEN, 0)
    lengths = jnp.where(heavy[:, None], heavy_len, light_len).reshape(-1)
    owners = jnp.arange(IMAGES) // IMG_GROUP
    shuffle = jax.random.permutation(jax.random.fold_in(key, 13), IMAGES)
    return (lengths[shuffle].astype(jnp.int32), owners[shuffle].astype(jnp.int32))


def draw_image_len(key, part):
    layout = group_layout(key)
    return layout[0]


def draw_image_group(key, part):
    layout = group_layout(key)
    return layout[1]


def level_of(own_key, extent, shards, low, high):
    def one(position, shards_of):
        heights = jax.random.uniform(jax.random.fold_in(jax.random.fold_in(own_key, 6), position), (shards_of,), jnp.float32, low / len(shards), high / len(shards))
        return jnp.repeat(jnp.exp(heights), extent[position] // shards_of).reshape((-1,) + (1,) * (len(extent) - position - 1))

    level = one(*shards[0])
    for cut in shards[1:]:
        level = level * one(*cut)
    return level


def normal_values(own_key, extent, width, bound, cuts=(), kind=jnp.bfloat16):
    result = jax.random.normal(own_key, extent, jnp.float32) * width
    if len(cuts) > 0:
        result = level_of(own_key, extent, cuts, -0.22, 0.18) * result
    return jnp.clip(result, min=-bound, max=bound).astype(kind)


def setup_inputs(seed: int = 0) -> dict:
    seeds = jax.random.split(jax.random.key(seed), 14)
    return {
        "tokens": normal_values(seeds[0], (TOKENS, D), 1.0, 6.0, ((0, 32),)),
        "out_cotangent": normal_values(seeds[1], (TOKENS, D), 1.0, 6.0, ((0, 32),)),
        "ln_gain": jnp.clip(1.0 + 0.15 * jax.random.normal(seeds[2], (D,), jnp.float32), 0.25, 1.75).astype(jnp.bfloat16),
        "qkv_weight": normal_values(seeds[3], (D, 3 * HEADS * DH), D ** -0.5, 0.21875, ((1, 4),)),
        "q_gain": jnp.clip(1.0 + 0.18 * jax.random.normal(seeds[4], (HEADS * DH,), jnp.float32), 0.099609375, 1.8984375).astype(jnp.bfloat16),
        "k_gain": jnp.clip(1.0 + 0.18 * jax.random.normal(seeds[5], (HEADS * DH,), jnp.float32), 0.099609375, 1.8984375).astype(jnp.bfloat16),
        "attn_out": normal_values(seeds[6], (HEADS * DH, D), (HEADS * DH // 64) ** -0.5, 1.75, ((0, 4),)),
        "mlp_in": normal_values(seeds[7], (D, FF), D ** -0.5, 0.21875, ((1, 4),)),
        "mlp_bias": normal_values(seeds[8], (FF,), 0.5, 3.0, ((0, 4),)),
        "mlp_out": normal_values(seeds[9], (FF, D), FF ** -0.5, 0.109375, ((0, 4),)),
        "out_bias": normal_values(seeds[10], (D,), 0.5, 3.0),
        "image_len": draw_image_len(jax.random.fold_in(seeds[13], 71), 0),
        "image_group": draw_image_group(jax.random.fold_in(seeds[13], 71), 0),
    }


@jax.custom_vjp
def low(v):
    return lax.optimization_barrier(v.astype(jnp.bfloat16)).astype(jnp.float32)

@jax.custom_vjp
def low_back(v):
    return v

def low_keep(v):
    return (low(v), None)

def low_pass(kept, grad):
    return (grad,)

def back_keep(v):
    return (v, None)

def back_low(kept, grad):
    return (low(grad),)
low.defvjp(low_keep, low_pass)
low_back.defvjp(back_keep, back_low)
epsilon = 1e-06

def matmul(left, right):
    return jnp.dot(left, right, precision=lax.Precision.HIGHEST, preferred_element_type=jnp.float32)

def layer_norm(inputs, gain):
    row_mean = lax.optimization_barrier(jnp.mean(inputs, axis=-1, keepdims=True))
    centred = inputs - row_mean
    variance = lax.optimization_barrier(jnp.mean(centred * centred, axis=-1, keepdims=True))
    return centred * lax.rsqrt(variance + epsilon) * gain

def group_segments(image_len, image_group, group):
    row_ids = jnp.arange(CAP, dtype=jnp.int32)
    token_order = row_ids % TOK_DEV * N_TENSOR + row_ids // TOK_DEV
    member = image_group == group
    run_ends = jnp.cumsum(jnp.where(member, image_len, 0)).astype(jnp.int32)
    before = member[None, :] & (run_ends[None, :] <= token_order[:, None])
    return lax.optimization_barrier(jnp.sum(before.astype(jnp.int32), axis=1)).astype(jnp.int32)

def forward(x_rows, params, segment):
    ln_gain, qkv_weight, q_gain, k_gain, attn_out, mlp_in, mlp_bias, mlp_out, out_bias = params
    normed = low(layer_norm(x_rows, ln_gain))
    qkv_pre = low_back(matmul(normed, qkv_weight)).reshape(CAP, HEADS, 3, DH)
    query_rows = low(layer_norm(qkv_pre[:, :, 0], q_gain.reshape(HEADS, DH)) * DH ** (-0.5))
    key_rows = low(layer_norm(qkv_pre[:, :, 1], k_gain.reshape(HEADS, DH)))
    value_rows = low(qkv_pre[:, :, 2])
    allowed = segment[:, None] == segment[None, :]

    def one_head(triple):
        q_head, k_head, v_head = triple
        scores = low_back(matmul(q_head, k_head.T))
        scores = jnp.where(allowed, scores, -1e+30)
        weights = low(jax.nn.softmax(scores, axis=-1))
        return matmul(weights, v_head)
    heads = lax.map(jax.checkpoint(one_head), (query_rows.transpose(1, 0, 2), key_rows.transpose(1, 0, 2), value_rows.transpose(1, 0, 2)))
    heads_out = low(low_back(heads.transpose(1, 0, 2).reshape(CAP, HEADS * DH)))
    hidden_pre = low_back(matmul(normed, mlp_in) + mlp_bias)
    activation = low(jax.nn.gelu(hidden_pre, approximate=False))
    return x_rows + matmul(heads_out, attn_out) + matmul(activation, mlp_out) + out_bias

def reference(tokens, out_cotangent, ln_gain, qkv_weight, q_gain, k_gain, attn_out, mlp_in, mlp_bias, mlp_out, out_bias, image_len, image_group):
    params = tuple((item.astype(jnp.float32) for item in (ln_gain, qkv_weight, q_gain, k_gain, attn_out, mlp_in, mlp_bias, mlp_out, out_bias)))
    segments = lax.map(lambda group: group_segments(image_len, image_group, group), jnp.arange(N_BATCH, dtype=jnp.int32))
    group_rows = tokens.reshape(N_BATCH, CAP, D)
    group_cot = out_cotangent.reshape(N_BATCH, CAP, D)

    def step(totals, item):
        x_group, cot_group, segment = item

        def apply(x_rows, *weights):
            return forward(x_rows, weights, segment)
        y_group, pull = jax.vjp(apply, x_group.astype(jnp.float32), *params)
        grads = pull(cot_group.astype(jnp.float32))
        totals = tuple((total + grad for total, grad in zip(totals, grads[1:])))
        return (totals, (y_group.astype(jnp.bfloat16), grads[0].astype(jnp.bfloat16)))
    zeros = tuple((jnp.zeros(item.shape, jnp.float32) for item in params))
    totals, (outputs, input_grads) = lax.scan(step, zeros, (group_rows, group_cot, segments))
    ln_g, qkv_g, qg_g, kg_g, attn_g, mlp_in_g, bias_g, mlp_out_g, out_bias_g = totals
    return (outputs.reshape(TOKENS, D), input_grads.reshape(TOKENS, D), ln_g, qkv_g, qg_g, kg_g, attn_g, mlp_in_g, bias_g, mlp_out_g, out_bias_g)
```

```python
import functools

import jax
import jax.numpy as jnp
from jax import lax
from jax.experimental import pallas as pl
from jax.experimental.pallas import tpu as pltpu
from jax.sharding import PartitionSpec as P

DH = 64
LANES = 128
WIN = 64
LOG2E = 1.4426950408889634
epsilon = 1e-06
F32 = jnp.float32
BF16 = jnp.bfloat16
VMEM = pl.BlockSpec(memory_space=pltpu.VMEM)
SMEM = pl.BlockSpec(memory_space=pltpu.SMEM)
ANY = pl.BlockSpec(memory_space=pl.ANY)


def nn(left, right):
    return lax.dot_general(left, right, (((1,), (0,)), ((), ())), preferred_element_type=F32)


def nt(left, right):
    return lax.dot_general(left, right, (((1,), (1,)), ((), ())), preferred_element_type=F32)


def tn(left, right):
    return lax.dot_general(left, right, (((0,), (0,)), ((), ())), preferred_element_type=F32)


def find_segments(len_ref, group_ref, seg_ref, strips, tok_dev):
    group = lax.axis_index("batch")

    def entry(i, carry):
        count, run = carry
        rows = jnp.where(group_ref[i] == group, len_ref[i] // strips, 0)

        @pl.when(rows > 0)
        def _():
            seg_ref[0, count] = run
            seg_ref[1, count] = run + rows

        return count + jnp.where(rows > 0, 1, 0), run + rows

    count, run = lax.fori_loop(0, len_ref.shape[0], entry, (jnp.int32(0), jnp.int32(0)))

    @pl.when(run < tok_dev)
    def _():
        seg_ref[0, count] = run
        seg_ref[1, count] = tok_dev

    return count + jnp.where(run < tok_dev, 1, 0)


def window(start, end, first, i, tok_dev):
    nominal = first + WIN * i
    at = pl.multiple_of(jnp.minimum(nominal, tok_dev - WIN), 16)
    return at, jnp.maximum(start, nominal) - at, jnp.minimum(end, nominal + WIN) - at


def row_mask(low, high, strips, width=LANES):
    j = lax.broadcasted_iota(jnp.int32, (strips, WIN, width), 1).reshape(strips * WIN, width)
    return (j >= low) & (j < high)


def tile(ref, at, h):
    strips = ref.shape[0]
    return ref[:, pl.ds(at, WIN), h * LANES : (h + 1) * LANES].reshape(strips * WIN, LANES)


def put_tile(ref, at, h, mask, value, width=LANES):
    strips = ref.shape[0]
    where = (slice(None), pl.ds(at, WIN), slice(h * LANES, h * LANES + width))
    old = ref[where].reshape(strips * WIN, width)
    ref[where] = jnp.where(mask, value.astype(ref.dtype), old).reshape(strips, WIN, width)


def attn_fwd_body(heads, len_ref, group_ref, qa, ka, va, do, qb, dob, ho, seg, acc):
    strips, tok_dev = qa.shape[0], qa.shape[1]
    count = find_segments(len_ref, group_ref, seg, strips, tok_dev)
    lane = lax.broadcasted_iota(jnp.int32, (strips * WIN, LANES), 1)
    left = lane < DH

    def finish(h, at, low, high, total):
        mask = row_mask(low, high, strips)
        rows_sum = jnp.where(left, pltpu.roll(total, DH, 1), total)
        out = jnp.where(left, total / rows_sum, 0.0)
        log_sum = jnp.log2(rows_sum)
        d_out = tile(do, at, h).astype(F32)
        out_low = out.astype(BF16)
        delta = jnp.sum(out * d_out, axis=-1, keepdims=True)
        log_hi = log_sum.astype(BF16).astype(F32)
        delta_hi = delta.astype(BF16).astype(F32)
        q = tile(qa, at, h).astype(F32)
        q = jnp.where(lane == DH, -log_hi, jnp.where(lane == DH + 1, log_hi - log_sum, q))
        d_out = jnp.where(lane == DH, -delta_hi, jnp.where(lane == DH + 1, delta_hi - delta, d_out))
        put_tile(ho, at, h, mask, out_low)
        put_tile(qb, at, h, mask, q)
        put_tile(dob, at, h, mask, d_out)

    def product(h, at_q, at_k, k_mask):
        scores = nt(tile(qa, at_q, h), tile(ka, at_k, h))
        weights = jnp.exp2(scores).astype(BF16)
        return nn(weights, jnp.where(k_mask, tile(va, at_k, h), jnp.zeros((), BF16)))

    def segment(index, _):
        start, end = seg[0, index], seg[1, index]
        first = (start // 16) * 16
        windows = (end - first + WIN - 1) // WIN

        @pl.when(windows == 1)
        def _():
            at, low, high = window(start, end, first, 0, tok_dev)
            mask = row_mask(low, high, strips)
            for h in range(heads):
                finish(h, at, low, high, product(h, at, at, mask))

        @pl.when(windows > 1)
        def _():
            def q_window(i, _):
                at_q, low_q, high_q = window(start, end, first, i, tok_dev)
                acc[...] = jnp.zeros_like(acc)

                def k_window(k, _):
                    at_k, low_k, high_k = window(start, end, first, k, tok_dev)
                    mask = row_mask(low_k, high_k, strips)
                    for h in range(heads):
                        acc[h] += product(h, at_q, at_k, mask)
                    return 0

                lax.fori_loop(0, windows, k_window, 0)
                for h in range(heads):
                    finish(h, at_q, low_q, high_q, acc[h])
                return 0

            lax.fori_loop(0, windows, q_window, 0)

        return 0

    lax.fori_loop(0, count, segment, 0)


def attn_fwd(image_len, image_group, qa, ka, va, do):
    strips, tok_dev, width = qa.shape
    heads = width // LANES
    like = jax.ShapeDtypeStruct(qa.shape, BF16)
    return pl.pallas_call(
        functools.partial(attn_fwd_body, heads),
        out_shape=(like, like, like),
        in_specs=[SMEM, SMEM] + [VMEM] * 4,
        out_specs=(VMEM,) * 3,
        scratch_shapes=[
            pltpu.SMEM((2, image_len.shape[0] + 1), jnp.int32),
            pltpu.VMEM((heads, strips * WIN, LANES), F32),
        ],
        compiler_params=pltpu.CompilerParams(vmem_limit_bytes=48 << 20),
        name="attention_forward",
    )(image_len, image_group, qa, ka, va, do)


def attn_bwd_body(
    heads, len_ref, group_ref, qb, ka, va, dob, uq, uk, gq, gk,
    d_qkv, gain_grad, seg, k_turned, dq_turned, dk_acc, dv_acc, dq, dk, dv,
):
    strips, tok_dev = qb.shape[0], qb.shape[1]
    count = find_segments(len_ref, group_ref, seg, strips, tok_dev)
    zero = jnp.zeros((), BF16)

    def products(h, at_q, at_k, q_mask, k_turned_h):
        q = tile(qb, at_q, h)
        d_out = jnp.where(q_mask, tile(dob, at_q, h), zero)
        weights = jnp.exp2(nt(tile(ka, at_k, h), q))
        d_weights = nt(tile(va, at_k, h), d_out)
        d_scores = (weights * d_weights).astype(BF16)
        return nn(k_turned_h, d_scores), nn(d_scores, q), nn(weights.astype(BF16), d_out)

    def turned(h, at_k, mask):
        return jnp.where(mask, tile(ka, at_k, h), zero).T[:DH]

    def segment(index, _):
        start, end = seg[0, index], seg[1, index]
        first = (start // 16) * 16
        windows = (end - first + WIN - 1) // WIN

        @pl.when(windows == 1)
        def _():
            at, low, high = window(start, end, first, 0, tok_dev)
            mask = row_mask(low, high, strips)
            half = row_mask(low, high, strips, DH)
            for h in range(heads):
                dq_t, dk_new, dv_new = products(h, at, at, mask, turned(h, at, mask))
                put_tile(dq, at, h, half, dq_t.T, DH)
                put_tile(dk, at, h, mask, dk_new)
                put_tile(dv, at, h, mask, dv_new)

        @pl.when(windows > 1)
        def _():
            def clear(i, _):
                for h in range(heads):
                    dq_turned[h, i] = jnp.zeros(dq_turned.shape[2:], F32)
                return 0

            lax.fori_loop(0, windows, clear, 0)

            def k_window(k, _):
                at_k, low_k, high_k = window(start, end, first, k, tok_dev)
                mask_k = row_mask(low_k, high_k, strips)
                for h in range(heads):
                    k_turned[h] = turned(h, at_k, mask_k)
                dk_acc[...] = jnp.zeros_like(dk_acc)
                dv_acc[...] = jnp.zeros_like(dv_acc)

                def q_window(i, _):
                    at_q, low_q, high_q = window(start, end, first, i, tok_dev)
                    mask_q = row_mask(low_q, high_q, strips)
                    for h in range(heads):
                        dq_t, dk_new, dv_new = products(h, at_q, at_k, mask_q, k_turned[h])
                        dq_turned[h, i] += dq_t
                        dk_acc[h] += dk_new
                        dv_acc[h] += dv_new
                    return 0

                lax.fori_loop(0, windows, q_window, 0)
                for h in range(heads):
                    put_tile(dk, at_k, h, mask_k, dk_acc[h])
                    put_tile(dv, at_k, h, mask_k, dv_acc[h])
                return 0

            lax.fori_loop(0, windows, k_window, 0)

            def q_out(i, _):
                at_q, low_q, high_q = window(start, end, first, i, tok_dev)
                half = row_mask(low_q, high_q, strips, DH)
                for h in range(heads):
                    put_tile(dq, at_q, h, half, dq_turned[h, i].T, DH)
                return 0

            lax.fori_loop(0, windows, q_out, 0)

        return 0

    lax.fori_loop(0, count, segment, 0)

    rows = strips * WIN
    lane = lax.broadcasted_iota(jnp.int32, (rows, LANES), 1)
    left = lane < DH

    def norm_back(d_rows, u_ref, gain, at, h):
        u = tile(u_ref, at, h).astype(F32)
        rstd = pltpu.roll(u, DH, 1)
        d_rows = jnp.where(left, d_rows, 0.0)
        scaled = d_rows * gain
        mean = jnp.sum(scaled, axis=-1, keepdims=True) * (1.0 / DH)
        mean_u = jnp.sum(scaled * u, axis=-1, keepdims=True) * (1.0 / DH)
        return (scaled - mean - u * mean_u) * rstd, jnp.sum(d_rows * u, axis=0, keepdims=True)

    gain_grad[...] = jnp.zeros_like(gain_grad)

    def chunk(i, _):
        at = pl.multiple_of(i * WIN, WIN)
        parts = []
        for h in range(heads):
            cols = slice(h * LANES, (h + 1) * LANES)
            d_q, g_q = norm_back(tile(dq, at, h), uq, gq[:, cols], at, h)
            d_k, g_k = norm_back(tile(dk, at, h) * (1.0 / LOG2E), uk, gk[:, cols], at, h)
            gain_grad[0:1, cols] += g_q * DH ** (-0.5)
            gain_grad[1:2, cols] += g_k
            parts += [d_q, d_k, tile(dv, at, h)]
        if len(parts) % 2:
            parts.append(jnp.zeros_like(parts[0]))
        for b in range(len(parts) // 2):
            block = jnp.where(left, parts[2 * b], pltpu.roll(parts[2 * b + 1], DH, 1))
            d_qkv[:, pl.ds(at, WIN), b * LANES : (b + 1) * LANES] = block.astype(BF16).reshape(strips, WIN, LANES)
        return 0

    lax.fori_loop(0, tok_dev // WIN, chunk, 0)


def attn_bwd(image_len, image_group, qb, ka, va, dob, uq, uk, gq, gk):
    strips, tok_dev, width = qb.shape
    heads = width // LANES
    blocks = (3 * heads + 1) // 2
    rows = strips * WIN
    windows = tok_dev // WIN + 1
    full = pltpu.VMEM((strips, tok_dev, width), F32)
    return pl.pallas_call(
        functools.partial(attn_bwd_body, heads),
        out_shape=(
            jax.ShapeDtypeStruct((strips, tok_dev, blocks * LANES), BF16),
            jax.ShapeDtypeStruct((8, width), F32),
        ),
        in_specs=[SMEM, SMEM] + [VMEM] * 8,
        out_specs=(VMEM, VMEM),
        scratch_shapes=[
            pltpu.SMEM((2, image_len.shape[0] + 1), jnp.int32),
            pltpu.VMEM((heads, DH, rows), BF16),
            pltpu.VMEM((heads, windows, DH, rows), F32),
            pltpu.VMEM((heads, rows, LANES), F32),
            pltpu.VMEM((heads, rows, LANES), F32),
            full, full, full,
        ],
        compiler_params=pltpu.CompilerParams(vmem_limit_bytes=56 << 20),
        name="attention_backward",
    )(image_len, image_group, qb, ka, va, dob, uq, uk, gq, gk)


def layer_norm(inputs, gain):
    row_mean = jnp.mean(inputs, axis=-1, keepdims=True)
    centred = inputs - row_mean
    variance = jnp.mean(centred * centred, axis=-1, keepdims=True)
    return centred * lax.rsqrt(variance + epsilon) * gain


def head_norm(part):
    centred = part - jnp.mean(part, axis=-1, keepdims=True)
    rstd = lax.rsqrt(jnp.mean(centred * centred, axis=-1, keepdims=True) + epsilon)
    return centred * rstd, rstd


def gelu_exact(hidden_pre):
    return jax.nn.gelu(hidden_pre, approximate=False)


def on_device(
    tokens, out_cotangent, ln_gain, qkv_weight, q_gain, k_gain, attn_out,
    mlp_in, mlp_bias, mlp_out, out_bias, image_len, image_group,
):
    tok_dev = tokens.shape[0]
    strips = lax.axis_size("tensor")
    cap = tok_dev * strips
    heads = q_gain.shape[0] // DH
    head_width = heads * DH
    qkv_cols = qkv_weight.shape[1]

    def pad_heads(x, fill):
        x = x.astype(BF16).reshape(strips, tok_dev, heads, DH)
        fill = jnp.broadcast_to(jnp.asarray(fill, BF16), x.shape)
        return jnp.concatenate([x, fill], axis=-1).reshape(strips, tok_dev, heads * LANES)

    def pad_gain(g):
        g = g.astype(F32).reshape(heads, DH)
        return jnp.concatenate([g, jnp.zeros_like(g)], axis=-1).reshape(1, heads * LANES)

    joined_weight = jnp.concatenate([qkv_weight, mlp_in], axis=1)
    x_full = tokens.astype(F32)
    normed_value, ln_pull = jax.vjp(layer_norm, x_full, ln_gain.astype(F32))
    normed = normed_value.astype(BF16)
    normed_all = lax.all_gather(normed, "tensor", axis=0, tiled=True)
    joined_pre = jnp.dot(normed_all, joined_weight, preferred_element_type=F32)
    parts = joined_pre[:, :qkv_cols].reshape(cap, heads, 3, DH)
    hidden_pre = joined_pre[:, qkv_cols:] + mlp_bias.astype(F32)
    u_q, r_q = head_norm(parts[:, :, 0])
    u_k, r_k = head_norm(parts[:, :, 1])
    gq = q_gain.astype(F32).reshape(heads, DH)
    gk = k_gain.astype(F32).reshape(heads, DH)
    qa = pad_heads(u_q * gq * (DH ** (-0.5) * LOG2E), 0.0)
    ka = pad_heads(u_k * gk, 1.0)
    va = pad_heads(parts[:, :, 2], 1.0)
    uq = pad_heads(u_q, r_q.reshape(strips, tok_dev, heads, 1))
    uk = pad_heads(u_k, r_k.reshape(strips, tok_dev, heads, 1))
    act_value, gelu_pull = jax.vjp(gelu_exact, hidden_pre)
    activation = act_value.astype(BF16)
    grad_rows = lax.all_gather(out_cotangent, "tensor", axis=0, tiled=True)
    d_heads = nt(grad_rows, attn_out).astype(BF16)
    do = pad_heads(d_heads, 0.0)

    qb, dob, ho = attn_fwd(image_len, image_group, qa, ka, va, do)
    heads_out = ho.reshape(cap, heads, LANES)[:, :, :DH].reshape(cap, head_width)
    summed = lax.psum_scatter(
        (nn(heads_out, attn_out) + nn(activation, mlp_out)).astype(BF16), "tensor", scatter_dimension=0, tiled=True
    )
    output = (x_full + summed.astype(F32) + out_bias.astype(F32)).astype(BF16)
    d_act = nt(grad_rows, mlp_out)
    attn_out_grad = tn(heads_out, grad_rows)
    mlp_out_grad = tn(activation, grad_rows)
    d_hidden = gelu_pull(d_act)[0].astype(BF16)

    d_qkv, gain_grad = attn_bwd(
        image_len, image_group, qb, ka, va, dob, uq, uk, pad_gain(q_gain) * DH ** (-0.5), pad_gain(k_gain)
    )
    d_qkv = d_qkv.reshape(cap, -1)[:, :qkv_cols]
    gain_grad = gain_grad.reshape(8, heads, LANES)[:, :, :DH].reshape(8, head_width)
    q_gain_grad, k_gain_grad = gain_grad[0], gain_grad[1]
    d_joined = jnp.concatenate([d_qkv, d_hidden], axis=1)
    mlp_bias_grad = jnp.sum(d_hidden.astype(F32), axis=0)
    joined_grad = tn(normed_all, d_joined)
    d_normed = lax.psum_scatter(nt(d_joined, joined_weight).astype(BF16), "tensor", scatter_dimension=0, tiled=True)
    d_x, ln_gain_part = ln_pull(d_normed.astype(F32))
    input_grad = (out_cotangent.astype(F32) + d_x).astype(BF16)
    out_bias_part = jnp.sum(out_cotangent.astype(F32), axis=0)
    ln_gain_grad, out_bias_grad = lax.psum((ln_gain_part, out_bias_part), ("batch", "tensor"))
    qkv_grad = joined_grad[:, :qkv_cols]
    mlp_in_grad = joined_grad[:, qkv_cols:]

    def over_batch(grad):
        return lax.psum(grad.astype(BF16), "batch").astype(F32)

    return (
        output,
        input_grad,
        ln_gain_grad,
        over_batch(qkv_grad),
        over_batch(q_gain_grad),
        over_batch(k_gain_grad),
        over_batch(attn_out_grad),
        over_batch(mlp_in_grad),
        over_batch(mlp_bias_grad),
        over_batch(mlp_out_grad),
        out_bias_grad,
    )


def solution(mesh):
    rows, cols, first = P(("batch", "tensor"), None), P(None, "tensor"), P("tensor", None)
    return jax.shard_map(
        on_device,
        mesh=mesh,
        in_specs=(rows, rows, P(), cols, P("tensor"), P("tensor"), first, cols, P("tensor"), first, P(), P(), P()),
        out_specs=(rows, rows, P(), cols, P("tensor"), P("tensor"), first, cols, P("tensor"), first, P()),
        check_vma=False,
    )
```

```python
import functools

import jax
import jax.numpy as jnp
from jax import lax
from jax.experimental import pallas as pl
from jax.experimental.pallas import tpu as pltpu
from jax.sharding import PartitionSpec as P

DH = 64
LANES = 128
WIN = 64
LOG2E = 1.4426950408889634
epsilon = 1e-06
F32 = jnp.float32
BF16 = jnp.bfloat16
VMEM = pl.BlockSpec(memory_space=pltpu.VMEM)
SMEM = pl.BlockSpec(memory_space=pltpu.SMEM)
ANY = pl.BlockSpec(memory_space=pl.ANY)


def nn(left, right):
    return lax.dot_general(left, right, (((1,), (0,)), ((), ())), preferred_element_type=F32)


def nt(left, right):
    return lax.dot_general(left, right, (((1,), (1,)), ((), ())), preferred_element_type=F32)


def tn(left, right):
    return lax.dot_general(left, right, (((0,), (0,)), ((), ())), preferred_element_type=F32)


def find_segments(len_ref, group_ref, seg_ref, strips, tok_dev):
    group = lax.axis_index("batch")

    def entry(i, carry):
        count, run = carry
        rows = jnp.where(group_ref[i] == group, len_ref[i] // strips, 0)

        @pl.when(rows > 0)
        def _():
            seg_ref[0, count] = run
            seg_ref[1, count] = run + rows

        return count + jnp.where(rows > 0, 1, 0), run + rows

    count, run = lax.fori_loop(0, len_ref.shape[0], entry, (jnp.int32(0), jnp.int32(0)))

    @pl.when(run < tok_dev)
    def _():
        seg_ref[0, count] = run
        seg_ref[1, count] = tok_dev

    return count + jnp.where(run < tok_dev, 1, 0)


def window(start, end, first, i, tok_dev):
    nominal = first + WIN * i
    at = pl.multiple_of(jnp.minimum(nominal, tok_dev - WIN), 16)
    return at, jnp.maximum(start, nominal) - at, jnp.minimum(end, nominal + WIN) - at


def row_mask(low, high, strips, width=LANES):
    j = lax.broadcasted_iota(jnp.int32, (strips, WIN, width), 1).reshape(strips * WIN, width)
    return (j >= low) & (j < high)


def tile(ref, at, h):
    strips = ref.shape[0]
    return ref[:, pl.ds(at, WIN), h * LANES : (h + 1) * LANES].reshape(strips * WIN, LANES)


def put_tile(ref, at, h, mask, value, width=LANES):
    strips = ref.shape[0]
    where = (slice(None), pl.ds(at, WIN), slice(h * LANES, h * LANES + width))
    old = ref[where].reshape(strips * WIN, width)
    ref[where] = jnp.where(mask, value.astype(ref.dtype), old).reshape(strips, WIN, width)


def attn_fwd_body(
    heads, len_ref, group_ref, qa, ka, va, do, attn_out, mlp_part_hbm, call_hbm,
    qb, dob, give, keep, attn_grad, seg, acc, ho, mlp_part, call, out_pad, grad_acc, sems,
):
    strips, tok_dev = qa.shape[0], qa.shape[1]
    loads = [pltpu.make_async_copy(mlp_part_hbm, mlp_part, sems.at[0]), pltpu.make_async_copy(call_hbm, call, sems.at[1])]
    for load in loads:
        load.start()
    count = find_segments(len_ref, group_ref, seg, strips, tok_dev)
    lane = lax.broadcasted_iota(jnp.int32, (strips * WIN, LANES), 1)
    left = lane < DH

    def finish(h, at, low, high, total):
        mask = row_mask(low, high, strips)
        rows_sum = jnp.where(left, pltpu.roll(total, DH, 1), total)
        out = jnp.where(left, total / rows_sum, 0.0)
        log_sum = jnp.log2(rows_sum)
        d_out = tile(do, at, h).astype(F32)
        out_low = out.astype(BF16)
        delta = jnp.sum(out * d_out, axis=-1, keepdims=True)
        log_hi = log_sum.astype(BF16).astype(F32)
        delta_hi = delta.astype(BF16).astype(F32)
        q = tile(qa, at, h).astype(F32)
        q = jnp.where(lane == DH, -log_hi, jnp.where(lane == DH + 1, log_hi - log_sum, q))
        d_out = jnp.where(lane == DH, -delta_hi, jnp.where(lane == DH + 1, delta_hi - delta, d_out))
        put_tile(ho, at, h, mask, out_low)
        put_tile(qb, at, h, mask, q)
        put_tile(dob, at, h, mask, d_out)

    def product(h, at_q, at_k, k_mask):
        scores = nt(tile(qa, at_q, h), tile(ka, at_k, h))
        weights = jnp.exp2(scores).astype(BF16)
        return nn(weights, jnp.where(k_mask, tile(va, at_k, h), jnp.zeros((), BF16)))

    def segment(index, _):
        start, end = seg[0, index], seg[1, index]
        first = (start // 16) * 16
        windows = (end - first + WIN - 1) // WIN

        @pl.when(windows == 1)
        def _():
            at, low, high = window(start, end, first, 0, tok_dev)
            mask = row_mask(low, high, strips)
            for h in range(heads):
                finish(h, at, low, high, product(h, at, at, mask))

        @pl.when(windows > 1)
        def _():
            def q_window(i, _):
                at_q, low_q, high_q = window(start, end, first, i, tok_dev)
                acc[...] = jnp.zeros_like(acc)

                def k_window(k, _):
                    at_k, low_k, high_k = window(start, end, first, k, tok_dev)
                    mask = row_mask(low_k, high_k, strips)
                    for h in range(heads):
                        acc[h] += product(h, at_q, at_k, mask)
                    return 0

                lax.fori_loop(0, windows, k_window, 0)
                for h in range(heads):
                    finish(h, at_q, low_q, high_q, acc[h])
                return 0

            lax.fori_loop(0, windows, q_window, 0)

        return 0

    lax.fori_loop(0, count, segment, 0)

    for h in range(heads):
        out_pad[h * LANES : h * LANES + DH, :] = attn_out[h * DH : (h + 1) * DH, :]
        out_pad[h * LANES + DH : (h + 1) * LANES, :] = jnp.zeros((DH, out_pad.shape[1]), BF16)
    for load in loads:
        load.wait()
    me = lax.axis_index("tensor")
    rows = 256
    per_strip = tok_dev // rows
    grad_acc[...] = jnp.zeros_like(grad_acc)

    def project(i, _):
        strip = i // per_strip
        at = pl.ds(pl.multiple_of(i % per_strip * rows, rows), rows)
        heads_rows = ho[strip, at]
        out = (nn(heads_rows, out_pad[...]) + mlp_part[strip, at].astype(F32)).astype(BF16)
        own = jnp.where(strip // 2 == me // 2, 1, 0)

        @pl.when(strip % 2 == me % 2)
        def _():
            keep[own, at] = out

        @pl.when(strip % 2 != me % 2)
        def _():
            give[own, at] = out

        grad_acc[...] += tn(heads_rows, call[strip, at])
        return 0

    lax.fori_loop(0, strips * per_strip, project, 0)
    for h in range(heads):
        attn_grad[h * DH : (h + 1) * DH, :] = grad_acc[h * LANES : h * LANES + DH, :].astype(BF16)


def attn_fwd(image_len, image_group, qa, ka, va, do, attn_out, mlp_part, call):
    strips, tok_dev, width = qa.shape
    heads = width // LANES
    features = call.shape[2]
    like = jax.ShapeDtypeStruct(qa.shape, BF16)
    half = jax.ShapeDtypeStruct((strips // 2, tok_dev, features), BF16)
    return pl.pallas_call(
        functools.partial(attn_fwd_body, heads),
        out_shape=(like, like, half, half, jax.ShapeDtypeStruct(attn_out.shape, BF16)),
        in_specs=[SMEM, SMEM] + [VMEM] * 5 + [ANY] * 2,
        out_specs=(VMEM,) * 5,
        scratch_shapes=[
            pltpu.SMEM((2, image_len.shape[0] + 1), jnp.int32),
            pltpu.VMEM((heads, strips * WIN, LANES), F32),
            pltpu.VMEM(qa.shape, BF16),
            pltpu.VMEM(call.shape, BF16),
            pltpu.VMEM(call.shape, BF16),
            pltpu.VMEM((width, features), BF16),
            pltpu.VMEM((width, features), F32),
            pltpu.SemaphoreType.DMA((2,)),
        ],
        compiler_params=pltpu.CompilerParams(vmem_limit_bytes=56 << 20),
        cost_estimate=pl.CostEstimate(flops=8 * 10**9, bytes_accessed=30 * 10**6, transcendentals=8 * 10**6),
        name="attention_forward",
    )(image_len, image_group, qa, ka, va, do, attn_out, mlp_part, call)


def attn_bwd_body(
    heads, len_ref, group_ref, qb, ka, va, dob, uq, uk, gq, gk,
    d_qkv, gain_grad, seg, k_turned, dq_turned, dk_acc, dv_acc, dq, dk, dv,
):
    strips, tok_dev = qb.shape[0], qb.shape[1]
    count = find_segments(len_ref, group_ref, seg, strips, tok_dev)
    zero = jnp.zeros((), BF16)

    def products(h, at_q, at_k, q_mask, k_turned_h):
        q = tile(qb, at_q, h)
        d_out = jnp.where(q_mask, tile(dob, at_q, h), zero)
        weights = jnp.exp2(nt(tile(ka, at_k, h), q))
        d_weights = nt(tile(va, at_k, h), d_out)
        d_scores = (weights * d_weights).astype(BF16)
        return nn(k_turned_h, d_scores), nn(d_scores, q), nn(weights.astype(BF16), d_out)

    def turned(h, at_k, mask):
        return jnp.where(mask, tile(ka, at_k, h), zero).T[:DH]

    def segment(index, _):
        start, end = seg[0, index], seg[1, index]
        first = (start // 16) * 16
        windows = (end - first + WIN - 1) // WIN

        @pl.when(windows == 1)
        def _():
            at, low, high = window(start, end, first, 0, tok_dev)
            mask = row_mask(low, high, strips)
            half = row_mask(low, high, strips, DH)
            for h in range(heads):
                dq_t, dk_new, dv_new = products(h, at, at, mask, turned(h, at, mask))
                put_tile(dq, at, h, half, dq_t.T, DH)
                put_tile(dk, at, h, mask, dk_new)
                put_tile(dv, at, h, mask, dv_new)

        @pl.when(windows > 1)
        def _():
            def clear(i, _):
                for h in range(heads):
                    dq_turned[h, i] = jnp.zeros(dq_turned.shape[2:], F32)
                return 0

            lax.fori_loop(0, windows, clear, 0)

            def k_window(k, _):
                at_k, low_k, high_k = window(start, end, first, k, tok_dev)
                mask_k = row_mask(low_k, high_k, strips)
                for h in range(heads):
                    k_turned[h] = turned(h, at_k, mask_k)
                dk_acc[...] = jnp.zeros_like(dk_acc)
                dv_acc[...] = jnp.zeros_like(dv_acc)

                def q_window(i, _):
                    at_q, low_q, high_q = window(start, end, first, i, tok_dev)
                    mask_q = row_mask(low_q, high_q, strips)
                    for h in range(heads):
                        dq_t, dk_new, dv_new = products(h, at_q, at_k, mask_q, k_turned[h])
                        dq_turned[h, i] += dq_t
                        dk_acc[h] += dk_new
                        dv_acc[h] += dv_new
                    return 0

                lax.fori_loop(0, windows, q_window, 0)
                for h in range(heads):
                    put_tile(dk, at_k, h, mask_k, dk_acc[h])
                    put_tile(dv, at_k, h, mask_k, dv_acc[h])
                return 0

            lax.fori_loop(0, windows, k_window, 0)

            def q_out(i, _):
                at_q, low_q, high_q = window(start, end, first, i, tok_dev)
                half = row_mask(low_q, high_q, strips, DH)
                for h in range(heads):
                    put_tile(dq, at_q, h, half, dq_turned[h, i].T, DH)
                return 0

            lax.fori_loop(0, windows, q_out, 0)

        return 0

    lax.fori_loop(0, count, segment, 0)

    rows = strips * WIN
    lane = lax.broadcasted_iota(jnp.int32, (rows, LANES), 1)
    left = lane < DH

    def norm_back(d_rows, u_ref, gain, at, h):
        u = tile(u_ref, at, h).astype(F32)
        rstd = pltpu.roll(u, DH, 1)
        d_rows = jnp.where(left, d_rows, 0.0)
        scaled = d_rows * gain
        mean = jnp.sum(scaled, axis=-1, keepdims=True) * (1.0 / DH)
        mean_u = jnp.sum(scaled * u, axis=-1, keepdims=True) * (1.0 / DH)
        return (scaled - mean - u * mean_u) * rstd, jnp.sum(d_rows * u, axis=0, keepdims=True)

    gain_grad[...] = jnp.zeros_like(gain_grad)

    def chunk(i, _):
        at = pl.multiple_of(i * WIN, WIN)
        parts = []
        for h in range(heads):
            cols = slice(h * LANES, (h + 1) * LANES)
            d_q, g_q = norm_back(tile(dq, at, h), uq, gq[:, cols], at, h)
            d_k, g_k = norm_back(tile(dk, at, h) * (1.0 / LOG2E), uk, gk[:, cols], at, h)
            gain_grad[0:1, cols] += g_q * DH ** (-0.5)
            gain_grad[1:2, cols] += g_k
            parts += [d_q, d_k, tile(dv, at, h)]
        if len(parts) % 2:
            parts.append(jnp.zeros_like(parts[0]))
        for b in range(len(parts) // 2):
            block = jnp.where(left, parts[2 * b], pltpu.roll(parts[2 * b + 1], DH, 1))
            d_qkv[:, pl.ds(at, WIN), b * LANES : (b + 1) * LANES] = block.astype(BF16).reshape(strips, WIN, LANES)
        return 0

    lax.fori_loop(0, tok_dev // WIN, chunk, 0)


def attn_bwd(image_len, image_group, qb, ka, va, dob, uq, uk, gq, gk):
    strips, tok_dev, width = qb.shape
    heads = width // LANES
    blocks = (3 * heads + 1) // 2
    rows = strips * WIN
    windows = tok_dev // WIN + 1
    full = pltpu.VMEM((strips, tok_dev, width), F32)
    return pl.pallas_call(
        functools.partial(attn_bwd_body, heads),
        out_shape=(
            jax.ShapeDtypeStruct((strips, tok_dev, blocks * LANES), BF16),
            jax.ShapeDtypeStruct((8, width), F32),
        ),
        in_specs=[SMEM, SMEM] + [VMEM] * 8,
        out_specs=(VMEM, VMEM),
        scratch_shapes=[
            pltpu.SMEM((2, image_len.shape[0] + 1), jnp.int32),
            pltpu.VMEM((heads, DH, rows), BF16),
            pltpu.VMEM((heads, windows, DH, rows), F32),
            pltpu.VMEM((heads, rows, LANES), F32),
            pltpu.VMEM((heads, rows, LANES), F32),
            full, full, full,
        ],
        compiler_params=pltpu.CompilerParams(vmem_limit_bytes=56 << 20),
        cost_estimate=pl.CostEstimate(flops=16 * 10**9, bytes_accessed=30 * 10**6, transcendentals=8 * 10**6),
        name="attention_backward",
    )(image_len, image_group, qb, ka, va, dob, uq, uk, gq, gk)


CHUNKS = 4


def remote(src, dst, send, recv, device):
    return pltpu.make_async_remote_copy(
        src_ref=src, dst_ref=dst, send_sem=send, recv_sem=recv, device_id=device, device_id_type=pl.DeviceIdType.MESH
    )


def front_body(
    heads, tokens, cot, ln_gain, qkv_weight, gq, gk, attn_out, mlp_in, mlp_bias, mlp_out,
    qa_out, ka_out, va_out, do_out, uq_out, uk_out, mlp_part_out, dn_part_out, nall_out, call_out,
    g_in_out, g_out_out, rows_out,
    both, wide, narrow, qkv_pad, mlp_out_t, mlp_in_t, attn_out_t, g_in, g_out,
    send_sem, recv_sem, save_sem,
):
    batch, me = lax.axis_index("batch"), lax.axis_index("tensor")
    sibling = me + 1 - 2 * (me % 2)
    across = (me + 2) % 4
    chip, far_chip = me // 2, 1 - me // 2
    tok_dev = tokens.shape[0]
    step = tok_dev // CHUNKS
    rows = 2 * step
    features = tokens.shape[1]
    heads_wide = heads * LANES

    def rows_of(c):
        return pl.ds(pl.multiple_of(c * step, step), step)

    def move(kind, route, c, strip, to):
        part = both.at[kind, strip, rows_of(c)]
        return remote(part, part, send_sem.at[kind, route, c], recv_sem.at[kind, route, c], (batch, to))

    barrier = pltpu.get_barrier_semaphore()
    for other in (sibling, across):
        pl.semaphore_signal(barrier, inc=1, device_id=(batch, other), device_id_type=pl.DeviceIdType.MESH)
    gain = ln_gain[...].astype(F32)

    def norm_chunk(c):
        both[0, me, rows_of(c)] = cot[rows_of(c)]
        x = tokens[rows_of(c)].astype(F32)
        centred = x - jnp.mean(x, axis=-1, keepdims=True)
        variance = jnp.mean(centred * centred, axis=-1, keepdims=True)
        both[1, me, rows_of(c)] = (centred * lax.rsqrt(variance + epsilon) * gain).astype(BF16)

    norm_chunk(0)
    pl.semaphore_wait(barrier, 2)

    def first_sends(c, _):
        for kind in range(2):
            move(kind, 1, c, me, across).start()
            move(kind, 0, c, me, sibling).start()

        @pl.when(c + 1 < CHUNKS)
        def _():
            norm_chunk(c + 1)

        return 0

    lax.fori_loop(0, CHUNKS, first_sends, 0)

    g_in[...] = jnp.zeros_like(g_in)
    g_out[...] = jnp.zeros_like(g_out)
    rows_out[...] = jnp.zeros_like(rows_out)
    total = jnp.zeros((1, features), F32)
    for c in range(CHUNKS):
        total += jnp.sum(cot[c * step : (c + 1) * step].astype(F32), axis=0, keepdims=True)
    rows_out[1:2, :] = total
    width = qkv_weight.shape[1]
    qkv_pad[:, width // LANES * LANES :] = jnp.zeros((features, qkv_pad.shape[1] - width // LANES * LANES), BF16)
    qkv_pad[:, :width] = qkv_weight[...]
    mlp_out_t[...] = mlp_out[...].T
    mlp_in_t[...] = mlp_in[...].T
    for h in range(heads):
        part = attn_out[h * DH : (h + 1) * DH, :]
        attn_out_t[:, h * LANES : (h + 1) * LANES] = jnp.concatenate([part, jnp.zeros_like(part)], axis=0).T

    lane = lax.broadcasted_iota(jnp.int32, (rows, LANES), 1)
    left = lane < DH
    bias = mlp_bias[...].astype(F32)

    def saves(c, at_chip):
        strips = pl.ds(2 * at_chip, 2)
        where = rows_of(c)
        index = at_chip * CHUNKS + c
        pairs = [(narrow.at[a, strips, where], ref.at[strips, where]) for a, ref in enumerate(
            (qa_out, ka_out, va_out, do_out, uq_out, uk_out))]
        pairs += [(wide.at[a, strips, where], ref.at[strips, where]) for a, ref in enumerate(
            (mlp_part_out, dn_part_out))]
        pairs += [(both.at[1, strips, where], nall_out.at[strips, where]), (both.at[0, strips, where], call_out.at[strips, where])]
        return [pltpu.make_async_copy(a, b, save_sem.at[n, index]) for n, (a, b) in enumerate(pairs)]

    def unit(i, _):
        far = i >= CHUNKS
        c = i % CHUNKS
        at_chip = jnp.where(far, far_chip, chip)

        @pl.when(jnp.logical_not(far))
        def _():
            for kind in range(2):
                move(kind, 0, c, sibling, sibling).wait_recv()

        def pass_on(k):
            for kind in range(2):
                move(kind, 1, k, across, across).wait_recv()
                move(kind, 2, k, across, sibling).start()

        @pl.when(i == CHUNKS - 1)
        def _():
            pass_on(0)

        @pl.when(i == CHUNKS)
        def _():
            pass_on(1)

        @pl.when(i > CHUNKS + 1)
        def _():
            pass_on(c)

        @pl.when(far)
        def _():
            for kind in range(2):
                move(kind, 2, c, across + 1 - 2 * (across % 2), sibling).wait_recv()

        strips = pl.ds(2 * at_chip, 2)
        where = rows_of(c)
        n = both[1, strips, where].reshape(rows, features)
        d = both[0, strips, where].reshape(rows, features)

        def save(ref, a, h, value):
            ref[a, strips, where, h * LANES : (h + 1) * LANES] = value.astype(BF16).reshape(2, step, LANES)

        qkv = nn(n, qkv_pad[...])

        def part(p):
            block = qkv[:, p // 2 * LANES : p // 2 * LANES + LANES]
            return pltpu.roll(block, DH, 1) if p % 2 else block

        def unit_norm(x):
            x = jnp.where(left, x, 0.0)
            centred = jnp.where(left, x - jnp.sum(x, axis=-1, keepdims=True) * (1.0 / DH), 0.0)
            rstd = lax.rsqrt(jnp.sum(centred * centred, axis=-1, keepdims=True) * (1.0 / DH) + epsilon)
            return centred * rstd, rstd

        for h in range(heads):
            cols = slice(h * LANES, (h + 1) * LANES)
            u, rstd = unit_norm(part(3 * h))
            save(narrow, 0, h, u * gq[:, cols])
            save(narrow, 4, h, jnp.where(left, u, rstd))
            u, rstd = unit_norm(part(3 * h + 1))
            save(narrow, 1, h, jnp.where(left, u * gk[:, cols], 1.0))
            save(narrow, 5, h, jnp.where(left, u, rstd))
            save(narrow, 2, h, jnp.where(left, part(3 * h + 2), 1.0))
        narrow[3, strips, where] = nn(d, attn_out_t[...]).astype(BF16).reshape(2, step, heads_wide)

        hidden = nn(n, mlp_in[...]) + bias
        cdf = 0.5 + 0.5 * lax.erf(hidden * 0.7071067811865476)
        act = (hidden * cdf).astype(BF16)
        slope = cdf + hidden * (0.3989422804014327 * jnp.exp(hidden * hidden * -0.5))
        wide[0, strips, where] = nn(act, mlp_out[...]).astype(BF16).reshape(2, step, features)
        d_hidden = nn(d, mlp_out_t[...]) * slope
        d_low = d_hidden.astype(BF16)
        rows_out[0:1, :] += jnp.sum(d_low.astype(F32), axis=0, keepdims=True)
        wide[1, strips, where] = nn(d_low, mlp_in_t[...]).astype(BF16).reshape(2, step, features)
        g_out[...] += tn(act, d)
        g_in[...] += tn(n, d_low)
        for copy in saves(c, at_chip):
            copy.start()
        return 0

    lax.fori_loop(0, 2 * CHUNKS, unit, 0)

    g_in_out[...] = g_in[...].astype(BF16)
    g_out_out[...] = g_out[...].astype(BF16)

    def finish(i, _):
        for copy in saves(i % CHUNKS, i // CHUNKS):
            copy.wait()
        return 0

    lax.fori_loop(0, 2 * CHUNKS, finish, 0)

    def sent(c, _):
        for kind in range(2):
            move(kind, 0, c, me, sibling).wait_send()
            move(kind, 1, c, me, across).wait_send()
            move(kind, 2, c, across, sibling).wait_send()
        return 0

    lax.fori_loop(0, CHUNKS, sent, 0)


def front(strips, tokens, cot, ln_gain, qkv_weight, gq, gk, attn_out, mlp_in, mlp_bias, mlp_out):
    tok_dev, features = tokens.shape
    width = gq.shape[1]
    heads = width // LANES
    hidden = mlp_in.shape[1]
    blocks = (3 * heads + 1) // 2
    like = jax.ShapeDtypeStruct((strips, tok_dev, width), BF16)
    rows = jax.ShapeDtypeStruct((strips, tok_dev, features), BF16)
    return pl.pallas_call(
        functools.partial(front_body, heads),
        out_shape=(like,) * 6 + (rows,) * 4 + (
            jax.ShapeDtypeStruct((features, hidden), BF16),
            jax.ShapeDtypeStruct((hidden, features), BF16),
            jax.ShapeDtypeStruct((8, features), F32),
        ),
        in_specs=[VMEM] * 10,
        out_specs=(ANY,) * 10 + (VMEM,) * 3,
        scratch_shapes=[
            pltpu.VMEM((2, strips, tok_dev, features), BF16),
            pltpu.VMEM((2, strips, tok_dev, features), BF16),
            pltpu.VMEM((6, strips, tok_dev, width), BF16),
            pltpu.VMEM((features, blocks * LANES), BF16),
            pltpu.VMEM((features, hidden), BF16),
            pltpu.VMEM((hidden, features), BF16),
            pltpu.VMEM((features, width), BF16),
            pltpu.VMEM((features, hidden), F32),
            pltpu.VMEM((hidden, features), F32),
            pltpu.SemaphoreType.DMA((2, 3, CHUNKS)),
            pltpu.SemaphoreType.DMA((2, 3, CHUNKS)),
            pltpu.SemaphoreType.DMA((10, 2 * CHUNKS)),
        ],
        compiler_params=pltpu.CompilerParams(collective_id=0, has_side_effects=True, vmem_limit_bytes=60 << 20),
        name="gather_and_project",
    )(tokens, cot, ln_gain, qkv_weight, gq, gk, attn_out, mlp_in, mlp_bias, mlp_out)


def layer_norm(inputs, gain):
    row_mean = jnp.mean(inputs, axis=-1, keepdims=True)
    centred = inputs - row_mean
    variance = jnp.mean(centred * centred, axis=-1, keepdims=True)
    return centred * lax.rsqrt(variance + epsilon) * gain


SIBLINGS = [(0, 1), (1, 0), (2, 3), (3, 2)]
ACROSS = [(0, 2), (1, 3), (2, 0), (3, 1)]


def on_device(
    tokens, out_cotangent, ln_gain, qkv_weight, q_gain, k_gain, attn_out,
    mlp_in, mlp_bias, mlp_out, out_bias, image_len, image_group,
):
    tok_dev, features = tokens.shape
    strips = lax.axis_size("tensor")
    cap = tok_dev * strips
    heads = q_gain.shape[0] // DH
    head_width = heads * DH
    qkv_cols = qkv_weight.shape[1]

    def pad_gain(g, factor):
        g = g.astype(F32).reshape(heads, DH) * factor
        return jnp.concatenate([g, jnp.zeros_like(g)], axis=-1).reshape(1, heads * LANES)

    scale = DH ** (-0.5)
    gq, gk = pad_gain(q_gain, scale), pad_gain(k_gain, 1.0)
    (qa, ka, va, do, uq, uk, mlp_part, dn_part, nall, call, g_in, g_out, rows_out) = front(
        strips, tokens, out_cotangent, ln_gain.reshape(1, -1), qkv_weight, gq * LOG2E, gk,
        attn_out, mlp_in, mlp_bias.reshape(1, -1), mlp_out,
    )

    def over_batch(grad):
        return lax.psum(grad.astype(BF16), "batch").astype(F32)

    mlp_in_grad, mlp_out_grad, mlp_bias_grad = over_batch(g_in), over_batch(g_out), over_batch(rows_out[0])
    qb, dob, give, keep, attn_grad = attn_fwd(image_len, image_group, qa, ka, va, do, attn_out, mlp_part, call)
    got = lax.ppermute(give, "tensor", SIBLINGS)
    mine = (keep.astype(F32) + got.astype(F32)).astype(BF16)
    got = lax.ppermute(mine[0], "tensor", ACROSS)
    output = (
        tokens.astype(F32) + mine[1].astype(F32) + got.astype(F32) + out_bias.astype(F32)
    ).astype(BF16)

    d_qkv, gain_grad = attn_bwd(image_len, image_group, qb, ka, va, dob, uq, uk, gq, gk)
    gain_grad = gain_grad.reshape(8, heads, LANES)[:, :, :DH].reshape(8, head_width)
    d_qkv = d_qkv.reshape(cap, -1)[:, :qkv_cols]
    qkv_grad = tn(nall.reshape(cap, features), d_qkv)
    d_normed = lax.psum_scatter(
        (nt(d_qkv, qkv_weight) + dn_part.reshape(cap, features).astype(F32)).astype(BF16),
        "tensor", scatter_dimension=0, tiled=True,
    )
    _, ln_pull = jax.vjp(layer_norm, tokens.astype(F32), ln_gain.astype(F32))
    d_x, ln_gain_part = ln_pull(d_normed.astype(F32))
    input_grad = (out_cotangent.astype(F32) + d_x).astype(BF16)
    ln_gain_grad, out_bias_grad = lax.psum((ln_gain_part, rows_out[1]), ("batch", "tensor"))
    return (
        output,
        input_grad,
        ln_gain_grad,
        over_batch(qkv_grad),
        over_batch(gain_grad[0]),
        over_batch(gain_grad[1]),
        over_batch(attn_grad),
        mlp_in_grad,
        mlp_bias_grad,
        mlp_out_grad,
        out_bias_grad,
    )


def solution(mesh):
    rows, cols, first = P(("batch", "tensor"), None), P(None, "tensor"), P("tensor", None)
    return jax.shard_map(
        on_device,
        mesh=mesh,
        in_specs=(rows, rows, P(), cols, P("tensor"), P("tensor"), first, cols, P("tensor"), first, P(), P(), P()),
        out_specs=(rows, rows, P(), cols, P("tensor"), P("tensor"), first, cols, P("tensor"), first, P()),
        check_vma=False,
    )
```

```python
import functools

import jax
import jax.numpy as jnp
from jax import lax
from jax.experimental import pallas as pl
from jax.experimental.pallas import tpu as pltpu
from jax.sharding import PartitionSpec as P

DH = 64
LANES = 128
WIN = 64
LOG2E = 1.4426950408889634
epsilon = 1e-06
F32 = jnp.float32
BF16 = jnp.bfloat16
VMEM = pl.BlockSpec(memory_space=pltpu.VMEM)
SMEM = pl.BlockSpec(memory_space=pltpu.SMEM)
ANY = pl.BlockSpec(memory_space=pl.ANY)


def nn(left, right):
    return lax.dot_general(left, right, (((1,), (0,)), ((), ())), preferred_element_type=F32)


def nt(left, right):
    return lax.dot_general(left, right, (((1,), (1,)), ((), ())), preferred_element_type=F32)


def tn(left, right):
    return lax.dot_general(left, right, (((0,), (0,)), ((), ())), preferred_element_type=F32)


def find_segments(len_ref, group_ref, seg_ref, strips, tok_dev):
    group = lax.axis_index("batch")

    def entry(i, carry):
        count, run = carry
        rows = jnp.where(group_ref[i] == group, len_ref[i] // strips, 0)

        @pl.when(rows > 0)
        def _():
            seg_ref[0, count] = run
            seg_ref[1, count] = run + rows

        return count + jnp.where(rows > 0, 1, 0), run + rows

    count, run = lax.fori_loop(0, len_ref.shape[0], entry, (jnp.int32(0), jnp.int32(0)))

    @pl.when(run < tok_dev)
    def _():
        seg_ref[0, count] = run
        seg_ref[1, count] = tok_dev

    return count + jnp.where(run < tok_dev, 1, 0)


def window(start, end, first, i, tok_dev):
    nominal = first + WIN * i
    at = pl.multiple_of(jnp.minimum(nominal, tok_dev - WIN), 16)
    return at, jnp.maximum(start, nominal) - at, jnp.minimum(end, nominal + WIN) - at


def row_mask(low, high, strips, width=LANES):
    j = lax.broadcasted_iota(jnp.int32, (strips, WIN, width), 1).reshape(strips * WIN, width)
    return (j >= low) & (j < high)


def tile(ref, at, h):
    strips = ref.shape[0]
    return ref[:, pl.ds(at, WIN), h * LANES : (h + 1) * LANES].reshape(strips * WIN, LANES)


def put_tile(ref, at, h, mask, value, width=LANES):
    strips = ref.shape[0]
    where = (slice(None), pl.ds(at, WIN), slice(h * LANES, h * LANES + width))
    old = ref[where].reshape(strips * WIN, width)
    ref[where] = jnp.where(mask, value.astype(ref.dtype), old).reshape(strips, WIN, width)


def attn_fwd_body(
    heads, len_ref, group_ref, qa, ka, va, do, attn_out, mlp_part_hbm, call_hbm,
    qb, dob, give, keep, attn_t, seg, acc, ho, mlp_part, call, out_pad, grad_acc, sems,
):
    strips, tok_dev = qa.shape[0], qa.shape[1]
    loads = [pltpu.make_async_copy(mlp_part_hbm, mlp_part, sems.at[0]), pltpu.make_async_copy(call_hbm, call, sems.at[1])]
    for load in loads:
        load.start()
    count = find_segments(len_ref, group_ref, seg, strips, tok_dev)
    lane = lax.broadcasted_iota(jnp.int32, (strips * WIN, LANES), 1)
    left = lane < DH

    def finish(h, at, low, high, total):
        mask = row_mask(low, high, strips)
        rows_sum = jnp.where(left, pltpu.roll(total, DH, 1), total)
        out = jnp.where(left, total / rows_sum, 0.0)
        log_sum = jnp.log2(rows_sum)
        d_out = tile(do, at, h).astype(F32)
        out_low = out.astype(BF16)
        delta = jnp.sum(out * d_out, axis=-1, keepdims=True)
        log_hi = log_sum.astype(BF16).astype(F32)
        delta_hi = delta.astype(BF16).astype(F32)
        q = tile(qa, at, h).astype(F32)
        q = jnp.where(lane == DH, -log_hi, jnp.where(lane == DH + 1, log_hi - log_sum, q))
        d_out = jnp.where(lane == DH, -delta_hi, jnp.where(lane == DH + 1, delta_hi - delta, d_out))
        put_tile(ho, at, h, mask, out_low)
        put_tile(qb, at, h, mask, q)
        put_tile(dob, at, h, mask, d_out)

    def product(h, at_q, at_k, k_mask):
        scores = nt(tile(qa, at_q, h), tile(ka, at_k, h))
        weights = jnp.exp2(scores).astype(BF16)
        return nn(weights, jnp.where(k_mask, tile(va, at_k, h), jnp.zeros((), BF16)))

    def segment(index, _):
        start, end = seg[0, index], seg[1, index]
        first = (start // 16) * 16
        windows = (end - first + WIN - 1) // WIN

        @pl.when(windows == 1)
        def _():
            at, low, high = window(start, end, first, 0, tok_dev)
            mask = row_mask(low, high, strips)
            for h in range(heads):
                finish(h, at, low, high, product(h, at, at, mask))

        @pl.when(windows > 1)
        def _():
            def q_window(i, _):
                at_q, low_q, high_q = window(start, end, first, i, tok_dev)
                acc[...] = jnp.zeros_like(acc)

                def k_window(k, _):
                    at_k, low_k, high_k = window(start, end, first, k, tok_dev)
                    mask = row_mask(low_k, high_k, strips)
                    for h in range(heads):
                        acc[h] += product(h, at_q, at_k, mask)
                    return 0

                lax.fori_loop(0, windows, k_window, 0)
                for h in range(heads):
                    finish(h, at_q, low_q, high_q, acc[h])
                return 0

            lax.fori_loop(0, windows, q_window, 0)

        return 0

    lax.fori_loop(0, count, segment, 0)

    for h in range(heads):
        out_pad[h * LANES : h * LANES + DH, :] = attn_out[h * DH : (h + 1) * DH, :]
        out_pad[h * LANES + DH : (h + 1) * LANES, :] = jnp.zeros((DH, out_pad.shape[1]), BF16)
    for load in loads:
        load.wait()
    me = lax.axis_index("tensor")
    rows = 256
    per_strip = tok_dev // rows
    grad_acc[...] = jnp.zeros_like(grad_acc)

    def project(i, _):
        strip = i // per_strip
        at = pl.ds(pl.multiple_of(i % per_strip * rows, rows), rows)
        heads_rows = ho[strip, at]
        out = (nn(heads_rows, out_pad[...]) + mlp_part[strip, at].astype(F32)).astype(BF16)
        own = jnp.where(strip // 2 == me // 2, 1, 0)

        @pl.when(strip % 2 == me % 2)
        def _():
            keep[own, at] = out

        @pl.when(strip % 2 != me % 2)
        def _():
            give[own, at] = out

        grad_acc[...] += tn(heads_rows, call[strip, at])
        return 0

    lax.fori_loop(0, strips * per_strip, project, 0)
    attn_t[...] = grad_acc[...].T.astype(BF16)


def attn_fwd(image_len, image_group, qa, ka, va, do, attn_out, mlp_part, call):
    strips, tok_dev, width = qa.shape
    heads = width // LANES
    features = call.shape[2]
    like = jax.ShapeDtypeStruct(qa.shape, BF16)
    half = jax.ShapeDtypeStruct((strips // 2, tok_dev, features), BF16)
    return pl.pallas_call(
        functools.partial(attn_fwd_body, heads),
        out_shape=(like, like, half, half, jax.ShapeDtypeStruct((features, width), BF16)),
        in_specs=[SMEM, SMEM] + [VMEM] * 5 + [ANY] * 2,
        out_specs=(VMEM,) * 5,
        scratch_shapes=[
            pltpu.SMEM((2, image_len.shape[0] + 1), jnp.int32),
            pltpu.VMEM((heads, strips * WIN, LANES), F32),
            pltpu.VMEM(qa.shape, BF16),
            pltpu.VMEM(call.shape, BF16),
            pltpu.VMEM(call.shape, BF16),
            pltpu.VMEM((width, features), BF16),
            pltpu.VMEM((width, features), F32),
            pltpu.SemaphoreType.DMA((2,)),
        ],
        compiler_params=pltpu.CompilerParams(vmem_limit_bytes=56 << 20),
        cost_estimate=pl.CostEstimate(flops=8 * 10**9, bytes_accessed=30 * 10**6, transcendentals=8 * 10**6),
        name="attention_forward",
    )(image_len, image_group, qa, ka, va, do, attn_out, mlp_part, call)


def attn_bwd_body(
    heads, len_ref, group_ref, qb, ka, va, dob, uq, uk, gq, gk,
    d_qkv, gain_grad, seg, k_turned, dq_turned, dk_acc, dv_acc, dq, dk, dv,
):
    strips, tok_dev = qb.shape[0], qb.shape[1]
    count = find_segments(len_ref, group_ref, seg, strips, tok_dev)
    zero = jnp.zeros((), BF16)

    def products(h, at_q, at_k, q_mask, k_turned_h):
        q = tile(qb, at_q, h)
        d_out = jnp.where(q_mask, tile(dob, at_q, h), zero)
        weights = jnp.exp2(nt(tile(ka, at_k, h), q))
        d_weights = nt(tile(va, at_k, h), d_out)
        d_scores = (weights * d_weights).astype(BF16)
        return nn(k_turned_h, d_scores), nn(d_scores, q), nn(weights.astype(BF16), d_out)

    def turned(h, at_k, mask):
        return jnp.where(mask, tile(ka, at_k, h), zero).T[:DH]

    def segment(index, _):
        start, end = seg[0, index], seg[1, index]
        first = (start // 16) * 16
        windows = (end - first + WIN - 1) // WIN

        @pl.when(windows == 1)
        def _():
            at, low, high = window(start, end, first, 0, tok_dev)
            mask = row_mask(low, high, strips)
            half = row_mask(low, high, strips, DH)
            for h in range(heads):
                dq_t, dk_new, dv_new = products(h, at, at, mask, turned(h, at, mask))
                put_tile(dq, at, h, half, dq_t.T, DH)
                put_tile(dk, at, h, mask, dk_new)
                put_tile(dv, at, h, mask, dv_new)

        @pl.when(windows > 1)
        def _():
            def clear(i, _):
                for h in range(heads):
                    dq_turned[h, i] = jnp.zeros(dq_turned.shape[2:], F32)
                return 0

            lax.fori_loop(0, windows, clear, 0)

            def k_window(k, _):
                at_k, low_k, high_k = window(start, end, first, k, tok_dev)
                mask_k = row_mask(low_k, high_k, strips)
                for h in range(heads):
                    k_turned[h] = turned(h, at_k, mask_k)
                dk_acc[...] = jnp.zeros_like(dk_acc)
                dv_acc[...] = jnp.zeros_like(dv_acc)

                def q_window(i, _):
                    at_q, low_q, high_q = window(start, end, first, i, tok_dev)
                    mask_q = row_mask(low_q, high_q, strips)
                    for h in range(heads):
                        dq_t, dk_new, dv_new = products(h, at_q, at_k, mask_q, k_turned[h])
                        dq_turned[h, i] += dq_t
                        dk_acc[h] += dk_new
                        dv_acc[h] += dv_new
                    return 0

                lax.fori_loop(0, windows, q_window, 0)
                for h in range(heads):
                    put_tile(dk, at_k, h, mask_k, dk_acc[h])
                    put_tile(dv, at_k, h, mask_k, dv_acc[h])
                return 0

            lax.fori_loop(0, windows, k_window, 0)

            def q_out(i, _):
                at_q, low_q, high_q = window(start, end, first, i, tok_dev)
                half = row_mask(low_q, high_q, strips, DH)
                for h in range(heads):
                    put_tile(dq, at_q, h, half, dq_turned[h, i].T, DH)
                return 0

            lax.fori_loop(0, windows, q_out, 0)

        return 0

    lax.fori_loop(0, count, segment, 0)

    rows = strips * WIN
    lane = lax.broadcasted_iota(jnp.int32, (rows, LANES), 1)
    left = lane < DH

    def norm_back(d_rows, u_ref, gain, at, h):
        u = tile(u_ref, at, h).astype(F32)
        rstd = pltpu.roll(u, DH, 1)
        d_rows = jnp.where(left, d_rows, 0.0)
        scaled = d_rows * gain
        mean = jnp.sum(scaled, axis=-1, keepdims=True) * (1.0 / DH)
        mean_u = jnp.sum(scaled * u, axis=-1, keepdims=True) * (1.0 / DH)
        return (scaled - mean - u * mean_u) * rstd, jnp.sum(d_rows * u, axis=0, keepdims=True)

    gain_grad[...] = jnp.zeros_like(gain_grad)

    def chunk(i, _):
        at = pl.multiple_of(i * WIN, WIN)
        parts = []
        for h in range(heads):
            cols = slice(h * LANES, (h + 1) * LANES)
            d_q, g_q = norm_back(tile(dq, at, h), uq, gq[:, cols], at, h)
            d_k, g_k = norm_back(tile(dk, at, h) * (1.0 / LOG2E), uk, gk[:, cols], at, h)
            gain_grad[0:1, cols] += g_q * DH ** (-0.5)
            gain_grad[1:2, cols] += g_k
            parts += [d_q, d_k, tile(dv, at, h)]
        if len(parts) % 2:
            parts.append(jnp.zeros_like(parts[0]))
        for b in range(len(parts) // 2):
            block = jnp.where(left, parts[2 * b], pltpu.roll(parts[2 * b + 1], DH, 1))
            d_qkv[:, pl.ds(at, WIN), b * LANES : (b + 1) * LANES] = block.astype(BF16).reshape(strips, WIN, LANES)
        return 0

    lax.fori_loop(0, tok_dev // WIN, chunk, 0)


def attn_bwd(image_len, image_group, qb, ka, va, dob, uq, uk, gq, gk):
    strips, tok_dev, width = qb.shape
    heads = width // LANES
    blocks = (3 * heads + 1) // 2
    rows = strips * WIN
    windows = tok_dev // WIN + 1
    full = pltpu.VMEM((strips, tok_dev, width), F32)
    return pl.pallas_call(
        functools.partial(attn_bwd_body, heads),
        out_shape=(
            jax.ShapeDtypeStruct((strips, tok_dev, blocks * LANES), BF16),
            jax.ShapeDtypeStruct((8, width), F32),
        ),
        in_specs=[SMEM, SMEM] + [VMEM] * 8,
        out_specs=(VMEM, VMEM),
        scratch_shapes=[
            pltpu.SMEM((2, image_len.shape[0] + 1), jnp.int32),
            pltpu.VMEM((heads, DH, rows), BF16),
            pltpu.VMEM((heads, windows, DH, rows), F32),
            pltpu.VMEM((heads, rows, LANES), F32),
            pltpu.VMEM((heads, rows, LANES), F32),
            full, full, full,
        ],
        compiler_params=pltpu.CompilerParams(vmem_limit_bytes=56 << 20),
        cost_estimate=pl.CostEstimate(flops=16 * 10**9, bytes_accessed=30 * 10**6, transcendentals=8 * 10**6),
        name="attention_backward",
    )(image_len, image_group, qb, ka, va, dob, uq, uk, gq, gk)


CHUNKS = 4


def remote(src, dst, send, recv, device):
    return pltpu.make_async_remote_copy(
        src_ref=src, dst_ref=dst, send_sem=send, recv_sem=recv, device_id=device, device_id_type=pl.DeviceIdType.MESH
    )


def front_body(
    heads, tokens, cot, ln_gain, qkv_weight, gq, gk, attn_out, mlp_in, mlp_bias, mlp_out,
    qa_out, ka_out, va_out, do_out, uq_out, uk_out, mlp_part_out, dn_part_out, nall_out, call_out,
    *rest,
):
    (rows_out, both, wide, narrow, qkv_pad, mlp_out_t, mlp_in_t, attn_out_t, g_in, g_out,
     send_sem, recv_sem, save_sem) = rest[-13:]
    grad_outs = rest[:-13]
    batch, me = lax.axis_index("batch"), lax.axis_index("tensor")
    sibling = me + 1 - 2 * (me % 2)
    across = (me + 2) % 4
    chip, far_chip = me // 2, 1 - me // 2
    tok_dev = tokens.shape[0]
    step = tok_dev // CHUNKS
    rows = 2 * step
    features = tokens.shape[1]
    heads_wide = heads * LANES

    def rows_of(c):
        return pl.ds(pl.multiple_of(c * step, step), step)

    def move(kind, route, c, strip, to):
        part = both.at[kind, strip, rows_of(c)]
        return remote(part, part, send_sem.at[kind, route, c], recv_sem.at[kind, route, c], (batch, to))

    barrier = pltpu.get_barrier_semaphore()
    for other in (sibling, across):
        pl.semaphore_signal(barrier, inc=1, device_id=(batch, other), device_id_type=pl.DeviceIdType.MESH)
    gain = ln_gain[...].astype(F32)

    def norm_chunk(c):
        both[0, me, rows_of(c)] = cot[rows_of(c)]
        x = tokens[rows_of(c)].astype(F32)
        centred = x - jnp.mean(x, axis=-1, keepdims=True)
        variance = jnp.mean(centred * centred, axis=-1, keepdims=True)
        both[1, me, rows_of(c)] = (centred * lax.rsqrt(variance + epsilon) * gain).astype(BF16)

    norm_chunk(0)
    pl.semaphore_wait(barrier, 2)

    def first_sends(c, _):
        for kind in range(2):
            move(kind, 1, c, me, across).start()
            move(kind, 0, c, me, sibling).start()

        @pl.when(c + 1 < CHUNKS)
        def _():
            norm_chunk(c + 1)

        return 0

    lax.fori_loop(0, CHUNKS, first_sends, 0)

    g_in[...] = jnp.zeros_like(g_in)
    g_out[...] = jnp.zeros_like(g_out)
    rows_out[...] = jnp.zeros_like(rows_out)
    total = jnp.zeros((1, features), F32)
    for c in range(CHUNKS):
        total += jnp.sum(cot[c * step : (c + 1) * step].astype(F32), axis=0, keepdims=True)
    rows_out[1:2, :] = total
    width = qkv_weight.shape[1]
    qkv_pad[:, width // LANES * LANES :] = jnp.zeros((features, qkv_pad.shape[1] - width // LANES * LANES), BF16)
    qkv_pad[:, :width] = qkv_weight[...]
    mlp_out_t[...] = mlp_out[...].T
    mlp_in_t[...] = mlp_in[...].T
    for h in range(heads):
        part = attn_out[h * DH : (h + 1) * DH, :]
        attn_out_t[:, h * LANES : (h + 1) * LANES] = jnp.concatenate([part, jnp.zeros_like(part)], axis=0).T

    lane = lax.broadcasted_iota(jnp.int32, (rows, LANES), 1)
    left = lane < DH
    bias = mlp_bias[...].astype(F32)

    def saves(c, at_chip):
        strips = pl.ds(2 * at_chip, 2)
        where = rows_of(c)
        index = at_chip * CHUNKS + c
        pairs = [(narrow.at[a, strips, where], ref.at[strips, where]) for a, ref in enumerate(
            (qa_out, ka_out, va_out, do_out, uq_out, uk_out))]
        pairs += [(wide.at[a, strips, where], ref.at[strips, where]) for a, ref in enumerate(
            (mlp_part_out, dn_part_out))]
        pairs += [(both.at[1, strips, where], nall_out.at[strips, where]), (both.at[0, strips, where], call_out.at[strips, where])]
        return [pltpu.make_async_copy(a, b, save_sem.at[n, index]) for n, (a, b) in enumerate(pairs)]

    def unit(i, _):
        far = i >= CHUNKS
        c = i % CHUNKS
        at_chip = jnp.where(far, far_chip, chip)

        @pl.when(jnp.logical_not(far))
        def _():
            for kind in range(2):
                move(kind, 0, c, sibling, sibling).wait_recv()

        def pass_on(k):
            for kind in range(2):
                move(kind, 1, k, across, across).wait_recv()
                move(kind, 2, k, across, sibling).start()

        @pl.when(i == CHUNKS - 1)
        def _():
            pass_on(0)

        @pl.when(i == CHUNKS)
        def _():
            pass_on(1)

        @pl.when(i > CHUNKS + 1)
        def _():
            pass_on(c)

        @pl.when(far)
        def _():
            for kind in range(2):
                move(kind, 2, c, across + 1 - 2 * (across % 2), sibling).wait_recv()

        strips = pl.ds(2 * at_chip, 2)
        where = rows_of(c)
        n = both[1, strips, where].reshape(rows, features)
        d = both[0, strips, where].reshape(rows, features)

        def save(ref, a, h, value):
            ref[a, strips, where, h * LANES : (h + 1) * LANES] = value.astype(BF16).reshape(2, step, LANES)

        qkv = nn(n, qkv_pad[...])

        def part(p):
            block = qkv[:, p // 2 * LANES : p // 2 * LANES + LANES]
            return pltpu.roll(block, DH, 1) if p % 2 else block

        def unit_norm(x):
            x = jnp.where(left, x, 0.0)
            centred = jnp.where(left, x - jnp.sum(x, axis=-1, keepdims=True) * (1.0 / DH), 0.0)
            rstd = lax.rsqrt(jnp.sum(centred * centred, axis=-1, keepdims=True) * (1.0 / DH) + epsilon)
            return centred * rstd, rstd

        for h in range(heads):
            cols = slice(h * LANES, (h + 1) * LANES)
            u, rstd = unit_norm(part(3 * h))
            save(narrow, 0, h, u * gq[:, cols])
            save(narrow, 4, h, jnp.where(left, u, rstd))
            u, rstd = unit_norm(part(3 * h + 1))
            save(narrow, 1, h, jnp.where(left, u * gk[:, cols], 1.0))
            save(narrow, 5, h, jnp.where(left, u, rstd))
            save(narrow, 2, h, jnp.where(left, part(3 * h + 2), 1.0))
        narrow[3, strips, where] = nn(d, attn_out_t[...]).astype(BF16).reshape(2, step, heads_wide)

        hidden = nn(n, mlp_in[...]) + bias
        cdf = 0.5 + 0.5 * lax.erf(hidden * 0.7071067811865476)
        act = (hidden * cdf).astype(BF16)
        slope = cdf + hidden * (0.3989422804014327 * jnp.exp(hidden * hidden * -0.5))
        wide[0, strips, where] = nn(act, mlp_out[...]).astype(BF16).reshape(2, step, features)
        d_hidden = nn(d, mlp_out_t[...]) * slope
        d_low = d_hidden.astype(BF16)
        rows_out[0:1, :] += jnp.sum(d_low.astype(F32), axis=0, keepdims=True)
        wide[1, strips, where] = nn(d_low, mlp_in_t[...]).astype(BF16).reshape(2, step, features)
        g_out[...] += tn(act, d)
        g_in[...] += tn(n, d_low)
        for copy in saves(c, at_chip):
            copy.start()
        return 0

    lax.fori_loop(0, 2 * CHUNKS, unit, 0)

    n_lo = len(grad_outs)
    n_hi, chunk_rows = grad_outs[0].shape[0], grad_outs[0].shape[1]
    hi, lo = batch // n_lo, batch % n_lo
    per_grad = features // chunk_rows
    for o in range(n_hi * n_lo):
        source = (g_in, g_out)[o // per_grad]
        row = o % per_grad * chunk_rows
        low = source[row : row + chunk_rows, :].astype(BF16)
        at_hi = (o // n_lo - hi + n_hi) % n_hi
        at_lo = (o % n_lo - lo + n_lo) % n_lo
        for m in range(n_lo):

            @pl.when(at_lo == m)
            def _():
                grad_outs[m][at_hi] = low

    grown = g_in[...] * mlp_in[...].astype(F32)
    grown_hi = grown.astype(BF16)
    ones = jnp.ones((8, grown.shape[1]), BF16)
    rows_out[2:3, :] = (nt(ones, grown_hi) + nt(ones, (grown - grown_hi.astype(F32)).astype(BF16)))[0:1]

    def finish(i, _):
        for copy in saves(i % CHUNKS, i // CHUNKS):
            copy.wait()
        return 0

    lax.fori_loop(0, 2 * CHUNKS, finish, 0)

    def sent(c, _):
        for kind in range(2):
            move(kind, 0, c, me, sibling).wait_send()
            move(kind, 1, c, me, across).wait_send()
            move(kind, 2, c, across, sibling).wait_send()
        return 0

    lax.fori_loop(0, CHUNKS, sent, 0)


def front(strips, n_batch, tokens, cot, ln_gain, qkv_weight, gq, gk, attn_out, mlp_in, mlp_bias, mlp_out):
    tok_dev, features = tokens.shape
    width = gq.shape[1]
    heads = width // LANES
    hidden = mlp_in.shape[1]
    blocks = (3 * heads + 1) // 2
    n_hi, n_lo = levels(n_batch)
    like = jax.ShapeDtypeStruct((strips, tok_dev, width), BF16)
    rows = jax.ShapeDtypeStruct((strips, tok_dev, features), BF16)
    return pl.pallas_call(
        functools.partial(front_body, heads),
        out_shape=(like,) * 6 + (rows,) * 4 + (
            jax.ShapeDtypeStruct((n_hi, 2 * features // n_batch, features), BF16),
        ) * n_lo + (jax.ShapeDtypeStruct((8, features), F32),),
        in_specs=[VMEM] * 10,
        out_specs=(ANY,) * 10 + (VMEM,) * (n_lo + 1),
        scratch_shapes=[
            pltpu.VMEM((2, strips, tok_dev, features), BF16),
            pltpu.VMEM((2, strips, tok_dev, features), BF16),
            pltpu.VMEM((6, strips, tok_dev, width), BF16),
            pltpu.VMEM((features, blocks * LANES), BF16),
            pltpu.VMEM((features, hidden), BF16),
            pltpu.VMEM((hidden, features), BF16),
            pltpu.VMEM((features, width), BF16),
            pltpu.VMEM((features, hidden), F32),
            pltpu.VMEM((hidden, features), F32),
            pltpu.SemaphoreType.DMA((2, 3, CHUNKS)),
            pltpu.SemaphoreType.DMA((2, 3, CHUNKS)),
            pltpu.SemaphoreType.DMA((10, 2 * CHUNKS)),
        ],
        compiler_params=pltpu.CompilerParams(collective_id=0, has_side_effects=True, vmem_limit_bytes=60 << 20),
        name="gather_and_project",
    )(tokens, cot, ln_gain, qkv_weight, gq, gk, attn_out, mlp_in, mlp_bias, mlp_out)


def back_body(
    heads, n_hi, n_lo, d_qkv_hbm, nall_hbm, dn_part_hbm, qkv_weight, tokens, cot, ln_gain, attn_t, mlp_own, front_rows,
    gain_rows, input_grad, mlp_all_out, joint_all_out, rows_out,
    d_qkv, nall, dn_part, weight_t, acc, joint, joint_low, joint_got, joint_sum, joint_got_hi, joint_all, mlp_all,
    near, core_give, core_got, x_give, x_got, vec, vec_lo, vec_hi, vec_pair,
    load_sem, mlp_s, mlp_r, joint_s, joint_r, hi_s, hi_r, all_s, all_r, core_s, core_r, x_s, x_r, vec_s, vec_r, save_sem,
):
    batch, me = lax.axis_index("batch"), lax.axis_index("tensor")
    hi, lo = batch // n_lo, batch % n_lo
    sibling = me + 1 - 2 * (me % 2)
    across = (me + 2) % 4
    chip, core = me // 2, me % 2
    tok_dev, features = tokens.shape
    step = tok_dev // CHUNKS
    chunk_rows, chunk_cols = joint.shape[2], joint.shape[3]
    half_cols = chunk_cols

    loads = [
        pltpu.make_async_copy(a, b, load_sem.at[i])
        for i, (a, b) in enumerate(((d_qkv_hbm, d_qkv), (nall_hbm, nall), (dn_part_hbm, dn_part)))
    ]
    for load in loads:
        load.start()

    def hi_peer(k):
        return (hi + k + n_hi) % n_hi

    def lo_peer(m):
        return (lo + m + n_lo) % n_lo

    def to_hi(k):
        return (hi_peer(k) * n_lo + lo, me)

    def to_lo(m):
        return (hi * n_lo + lo_peer(m), me)

    barrier = pltpu.get_barrier_semaphore()
    peers = [to_hi(k) for k in range(1, n_hi)] + [to_lo(m) for m in range(1, n_lo)] + [(batch, sibling), (batch, across)]
    for peer in peers:
        pl.semaphore_signal(barrier, inc=1, device_id=peer, device_id_type=pl.DeviceIdType.MESH)
    mlp_all[hi, lo] = mlp_own[...]
    pl.semaphore_wait(barrier, len(peers))

    def gather_hi(buf, sends, recvs, k, back=0):
        part = buf.at[hi_peer(back), lo]
        return remote(part, part, sends.at[0, k], recvs.at[0, k], to_hi(k))

    def gather_lo(buf, sends, recvs, m, k, back=0):
        part = buf.at[hi_peer(-k), lo_peer(back)]
        return remote(part, part, sends.at[m, k], recvs.at[m, k], to_lo(m))

    def gather_start(buf, sends, recvs):
        for k in range(1, n_hi):
            gather_hi(buf, sends, recvs, k).start()
        for m in range(1, n_lo):
            gather_lo(buf, sends, recvs, m, 0).start()

    def gather_pass(buf, sends, recvs, k):
        gather_hi(buf, sends, recvs, k, -k).wait_recv()
        for m in range(1, n_lo):
            gather_lo(buf, sends, recvs, m, k).start()

    def gather_end(buf, sends, recvs):
        for m in range(1, n_lo):
            for k in range(n_hi):
                gather_lo(buf, sends, recvs, m, k, -m).wait_recv()
        for k in range(1, n_hi):
            gather_hi(buf, sends, recvs, k).wait_send()
        for m in range(1, n_lo):
            for k in range(n_hi):
                gather_lo(buf, sends, recvs, m, k).wait_send()

    gather_start(mlp_all, mlp_s, mlp_r)

    loads[0].wait()
    loads[1].wait()
    acc[...] = jnp.zeros_like(acc)

    def add_strip(i, _):
        acc[...] += tn(nall[i], d_qkv[i])
        return 0

    lax.fori_loop(0, nall.shape[0], add_strip, 0)
    width = qkv_weight.shape[1]
    whole = width // LANES * LANES
    left = lax.broadcasted_iota(jnp.int32, (features, LANES), 1) < DH
    joint_low[:, :whole] = acc[:, :whole].astype(BF16)
    parts = [attn_t[:, h * LANES : (h + 1) * LANES].astype(F32) for h in range(heads)]
    if width % LANES:
        parts = [acc[:, whole : whole + LANES]] + parts
    for b in range(len(parts) // 2):
        block = jnp.where(left, parts[2 * b], pltpu.roll(parts[2 * b + 1], DH, 1))
        joint_low[:, whole + b * LANES : whole + (b + 1) * LANES] = block.astype(BF16)
    per_half = features // chunk_rows
    for o in range(n_hi * n_lo):
        row = o % per_half * chunk_rows
        col = o // per_half * half_cols
        joint[o // n_lo, o % n_lo] = joint_low[row : row + chunk_rows, col : col + half_cols]

    def joint_move(m, k, back=0):
        return remote(
            joint.at[hi_peer(k), lo_peer(m)], joint_got.at[lo_peer(back), hi_peer(k)],
            joint_s.at[m, k], joint_r.at[m, k], to_lo(m),
        )

    for k in list(range(1, n_hi)) + [0]:
        for m in range(1, n_lo):
            joint_move(m, k).start()

    weight = qkv_weight[...].astype(F32)
    grown = acc[:, :width] * weight
    grown_hi = grown.astype(BF16)
    ones = jnp.ones((8, width), BF16)
    ln_row = (nt(ones, grown_hi) + nt(ones, (grown - grown_hi.astype(F32)).astype(BF16)))[0:1]
    vec_lo[lo] = front_rows[...]
    vec_lo[lo, 2:3, :] = (front_rows[2:3, :] + ln_row) / ln_gain[...].astype(F32)
    vec_lo[lo, 3:5, 0 : heads * LANES] = gain_rows[0:2, :]

    def vec_lo_move(m, back=0):
        part = vec_lo.at[lo_peer(back)]
        return remote(part, part, vec_s.at[m], vec_r.at[m], to_lo(m))

    def vec_hi_move(k, back=0):
        part = vec_hi.at[hi_peer(back)]
        return remote(part, part, vec_s.at[n_lo + k], vec_r.at[n_lo + k], to_hi(k))

    def vec_pair_move(i, to):
        return remote(vec.at[i], vec_pair.at[i], vec_s.at[n_lo + n_hi + i], vec_r.at[n_lo + n_hi + i], (batch, to))

    for m in range(1, n_lo):
        vec_lo_move(m).start()

    weight_t[...] = jnp.zeros_like(weight_t)
    weight_t[:width, :] = qkv_weight[...].T
    loads[2].wait()

    def rows_of(c):
        return pl.ds(pl.multiple_of(c * step, step), step)

    def partial_rows(strip, c):
        return nn(d_qkv[strip, rows_of(c)], weight_t[...]) + dn_part[strip, rows_of(c)].astype(F32)

    def core_move(side, c):
        return remote(
            core_give.at[side, rows_of(c)], core_got.at[side, rows_of(c)], core_s.at[side, c], core_r.at[side, c], (batch, sibling)
        )

    def x_move(c):
        return remote(x_give.at[rows_of(c)], x_got.at[rows_of(c)], x_s.at[c], x_r.at[c], (batch, across))

    def give_far(c, _):
        core_give[0, rows_of(c)] = partial_rows(across + sibling - me, c).astype(BF16)
        core_move(0, c).start()
        return 0

    def send_far(c, _):
        mine = partial_rows(across, c)
        core_move(0, c).wait_recv()
        x_give[rows_of(c)] = (mine + core_got[0, rows_of(c)].astype(F32)).astype(BF16)
        x_move(c).start()
        return 0

    def give_near(c, _):
        core_give[1, rows_of(c)] = partial_rows(sibling, c).astype(BF16)
        core_move(1, c).start()
        return 0

    def keep_near(c, _):
        mine = partial_rows(me, c)
        core_move(1, c).wait_recv()
        near[rows_of(c)] = mine + core_got[1, rows_of(c)].astype(F32)
        return 0

    for loop in (give_far, send_far, give_near, keep_near):
        lax.fori_loop(0, CHUNKS, loop, 0)

    for m in range(1, n_lo):
        vec_lo_move(m, -m).wait_recv()
    total = vec_lo[0]
    for i in range(1, n_lo):
        total = total + vec_lo[i]
    vec_hi[hi] = total
    for k in range(1, n_hi):
        vec_hi_move(k).start()

    def hi_move(k, back=0):
        return remote(joint_sum.at[hi_peer(k)], joint_got_hi.at[hi_peer(back)], hi_s.at[k], hi_r.at[k], to_hi(k))

    for k in list(range(1, n_hi)) + [0]:
        for m in range(1, n_lo):
            joint_move(m, k, -m).wait_recv()
        where = hi_peer(k)
        total = joint[where, lo].astype(F32)
        for m in range(1, n_lo):
            total = total + joint_got[lo_peer(m), where].astype(F32)
        joint_sum[where] = total.astype(BF16)
        if k:
            hi_move(k).start()

    for k in range(1, n_hi):
        vec_hi_move(k, -k).wait_recv()
    total = vec_hi[0]
    for i in range(1, n_hi):
        total = total + vec_hi[i]
    vec[0] = total
    vec_pair_move(0, sibling).start()

    gain = ln_gain[...].astype(F32)

    def last_rows(c, _):
        x_move(c).wait_recv()
        d_normed = near[rows_of(c)] + x_got[rows_of(c)].astype(F32)
        x = tokens[rows_of(c)].astype(F32)
        centred = x - jnp.mean(x, axis=-1, keepdims=True)
        r = lax.rsqrt(jnp.mean(centred * centred, axis=-1, keepdims=True) + epsilon)
        xhat = centred * r
        e = d_normed * gain
        d_x = r * (e - jnp.mean(e, axis=-1, keepdims=True) - xhat * jnp.mean(e * xhat, axis=-1, keepdims=True))
        input_grad[rows_of(c)] = (cot[rows_of(c)].astype(F32) + d_x).astype(BF16)
        return 0

    for k in range(1, n_hi):
        gather_pass(mlp_all, mlp_s, mlp_r, k)
    lax.fori_loop(0, CHUNKS, last_rows, 0)

    vec_pair_move(0, sibling).wait_recv()
    vec[1] = vec[0] + vec_pair[0]
    vec_pair_move(1, across).start()

    total = joint_sum[hi].astype(F32)
    for k in range(1, n_hi):
        hi_move(k, -k).wait_recv()
        total = total + joint_got_hi[hi_peer(-k)].astype(F32)
    joint_all[hi, lo] = total.astype(BF16)
    gather_start(joint_all, all_s, all_r)

    vec_pair_move(1, across).wait_recv()
    rows_out[...] = vec[0]
    rows_out[1:3, :] = vec[1, 1:3, :] + vec_pair[1, 1:3, :]

    for k in range(1, n_hi):
        gather_pass(joint_all, all_s, all_r, k)
    gather_end(mlp_all, mlp_s, mlp_r)
    save_mlp = pltpu.make_async_copy(mlp_all, mlp_all_out, save_sem.at[0])
    save_mlp.start()

    for m in range(1, n_lo):
        for k in range(n_hi):
            joint_move(m, k).wait_send()
        vec_lo_move(m).wait_send()
    for k in range(1, n_hi):
        hi_move(k).wait_send()
        vec_hi_move(k).wait_send()
    vec_pair_move(0, sibling).wait_send()
    vec_pair_move(1, across).wait_send()

    def sent(c, _):
        core_move(0, c).wait_send()
        core_move(1, c).wait_send()
        x_move(c).wait_send()
        return 0

    lax.fori_loop(0, CHUNKS, sent, 0)
    gather_end(joint_all, all_s, all_r)
    save_joint = pltpu.make_async_copy(joint_all, joint_all_out, save_sem.at[1])
    save_joint.start()
    save_mlp.wait()
    save_joint.wait()


def levels(n_batch):
    lo = 2 if n_batch <= 8 else 4
    return n_batch // lo, lo


def back(n_batch, d_qkv, nall, dn_part, qkv_weight, tokens, cot, ln_gain, attn_t, mlp_own, front_rows, gain_rows):
    n_hi, n_lo = levels(n_batch)
    strips, tok_dev, features = nall.shape
    wide = d_qkv.shape[2]
    heads = attn_t.shape[1] // LANES
    chunk = (2 * features // n_batch, features // 2)
    dma = pltpu.SemaphoreType.DMA
    rows = pltpu.VMEM((8, features), F32)
    return pl.pallas_call(
        functools.partial(back_body, heads, n_hi, n_lo),
        out_shape=(
            jax.ShapeDtypeStruct(tokens.shape, BF16),
            jax.ShapeDtypeStruct((n_hi, n_lo) + mlp_own.shape, BF16),
            jax.ShapeDtypeStruct((n_hi, n_lo) + chunk, BF16),
            jax.ShapeDtypeStruct((8, features), F32),
        ),
        in_specs=[ANY] * 3 + [VMEM] * 8,
        out_specs=(VMEM, ANY, ANY, VMEM),
        scratch_shapes=[
            pltpu.VMEM(d_qkv.shape, BF16),
            pltpu.VMEM(nall.shape, BF16),
            pltpu.VMEM(dn_part.shape, BF16),
            pltpu.VMEM((wide, features), BF16),
            pltpu.VMEM((features, wide), F32),
            pltpu.VMEM((n_hi, n_lo) + chunk, BF16),
            pltpu.VMEM((features, features), BF16),
            pltpu.VMEM((n_lo, n_hi) + chunk, BF16),
            pltpu.VMEM((n_hi,) + chunk, BF16),
            pltpu.VMEM((n_hi,) + chunk, BF16),
            pltpu.VMEM((n_hi, n_lo) + chunk, BF16),
            pltpu.VMEM((n_hi, n_lo) + mlp_own.shape, BF16),
            pltpu.VMEM(tokens.shape, F32),
            pltpu.VMEM((2,) + tokens.shape, BF16),
            pltpu.VMEM((2,) + tokens.shape, BF16),
            pltpu.VMEM(tokens.shape, BF16),
            pltpu.VMEM(tokens.shape, BF16),
            pltpu.VMEM((2, 8, features), F32),
            pltpu.VMEM((n_lo, 8, features), F32),
            pltpu.VMEM((n_hi, 8, features), F32),
            pltpu.VMEM((2, 8, features), F32),
            dma((3,)),
            dma((n_lo, n_hi)), dma((n_lo, n_hi)),
            dma((n_lo, n_hi)), dma((n_lo, n_hi)),
            dma((n_hi,)), dma((n_hi,)),
            dma((n_lo, n_hi)), dma((n_lo, n_hi)),
            dma((2, CHUNKS)), dma((2, CHUNKS)),
            dma((CHUNKS,)), dma((CHUNKS,)),
            dma((n_lo + n_hi + 2,)), dma((n_lo + n_hi + 2,)),
            dma((2,)),
        ],
        compiler_params=pltpu.CompilerParams(collective_id=1, has_side_effects=True, vmem_limit_bytes=60 << 20),
        name="reduce_gradients",
    )(d_qkv, nall, dn_part, qkv_weight, tokens, cot, ln_gain, attn_t, mlp_own, front_rows, gain_rows)


SIBLINGS = [(0, 1), (1, 0), (2, 3), (3, 2)]
ACROSS = [(0, 2), (1, 3), (2, 0), (3, 1)]


def on_device(
    tokens, out_cotangent, ln_gain, qkv_weight, q_gain, k_gain, attn_out,
    mlp_in, mlp_bias, mlp_out, out_bias, image_len, image_group,
):
    tok_dev, features = tokens.shape
    strips = lax.axis_size("tensor")
    n_batch = lax.axis_size("batch")
    n_hi, n_lo = levels(n_batch)
    heads = q_gain.shape[0] // DH
    qkv_cols = qkv_weight.shape[1]

    def pad_gain(g, factor):
        g = g.astype(F32).reshape(heads, DH) * factor
        return jnp.concatenate([g, jnp.zeros_like(g)], axis=-1).reshape(1, heads * LANES)

    scale = DH ** (-0.5)
    gq, gk = pad_gain(q_gain, scale), pad_gain(k_gain, 1.0)
    ln_row = ln_gain.reshape(1, -1)
    (qa, ka, va, do, uq, uk, mlp_part, dn_part, nall, call, *mlp_grad, front_rows) = front(
        strips, n_batch, tokens, out_cotangent, ln_row, qkv_weight, gq * LOG2E, gk,
        attn_out, mlp_in, mlp_bias.reshape(1, -1), mlp_out,
    )

    def along_lo(x, m):
        pairs = [(h * n_lo + i, h * n_lo + (i + m) % n_lo) for h in range(n_hi) for i in range(n_lo)]
        return lax.ppermute(x, "batch", pairs)

    def along_hi(x, k):
        pairs = [(h * n_lo + i, (h + k) % n_hi * n_lo + i) for h in range(n_hi) for i in range(n_lo)]
        return lax.ppermute(x, "batch", pairs)

    def add(first, others):
        total = first.astype(F32)
        for other in others:
            total = total + other.astype(F32)
        return total.astype(BF16)

    lo_got = [along_lo(mlp_grad[m], m) for m in range(1, n_lo)]
    qb, dob, give, keep, attn_t = attn_fwd(image_len, image_group, qa, ka, va, do, attn_out, mlp_part, call)
    lo_sum = [add(mlp_grad[0][k], [got[k] for got in lo_got]) for k in range(n_hi)]
    core_got = lax.ppermute(give, "tensor", SIBLINGS)
    hi_got = [along_hi(lo_sum[k], k) for k in range(1, n_hi)]
    mine = add(keep, [core_got])
    x_got = lax.ppermute(mine[0], "tensor", ACROSS)
    d_qkv, gain_rows = attn_bwd(image_len, image_group, qb, ka, va, dob, uq, uk, gq, gk)
    output = (
        tokens.astype(F32) + mine[1].astype(F32) + x_got.astype(F32) + out_bias.astype(F32)
    ).astype(BF16)
    mlp_own = add(lo_sum[0], hi_got)
    input_grad, mlp_all, joint_all, rows = back(
        n_batch, d_qkv, nall, dn_part, qkv_weight, tokens, out_cotangent, ln_row, attn_t, mlp_own, front_rows, gain_rows
    )
    mlp_all = mlp_all.reshape(-1, features).astype(F32)
    joint = joint_all.reshape(2, features, features // 2).astype(F32)
    hidden = mlp_in.shape[1]
    left_cols = features // 2

    def gain_grad(row):
        return row[: heads * LANES].reshape(heads, LANES)[:, :DH].reshape(heads * DH)

    return (
        output,
        input_grad,
        rows[2],
        jnp.concatenate([joint[0], joint[1][:, : qkv_cols - left_cols]], axis=1),
        gain_grad(rows[3]),
        gain_grad(rows[4]),
        joint[1][:, qkv_cols - left_cols :].T,
        mlp_all[:features],
        rows[0],
        mlp_all[features:],
        rows[1],
    )


def solution(mesh):
    rows, cols, first = P(("batch", "tensor"), None), P(None, "tensor"), P("tensor", None)
    return jax.shard_map(
        on_device,
        mesh=mesh,
        in_specs=(rows, rows, P(), cols, P("tensor"), P("tensor"), first, cols, P("tensor"), first, P(), P(), P()),
        out_specs=(rows, rows, P(), cols, P("tensor"), P("tensor"), first, cols, P("tensor"), first, P()),
        check_vma=False,
    )
```

```python
import functools

import jax
import jax.numpy as jnp
from jax import lax
from jax.experimental import pallas as pl
from jax.experimental.pallas import tpu as pltpu
from jax.sharding import PartitionSpec as P

DH = 64
LANES = 128
WIN = 64
ALIGN = 16
LOG2E = 1.4426950408889634
epsilon = 1e-06
F32 = jnp.float32
BF16 = jnp.bfloat16
VMEM = pl.BlockSpec(memory_space=pltpu.VMEM)
SMEM = pl.BlockSpec(memory_space=pltpu.SMEM)
ANY = pl.BlockSpec(memory_space=pl.ANY)


def nn(left, right):
    return lax.dot_general(left, right, (((1,), (0,)), ((), ())), preferred_element_type=F32)


def nt(left, right):
    return lax.dot_general(left, right, (((1,), (1,)), ((), ())), preferred_element_type=F32)


def tn(left, right):
    return lax.dot_general(left, right, (((0,), (0,)), ((), ())), preferred_element_type=F32)


def row_of(vector):
    return vector[...].astype(F32).reshape(1, -1)


def pair_row(q_vector, k_vector, heads):
    q, k = row_of(q_vector), row_of(k_vector)
    parts = []
    for h in range(heads):
        parts += [q[:, h * DH : (h + 1) * DH], k[:, h * DH : (h + 1) * DH]]
    return jnp.concatenate(parts, axis=1)


def half_sums():
    row = lax.broadcasted_iota(jnp.int32, (LANES, LANES), 0) // DH
    col = lax.broadcasted_iota(jnp.int32, (LANES, LANES), 1) // DH
    return jnp.where(row == col, 1.0, 0.0).astype(BF16)


def left_half(rows):
    return lax.broadcasted_iota(jnp.int32, (rows, LANES), 1) < DH


def find_segments(len_ref, group_ref, seg_ref, strips, tok_dev):
    group = lax.axis_index("batch")

    def entry(i, carry):
        count, run = carry
        rows = jnp.where(group_ref[i] == group, len_ref[i] // strips, 0)

        @pl.when(rows > 0)
        def _():
            seg_ref[0, count] = run
            seg_ref[1, count] = run + rows

        return count + jnp.where(rows > 0, 1, 0), run + rows

    count, run = lax.fori_loop(0, len_ref.shape[0], entry, (jnp.int32(0), jnp.int32(0)))

    @pl.when(run < tok_dev)
    def _():
        seg_ref[0, count] = run
        seg_ref[1, count] = tok_dev

    return count + jnp.where(run < tok_dev, 1, 0)


def window(start, end, first, i, tok_dev):
    nominal = first + WIN * i
    at = pl.multiple_of(jnp.minimum(nominal, tok_dev - WIN), ALIGN)
    return at, jnp.maximum(start, nominal) - at, jnp.minimum(end, nominal + WIN) - at


def row_mask(low, high, strips, win=WIN, width=LANES):
    j = lax.broadcasted_iota(jnp.int32, (strips, win, width), 1).reshape(strips * win, width)
    return (j >= low) & (j < high)


def tile(ref, at, h, win=WIN):
    strips = ref.shape[0]
    return ref[:, pl.ds(at, win), h * LANES : (h + 1) * LANES].reshape(strips * win, LANES)


def put_tile(ref, at, h, mask, value, win=WIN, width=LANES):
    strips = ref.shape[0]
    where = (slice(None), pl.ds(at, win), slice(h * LANES, h * LANES + width))
    old = ref[where].reshape(strips * win, width)
    ref[where] = jnp.where(mask, value.astype(ref.dtype), old).reshape(strips, win, width)


def for_segments(len_ref, group_ref, seg, strips, tok_dev, small, middle, large):
    count = find_segments(len_ref, group_ref, seg, strips, tok_dev)
    big = middle_rows(tok_dev)

    def segment(index, _):
        start, end = seg[0, index], seg[1, index]
        first = (start // ALIGN) * ALIGN
        windows = (end - first + WIN - 1) // WIN
        fits = end - first <= big

        @pl.when(windows == 1)
        def _():
            small(*window(start, end, first, 0, tok_dev))

        @pl.when((windows > 1) & fits)
        def _():
            at = pl.multiple_of(jnp.minimum(first, tok_dev - big), ALIGN)
            middle(at, start - at, end - at)

        @pl.when(jnp.logical_not(fits))
        def _():
            large(start, end, first, windows)

        return 0

    lax.fori_loop(0, count, segment, 0)


def middle_rows(tok_dev):
    return min(tok_dev, tok_dev // 2 + ALIGN)


def attn_fwd_body(
    heads, len_ref, group_ref, qa, ka, va, do, attn_out, mlp_part_hbm, call_hbm,
    qb, dob, give, keep, attn_grad, seg, acc, ho, mlp_part, call, out_pad, grad_acc, sems,
):
    strips, tok_dev = qa.shape[0], qa.shape[1]
    loads = [pltpu.make_async_copy(mlp_part_hbm, mlp_part, sems.at[0]), pltpu.make_async_copy(call_hbm, call, sems.at[1])]
    for load in loads:
        load.start()
    zero = jnp.zeros((), BF16)
    big = middle_rows(tok_dev)

    def finish(at, low, high, totals, win=WIN):
        rows = strips * win
        mask = row_mask(low, high, strips, win)
        lane = lax.broadcasted_iota(jnp.int32, (rows, LANES), 1)
        left = lane < DH
        outs = []
        for h in range(heads):
            total = totals[h]
            rows_sum = jnp.where(left, pltpu.roll(total, DH, 1), total)
            out = jnp.where(left, total / rows_sum, 0.0)
            log_sum = jnp.log2(rows_sum)
            d_out = tile(do, at, h, win).astype(F32)
            delta = jnp.sum(out * d_out, axis=-1, keepdims=True)
            log_hi = log_sum.astype(BF16).astype(F32)
            delta_hi = delta.astype(BF16).astype(F32)
            q = tile(qa, at, h, win).astype(F32)
            q = jnp.where(lane == DH, -log_hi, jnp.where(lane == DH + 1, log_hi - log_sum, q))
            d_out = jnp.where(lane == DH, -delta_hi, jnp.where(lane == DH + 1, delta_hi - delta, d_out))
            put_tile(qb, at, h, mask, q, win)
            put_tile(dob, at, h, mask, d_out, win)
            outs.append(out)
        if heads % 2:
            outs.append(jnp.zeros_like(outs[0]))
        for b in range(len(outs) // 2):
            put_tile(ho, at, b, mask, jnp.where(left, outs[2 * b], pltpu.roll(outs[2 * b + 1], DH, 1)), win)

    def products(at_q, at_k, k_mask, win_q=WIN, win_k=WIN):
        scores = [nt(tile(qa, at_q, h, win_q), tile(ka, at_k, h, win_k)) for h in range(heads)]
        weights = [jnp.exp2(s).astype(BF16) for s in scores]
        return [nn(weights[h], jnp.where(k_mask, tile(va, at_k, h, win_k), zero)) for h in range(heads)]

    def small(at, low, high):
        finish(at, low, high, products(at, at, row_mask(low, high, strips)))

    def middle(at, low, high):
        def add(at_k, k_mask, win, first=False):
            for h, new in enumerate(products(at, at_k, k_mask, big, win)):
                acc[h] = new if first else acc[h] + new

        rest = big % WIN
        base = at + big - rest
        if rest:
            add(base, row_mask(low - (big - rest), high - (big - rest), strips, rest), rest, True)
        else:
            acc[...] = jnp.zeros_like(acc)

        def k_window(k, _):
            add(pl.multiple_of(at + k * WIN, ALIGN), row_mask(low - k * WIN, high - k * WIN, strips), WIN)
            return 0

        lax.fori_loop(0, big // WIN, k_window, 0)

        def total(h, offset, win):
            return acc[h].reshape(strips, big, LANES)[:, offset : offset + win].reshape(strips * win, LANES)

        for w in range(big // WIN):
            offset = w * WIN
            finish(
                pl.multiple_of(at + offset, ALIGN), low - offset, high - offset, [total(h, offset, WIN) for h in range(heads)]
            )
        if rest:
            offset = big - rest
            finish(base, low - offset, high - offset, [total(h, offset, rest) for h in range(heads)], rest)

    def large(start, end, first, windows):
        def q_window(i, _):
            at_q, low_q, high_q = window(start, end, first, i, tok_dev)
            rows = strips * WIN
            acc[:, :rows] = jnp.zeros((heads, rows, LANES), F32)

            def k_window(k, _):
                at_k, low_k, high_k = window(start, end, first, k, tok_dev)
                for h, new in enumerate(products(at_q, at_k, row_mask(low_k, high_k, strips))):
                    acc[h, :rows] += new
                return 0

            lax.fori_loop(0, windows, k_window, 0)
            finish(at_q, low_q, high_q, [acc[h, :rows] for h in range(heads)])
            return 0

        lax.fori_loop(0, windows, q_window, 0)

    for_segments(len_ref, group_ref, seg, strips, tok_dev, small, middle, large)

    width = attn_out.shape[0]
    out_pad[:width] = attn_out[...]
    out_pad[width:] = jnp.zeros((out_pad.shape[0] - width, out_pad.shape[1]), BF16)
    for load in loads:
        load.wait()
    me = lax.axis_index("tensor")
    grad_acc[...] = jnp.zeros_like(grad_acc)

    def project(strip, _):
        heads_rows = ho[strip]
        out = (nn(heads_rows, out_pad[...]) + mlp_part[strip].astype(F32)).astype(BF16)
        own = jnp.where(strip // 2 == me // 2, 1, 0)

        @pl.when(strip % 2 == me % 2)
        def _():
            keep[own] = out

        @pl.when(strip % 2 != me % 2)
        def _():
            give[own] = out

        grad_acc[...] += tn(heads_rows, call[strip])
        return 0

    lax.fori_loop(0, strips, project, 0)
    attn_grad[...] = grad_acc[:width].astype(BF16)


def attn_fwd(image_len, image_group, qa, ka, va, do, attn_out, mlp_part, call):
    strips, tok_dev, width = qa.shape
    heads = width // LANES
    features = call.shape[2]
    packed = (heads + 1) // 2 * LANES
    like = jax.ShapeDtypeStruct(qa.shape, BF16)
    half = jax.ShapeDtypeStruct((strips // 2, tok_dev, features), BF16)
    return pl.pallas_call(
        functools.partial(attn_fwd_body, heads),
        out_shape=(like, like, half, half, jax.ShapeDtypeStruct(attn_out.shape, BF16)),
        in_specs=[SMEM, SMEM] + [VMEM] * 5 + [ANY] * 2,
        out_specs=(VMEM,) * 5,
        scratch_shapes=[
            pltpu.SMEM((2, image_len.shape[0] + 1), jnp.int32),
            pltpu.VMEM((heads, strips * middle_rows(tok_dev), LANES), F32),
            pltpu.VMEM((strips, tok_dev, packed), BF16),
            pltpu.VMEM(call.shape, BF16),
            pltpu.VMEM(call.shape, BF16),
            pltpu.VMEM((packed, features), BF16),
            pltpu.VMEM((packed, features), F32),
            pltpu.SemaphoreType.DMA((2,)),
        ],
        compiler_params=pltpu.CompilerParams(vmem_limit_bytes=60 << 20),
        cost_estimate=pl.CostEstimate(flops=8 * 10**9, bytes_accessed=30 * 10**6, transcendentals=8 * 10**6),
        name="attention_forward",
    )(image_len, image_group, qa, ka, va, do, attn_out, mlp_part, call)


def attn_bwd_body(
    heads, len_ref, group_ref, qb, ka, va, dob, u_hbm, r_hbm, q_gain, k_gain,
    d_qkv, gain_grad, seg, k_turned, dq_turned, dk_acc, dv_acc, dq, dk, dv, u_rows, r_rows, sems,
):
    strips, tok_dev = qb.shape[0], qb.shape[1]
    loads = [pltpu.make_async_copy(u_hbm, u_rows, sems.at[0]), pltpu.make_async_copy(r_hbm, r_rows, sems.at[1])]
    for load in loads:
        load.start()
    zero = jnp.zeros((), BF16)
    big = middle_rows(tok_dev)

    def products(at_q, at_k, q_mask, k_turned_of, win_q=WIN, win_k=WIN):
        every = range(heads)
        qs = [tile(qb, at_q, h, win_q) for h in every]
        d_outs = [jnp.where(q_mask, tile(dob, at_q, h, win_q), zero) for h in every]
        scores = [nt(tile(ka, at_k, h, win_k), qs[h]) for h in every]
        d_weights = [nt(tile(va, at_k, h, win_k), d_outs[h]) for h in every]
        weights = [jnp.exp2(s) for s in scores]
        d_scores = [(weights[h] * d_weights[h]).astype(BF16) for h in every]
        dv_new = [nn(weights[h].astype(BF16), d_outs[h]) for h in every]
        dk_new = [nn(d_scores[h], qs[h]) for h in every]
        dq_new = [nn(k_turned_of(h), d_scores[h]) for h in every]
        return dq_new, dk_new, dv_new

    def turned(h, at_k, mask, win=WIN):
        return jnp.where(mask, tile(ka, at_k, h, win), zero).T[:DH]

    def small(at, low, high):
        mask = row_mask(low, high, strips)
        half = row_mask(low, high, strips, width=DH)
        dq_t, dk_new, dv_new = products(at, at, mask, lambda h: turned(h, at, mask))
        for h in range(heads):
            put_tile(dq, at, h, half, dq_t[h].T, width=DH)
            put_tile(dk, at, h, mask, dk_new[h])
            put_tile(dv, at, h, mask, dv_new[h])

    def middle(at, low, high):
        mask = row_mask(low, high, strips, big)
        for h in range(heads):
            k_turned[h] = turned(h, at, mask, big)

        def q_window(at_q, low_q, high_q, win, first=False):
            mask_q = row_mask(low_q, high_q, strips, win)
            half = row_mask(low_q, high_q, strips, win, DH)
            dq_t, dk_new, dv_new = products(at_q, at, mask_q, lambda h: k_turned[h], win, big)
            for h in range(heads):
                put_tile(dq, at_q, h, half, dq_t[h].T, win, DH)
                dk_acc[h] = dk_new[h] if first else dk_acc[h] + dk_new[h]
                dv_acc[h] = dv_new[h] if first else dv_acc[h] + dv_new[h]

        rest = big % WIN
        offset = big - rest
        if rest:
            q_window(at + offset, low - offset, high - offset, rest, True)
        else:
            dk_acc[...] = jnp.zeros_like(dk_acc)
            dv_acc[...] = jnp.zeros_like(dv_acc)

        def each(i, _):
            q_window(pl.multiple_of(at + i * WIN, ALIGN), low - i * WIN, high - i * WIN, WIN)
            return 0

        lax.fori_loop(0, big // WIN, each, 0)
        for h in range(heads):
            put_tile(dk, at, h, mask, dk_acc[h], big)
            put_tile(dv, at, h, mask, dv_acc[h], big)

    def large(start, end, first, windows):
        rows = strips * WIN

        def clear(i, _):
            for h in range(heads):
                dq_turned[h, i] = jnp.zeros(dq_turned.shape[2:], F32)
            return 0

        lax.fori_loop(0, windows, clear, 0)

        def k_window(k, _):
            at_k, low_k, high_k = window(start, end, first, k, tok_dev)
            mask_k = row_mask(low_k, high_k, strips)
            for h in range(heads):
                k_turned[h, :, :rows] = turned(h, at_k, mask_k)
            dk_acc[:, :rows] = jnp.zeros((heads, rows, LANES), F32)
            dv_acc[:, :rows] = jnp.zeros((heads, rows, LANES), F32)

            def q_window(i, _):
                at_q, low_q, high_q = window(start, end, first, i, tok_dev)
                mask_q = row_mask(low_q, high_q, strips)
                dq_t, dk_new, dv_new = products(at_q, at_k, mask_q, lambda h: k_turned[h, :, :rows])
                for h in range(heads):
                    dq_turned[h, i] += dq_t[h]
                    dk_acc[h, :rows] += dk_new[h]
                    dv_acc[h, :rows] += dv_new[h]
                return 0

            lax.fori_loop(0, windows, q_window, 0)
            for h in range(heads):
                put_tile(dk, at_k, h, mask_k, dk_acc[h, :rows])
                put_tile(dv, at_k, h, mask_k, dv_acc[h, :rows])
            return 0

        lax.fori_loop(0, windows, k_window, 0)

        def q_out(i, _):
            at_q, low_q, high_q = window(start, end, first, i, tok_dev)
            half = row_mask(low_q, high_q, strips, width=DH)
            for h in range(heads):
                put_tile(dq, at_q, h, half, dq_turned[h, i].T, width=DH)
            return 0

        lax.fori_loop(0, windows, q_out, 0)

    for_segments(len_ref, group_ref, seg, strips, tok_dev, small, middle, large)

    rows = strips * WIN
    left = left_half(rows)
    sums = half_sums()
    gains = pair_row(q_gain, k_gain, heads)
    for load in loads:
        load.wait()

    def chunk(i, totals):
        at = pl.multiple_of(i * WIN, WIN)
        scaled, new_totals, us = [], [], []
        for h in range(heads):
            cols = slice(h * LANES, (h + 1) * LANES)
            d_q, d_k = tile(dq, at, h), tile(dk, at, h) * (1.0 / LOG2E)
            both = jnp.where(left, d_q * DH ** (-0.5), pltpu.roll(d_k, DH, 1))
            u = tile(u_rows, at, h).astype(F32)
            new_totals.append(totals[h] + jnp.sum(both * u, axis=0, keepdims=True))
            scaled.append(both * gains[:, cols])
            us.append(u)
        stacked = [s.astype(BF16) for s in scaled] + [(scaled[h] * us[h]).astype(BF16) for h in range(heads)]
        means = nn(jnp.concatenate(stacked, axis=0), sums) * (1.0 / DH)
        parts = []
        for h in range(heads):
            mean = means[h * rows : (h + 1) * rows]
            mean_u = means[(heads + h) * rows : (heads + h + 1) * rows]
            parts.append((scaled[h] - mean - us[h] * mean_u) * tile(r_rows, at, h).astype(F32))
        values = [tile(dv, at, h) for h in range(heads)]
        if heads % 2:
            values.append(jnp.zeros_like(values[0]))
        for b in range(len(values) // 2):
            parts.append(jnp.where(left, values[2 * b], pltpu.roll(values[2 * b + 1], DH, 1)))
        for b, part in enumerate(parts):
            d_qkv[:, pl.ds(at, WIN), b * LANES : (b + 1) * LANES] = part.astype(BF16).reshape(strips, WIN, LANES)
        return tuple(new_totals)

    totals = lax.fori_loop(0, tok_dev // WIN, chunk, tuple(jnp.zeros((1, LANES), F32) for _ in range(heads)))
    gain_grad[...] = jnp.zeros_like(gain_grad)
    for h in range(heads):
        gain_grad[0:1, h * LANES : (h + 1) * LANES] = totals[h]


def attn_bwd(image_len, image_group, qb, ka, va, dob, u, r, q_gain, k_gain):
    strips, tok_dev, width = qb.shape
    heads = width // LANES
    blocks = heads + (heads + 1) // 2
    rows = strips * WIN
    big = strips * middle_rows(tok_dev)
    windows = tok_dev // WIN + 1
    full = pltpu.VMEM((strips, tok_dev, width), F32)
    return pl.pallas_call(
        functools.partial(attn_bwd_body, heads),
        out_shape=(
            jax.ShapeDtypeStruct((strips, tok_dev, blocks * LANES), BF16),
            jax.ShapeDtypeStruct((8, width), F32),
        ),
        in_specs=[SMEM, SMEM] + [VMEM] * 4 + [ANY] * 2 + [VMEM] * 2,
        out_specs=(VMEM, VMEM),
        scratch_shapes=[
            pltpu.SMEM((2, image_len.shape[0] + 1), jnp.int32),
            pltpu.VMEM((heads, DH, big), BF16),
            pltpu.VMEM((heads, windows, DH, rows), F32),
            pltpu.VMEM((heads, big, LANES), F32),
            pltpu.VMEM((heads, big, LANES), F32),
            full, full, full,
            pltpu.VMEM(u.shape, BF16),
            pltpu.VMEM(r.shape, BF16),
            pltpu.SemaphoreType.DMA((2,)),
        ],
        compiler_params=pltpu.CompilerParams(vmem_limit_bytes=60 << 20),
        cost_estimate=pl.CostEstimate(flops=16 * 10**9, bytes_accessed=30 * 10**6, transcendentals=8 * 10**6),
        name="attention_backward",
    )(image_len, image_group, qb, ka, va, dob, u, r, q_gain, k_gain)


CHUNKS = 4


def by_kind(weight_t, heads, rows):
    parts = [weight_t[3 * h * DH : (3 * h + 2) * DH, :] for h in range(heads)]
    parts += [weight_t[(3 * h + 2) * DH : (3 * h + 3) * DH, :] for h in range(heads)]
    spare = rows - weight_t.shape[0]
    if spare:
        parts.append(jnp.zeros((spare, weight_t.shape[1]), BF16))
    return jnp.concatenate(parts, axis=0)


def remote(src, dst, send, recv, device):
    return pltpu.make_async_remote_copy(
        src_ref=src, dst_ref=dst, send_sem=send, recv_sem=recv, device_id=device, device_id_type=pl.DeviceIdType.MESH
    )


def front_body(
    heads, tokens, cot, ln_gain, qkv_weight_t, q_gain, k_gain, attn_out, mlp_in, mlp_bias, mlp_out,
    qa_out, ka_out, va_out, do_out, u_out, r_out, mlp_part_out, dn_part_out, nall_out, call_out,
    *rest,
):
    (rows_out, both, wide, narrow, qkv_pad, mlp_out_t, mlp_in_t, attn_out_t, g_in, g_out,
     send_sem, recv_sem, save_sem) = rest[-13:]
    grad_outs = rest[:-13]
    batch, me = lax.axis_index("batch"), lax.axis_index("tensor")
    sibling = me + 1 - 2 * (me % 2)
    across = (me + 2) % 4
    chip, far_chip = me // 2, 1 - me // 2
    tok_dev = tokens.shape[0]
    step = tok_dev // CHUNKS
    rows = 2 * step
    features = tokens.shape[1]
    heads_wide = heads * LANES

    def rows_of(c):
        return pl.ds(pl.multiple_of(c * step, step), step)

    def move(kind, route, c, strip, to):
        part = both.at[kind, strip, rows_of(c)]
        return remote(part, part, send_sem.at[kind, route, c], recv_sem.at[kind, route, c], (batch, to))

    barrier = pltpu.get_barrier_semaphore()
    for other in (sibling, across):
        pl.semaphore_signal(barrier, inc=1, device_id=(batch, other), device_id_type=pl.DeviceIdType.MESH)
    gain = row_of(ln_gain)
    gains = pair_row(q_gain, k_gain, heads)

    def norm_chunk(c):
        both[0, me, rows_of(c)] = cot[rows_of(c)]
        x = tokens[rows_of(c)].astype(F32)
        centred = x - jnp.mean(x, axis=-1, keepdims=True)
        variance = jnp.mean(centred * centred, axis=-1, keepdims=True)
        both[1, me, rows_of(c)] = (centred * lax.rsqrt(variance + epsilon) * gain).astype(BF16)

    norm_chunk(0)
    pl.semaphore_wait(barrier, 2)

    def first_sends(c, _):
        for kind in range(2):
            move(kind, 1, c, me, across).start()
            move(kind, 0, c, me, sibling).start()

        @pl.when(c + 1 < CHUNKS)
        def _():
            norm_chunk(c + 1)

        return 0

    lax.fori_loop(0, CHUNKS, first_sends, 0)

    g_in[...] = jnp.zeros_like(g_in)
    g_out[...] = jnp.zeros_like(g_out)
    rows_out[...] = jnp.zeros_like(rows_out)
    total = jnp.zeros((1, features), F32)
    for c in range(CHUNKS):
        total += jnp.sum(cot[c * step : (c + 1) * step].astype(F32), axis=0, keepdims=True)
    rows_out[1:2, :] = total
    qkv_pad[...] = by_kind(qkv_weight_t, heads, qkv_pad.shape[1]).T
    mlp_out_t[...] = mlp_out[...].T
    mlp_in_t[...] = mlp_in[...].T
    for h in range(heads):
        part = attn_out[h * DH : (h + 1) * DH, :]
        attn_out_t[:, h * LANES : (h + 1) * LANES] = jnp.concatenate([part, jnp.zeros_like(part)], axis=0).T

    left = left_half(rows)
    sums = half_sums()
    bias = row_of(mlp_bias)

    def saves(c, at_chip):
        strips = pl.ds(2 * at_chip, 2)
        where = rows_of(c)
        index = at_chip * CHUNKS + c
        pairs = [(narrow.at[a, strips, where], ref.at[strips, where]) for a, ref in enumerate(
            (qa_out, ka_out, va_out, do_out, u_out, r_out))]
        pairs += [(wide.at[a, strips, where], ref.at[strips, where]) for a, ref in enumerate(
            (mlp_part_out, dn_part_out))]
        pairs += [(both.at[1, strips, where], nall_out.at[strips, where]), (both.at[0, strips, where], call_out.at[strips, where])]
        return [pltpu.make_async_copy(a, b, save_sem.at[n, index]) for n, (a, b) in enumerate(pairs)]

    def unit(i, _):
        far = i >= CHUNKS
        c = i % CHUNKS
        at_chip = jnp.where(far, far_chip, chip)

        @pl.when(jnp.logical_not(far))
        def _():
            for kind in range(2):
                move(kind, 0, c, sibling, sibling).wait_recv()

        def pass_on(k):
            for kind in range(2):
                move(kind, 1, k, across, across).wait_recv()
                move(kind, 2, k, across, sibling).start()

        @pl.when(i == CHUNKS - 1)
        def _():
            pass_on(0)

        @pl.when(i == CHUNKS)
        def _():
            pass_on(1)

        @pl.when(i > CHUNKS + 1)
        def _():
            pass_on(c)

        @pl.when(far)
        def _():
            for kind in range(2):
                move(kind, 2, c, across + 1 - 2 * (across % 2), sibling).wait_recv()

        strips = pl.ds(2 * at_chip, 2)
        where = rows_of(c)
        n = both[1, strips, where].reshape(rows, features)
        d = both[0, strips, where].reshape(rows, features)

        def save(ref, a, h, value):
            ref[a, strips, where, h * LANES : (h + 1) * LANES] = value.astype(BF16).reshape(2, step, LANES)

        qkv = nn(n, qkv_pad[...])

        def block(b):
            return qkv[:, b * LANES : (b + 1) * LANES]

        def stacked_means(parts):
            stacked = jnp.concatenate([p.astype(BF16) for p in parts], axis=0)
            means = nn(stacked, sums) * (1.0 / DH)
            return [means[h * rows : (h + 1) * rows] for h in range(heads)]

        pairs = [block(h) for h in range(heads)]
        means = stacked_means(pairs)
        centred = [pairs[h] - means[h] for h in range(heads)]
        variances = stacked_means([x * x for x in centred])
        for h in range(heads):
            rstd = lax.rsqrt(variances[h] + epsilon)
            u = centred[h] * rstd
            scaled = u * gains[:, h * LANES : (h + 1) * LANES]
            save(narrow, 0, h, jnp.where(left, scaled * (DH ** (-0.5) * LOG2E), 0.0))
            save(narrow, 1, h, jnp.where(left, pltpu.roll(scaled, DH, 1), 1.0))
            value = block(heads + h // 2)
            save(narrow, 2, h, jnp.where(left, pltpu.roll(value, DH, 1) if h % 2 else value, 1.0))
            save(narrow, 4, h, u)
            save(narrow, 5, h, rstd)
        narrow[3, strips, where] = nn(d, attn_out_t[...]).astype(BF16).reshape(2, step, heads_wide)

        hidden = nn(n, mlp_in[...]) + bias
        cdf = 0.5 + 0.5 * lax.erf(hidden * 0.7071067811865476)
        act = (hidden * cdf).astype(BF16)
        slope = cdf + hidden * (0.3989422804014327 * jnp.exp(hidden * hidden * -0.5))
        wide[0, strips, where] = nn(act, mlp_out[...]).astype(BF16).reshape(2, step, features)
        d_hidden = nn(d, mlp_out_t[...]) * slope
        d_low = d_hidden.astype(BF16)
        rows_out[0:1, :] += jnp.sum(d_low.astype(F32), axis=0, keepdims=True)
        wide[1, strips, where] = nn(d_low, mlp_in_t[...]).astype(BF16).reshape(2, step, features)
        g_out[...] += tn(act, d)
        g_in[...] += tn(n, d_low)
        for copy in saves(c, at_chip):
            copy.start()
        return 0

    lax.fori_loop(0, 2 * CHUNKS, unit, 0)

    n_lo = len(grad_outs)
    n_hi, chunk_rows = grad_outs[0].shape[0], grad_outs[0].shape[1]
    hi, lo = batch // n_lo, batch % n_lo
    per_grad = features // chunk_rows
    for o in range(n_hi * n_lo):
        source = (g_in, g_out)[o // per_grad]
        row = o % per_grad * chunk_rows
        low = source[row : row + chunk_rows, :].astype(BF16)
        at_hi = (o // n_lo - hi + n_hi) % n_hi
        at_lo = (o % n_lo - lo + n_lo) % n_lo
        for m in range(n_lo):

            @pl.when(at_lo == m)
            def _():
                grad_outs[m][at_hi] = low

    grown = g_in[...] * mlp_in[...].astype(F32)
    grown_hi = grown.astype(BF16)
    ones = jnp.ones((8, grown.shape[1]), BF16)
    rows_out[2:3, :] = (nt(ones, grown_hi) + nt(ones, (grown - grown_hi.astype(F32)).astype(BF16)))[0:1]

    def finish(i, _):
        for copy in saves(i % CHUNKS, i // CHUNKS):
            copy.wait()
        return 0

    lax.fori_loop(0, 2 * CHUNKS, finish, 0)

    def sent(c, _):
        for kind in range(2):
            move(kind, 0, c, me, sibling).wait_send()
            move(kind, 1, c, me, across).wait_send()
            move(kind, 2, c, across, sibling).wait_send()
        return 0

    lax.fori_loop(0, CHUNKS, sent, 0)


def front(strips, n_batch, tokens, cot, ln_gain, qkv_weight_t, q_gain, k_gain, attn_out, mlp_in, mlp_bias, mlp_out):
    tok_dev, features = tokens.shape
    heads = q_gain.shape[0] // DH
    width = heads * LANES
    hidden = mlp_in.shape[1]
    blocks = heads + (heads + 1) // 2
    n_hi, n_lo = levels(n_batch)
    like = jax.ShapeDtypeStruct((strips, tok_dev, width), BF16)
    rows = jax.ShapeDtypeStruct((strips, tok_dev, features), BF16)
    return pl.pallas_call(
        functools.partial(front_body, heads),
        out_shape=(like,) * 6 + (rows,) * 4 + (
            jax.ShapeDtypeStruct((n_hi, 2 * features // n_batch, features), BF16),
        ) * n_lo + (jax.ShapeDtypeStruct((8, features), F32),),
        in_specs=[VMEM] * 10,
        out_specs=(ANY,) * 10 + (VMEM,) * (n_lo + 1),
        scratch_shapes=[
            pltpu.VMEM((2, strips, tok_dev, features), BF16),
            pltpu.VMEM((2, strips, tok_dev, features), BF16),
            pltpu.VMEM((6, strips, tok_dev, width), BF16),
            pltpu.VMEM((features, blocks * LANES), BF16),
            pltpu.VMEM((features, hidden), BF16),
            pltpu.VMEM((hidden, features), BF16),
            pltpu.VMEM((features, width), BF16),
            pltpu.VMEM((features, hidden), F32),
            pltpu.VMEM((hidden, features), F32),
            pltpu.SemaphoreType.DMA((2, 3, CHUNKS)),
            pltpu.SemaphoreType.DMA((2, 3, CHUNKS)),
            pltpu.SemaphoreType.DMA((10, 2 * CHUNKS)),
        ],
        compiler_params=pltpu.CompilerParams(collective_id=0, has_side_effects=True, vmem_limit_bytes=60 << 20),
        name="gather_and_project",
    )(tokens, cot, ln_gain, qkv_weight_t, q_gain, k_gain, attn_out, mlp_in, mlp_bias, mlp_out)


def back_body(
    heads, n_hi, n_lo, d_qkv_hbm, nall_hbm, dn_part_hbm, give, keep, qkv_weight_t, tokens, cot, ln_gain, out_bias, attn_grad,
    mlp_own, front_rows, gain_rows, output, input_grad, mlp_all_out, joint_all_out, rows_out,
    d_qkv, nall, dn_part, weight_t, acc, joint, joint_low, joint_got, joint_sum, joint_got_hi, joint_all, mlp_all,
    near, core_give, core_got, x_give, x_got, out_got, out_give, out_far, vec, vec_lo, vec_hi, vec_pair,
    load_sem, mlp_s, mlp_r, joint_s, joint_r, hi_s, hi_r, all_s, all_r, core_s, core_r, x_s, x_r, out_core_s, out_core_r, out_x_s, out_x_r, vec_s, vec_r, save_sem,
):
    batch, me = lax.axis_index("batch"), lax.axis_index("tensor")
    hi, lo = batch // n_lo, batch % n_lo
    sibling = me + 1 - 2 * (me % 2)
    across = (me + 2) % 4
    chip, core = me // 2, me % 2
    tok_dev, features = tokens.shape
    step = tok_dev // CHUNKS
    chunk_rows, chunk_cols = joint.shape[2], joint.shape[3]
    half_cols = chunk_cols

    loads = [
        pltpu.make_async_copy(a, b, load_sem.at[i])
        for i, (a, b) in enumerate(((d_qkv_hbm, d_qkv), (nall_hbm, nall), (dn_part_hbm, dn_part)))
    ]
    for load in loads:
        load.start()

    def hi_peer(k):
        return (hi + k + n_hi) % n_hi

    def lo_peer(m):
        return (lo + m + n_lo) % n_lo

    def to_hi(k):
        return (hi_peer(k) * n_lo + lo, me)

    def to_lo(m):
        return (hi * n_lo + lo_peer(m), me)

    barrier = pltpu.get_barrier_semaphore()
    peers = [to_hi(k) for k in range(1, n_hi)] + [to_lo(m) for m in range(1, n_lo)] + [(batch, sibling), (batch, across)]
    for peer in peers:
        pl.semaphore_signal(barrier, inc=1, device_id=peer, device_id_type=pl.DeviceIdType.MESH)
    mlp_all[hi, lo] = mlp_own[...]
    pl.semaphore_wait(barrier, len(peers))

    def gather_hi(buf, sends, recvs, k, back=0):
        part = buf.at[hi_peer(back), lo]
        return remote(part, part, sends.at[0, k], recvs.at[0, k], to_hi(k))

    def gather_lo(buf, sends, recvs, m, k, back=0):
        part = buf.at[hi_peer(-k), lo_peer(back)]
        return remote(part, part, sends.at[m, k], recvs.at[m, k], to_lo(m))

    def gather_start(buf, sends, recvs):
        for k in range(1, n_hi):
            gather_hi(buf, sends, recvs, k).start()
        for m in range(1, n_lo):
            gather_lo(buf, sends, recvs, m, 0).start()

    def gather_pass(buf, sends, recvs, k):
        gather_hi(buf, sends, recvs, k, -k).wait_recv()
        for m in range(1, n_lo):
            gather_lo(buf, sends, recvs, m, k).start()

    def gather_end(buf, sends, recvs):
        for m in range(1, n_lo):
            for k in range(n_hi):
                gather_lo(buf, sends, recvs, m, k, -m).wait_recv()
        for k in range(1, n_hi):
            gather_hi(buf, sends, recvs, k).wait_send()
        for m in range(1, n_lo):
            for k in range(n_hi):
                gather_lo(buf, sends, recvs, m, k).wait_send()

    def rows_of(c):
        return pl.ds(pl.multiple_of(c * step, step), step)

    def out_core(c):
        where = rows_of(c)
        return remote(give.at[:, where], out_got.at[:, where], out_core_s.at[c], out_core_r.at[c], (batch, sibling))

    def out_across(c):
        return remote(out_give.at[rows_of(c)], out_far.at[rows_of(c)], out_x_s.at[c], out_x_r.at[c], (batch, across))

    def out_start(c, _):
        out_core(c).start()
        return 0

    def out_send(c, _):
        out_core(c).wait_recv()
        where = rows_of(c)
        out_give[where] = (keep[0, where].astype(F32) + out_got[0, where].astype(F32)).astype(BF16)
        out_across(c).start()
        return 0

    def out_rows(c, _):
        out_across(c).wait_recv()
        where = rows_of(c)
        total = keep[1, where].astype(F32) + out_got[1, where].astype(F32) + out_far[where].astype(F32)
        output[where] = (tokens[where].astype(F32) + total + bias).astype(BF16)
        return 0

    bias = row_of(out_bias)
    lax.fori_loop(0, CHUNKS, out_start, 0)
    gather_start(mlp_all, mlp_s, mlp_r)
    lax.fori_loop(0, CHUNKS, out_send, 0)

    weight_t[...] = by_kind(qkv_weight_t, heads, weight_t.shape[0])

    loads[0].wait()
    loads[1].wait()
    acc[...] = jnp.zeros_like(acc)

    def add_strip(i, _):
        acc[...] += tn(d_qkv[i], nall[i])
        return 0

    lax.fori_loop(0, nall.shape[0], add_strip, 0)
    width = qkv_weight_t.shape[0]
    joint_low[:width] = acc[:width].astype(BF16)
    joint_low[width:] = attn_grad[...]
    per_half = features // chunk_rows
    for o in range(n_hi * n_lo):
        row = o % per_half * chunk_rows
        col = o // per_half * half_cols
        joint[o // n_lo, o % n_lo] = joint_low[row : row + chunk_rows, col : col + half_cols]

    def joint_move(m, k, back=0):
        return remote(
            joint.at[hi_peer(k), lo_peer(m)], joint_got.at[lo_peer(back), hi_peer(k)],
            joint_s.at[m, k], joint_r.at[m, k], to_lo(m),
        )

    for k in list(range(1, n_hi)) + [0]:
        for m in range(1, n_lo):
            joint_move(m, k).start()

    ln_row = jnp.sum(acc[...] * weight_t[...].astype(F32), axis=0, keepdims=True)
    gain = row_of(ln_gain)
    vec_lo[lo] = front_rows[...]
    vec_lo[lo, 2:3, :] = (front_rows[2:3, :] + ln_row) / gain
    vec_lo[lo, 3:4, 0 : heads * LANES] = gain_rows[0:1, :]

    def vec_lo_move(m, back=0):
        part = vec_lo.at[lo_peer(back)]
        return remote(part, part, vec_s.at[m], vec_r.at[m], to_lo(m))

    def vec_hi_move(k, back=0):
        part = vec_hi.at[hi_peer(back)]
        return remote(part, part, vec_s.at[n_lo + k], vec_r.at[n_lo + k], to_hi(k))

    def vec_pair_move(i, to):
        return remote(vec.at[i], vec_pair.at[i], vec_s.at[n_lo + n_hi + i], vec_r.at[n_lo + n_hi + i], (batch, to))

    for m in range(1, n_lo):
        vec_lo_move(m).start()

    loads[2].wait()

    def partial_rows(strip, c):
        return nn(d_qkv[strip, rows_of(c)], weight_t[...]) + dn_part[strip, rows_of(c)].astype(F32)

    def core_move(side, c):
        return remote(
            core_give.at[side, rows_of(c)], core_got.at[side, rows_of(c)], core_s.at[side, c], core_r.at[side, c], (batch, sibling)
        )

    def x_move(c):
        return remote(x_give.at[rows_of(c)], x_got.at[rows_of(c)], x_s.at[c], x_r.at[c], (batch, across))

    def give_far(c, _):
        core_give[0, rows_of(c)] = partial_rows(across + sibling - me, c).astype(BF16)
        core_move(0, c).start()
        return 0

    def send_far(c, _):
        mine = partial_rows(across, c)
        core_move(0, c).wait_recv()
        x_give[rows_of(c)] = (mine + core_got[0, rows_of(c)].astype(F32)).astype(BF16)
        x_move(c).start()
        return 0

    def give_near(c, _):
        core_give[1, rows_of(c)] = partial_rows(sibling, c).astype(BF16)
        core_move(1, c).start()
        return 0

    def keep_near(c, _):
        mine = partial_rows(me, c)
        core_move(1, c).wait_recv()
        near[rows_of(c)] = mine + core_got[1, rows_of(c)].astype(F32)
        return 0

    for loop in (give_far, send_far, give_near, keep_near):
        lax.fori_loop(0, CHUNKS, loop, 0)

    for m in range(1, n_lo):
        vec_lo_move(m, -m).wait_recv()
    total = vec_lo[0]
    for i in range(1, n_lo):
        total = total + vec_lo[i]
    vec_hi[hi] = total
    for k in range(1, n_hi):
        vec_hi_move(k).start()

    def hi_move(k, back=0):
        return remote(joint_sum.at[hi_peer(k)], joint_got_hi.at[hi_peer(back)], hi_s.at[k], hi_r.at[k], to_hi(k))

    for k in list(range(1, n_hi)) + [0]:
        for m in range(1, n_lo):
            joint_move(m, k, -m).wait_recv()
        where = hi_peer(k)
        total = joint[where, lo].astype(F32)
        for m in range(1, n_lo):
            total = total + joint_got[lo_peer(m), where].astype(F32)
        joint_sum[where] = total.astype(BF16)
        if k:
            hi_move(k).start()

    for k in range(1, n_hi):
        vec_hi_move(k, -k).wait_recv()
    total = vec_hi[0]
    for i in range(1, n_hi):
        total = total + vec_hi[i]
    vec[0] = total
    vec_pair_move(0, sibling).start()

    def last_rows(c, _):
        x_move(c).wait_recv()
        d_normed = near[rows_of(c)] + x_got[rows_of(c)].astype(F32)
        x = tokens[rows_of(c)].astype(F32)
        centred = x - jnp.mean(x, axis=-1, keepdims=True)
        r = lax.rsqrt(jnp.mean(centred * centred, axis=-1, keepdims=True) + epsilon)
        xhat = centred * r
        e = d_normed * gain
        d_x = r * (e - jnp.mean(e, axis=-1, keepdims=True) - xhat * jnp.mean(e * xhat, axis=-1, keepdims=True))
        input_grad[rows_of(c)] = (cot[rows_of(c)].astype(F32) + d_x).astype(BF16)
        return 0

    for k in range(1, n_hi):
        gather_pass(mlp_all, mlp_s, mlp_r, k)
    lax.fori_loop(0, CHUNKS, out_rows, 0)
    lax.fori_loop(0, CHUNKS, last_rows, 0)

    vec_pair_move(0, sibling).wait_recv()
    vec[1] = vec[0] + vec_pair[0]
    vec_pair_move(1, across).start()

    total = joint_sum[hi].astype(F32)
    for k in range(1, n_hi):
        hi_move(k, -k).wait_recv()
        total = total + joint_got_hi[hi_peer(-k)].astype(F32)
    joint_all[hi, lo] = total.astype(BF16)
    gather_start(joint_all, all_s, all_r)

    vec_pair_move(1, across).wait_recv()
    rows_out[...] = vec[0]
    rows_out[1:3, :] = vec[1, 1:3, :] + vec_pair[1, 1:3, :]

    for k in range(1, n_hi):
        gather_pass(joint_all, all_s, all_r, k)
    gather_end(mlp_all, mlp_s, mlp_r)
    save_mlp = pltpu.make_async_copy(mlp_all, mlp_all_out, save_sem.at[0])
    save_mlp.start()

    for m in range(1, n_lo):
        for k in range(n_hi):
            joint_move(m, k).wait_send()
        vec_lo_move(m).wait_send()
    for k in range(1, n_hi):
        hi_move(k).wait_send()
        vec_hi_move(k).wait_send()
    vec_pair_move(0, sibling).wait_send()
    vec_pair_move(1, across).wait_send()

    def sent(c, _):
        core_move(0, c).wait_send()
        core_move(1, c).wait_send()
        x_move(c).wait_send()
        out_core(c).wait_send()
        out_across(c).wait_send()
        return 0

    lax.fori_loop(0, CHUNKS, sent, 0)
    gather_end(joint_all, all_s, all_r)
    save_joint = pltpu.make_async_copy(joint_all, joint_all_out, save_sem.at[1])
    save_joint.start()
    save_mlp.wait()
    save_joint.wait()


def levels(n_batch):
    lo = 2 if n_batch <= 8 else 4
    return n_batch // lo, lo


def back(n_batch, d_qkv, nall, dn_part, give, keep, qkv_weight_t, tokens, cot, ln_gain, out_bias, attn_grad,
    mlp_own, front_rows, gain_rows):
    n_hi, n_lo = levels(n_batch)
    strips, tok_dev, features = nall.shape
    wide = d_qkv.shape[2]
    heads = attn_grad.shape[0] // DH
    chunk = (2 * features // n_batch, features // 2)
    dma = pltpu.SemaphoreType.DMA
    rows = pltpu.VMEM((8, features), F32)
    return pl.pallas_call(
        functools.partial(back_body, heads, n_hi, n_lo),
        out_shape=(
            jax.ShapeDtypeStruct(tokens.shape, BF16),
            jax.ShapeDtypeStruct(tokens.shape, BF16),
            jax.ShapeDtypeStruct((n_hi, n_lo) + mlp_own.shape, BF16),
            jax.ShapeDtypeStruct((n_hi, n_lo) + chunk, BF16),
            jax.ShapeDtypeStruct((8, features), F32),
        ),
        in_specs=[ANY] * 3 + [VMEM] * 11,
        out_specs=(VMEM, VMEM, ANY, ANY, VMEM),
        scratch_shapes=[
            pltpu.VMEM(d_qkv.shape, BF16),
            pltpu.VMEM(nall.shape, BF16),
            pltpu.VMEM(dn_part.shape, BF16),
            pltpu.VMEM((wide, features), BF16),
            pltpu.VMEM((wide, features), F32),
            pltpu.VMEM((n_hi, n_lo) + chunk, BF16),
            pltpu.VMEM((features, features), BF16),
            pltpu.VMEM((n_lo, n_hi) + chunk, BF16),
            pltpu.VMEM((n_hi,) + chunk, BF16),
            pltpu.VMEM((n_hi,) + chunk, BF16),
            pltpu.VMEM((n_hi, n_lo) + chunk, BF16),
            pltpu.VMEM((n_hi, n_lo) + mlp_own.shape, BF16),
            pltpu.VMEM(tokens.shape, F32),
            pltpu.VMEM((2,) + tokens.shape, BF16),
            pltpu.VMEM((2,) + tokens.shape, BF16),
            pltpu.VMEM(tokens.shape, BF16),
            pltpu.VMEM(tokens.shape, BF16),
            pltpu.VMEM((2,) + tokens.shape, BF16),
            pltpu.VMEM(tokens.shape, BF16),
            pltpu.VMEM(tokens.shape, BF16),
            pltpu.VMEM((2, 8, features), F32),
            pltpu.VMEM((n_lo, 8, features), F32),
            pltpu.VMEM((n_hi, 8, features), F32),
            pltpu.VMEM((2, 8, features), F32),
            dma((3,)),
            dma((n_lo, n_hi)), dma((n_lo, n_hi)),
            dma((n_lo, n_hi)), dma((n_lo, n_hi)),
            dma((n_hi,)), dma((n_hi,)),
            dma((n_lo, n_hi)), dma((n_lo, n_hi)),
            dma((2, CHUNKS)), dma((2, CHUNKS)),
            dma((CHUNKS,)), dma((CHUNKS,)),
            dma((CHUNKS,)), dma((CHUNKS,)),
            dma((CHUNKS,)), dma((CHUNKS,)),
            dma((n_lo + n_hi + 2,)), dma((n_lo + n_hi + 2,)),
            dma((2,)),
        ],
        compiler_params=pltpu.CompilerParams(collective_id=1, has_side_effects=True, vmem_limit_bytes=60 << 20),
        name="reduce_gradients",
    )(d_qkv, nall, dn_part, give, keep, qkv_weight_t, tokens, cot, ln_gain, out_bias, attn_grad,
    mlp_own, front_rows, gain_rows)


def widen_body(heads, mlp_all, joint_all, rows, qkv_t, attn, mlp_in, mlp_out, ln_gain, q_gain, k_gain, mlp_bias, out_bias):
    features = rows.shape[1]
    chunks = mlp_all.shape[0]
    chunk_rows = mlp_all.shape[1]
    per_grad = features // chunk_rows
    width = qkv_t.shape[0]
    cols = joint_all.shape[2]
    for o in range(chunks):
        low = o % per_grad * chunk_rows
        (mlp_in, mlp_out)[o // per_grad][low : low + chunk_rows, :] = mlp_all[o].astype(F32)
    for half in range(2):
        at = slice(half * cols, (half + 1) * cols)
        kinds = [(3 * h + i) * DH for h in range(heads) for i in range(2)] + [(3 * h + 2) * DH for h in range(heads)]
        for i, to in enumerate(kinds):
            qkv_t[to : to + DH, at] = joint_all[half, i * DH : (i + 1) * DH].astype(F32)
        attn[:, at] = joint_all[half, width:].astype(F32)
    mlp_bias[...] = rows[0:1, :].reshape(features)
    out_bias[...] = rows[1:2, :].reshape(features)
    ln_gain[...] = rows[2:3, :].reshape(features)
    for offset, ref in ((0, q_gain), (DH, k_gain)):
        parts = [rows[3:4, h * LANES + offset : h * LANES + offset + DH] for h in range(heads)]
        ref[...] = jnp.concatenate(parts, axis=1).reshape(heads * DH)


def widen(heads, width, mlp_all, joint_all, rows):
    features = rows.shape[1]
    head_width = heads * DH

    def out(*shape):
        return jax.ShapeDtypeStruct(shape, F32)

    return pl.pallas_call(
        functools.partial(widen_body, heads),
        out_shape=(
            out(width, features), out(head_width, features), out(features, features), out(features, features),
            out(features), out(head_width), out(head_width), out(features), out(features),
        ),
        in_specs=[VMEM] * 3,
        out_specs=(VMEM,) * 9,
        compiler_params=pltpu.CompilerParams(vmem_limit_bytes=40 << 20),
        name="widen_gradients",
    )(mlp_all, joint_all, rows)


def on_device(
    tokens, out_cotangent, ln_gain, qkv_weight, q_gain, k_gain, attn_out,
    mlp_in, mlp_bias, mlp_out, out_bias, image_len, image_group,
):
    tok_dev, features = tokens.shape
    strips = lax.axis_size("tensor")
    n_batch = lax.axis_size("batch")
    n_hi, n_lo = levels(n_batch)
    heads = q_gain.shape[0] // DH
    qkv_cols = qkv_weight.shape[1]

    weight_t = qkv_weight.T
    (qa, ka, va, do, u, r, mlp_part, dn_part, nall, call, *mlp_grad, front_rows) = front(
        strips, n_batch, tokens, out_cotangent, ln_gain, weight_t, q_gain, k_gain, attn_out, mlp_in, mlp_bias, mlp_out
    )

    def along_lo(x, m):
        pairs = [(h * n_lo + i, h * n_lo + (i + m) % n_lo) for h in range(n_hi) for i in range(n_lo)]
        return lax.ppermute(x, "batch", pairs)

    def along_hi(x, k):
        pairs = [(h * n_lo + i, (h + k) % n_hi * n_lo + i) for h in range(n_hi) for i in range(n_lo)]
        return lax.ppermute(x, "batch", pairs)

    def add(first, others):
        total = first.astype(F32)
        for other in others:
            total = total + other.astype(F32)
        return total.astype(BF16)

    lo_got = [along_lo(mlp_grad[m], m) for m in range(1, n_lo)]
    qb, dob, give, keep, attn_grad = attn_fwd(image_len, image_group, qa, ka, va, do, attn_out, mlp_part, call)
    lo_sum = [add(mlp_grad[0][k], [got[k] for got in lo_got]) for k in range(n_hi)]
    hi_got = [along_hi(lo_sum[k], k) for k in range(1, n_hi)]
    d_qkv, gain_rows = attn_bwd(image_len, image_group, qb, ka, va, dob, u, r, q_gain, k_gain)
    mlp_own = add(lo_sum[0], hi_got)
    output, input_grad, mlp_all, joint_all, rows = back(
        n_batch, d_qkv, nall, dn_part, give, keep, weight_t, tokens, out_cotangent, ln_gain, out_bias, attn_grad,
        mlp_own, front_rows, gain_rows,
    )
    qkv_t, attn, mlp_in_grad, mlp_out_grad, ln, q, k, bias, out_bias_grad = widen(
        heads, qkv_cols, mlp_all.reshape((n_batch,) + mlp_all.shape[2:]), joint_all.reshape(2, features, -1), rows
    )
    return output, input_grad, ln, qkv_t.T, q, k, attn, mlp_in_grad, bias, mlp_out_grad, out_bias_grad


def solution(mesh):
    rows, cols, first = P(("batch", "tensor"), None), P(None, "tensor"), P("tensor", None)
    return jax.shard_map(
        on_device,
        mesh=mesh,
        in_specs=(rows, rows, P(), cols, P("tensor"), P("tensor"), first, cols, P("tensor"), first, P(), P(), P()),
        out_specs=(rows, rows, P(), cols, P("tensor"), P("tensor"), first, cols, P("tensor"), first, P()),
        check_vma=False,
    )
```

```python
import functools

import jax
import jax.numpy as jnp
from jax import lax
from jax.experimental import pallas as pl
from jax.experimental.pallas import tpu as pltpu
from jax.sharding import PartitionSpec as P

DH = 64
LANES = 128
WIN = 64
ALIGN = 16
LOG2E = 1.4426950408889634
epsilon = 1e-06
F32 = jnp.float32
BF16 = jnp.bfloat16
VMEM = pl.BlockSpec(memory_space=pltpu.VMEM)
SMEM = pl.BlockSpec(memory_space=pltpu.SMEM)
ANY = pl.BlockSpec(memory_space=pl.ANY)


def nn(left, right):
    return lax.dot_general(left, right, (((1,), (0,)), ((), ())), preferred_element_type=F32)


def nt(left, right):
    return lax.dot_general(left, right, (((1,), (1,)), ((), ())), preferred_element_type=F32)


def tn(left, right):
    return lax.dot_general(left, right, (((0,), (0,)), ((), ())), preferred_element_type=F32)


def row_of(vector):
    return vector[...].astype(F32).reshape(1, -1)


def pair_row(q_vector, k_vector, heads):
    q, k = row_of(q_vector), row_of(k_vector)
    parts = []
    for h in range(heads):
        parts += [q[:, h * DH : (h + 1) * DH], k[:, h * DH : (h + 1) * DH]]
    return jnp.concatenate(parts, axis=1)


def half_sums():
    row = lax.broadcasted_iota(jnp.int32, (LANES, LANES), 0) // DH
    col = lax.broadcasted_iota(jnp.int32, (LANES, LANES), 1) // DH
    return jnp.where(row == col, 1.0, 0.0).astype(BF16)


def left_half(rows):
    return lax.broadcasted_iota(jnp.int32, (rows, LANES), 1) < DH


def find_segments(len_ref, group_ref, seg_ref, strips, tok_dev):
    group = lax.axis_index("batch")

    def entry(i, carry):
        count, run = carry
        rows = jnp.where(group_ref[i] == group, len_ref[i] // strips, 0)

        @pl.when(rows > 0)
        def _():
            seg_ref[0, count] = run
            seg_ref[1, count] = run + rows

        return count + jnp.where(rows > 0, 1, 0), run + rows

    count, run = lax.fori_loop(0, len_ref.shape[0], entry, (jnp.int32(0), jnp.int32(0)))

    @pl.when(run < tok_dev)
    def _():
        seg_ref[0, count] = run
        seg_ref[1, count] = tok_dev

    return count + jnp.where(run < tok_dev, 1, 0)


def window(start, end, first, i, tok_dev):
    nominal = first + WIN * i
    at = pl.multiple_of(jnp.minimum(nominal, tok_dev - WIN), ALIGN)
    return at, jnp.maximum(start, nominal) - at, jnp.minimum(end, nominal + WIN) - at


def row_mask(low, high, strips, win=WIN, width=LANES):
    j = lax.broadcasted_iota(jnp.int32, (strips, win, width), 1).reshape(strips * win, width)
    return (j >= low) & (j < high)


def tile(ref, at, h, win=WIN):
    strips = ref.shape[0]
    return ref[:, pl.ds(at, win), h * LANES : (h + 1) * LANES].reshape(strips * win, LANES)


def put_tile(ref, at, h, mask, value, win=WIN, width=LANES):
    strips = ref.shape[0]
    where = (slice(None), pl.ds(at, win), slice(h * LANES, h * LANES + width))
    old = ref[where].reshape(strips * win, width)
    ref[where] = jnp.where(mask, value.astype(ref.dtype), old).reshape(strips, win, width)


def for_segments(len_ref, group_ref, seg, strips, tok_dev, small, middle, large):
    count = find_segments(len_ref, group_ref, seg, strips, tok_dev)
    big = middle_rows(tok_dev)

    def segment(index, _):
        start, end = seg[0, index], seg[1, index]
        first = (start // ALIGN) * ALIGN
        windows = (end - first + WIN - 1) // WIN
        fits = end - first <= big

        @pl.when(windows == 1)
        def _():
            small(*window(start, end, first, 0, tok_dev))

        @pl.when((windows > 1) & fits)
        def _():
            at = pl.multiple_of(jnp.minimum(first, tok_dev - big), ALIGN)
            middle(at, start - at, end - at)

        @pl.when(jnp.logical_not(fits))
        def _():
            large(start, end, first, windows)

        return 0

    lax.fori_loop(0, count, segment, 0)


def middle_rows(tok_dev):
    return min(tok_dev, tok_dev // 2 + ALIGN)


def attn_fwd_body(
    heads, len_ref, group_ref, qa, ka, va, do, qb, dob, ho, seg, acc,
):
    strips, tok_dev = qa.shape[0], qa.shape[1]
    zero = jnp.zeros((), BF16)
    big = middle_rows(tok_dev)

    def finish(at, low, high, totals, win=WIN):
        rows = strips * win
        mask = row_mask(low, high, strips, win)
        lane = lax.broadcasted_iota(jnp.int32, (rows, LANES), 1)
        left = lane < DH
        outs = []
        for h in range(heads):
            total = totals[h]
            rows_sum = jnp.where(left, pltpu.roll(total, DH, 1), total)
            out = jnp.where(left, total / rows_sum, 0.0)
            log_sum = jnp.log2(rows_sum)
            d_out = tile(do, at, h, win).astype(F32)
            delta = jnp.sum(out * d_out, axis=-1, keepdims=True)
            log_hi = log_sum.astype(BF16).astype(F32)
            delta_hi = delta.astype(BF16).astype(F32)
            q = tile(qa, at, h, win).astype(F32)
            q = jnp.where(lane == DH, -log_hi, jnp.where(lane == DH + 1, log_hi - log_sum, q))
            d_out = jnp.where(lane == DH, -delta_hi, jnp.where(lane == DH + 1, delta_hi - delta, d_out))
            put_tile(qb, at, h, mask, q, win)
            put_tile(dob, at, h, mask, d_out, win)
            outs.append(out)
        if heads % 2:
            outs.append(jnp.zeros_like(outs[0]))
        for b in range(len(outs) // 2):
            put_tile(ho, at, b, mask, jnp.where(left, outs[2 * b], pltpu.roll(outs[2 * b + 1], DH, 1)), win)

    def products(at_q, at_k, k_mask, win_q=WIN, win_k=WIN):
        scores = [nt(tile(qa, at_q, h, win_q), tile(ka, at_k, h, win_k)) for h in range(heads)]
        weights = [jnp.exp2(s).astype(BF16) for s in scores]
        return [nn(weights[h], jnp.where(k_mask, tile(va, at_k, h, win_k), zero)) for h in range(heads)]

    def small(at, low, high):
        finish(at, low, high, products(at, at, row_mask(low, high, strips)))

    def middle(at, low, high):
        def add(at_k, k_mask, win, first=False):
            for h, new in enumerate(products(at, at_k, k_mask, big, win)):
                acc[h] = new if first else acc[h] + new

        rest = big % WIN
        base = at + big - rest
        if rest:
            add(base, row_mask(low - (big - rest), high - (big - rest), strips, rest), rest, True)
        else:
            acc[...] = jnp.zeros_like(acc)

        def k_window(k, _):
            add(pl.multiple_of(at + k * WIN, ALIGN), row_mask(low - k * WIN, high - k * WIN, strips), WIN)
            return 0

        lax.fori_loop(0, big // WIN, k_window, 0)

        def total(h, offset, win):
            return acc[h].reshape(strips, big, LANES)[:, offset : offset + win].reshape(strips * win, LANES)

        for w in range(big // WIN):
            offset = w * WIN
            finish(
                pl.multiple_of(at + offset, ALIGN), low - offset, high - offset, [total(h, offset, WIN) for h in range(heads)]
            )
        if rest:
            offset = big - rest
            finish(base, low - offset, high - offset, [total(h, offset, rest) for h in range(heads)], rest)

    def large(start, end, first, windows):
        def q_window(i, _):
            at_q, low_q, high_q = window(start, end, first, i, tok_dev)
            rows = strips * WIN
            acc[:, :rows] = jnp.zeros((heads, rows, LANES), F32)

            def k_window(k, _):
                at_k, low_k, high_k = window(start, end, first, k, tok_dev)
                for h, new in enumerate(products(at_q, at_k, row_mask(low_k, high_k, strips))):
                    acc[h, :rows] += new
                return 0

            lax.fori_loop(0, windows, k_window, 0)
            finish(at_q, low_q, high_q, [acc[h, :rows] for h in range(heads)])
            return 0

        lax.fori_loop(0, windows, q_window, 0)

    for_segments(len_ref, group_ref, seg, strips, tok_dev, small, middle, large)


def attn_fwd(image_len, image_group, qa, ka, va, do):
    strips, tok_dev, width = qa.shape
    heads = width // LANES
    packed = (heads + 1) // 2 * LANES
    like = jax.ShapeDtypeStruct(qa.shape, BF16)
    return pl.pallas_call(
        functools.partial(attn_fwd_body, heads),
        out_shape=(like, like, jax.ShapeDtypeStruct((strips, tok_dev, packed), BF16)),
        in_specs=[SMEM, SMEM] + [VMEM] * 4,
        out_specs=(VMEM,) * 3,
        scratch_shapes=[
            pltpu.SMEM((2, image_len.shape[0] + 1), jnp.int32),
            pltpu.VMEM((heads, strips * middle_rows(tok_dev), LANES), F32),
        ],
        compiler_params=pltpu.CompilerParams(vmem_limit_bytes=60 << 20),
        cost_estimate=pl.CostEstimate(flops=8 * 10**9, bytes_accessed=30 * 10**6, transcendentals=8 * 10**6),
        name="attention_forward",
    )(image_len, image_group, qa, ka, va, do)


def attn_bwd_body(
    heads, len_ref, group_ref, qb, ka, va, dob, u_hbm, r_hbm, q_gain, k_gain,
    d_qkv, gain_grad, seg, k_turned, dq_turned, dk_acc, dv_acc, dq, dk, dv, u_rows, r_rows, sems,
):
    strips, tok_dev = qb.shape[0], qb.shape[1]
    loads = [pltpu.make_async_copy(u_hbm, u_rows, sems.at[0]), pltpu.make_async_copy(r_hbm, r_rows, sems.at[1])]
    for load in loads:
        load.start()
    zero = jnp.zeros((), BF16)
    big = middle_rows(tok_dev)

    def products(at_q, at_k, q_mask, k_turned_of, win_q=WIN, win_k=WIN):
        every = range(heads)
        qs = [tile(qb, at_q, h, win_q) for h in every]
        d_outs = [jnp.where(q_mask, tile(dob, at_q, h, win_q), zero) for h in every]
        scores = [nt(tile(ka, at_k, h, win_k), qs[h]) for h in every]
        d_weights = [nt(tile(va, at_k, h, win_k), d_outs[h]) for h in every]
        weights = [jnp.exp2(s) for s in scores]
        d_scores = [(weights[h] * d_weights[h]).astype(BF16) for h in every]
        dv_new = [nn(weights[h].astype(BF16), d_outs[h]) for h in every]
        dk_new = [nn(d_scores[h], qs[h]) for h in every]
        dq_new = [nn(k_turned_of(h), d_scores[h]) for h in every]
        return dq_new, dk_new, dv_new

    def turned(h, at_k, mask, win=WIN):
        return jnp.where(mask, tile(ka, at_k, h, win), zero).T[:DH]

    def small(at, low, high):
        mask = row_mask(low, high, strips)
        half = row_mask(low, high, strips, width=DH)
        dq_t, dk_new, dv_new = products(at, at, mask, lambda h: turned(h, at, mask))
        for h in range(heads):
            put_tile(dq, at, h, half, dq_t[h].T, width=DH)
            put_tile(dk, at, h, mask, dk_new[h])
            put_tile(dv, at, h, mask, dv_new[h])

    def middle(at, low, high):
        mask = row_mask(low, high, strips, big)
        for h in range(heads):
            k_turned[h] = turned(h, at, mask, big)

        def q_window(at_q, low_q, high_q, win, first=False):
            mask_q = row_mask(low_q, high_q, strips, win)
            half = row_mask(low_q, high_q, strips, win, DH)
            dq_t, dk_new, dv_new = products(at_q, at, mask_q, lambda h: k_turned[h], win, big)
            for h in range(heads):
                put_tile(dq, at_q, h, half, dq_t[h].T, win, DH)
                dk_acc[h] = dk_new[h] if first else dk_acc[h] + dk_new[h]
                dv_acc[h] = dv_new[h] if first else dv_acc[h] + dv_new[h]

        rest = big % WIN
        offset = big - rest
        if rest:
            q_window(at + offset, low - offset, high - offset, rest, True)
        else:
            dk_acc[...] = jnp.zeros_like(dk_acc)
            dv_acc[...] = jnp.zeros_like(dv_acc)

        def each(i, _):
            q_window(pl.multiple_of(at + i * WIN, ALIGN), low - i * WIN, high - i * WIN, WIN)
            return 0

        lax.fori_loop(0, big // WIN, each, 0)
        for h in range(heads):
            put_tile(dk, at, h, mask, dk_acc[h], big)
            put_tile(dv, at, h, mask, dv_acc[h], big)

    def large(start, end, first, windows):
        rows = strips * WIN

        def clear(i, _):
            for h in range(heads):
                dq_turned[h, i] = jnp.zeros(dq_turned.shape[2:], F32)
            return 0

        lax.fori_loop(0, windows, clear, 0)

        def k_window(k, _):
            at_k, low_k, high_k = window(start, end, first, k, tok_dev)
            mask_k = row_mask(low_k, high_k, strips)
            for h in range(heads):
                k_turned[h, :, :rows] = turned(h, at_k, mask_k)
            dk_acc[:, :rows] = jnp.zeros((heads, rows, LANES), F32)
            dv_acc[:, :rows] = jnp.zeros((heads, rows, LANES), F32)

            def q_window(i, _):
                at_q, low_q, high_q = window(start, end, first, i, tok_dev)
                mask_q = row_mask(low_q, high_q, strips)
                dq_t, dk_new, dv_new = products(at_q, at_k, mask_q, lambda h: k_turned[h, :, :rows])
                for h in range(heads):
                    dq_turned[h, i] += dq_t[h]
                    dk_acc[h, :rows] += dk_new[h]
                    dv_acc[h, :rows] += dv_new[h]
                return 0

            lax.fori_loop(0, windows, q_window, 0)
            for h in range(heads):
                put_tile(dk, at_k, h, mask_k, dk_acc[h, :rows])
                put_tile(dv, at_k, h, mask_k, dv_acc[h, :rows])
            return 0

        lax.fori_loop(0, windows, k_window, 0)

        def q_out(i, _):
            at_q, low_q, high_q = window(start, end, first, i, tok_dev)
            half = row_mask(low_q, high_q, strips, width=DH)
            for h in range(heads):
                put_tile(dq, at_q, h, half, dq_turned[h, i].T, width=DH)
            return 0

        lax.fori_loop(0, windows, q_out, 0)

    for_segments(len_ref, group_ref, seg, strips, tok_dev, small, middle, large)

    rows = strips * WIN
    left = left_half(rows)
    sums = half_sums()
    gains = pair_row(q_gain, k_gain, heads)
    for load in loads:
        load.wait()

    def chunk(i, totals):
        at = pl.multiple_of(i * WIN, WIN)
        scaled, new_totals, us = [], [], []
        for h in range(heads):
            cols = slice(h * LANES, (h + 1) * LANES)
            d_q, d_k = tile(dq, at, h), tile(dk, at, h) * (1.0 / LOG2E)
            both = jnp.where(left, d_q * DH ** (-0.5), pltpu.roll(d_k, DH, 1))
            u = tile(u_rows, at, h).astype(F32)
            new_totals.append(totals[h] + jnp.sum(both * u, axis=0, keepdims=True))
            scaled.append(both * gains[:, cols])
            us.append(u)
        stacked = [s.astype(BF16) for s in scaled] + [(scaled[h] * us[h]).astype(BF16) for h in range(heads)]
        means = nn(jnp.concatenate(stacked, axis=0), sums) * (1.0 / DH)
        parts = []
        for h in range(heads):
            mean = means[h * rows : (h + 1) * rows]
            mean_u = means[(heads + h) * rows : (heads + h + 1) * rows]
            parts.append((scaled[h] - mean - us[h] * mean_u) * tile(r_rows, at, h).astype(F32))
        values = [tile(dv, at, h) for h in range(heads)]
        if heads % 2:
            values.append(jnp.zeros_like(values[0]))
        for b in range(len(values) // 2):
            parts.append(jnp.where(left, values[2 * b], pltpu.roll(values[2 * b + 1], DH, 1)))
        for b, part in enumerate(parts):
            d_qkv[:, pl.ds(at, WIN), b * LANES : (b + 1) * LANES] = part.astype(BF16).reshape(strips, WIN, LANES)
        return tuple(new_totals)

    totals = lax.fori_loop(0, tok_dev // WIN, chunk, tuple(jnp.zeros((1, LANES), F32) for _ in range(heads)))
    gain_grad[...] = jnp.zeros_like(gain_grad)
    for h in range(heads):
        gain_grad[0:1, h * LANES : (h + 1) * LANES] = totals[h]


def attn_bwd(image_len, image_group, qb, ka, va, dob, u, r, q_gain, k_gain):
    strips, tok_dev, width = qb.shape
    heads = width // LANES
    blocks = heads + (heads + 1) // 2
    rows = strips * WIN
    big = strips * middle_rows(tok_dev)
    windows = tok_dev // WIN + 1
    full = pltpu.VMEM((strips, tok_dev, width), F32)
    return pl.pallas_call(
        functools.partial(attn_bwd_body, heads),
        out_shape=(
            jax.ShapeDtypeStruct((strips, tok_dev, blocks * LANES), BF16),
            jax.ShapeDtypeStruct((8, width), F32),
        ),
        in_specs=[SMEM, SMEM] + [VMEM] * 4 + [ANY] * 2 + [VMEM] * 2,
        out_specs=(VMEM, VMEM),
        scratch_shapes=[
            pltpu.SMEM((2, image_len.shape[0] + 1), jnp.int32),
            pltpu.VMEM((heads, DH, big), BF16),
            pltpu.VMEM((heads, windows, DH, rows), F32),
            pltpu.VMEM((heads, big, LANES), F32),
            pltpu.VMEM((heads, big, LANES), F32),
            full, full, full,
            pltpu.VMEM(u.shape, BF16),
            pltpu.VMEM(r.shape, BF16),
            pltpu.SemaphoreType.DMA((2,)),
        ],
        compiler_params=pltpu.CompilerParams(vmem_limit_bytes=60 << 20),
        cost_estimate=pl.CostEstimate(flops=16 * 10**9, bytes_accessed=30 * 10**6, transcendentals=8 * 10**6),
        name="attention_backward",
    )(image_len, image_group, qb, ka, va, dob, u, r, q_gain, k_gain)


CHUNKS = 4


def by_kind(weight_t, heads, rows):
    parts = [weight_t[3 * h * DH : (3 * h + 2) * DH, :] for h in range(heads)]
    parts += [weight_t[(3 * h + 2) * DH : (3 * h + 3) * DH, :] for h in range(heads)]
    spare = rows - weight_t.shape[0]
    if spare:
        parts.append(jnp.zeros((spare, weight_t.shape[1]), BF16))
    return jnp.concatenate(parts, axis=0)


def remote(src, dst, send, recv, device):
    return pltpu.make_async_remote_copy(
        src_ref=src, dst_ref=dst, send_sem=send, recv_sem=recv, device_id=device, device_id_type=pl.DeviceIdType.MESH
    )


def lo_rows(features):
    return 2 * features * 2 // 3


def front_body(
    heads, n_hi, n_lo, tokens, cot, ln_gain, qkv_weight_t, q_gain, k_gain, attn_out, mlp_in, mlp_bias, mlp_out,
    qa_out, ka_out, va_out, do_out, u_out, r_out, mlp_part_out, dn_part_out, nall_out, call_out,
    *rest,
):
    (rows_out, both, wide, narrow, qkv_pad, mlp_out_t, mlp_in_t, attn_out_t, g_in, g_out,
     send_sem, recv_sem, save_sem) = rest[-13:]
    lo_first, hi_first = rest[:n_lo], rest[n_lo : n_lo + n_hi]
    batch, me = lax.axis_index("batch"), lax.axis_index("tensor")
    sibling = me + 1 - 2 * (me % 2)
    across = (me + 2) % 4
    chip, far_chip = me // 2, 1 - me // 2
    tok_dev = tokens.shape[0]
    step = tok_dev // CHUNKS
    rows = 2 * step
    features = tokens.shape[1]
    heads_wide = heads * LANES

    def rows_of(c):
        return pl.ds(pl.multiple_of(c * step, step), step)

    def move(kind, route, c, strip, to):
        part = both.at[kind, strip, rows_of(c)]
        return remote(part, part, send_sem.at[kind, route, c], recv_sem.at[kind, route, c], (batch, to))

    barrier = pltpu.get_barrier_semaphore()
    for other in (sibling, across):
        pl.semaphore_signal(barrier, inc=1, device_id=(batch, other), device_id_type=pl.DeviceIdType.MESH)
    gain = row_of(ln_gain)
    gains = pair_row(q_gain, k_gain, heads)

    def norm_chunk(c):
        both[0, me, rows_of(c)] = cot[rows_of(c)]
        x = tokens[rows_of(c)].astype(F32)
        centred = x - jnp.mean(x, axis=-1, keepdims=True)
        variance = jnp.mean(centred * centred, axis=-1, keepdims=True)
        both[1, me, rows_of(c)] = (centred * lax.rsqrt(variance + epsilon) * gain).astype(BF16)

    norm_chunk(0)
    pl.semaphore_wait(barrier, 2)

    def first_sends(c, _):
        for kind in range(2):
            move(kind, 1, c, me, across).start()
            move(kind, 0, c, me, sibling).start()

        @pl.when(c + 1 < CHUNKS)
        def _():
            norm_chunk(c + 1)

        return 0

    lax.fori_loop(0, CHUNKS, first_sends, 0)

    g_in[...] = jnp.zeros_like(g_in)
    g_out[...] = jnp.zeros_like(g_out)
    rows_out[...] = jnp.zeros_like(rows_out)
    total = jnp.zeros((1, features), F32)
    for c in range(CHUNKS):
        total += jnp.sum(cot[c * step : (c + 1) * step].astype(F32), axis=0, keepdims=True)
    rows_out[1:2, :] = total
    qkv_pad[...] = by_kind(qkv_weight_t, heads, qkv_pad.shape[1]).T
    mlp_out_t[...] = mlp_out[...].T
    mlp_in_t[...] = mlp_in[...].T
    for h in range(heads):
        part = attn_out[h * DH : (h + 1) * DH, :]
        attn_out_t[:, h * LANES : (h + 1) * LANES] = jnp.concatenate([part, jnp.zeros_like(part)], axis=0).T

    left = left_half(rows)
    sums = half_sums()
    bias = row_of(mlp_bias)

    def saves(c, at_chip):
        strips = pl.ds(2 * at_chip, 2)
        where = rows_of(c)
        index = at_chip * CHUNKS + c
        pairs = [(narrow.at[a, strips, where], ref.at[strips, where]) for a, ref in enumerate(
            (qa_out, ka_out, va_out, do_out, u_out, r_out))]
        pairs += [(wide.at[a, strips, where], ref.at[strips, where]) for a, ref in enumerate(
            (mlp_part_out, dn_part_out))]
        pairs += [(both.at[1, strips, where], nall_out.at[strips, where]), (both.at[0, strips, where], call_out.at[strips, where])]
        return [pltpu.make_async_copy(a, b, save_sem.at[n, index]) for n, (a, b) in enumerate(pairs)]

    def unit(i, _):
        far = i >= CHUNKS
        c = i % CHUNKS
        at_chip = jnp.where(far, far_chip, chip)

        @pl.when(jnp.logical_not(far))
        def _():
            for kind in range(2):
                move(kind, 0, c, sibling, sibling).wait_recv()

        def pass_on(k):
            for kind in range(2):
                move(kind, 1, k, across, across).wait_recv()
                move(kind, 2, k, across, sibling).start()

        @pl.when(i == CHUNKS - 1)
        def _():
            pass_on(0)

        @pl.when(i == CHUNKS)
        def _():
            pass_on(1)

        @pl.when(i > CHUNKS + 1)
        def _():
            pass_on(c)

        @pl.when(far)
        def _():
            for kind in range(2):
                move(kind, 2, c, across + 1 - 2 * (across % 2), sibling).wait_recv()

        strips = pl.ds(2 * at_chip, 2)
        where = rows_of(c)
        n = both[1, strips, where].reshape(rows, features)
        d = both[0, strips, where].reshape(rows, features)

        def save(ref, a, h, value):
            ref[a, strips, where, h * LANES : (h + 1) * LANES] = value.astype(BF16).reshape(2, step, LANES)

        qkv = nn(n, qkv_pad[...])

        def block(b):
            return qkv[:, b * LANES : (b + 1) * LANES]

        def stacked_means(parts):
            stacked = jnp.concatenate([p.astype(BF16) for p in parts], axis=0)
            means = nn(stacked, sums) * (1.0 / DH)
            return [means[h * rows : (h + 1) * rows] for h in range(heads)]

        pairs = [block(h) for h in range(heads)]
        means = stacked_means(pairs)
        centred = [pairs[h] - means[h] for h in range(heads)]
        variances = stacked_means([x * x for x in centred])
        for h in range(heads):
            rstd = lax.rsqrt(variances[h] + epsilon)
            u = centred[h] * rstd
            scaled = u * gains[:, h * LANES : (h + 1) * LANES]
            save(narrow, 0, h, jnp.where(left, scaled * (DH ** (-0.5) * LOG2E), 0.0))
            save(narrow, 1, h, jnp.where(left, pltpu.roll(scaled, DH, 1), 1.0))
            value = block(heads + h // 2)
            save(narrow, 2, h, jnp.where(left, pltpu.roll(value, DH, 1) if h % 2 else value, 1.0))
            save(narrow, 4, h, u)
            save(narrow, 5, h, rstd)
        narrow[3, strips, where] = nn(d, attn_out_t[...]).astype(BF16).reshape(2, step, heads_wide)

        hidden = nn(n, mlp_in[...]) + bias
        cdf = 0.5 + 0.5 * lax.erf(hidden * 0.7071067811865476)
        act = (hidden * cdf).astype(BF16)
        slope = cdf + hidden * (0.3989422804014327 * jnp.exp(hidden * hidden * -0.5))
        wide[0, strips, where] = nn(act, mlp_out[...]).astype(BF16).reshape(2, step, features)
        d_hidden = nn(d, mlp_out_t[...]) * slope
        d_low = d_hidden.astype(BF16)
        rows_out[0:1, :] += jnp.sum(d_low.astype(F32), axis=0, keepdims=True)
        wide[1, strips, where] = nn(d_low, mlp_in_t[...]).astype(BF16).reshape(2, step, features)
        g_out[...] += tn(act, d)
        g_in[...] += tn(n, d_low)
        for copy in saves(c, at_chip):
            copy.start()
        return 0

    lax.fori_loop(0, 2 * CHUNKS, unit, 0)

    hi, lo = batch // n_lo, batch % n_lo
    for o in range(n_hi * n_lo):
        at_hi = (o // n_lo - hi + n_hi) % n_hi
        at_lo = (o % n_lo - lo + n_lo) % n_lo
        for first, part in ((0, lo_first), (lo_rows(features), hi_first)):
            chunk_rows = part[0].shape[1]
            row = first + o * chunk_rows
            source = (g_in, g_out)[row // features]
            row = row % features
            low = source[row : row + chunk_rows, :].astype(BF16)
            slot, place = (at_lo, at_hi) if first == 0 else (at_hi, at_lo)
            for m in range(len(part)):

                @pl.when(slot == m)
                def _():
                    part[m][place] = low

    grown = g_in[...] * mlp_in[...].astype(F32)
    grown_hi = grown.astype(BF16)
    ones = jnp.ones((8, grown.shape[1]), BF16)
    rows_out[2:3, :] = (nt(ones, grown_hi) + nt(ones, (grown - grown_hi.astype(F32)).astype(BF16)))[0:1]

    def finish(i, _):
        for copy in saves(i % CHUNKS, i // CHUNKS):
            copy.wait()
        return 0

    lax.fori_loop(0, 2 * CHUNKS, finish, 0)

    def sent(c, _):
        for kind in range(2):
            move(kind, 0, c, me, sibling).wait_send()
            move(kind, 1, c, me, across).wait_send()
            move(kind, 2, c, across, sibling).wait_send()
        return 0

    lax.fori_loop(0, CHUNKS, sent, 0)


def front(strips, n_batch, tokens, cot, ln_gain, qkv_weight_t, q_gain, k_gain, attn_out, mlp_in, mlp_bias, mlp_out):
    tok_dev, features = tokens.shape
    heads = q_gain.shape[0] // DH
    width = heads * LANES
    hidden = mlp_in.shape[1]
    blocks = heads + (heads + 1) // 2
    n_hi, n_lo = levels(n_batch)
    like = jax.ShapeDtypeStruct((strips, tok_dev, width), BF16)
    rows = jax.ShapeDtypeStruct((strips, tok_dev, features), BF16)
    return pl.pallas_call(
        functools.partial(front_body, heads, n_hi, n_lo),
        out_shape=(like,) * 6 + (rows,) * 4 + (
            jax.ShapeDtypeStruct((n_hi, lo_rows(features) // n_batch, features), BF16),
        ) * n_lo + (
            jax.ShapeDtypeStruct((n_lo, (2 * features - lo_rows(features)) // n_batch, features), BF16),
        ) * n_hi + (jax.ShapeDtypeStruct((8, features), F32),),
        in_specs=[VMEM] * 10,
        out_specs=(ANY,) * 10 + (VMEM,) * (n_lo + n_hi + 1),
        scratch_shapes=[
            pltpu.VMEM((2, strips, tok_dev, features), BF16),
            pltpu.VMEM((2, strips, tok_dev, features), BF16),
            pltpu.VMEM((6, strips, tok_dev, width), BF16),
            pltpu.VMEM((features, blocks * LANES), BF16),
            pltpu.VMEM((features, hidden), BF16),
            pltpu.VMEM((hidden, features), BF16),
            pltpu.VMEM((features, width), BF16),
            pltpu.VMEM((features, hidden), F32),
            pltpu.VMEM((hidden, features), F32),
            pltpu.SemaphoreType.DMA((2, 3, CHUNKS)),
            pltpu.SemaphoreType.DMA((2, 3, CHUNKS)),
            pltpu.SemaphoreType.DMA((10, 2 * CHUNKS)),
        ],
        compiler_params=pltpu.CompilerParams(collective_id=0, has_side_effects=True, vmem_limit_bytes=60 << 20),
        name="gather_and_project",
    )(tokens, cot, ln_gain, qkv_weight_t, q_gain, k_gain, attn_out, mlp_in, mlp_bias, mlp_out)


def back_body(
    heads, n_hi, n_lo, d_qkv_hbm, nall_hbm, dn_part_hbm, ho_hbm, call_hbm, mlp_part_hbm, qkv_weight_t, attn_out, tokens, cot,
    ln_gain, out_bias, own_lo, own_hi, front_rows, gain_rows, output, input_grad, mlp_all_out, joint_all_out, rows_out,
    d_qkv, nall, dn_part, ho, call, mlp_part, weight_t, attn_pad, acc, attn_acc, joint, joint_low, joint_got, joint_sum,
    joint_got_hi, joint_all, mlp_all, near, core_give, core_got, x_give, x_got, vec, vec_lo, vec_hi, vec_pair,
    load_sem, mlp_z_s, mlp_z_r, mlp_y_s, mlp_y_r, joint_s, joint_r, hi_s, hi_r, all_z_s, all_z_r, all_y_s, all_y_r,
    core_s, core_r, x_s, x_r, vec_s, vec_r, save_sem,
):
    batch, me = lax.axis_index("batch"), lax.axis_index("tensor")
    hi, lo = batch // n_lo, batch % n_lo
    sibling = me + 1 - 2 * (me % 2)
    across = (me + 2) % 4
    far_sibling = (sibling + 2) % 4
    tok_dev, features = tokens.shape
    step = tok_dev // CHUNKS
    chunk_rows, half_cols = joint.shape[2], joint.shape[3]
    every_k, every_m = range(1, n_hi), range(1, n_lo)
    cut = chunk_rows // 2 // 16 * 16
    parts = [pl.ds(0, cut), pl.ds(cut, chunk_rows - cut)]

    sources = (
        (d_qkv_hbm, d_qkv), (nall_hbm, nall), (ho_hbm, ho), (call_hbm, call), (dn_part_hbm, dn_part), (mlp_part_hbm, mlp_part)
    )
    loads = [pltpu.make_async_copy(a, b, load_sem.at[i]) for i, (a, b) in enumerate(sources)]
    for load in loads:
        load.start()

    def hi_peer(k):
        return (hi + k + n_hi) % n_hi

    def lo_peer(m):
        return (lo + m + n_lo) % n_lo

    def to_hi(k):
        return (hi_peer(k) * n_lo + lo, me)

    def to_lo(m):
        return (hi * n_lo + lo_peer(m), me)

    barrier = pltpu.get_barrier_semaphore()
    peers = [to_hi(k) for k in every_k] + [to_lo(m) for m in every_m] + [(batch, sibling), (batch, across)]
    for peer in peers:
        pl.semaphore_signal(barrier, inc=1, device_id=peer, device_id_type=pl.DeviceIdType.MESH)
    mlp_all[hi, lo] = jnp.concatenate([own_lo[...], own_hi[...]], axis=0)
    pl.semaphore_wait(barrier, len(peers))

    def mlp_hop(s, up, origin):
        part = mlp_all.at[origin, lo]
        to = ((hi + (1 if up else -1) + n_hi) % n_hi * n_lo + lo, me)
        return remote(part, part, mlp_z_s.at[up, s], mlp_z_r.at[up, s], to)

    def mlp_send_hop(s, wait=False):
        for up in range(2):
            origin = hi - (s - 1) if up else hi + (s - 1)
            there = (origin >= 0) & (hi + 1 < n_hi) if up else (origin < n_hi) & (hi >= 1)

            @pl.when(there)
            def _():
                hop = mlp_hop(s, up, (origin + n_hi) % n_hi)
                hop.wait_send() if wait else hop.start()

    def mlp_wait_hop(s):
        for up in range(2):
            origin = hi - s if up else hi + s

            @pl.when((origin >= 0) if up else (origin < n_hi))
            def _():
                mlp_hop(s, up, (origin + n_hi) % n_hi).wait_recv()

    def mlp_lo(m, k, back=0):
        part = mlp_all.at[hi_peer(k), lo_peer(back)]
        return remote(part, part, mlp_y_s.at[m, k], mlp_y_r.at[m, k], to_lo(m))

    def mlp_send_lo(s):
        for m in every_m:
            for k, there in ((s, hi + s < n_hi), (n_hi - s, hi >= s)):

                @pl.when(there)
                def _():
                    mlp_lo(m, k).start()

    for m in every_m:
        mlp_lo(m, 0).start()
    mlp_send_hop(1)

    weight_t[...] = by_kind(qkv_weight_t, heads, weight_t.shape[0])
    head_width = attn_out.shape[0]
    attn_pad[:head_width] = attn_out[...]
    attn_pad[head_width:] = jnp.zeros((attn_pad.shape[0] - head_width, features), BF16)
    acc[...] = jnp.zeros_like(acc)
    attn_acc[...] = jnp.zeros_like(attn_acc)
    for load in loads[:4]:
        load.wait()

    def add_strip(i, _):
        acc[...] += tn(d_qkv[i], nall[i])
        attn_acc[...] += tn(ho[i], call[i])
        return 0

    lax.fori_loop(0, nall.shape[0], add_strip, 0)
    width = qkv_weight_t.shape[0]
    joint_low[:width] = acc[:width].astype(BF16)
    joint_low[width:] = attn_acc[:head_width].astype(BF16)
    per_half = features // chunk_rows
    for o in range(n_hi * n_lo):
        row = o % per_half * chunk_rows
        col = o // per_half * half_cols
        joint[o % n_lo, o // n_lo] = joint_low[row : row + chunk_rows, col : col + half_cols]

    def joint_lo(p, m, back=0):
        return remote(
            joint.at[lo_peer(m), :, parts[p]], joint_got.at[lo_peer(back), :, parts[p]], joint_s.at[m, p], joint_r.at[m, p], to_lo(m)
        )

    def joint_hi(p, k, back=0):
        return remote(
            joint_sum.at[hi_peer(k), parts[p]], joint_got_hi.at[hi_peer(back), parts[p]], hi_s.at[k, p], hi_r.at[k, p], to_hi(k)
        )

    def joint_sum_lo(p):
        for m in every_m:
            joint_lo(p, m, -m).wait_recv()
        total = joint[lo, :, parts[p]].astype(F32)
        for m in every_m:
            total = total + joint_got[lo_peer(m), :, parts[p]].astype(F32)
        joint_sum[:, parts[p]] = total.astype(BF16)
        for k in every_k:
            joint_hi(p, k).start()

    def all_hi(p, k, back=0):
        part = joint_all.at[lo, hi_peer(back), parts[p]]
        return remote(part, part, all_z_s.at[k, p], all_z_r.at[k, p], to_hi(k))

    def all_lo(p, m, back=0):
        part = joint_all.at[lo_peer(back), :, parts[p]]
        return remote(part, part, all_y_s.at[m, p], all_y_r.at[m, p], to_lo(m))

    def joint_sum_hi(p):
        total = joint_sum[hi, parts[p]].astype(F32)
        for k in every_k:
            joint_hi(p, k, -k).wait_recv()
            total = total + joint_got_hi[hi_peer(-k), parts[p]].astype(F32)
        joint_all[lo, hi, parts[p]] = total.astype(BF16)
        for k in every_k:
            all_hi(p, k).start()

    def joint_pass(p):
        for k in every_k:
            all_hi(p, k, -k).wait_recv()
        for m in every_m:
            all_lo(p, m).start()

    for m in every_m:
        joint_lo(0, m).start()

    ln_row = jnp.sum(acc[...] * weight_t[...].astype(F32), axis=0, keepdims=True)
    gain = row_of(ln_gain)
    vec_lo[lo] = front_rows[...]
    vec_lo[lo, 2:3, :] = (front_rows[2:3, :] + ln_row) / gain
    vec_lo[lo, 3:4, 0 : heads * LANES] = gain_rows[0:1, :]

    def vec_lo_move(m, back=0):
        part = vec_lo.at[lo_peer(back)]
        return remote(part, part, vec_s.at[m], vec_r.at[m], to_lo(m))

    def vec_hi_move(k, back=0):
        part = vec_hi.at[hi_peer(back)]
        return remote(part, part, vec_s.at[n_lo + k], vec_r.at[n_lo + k], to_hi(k))

    def vec_pair_move(i, to):
        return remote(vec.at[i], vec_pair.at[i], vec_s.at[n_lo + n_hi + i], vec_r.at[n_lo + n_hi + i], (batch, to))

    for m in every_m:
        vec_lo_move(m).start()
    mlp_wait_hop(1)
    mlp_send_hop(2)

    def rows_of(c):
        return pl.ds(pl.multiple_of(c * step, step), step)

    def partial_rows(which, strip, c):
        if which == 0:
            return nn(d_qkv[strip, rows_of(c)], weight_t[...]) + dn_part[strip, rows_of(c)].astype(F32)
        return nn(ho[strip, rows_of(c)], attn_pad[...]) + mlp_part[strip, rows_of(c)].astype(F32)

    def core_move(which, side, c):
        where = rows_of(c)
        return remote(
            core_give.at[which, side, where], core_got.at[which, side, where],
            core_s.at[which, side, c], core_r.at[which, side, c], (batch, sibling),
        )

    def x_move(which, c):
        where = rows_of(c)
        return remote(x_give.at[which, where], x_got.at[which, where], x_s.at[which, c], x_r.at[which, c], (batch, across))

    def far(which):
        def give(c, _):
            core_give[which, 0, rows_of(c)] = partial_rows(which, far_sibling, c).astype(BF16)
            core_move(which, 0, c).start()
            return 0

        def send(c, _):
            mine = partial_rows(which, across, c)
            core_move(which, 0, c).wait_recv()
            x_give[which, rows_of(c)] = (mine + core_got[which, 0, rows_of(c)].astype(F32)).astype(BF16)
            x_move(which, c).start()
            return 0

        lax.fori_loop(0, CHUNKS, give, 0)
        lax.fori_loop(0, CHUNKS, send, 0)

    def close(which):
        def give(c, _):
            core_give[which, 1, rows_of(c)] = partial_rows(which, sibling, c).astype(BF16)
            core_move(which, 1, c).start()
            return 0

        def keep(c, _):
            mine = partial_rows(which, me, c)
            core_move(which, 1, c).wait_recv()
            near[which, rows_of(c)] = mine + core_got[which, 1, rows_of(c)].astype(F32)
            return 0

        lax.fori_loop(0, CHUNKS, give, 0)
        lax.fori_loop(0, CHUNKS, keep, 0)

    for load in loads[4:]:
        load.wait()
    far(0)
    for m in every_m:
        joint_lo(1, m).start()
    far(1)
    joint_sum_lo(0)
    for s in range(2, n_hi - 1):
        mlp_wait_hop(s)
        mlp_send_hop(s + 1)
    close(0)
    joint_sum_lo(1)
    mlp_send_lo(1)
    close(1)

    for m in every_m:
        vec_lo_move(m, -m).wait_recv()
    total = vec_lo[0]
    for i in range(1, n_lo):
        total = total + vec_lo[i]
    vec_hi[hi] = total
    for k in every_k:
        vec_hi_move(k).start()

    joint_sum_hi(0)
    for s in range(2, n_hi - 1):
        mlp_send_lo(s)
    joint_sum_hi(1)
    if n_hi > 2:
        mlp_wait_hop(n_hi - 1)
        mlp_send_lo(n_hi - 1)

    for k in every_k:
        vec_hi_move(k, -k).wait_recv()
    total = vec_hi[0]
    for i in range(1, n_hi):
        total = total + vec_hi[i]
    vec[0] = total
    vec_pair_move(0, sibling).start()

    joint_pass(0)
    vec_pair_move(0, sibling).wait_recv()
    vec[1] = vec[0] + vec_pair[0]
    vec_pair_move(1, across).start()

    def last_rows(c, _):
        x_move(0, c).wait_recv()
        where = rows_of(c)
        d_normed = near[0, where] + x_got[0, where].astype(F32)
        x = tokens[where].astype(F32)
        centred = x - jnp.mean(x, axis=-1, keepdims=True)
        r = lax.rsqrt(jnp.mean(centred * centred, axis=-1, keepdims=True) + epsilon)
        xhat = centred * r
        e = d_normed * gain
        d_x = r * (e - jnp.mean(e, axis=-1, keepdims=True) - xhat * jnp.mean(e * xhat, axis=-1, keepdims=True))
        input_grad[where] = (cot[where].astype(F32) + d_x).astype(BF16)
        return 0

    lax.fori_loop(0, CHUNKS, last_rows, 0)
    joint_pass(1)
    bias = row_of(out_bias)

    def out_rows(c, _):
        x_move(1, c).wait_recv()
        where = rows_of(c)
        output[where] = (tokens[where].astype(F32) + near[1, where] + x_got[1, where].astype(F32) + bias).astype(BF16)
        return 0

    lax.fori_loop(0, CHUNKS, out_rows, 0)
    vec_pair_move(1, across).wait_recv()
    rows_out[...] = vec[0]
    rows_out[1:3, :] = vec[1, 1:3, :] + vec_pair[1, 1:3, :]

    for m in every_m:
        for k in range(n_hi):
            mlp_lo(m, k, -m).wait_recv()
    save_mlp = pltpu.make_async_copy(mlp_all, mlp_all_out, save_sem.at[0])
    save_mlp.start()
    for s in range(1, n_hi):
        mlp_send_hop(s, wait=True)
    for m in every_m:
        for k in range(n_hi):
            mlp_lo(m, k).wait_send()
        for p in range(2):
            joint_lo(p, m).wait_send()
        vec_lo_move(m).wait_send()
    for k in every_k:
        for p in range(2):
            joint_hi(p, k).wait_send()
            all_hi(p, k).wait_send()
        vec_hi_move(k).wait_send()
    vec_pair_move(0, sibling).wait_send()
    vec_pair_move(1, across).wait_send()

    def sent(c, _):
        for which in range(2):
            core_move(which, 0, c).wait_send()
            core_move(which, 1, c).wait_send()
            x_move(which, c).wait_send()
        return 0

    lax.fori_loop(0, CHUNKS, sent, 0)
    for m in every_m:
        for p in range(2):
            all_lo(p, m, -m).wait_recv()
            all_lo(p, m).wait_send()
    save_joint = pltpu.make_async_copy(joint_all, joint_all_out, save_sem.at[1])
    save_joint.start()
    save_mlp.wait()
    save_joint.wait()


def levels(n_batch):
    lo = 2 if n_batch <= 8 else 4
    return n_batch // lo, lo


def back(
    n_batch, d_qkv, nall, dn_part, ho, call, mlp_part, qkv_weight_t, attn_out, tokens, cot, ln_gain, out_bias,
    own_lo, own_hi, front_rows, gain_rows,
):
    n_hi, n_lo = levels(n_batch)
    strips, tok_dev, features = nall.shape
    own = (own_lo.shape[0] + own_hi.shape[0], features)
    wide, packed = d_qkv.shape[2], ho.shape[2]
    heads = attn_out.shape[0] // DH
    chunk = (2 * features // n_batch, features // 2)
    dma = pltpu.SemaphoreType.DMA
    vmem = pltpu.VMEM
    return pl.pallas_call(
        functools.partial(back_body, heads, n_hi, n_lo),
        out_shape=(
            jax.ShapeDtypeStruct(tokens.shape, BF16),
            jax.ShapeDtypeStruct(tokens.shape, BF16),
            jax.ShapeDtypeStruct((n_hi, n_lo) + own, BF16),
            jax.ShapeDtypeStruct((n_lo, n_hi) + chunk, BF16),
            jax.ShapeDtypeStruct((8, features), F32),
        ),
        in_specs=[ANY] * 6 + [VMEM] * 10,
        out_specs=(VMEM, VMEM, ANY, ANY, VMEM),
        scratch_shapes=[
            vmem(d_qkv.shape, BF16), vmem(nall.shape, BF16), vmem(dn_part.shape, BF16),
            vmem(ho.shape, BF16), vmem(call.shape, BF16), vmem(mlp_part.shape, BF16),
            vmem((wide, features), BF16),
            vmem((packed, features), BF16),
            vmem((wide, features), F32),
            vmem((packed, features), F32),
            vmem((n_lo, n_hi) + chunk, BF16),
            vmem((features, features), BF16),
            vmem((n_lo, n_hi) + chunk, BF16),
            vmem((n_hi,) + chunk, BF16),
            vmem((n_hi,) + chunk, BF16),
            vmem((n_lo, n_hi) + chunk, BF16),
            vmem((n_hi, n_lo) + own, BF16),
            vmem((2,) + tokens.shape, F32),
            vmem((2, 2) + tokens.shape, BF16),
            vmem((2, 2) + tokens.shape, BF16),
            vmem((2,) + tokens.shape, BF16),
            vmem((2,) + tokens.shape, BF16),
            vmem((2, 8, features), F32),
            vmem((n_lo, 8, features), F32),
            vmem((n_hi, 8, features), F32),
            vmem((2, 8, features), F32),
            dma((6,)),
            dma((2, n_hi)), dma((2, n_hi)),
            dma((n_lo, n_hi)), dma((n_lo, n_hi)),
            dma((n_lo, 2)), dma((n_lo, 2)),
            dma((n_hi, 2)), dma((n_hi, 2)),
            dma((n_hi, 2)), dma((n_hi, 2)),
            dma((n_lo, 2)), dma((n_lo, 2)),
            dma((2, 2, CHUNKS)), dma((2, 2, CHUNKS)),
            dma((2, CHUNKS)), dma((2, CHUNKS)),
            dma((n_lo + n_hi + 2,)), dma((n_lo + n_hi + 2,)),
            dma((2,)),
        ],
        compiler_params=pltpu.CompilerParams(collective_id=1, has_side_effects=True, vmem_limit_bytes=60 << 20),
        name="reduce_gradients",
    )(
        d_qkv, nall, dn_part, ho, call, mlp_part, qkv_weight_t, attn_out, tokens, cot, ln_gain, out_bias,
        own_lo, own_hi, front_rows, gain_rows,
    )


def widen_body(
    heads, mlp_hbm, joint_hbm, output_in, input_grad_in, rows,
    output, input_grad, qkv_out, attn_out, mlp_in_out, mlp_out_out, ln_gain, q_gain, k_gain, mlp_bias, out_bias,
    mlp_all, joint_all, joint, qkv_t, attn, mlp, sems,
):
    def copy(i, source, to):
        made = pltpu.make_async_copy(source, to, sems.at[i])
        made.start()
        return made

    load_joint = copy(0, joint_hbm, joint_all)
    load_mlp = copy(1, mlp_hbm, mlp_all)
    features = rows.shape[1]
    mlp_bias[...] = rows[0:1, :].reshape(features)
    out_bias[...] = rows[1:2, :].reshape(features)
    ln_gain[...] = rows[2:3, :].reshape(features)
    for offset, ref in ((0, q_gain), (DH, k_gain)):
        parts = [rows[3:4, h * LANES + offset : h * LANES + offset + DH] for h in range(heads)]
        ref[...] = jnp.concatenate(parts, axis=1).reshape(heads * DH)
    output[...] = output_in[...]
    input_grad[...] = input_grad_in[...]
    load_joint.wait()
    n_lo, n_hi, chunk_rows, cols = joint_all.shape
    width = qkv_t.shape[0]
    per_half = features // chunk_rows
    for o in range(n_lo * n_hi):
        row = o % per_half * chunk_rows
        joint[o // per_half, row : row + chunk_rows] = joint_all[o % n_lo, o // n_lo].astype(F32)
    kinds = [(3 * h + i) * DH for h in range(heads) for i in range(2)] + [(3 * h + 2) * DH for h in range(heads)]
    for half in range(2):
        at = slice(half * cols, (half + 1) * cols)
        for i, to in enumerate(kinds):
            qkv_t[to : to + DH, at] = joint[half, i * DH : (i + 1) * DH]
        attn[:, at] = joint[half, width:]
    pending = [copy(4, qkv_t, qkv_out), copy(5, attn, attn_out)]
    load_mlp.wait()
    chunks = mlp_all.shape[0]
    cut = lo_rows(features) // chunks
    rest = mlp_all.shape[1] - cut
    for o in range(chunks):
        mlp[o * cut : (o + 1) * cut] = mlp_all[o, :cut].astype(F32)
        row = lo_rows(features) + o * rest
        mlp[row : row + rest] = mlp_all[o, cut:].astype(F32)
    pending += [copy(6, mlp.at[:features], mlp_in_out), copy(7, mlp.at[features:], mlp_out_out)]
    for made in pending:
        made.wait()


def widen(heads, width, mlp_all, joint_all, output, input_grad, rows):
    features = rows.shape[1]
    head_width = heads * DH

    def out(*shape):
        return jax.ShapeDtypeStruct(shape, F32)

    like = jax.ShapeDtypeStruct(output.shape, BF16)
    return pl.pallas_call(
        functools.partial(widen_body, heads),
        out_shape=(
            like, like, out(width, features), out(head_width, features), out(features, features), out(features, features),
            out(features), out(head_width), out(head_width), out(features), out(features),
        ),
        in_specs=[ANY] * 2 + [VMEM] * 3,
        out_specs=(VMEM,) * 2 + (ANY,) * 4 + (VMEM,) * 5,
        scratch_shapes=[
            pltpu.VMEM(mlp_all.shape, BF16),
            pltpu.VMEM(joint_all.shape, BF16),
            pltpu.VMEM((2, features, features // 2), F32),
            pltpu.VMEM((width, features), F32),
            pltpu.VMEM((head_width, features), F32),
            pltpu.VMEM((2 * features, features), F32),
            pltpu.SemaphoreType.DMA((8,)),
        ],
        compiler_params=pltpu.CompilerParams(vmem_limit_bytes=60 << 20),
        name="widen_gradients",
    )(mlp_all, joint_all, output, input_grad, rows)


def on_device(
    tokens, out_cotangent, ln_gain, qkv_weight, q_gain, k_gain, attn_out,
    mlp_in, mlp_bias, mlp_out, out_bias, image_len, image_group,
):
    tok_dev, features = tokens.shape
    strips = lax.axis_size("tensor")
    n_batch = lax.axis_size("batch")
    n_hi, n_lo = levels(n_batch)
    heads = q_gain.shape[0] // DH
    qkv_cols = qkv_weight.shape[1]

    weight_t = qkv_weight.T
    (qa, ka, va, do, u, r, mlp_part, dn_part, nall, call, *mlp_grad, front_rows) = front(
        strips, n_batch, tokens, out_cotangent, ln_gain, weight_t, q_gain, k_gain, attn_out, mlp_in, mlp_bias, mlp_out
    )

    def along_lo(x, m):
        pairs = [(h * n_lo + i, h * n_lo + (i + m) % n_lo) for h in range(n_hi) for i in range(n_lo)]
        return lax.ppermute(x, "batch", pairs)

    def along_hi(x, k):
        pairs = [(h * n_lo + i, (h + k) % n_hi * n_lo + i) for h in range(n_hi) for i in range(n_lo)]
        return lax.ppermute(x, "batch", pairs)

    def add(first, others):
        total = first.astype(F32)
        for other in others:
            total = total + other.astype(F32)
        return total.astype(BF16)

    lo_first, hi_first = mlp_grad[:n_lo], mlp_grad[n_lo:]
    lo_got = [along_lo(lo_first[m], m) for m in range(1, n_lo)]
    hi_got = [along_hi(hi_first[k], k) for k in range(1, n_hi)]
    qb, dob, ho = attn_fwd(image_len, image_group, qa, ka, va, do)
    lo_sum = [add(lo_first[0][k], [got[k] for got in lo_got]) for k in range(n_hi)]
    hi_sum = [add(hi_first[0][m], [got[m] for got in hi_got]) for m in range(n_lo)]
    qb, lo_sum, hi_sum = lax.optimization_barrier((qb, lo_sum, hi_sum))
    lo_got = [along_hi(lo_sum[k], k) for k in range(1, n_hi)]
    hi_got = [along_lo(hi_sum[m], m) for m in range(1, n_lo)]
    d_qkv, gain_rows = attn_bwd(image_len, image_group, qb, ka, va, dob, u, r, q_gain, k_gain)
    own_lo, own_hi = add(lo_sum[0], lo_got), add(hi_sum[0], hi_got)
    output, input_grad, mlp_all, joint_all, rows = back(
        n_batch, d_qkv, nall, dn_part, ho, call, mlp_part, weight_t, attn_out, tokens, out_cotangent, ln_gain, out_bias,
        own_lo, own_hi, front_rows, gain_rows,
    )
    output, input_grad, qkv_t, attn, mlp_in_grad, mlp_out_grad, ln, q, k, bias, out_bias_grad = widen(
        heads, qkv_cols, mlp_all.reshape((n_batch,) + mlp_all.shape[2:]), joint_all,
        output, input_grad, rows,
    )
    return output, input_grad, ln, qkv_t.T, q, k, attn, mlp_in_grad, bias, mlp_out_grad, out_bias_grad


def solution(mesh):
    rows, cols, first = P(("batch", "tensor"), None), P(None, "tensor"), P("tensor", None)
    return jax.shard_map(
        on_device,
        mesh=mesh,
        in_specs=(rows, rows, P(), cols, P("tensor"), P("tensor"), first, cols, P("tensor"), first, P(), P(), P()),
        out_specs=(rows, rows, P(), cols, P("tensor"), P("tensor"), first, cols, P("tensor"), first, P()),
        check_vma=False,
    )
```

```python
import functools

import jax
import jax.numpy as jnp
from jax import lax
from jax.experimental import pallas as pl
from jax.experimental.pallas import tpu as pltpu
from jax.sharding import PartitionSpec as P

DH = 64
LANES = 128
WIN = 64
ALIGN = 16
LOG2E = 1.4426950408889634
epsilon = 1e-06
F32 = jnp.float32
BF16 = jnp.bfloat16
VMEM = pl.BlockSpec(memory_space=pltpu.VMEM)
SMEM = pl.BlockSpec(memory_space=pltpu.SMEM)
ANY = pl.BlockSpec(memory_space=pl.ANY)


def nn(left, right):
    return lax.dot_general(left, right, (((1,), (0,)), ((), ())), preferred_element_type=F32)


def nt(left, right):
    return lax.dot_general(left, right, (((1,), (1,)), ((), ())), preferred_element_type=F32)


def tn(left, right):
    return lax.dot_general(left, right, (((0,), (0,)), ((), ())), preferred_element_type=F32)


def row_of(vector):
    return vector[...].astype(F32).reshape(1, -1)


def pair_row(q_vector, k_vector, heads):
    q, k = row_of(q_vector), row_of(k_vector)
    parts = []
    for h in range(heads):
        parts += [q[:, h * DH : (h + 1) * DH], k[:, h * DH : (h + 1) * DH]]
    return jnp.concatenate(parts, axis=1)


def half_sums():
    row = lax.broadcasted_iota(jnp.int32, (LANES, LANES), 0) // DH
    col = lax.broadcasted_iota(jnp.int32, (LANES, LANES), 1) // DH
    return jnp.where(row == col, 1.0, 0.0).astype(BF16)


def left_half(rows):
    return lax.broadcasted_iota(jnp.int32, (rows, LANES), 1) < DH


def find_segments(len_ref, group_ref, seg_ref, strips, tok_dev):
    group = lax.axis_index("batch")

    def entry(i, carry):
        count, run = carry
        rows = jnp.where(group_ref[i] == group, len_ref[i] // strips, 0)

        @pl.when(rows > 0)
        def _():
            seg_ref[0, count] = run
            seg_ref[1, count] = run + rows

        return count + jnp.where(rows > 0, 1, 0), run + rows

    count, run = lax.fori_loop(0, len_ref.shape[0], entry, (jnp.int32(0), jnp.int32(0)))

    @pl.when(run < tok_dev)
    def _():
        seg_ref[0, count] = run
        seg_ref[1, count] = tok_dev

    return count + jnp.where(run < tok_dev, 1, 0)


def window(start, end, first, i, tok_dev):
    nominal = first + WIN * i
    at = pl.multiple_of(jnp.minimum(nominal, tok_dev - WIN), ALIGN)
    return at, jnp.maximum(start, nominal) - at, jnp.minimum(end, nominal + WIN) - at


def row_mask(low, high, strips, win=WIN, width=LANES):
    j = lax.broadcasted_iota(jnp.int32, (strips, win, width), 1).reshape(strips * win, width)
    return (j >= low) & (j < high)


def tile(ref, at, h, win=WIN):
    strips = ref.shape[0]
    return ref[:, pl.ds(at, win), h * LANES : (h + 1) * LANES].reshape(strips * win, LANES)


def put_tile(ref, at, h, mask, value, win=WIN, width=LANES):
    strips = ref.shape[0]
    where = (slice(None), pl.ds(at, win), slice(h * LANES, h * LANES + width))
    old = ref[where].reshape(strips * win, width)
    ref[where] = jnp.where(mask, value.astype(ref.dtype), old).reshape(strips, win, width)


PIECES = 4


def pieces_of(pairs, sem, tok_dev):
    rows = tok_dev // PIECES
    return [
        [
            pltpu.make_async_copy(a.at[:, pl.ds(p * rows, rows)], b.at[:, pl.ds(p * rows, rows)], sem.at[i, p])
            for i, (a, b) in enumerate(pairs)
        ]
        for p in range(PIECES)
    ]


def for_segments(len_ref, group_ref, seg, strips, tok_dev, loads, later, stores, small, middle, large):
    for piece in loads:
        for copy in piece:
            copy.start()
    for copy in later:
        copy.start()
    count = find_segments(len_ref, group_ref, seg, strips, tok_dev)
    big = middle_rows(tok_dev)
    rows = tok_dev // PIECES

    def segment(index, ready):
        start, end = seg[0, index], seg[1, index]
        first = (start // ALIGN) * ALIGN
        windows = (end - first + WIN - 1) // WIN
        fits = end - first <= big
        reach = jnp.where(windows == 1, first + WIN, jnp.where(fits, first + big, first + windows * WIN))
        needed = jnp.minimum((reach + rows - 1) // rows, PIECES)
        for p in range(PIECES):

            @pl.when((p >= ready) & (p < needed))
            def _():
                for copy in loads[p]:
                    copy.wait()

        @pl.when(windows == 1)
        def _():
            small(*window(start, end, first, 0, tok_dev))

        @pl.when((windows > 1) & fits)
        def _():
            at = pl.multiple_of(jnp.minimum(first, tok_dev - big), ALIGN)
            middle(at, start - at, end - at)

        @pl.when(jnp.logical_not(fits))
        def _():
            large(start, end, first, windows)

        for p, piece in enumerate(stores):

            @pl.when((start < (p + 1) * rows) & ((p + 1) * rows <= end))
            def _():
                for copy in piece:
                    copy.start()

        return jnp.maximum(ready, needed)

    lax.fori_loop(0, count, segment, jnp.int32(0))


def middle_rows(tok_dev):
    return min(tok_dev, tok_dev // 2 + ALIGN)


def attn_fwd_body(
    heads, len_ref, group_ref, qa_hbm, ka_hbm, va_hbm, do_hbm, qb_hbm, dob_hbm, ho_hbm,
    qa, ka, va, do, qb, dob, ho, seg, acc, in_sem, out_sem,
):
    strips, tok_dev = qa.shape[0], qa.shape[1]
    loads = pieces_of([(qa_hbm, qa), (ka_hbm, ka), (va_hbm, va), (do_hbm, do)], in_sem, tok_dev)
    stores = pieces_of([(qb, qb_hbm), (dob, dob_hbm), (ho, ho_hbm)], out_sem, tok_dev)
    zero = jnp.zeros((), BF16)
    big = middle_rows(tok_dev)

    def finish(at, low, high, totals, win=WIN):
        rows = strips * win
        mask = row_mask(low, high, strips, win)
        lane = lax.broadcasted_iota(jnp.int32, (rows, LANES), 1)
        left = lane < DH
        outs = []
        for h in range(heads):
            total = totals[h]
            rows_sum = jnp.where(left, pltpu.roll(total, DH, 1), total)
            out = jnp.where(left, total / rows_sum, 0.0)
            log_sum = jnp.log2(rows_sum)
            d_out = tile(do, at, h, win).astype(F32)
            delta = jnp.sum(out * d_out, axis=-1, keepdims=True)
            log_hi = log_sum.astype(BF16).astype(F32)
            delta_hi = delta.astype(BF16).astype(F32)
            q = tile(qa, at, h, win).astype(F32)
            q = jnp.where(lane == DH, -log_hi, jnp.where(lane == DH + 1, log_hi - log_sum, q))
            d_out = jnp.where(lane == DH, -delta_hi, jnp.where(lane == DH + 1, delta_hi - delta, d_out))
            put_tile(qb, at, h, mask, q, win)
            put_tile(dob, at, h, mask, d_out, win)
            outs.append(out)
        if heads % 2:
            outs.append(jnp.zeros_like(outs[0]))
        for b in range(len(outs) // 2):
            put_tile(ho, at, b, mask, jnp.where(left, outs[2 * b], pltpu.roll(outs[2 * b + 1], DH, 1)), win)

    def products(at_q, at_k, k_mask, win_q=WIN, win_k=WIN):
        scores = [nt(tile(qa, at_q, h, win_q), tile(ka, at_k, h, win_k)) for h in range(heads)]
        weights = [jnp.exp2(s).astype(BF16) for s in scores]
        return [nn(weights[h], jnp.where(k_mask, tile(va, at_k, h, win_k), zero)) for h in range(heads)]

    def small(at, low, high):
        finish(at, low, high, products(at, at, row_mask(low, high, strips)))

    def middle(at, low, high):
        def add(at_k, k_mask, win, first=False):
            for h, new in enumerate(products(at, at_k, k_mask, big, win)):
                acc[h] = new if first else acc[h] + new

        rest = big % WIN
        base = at + big - rest
        if rest:
            add(base, row_mask(low - (big - rest), high - (big - rest), strips, rest), rest, True)
        else:
            acc[...] = jnp.zeros_like(acc)

        def k_window(k, _):
            add(pl.multiple_of(at + k * WIN, ALIGN), row_mask(low - k * WIN, high - k * WIN, strips), WIN)
            return 0

        lax.fori_loop(0, big // WIN, k_window, 0)

        def total(h, offset, win):
            return acc[h].reshape(strips, big, LANES)[:, offset : offset + win].reshape(strips * win, LANES)

        for w in range(big // WIN):
            offset = w * WIN
            finish(
                pl.multiple_of(at + offset, ALIGN), low - offset, high - offset, [total(h, offset, WIN) for h in range(heads)]
            )
        if rest:
            offset = big - rest
            finish(base, low - offset, high - offset, [total(h, offset, rest) for h in range(heads)], rest)

    def large(start, end, first, windows):
        def q_window(i, _):
            at_q, low_q, high_q = window(start, end, first, i, tok_dev)
            rows = strips * WIN
            acc[:, :rows] = jnp.zeros((heads, rows, LANES), F32)

            def k_window(k, _):
                at_k, low_k, high_k = window(start, end, first, k, tok_dev)
                for h, new in enumerate(products(at_q, at_k, row_mask(low_k, high_k, strips))):
                    acc[h, :rows] += new
                return 0

            lax.fori_loop(0, windows, k_window, 0)
            finish(at_q, low_q, high_q, [acc[h, :rows] for h in range(heads)])
            return 0

        lax.fori_loop(0, windows, q_window, 0)

    for_segments(len_ref, group_ref, seg, strips, tok_dev, loads, [], stores, small, middle, large)
    for piece in stores:
        for copy in piece:
            copy.wait()


def attn_fwd(image_len, image_group, qa, ka, va, do):
    strips, tok_dev, width = qa.shape
    heads = width // LANES
    packed = (heads + 1) // 2 * LANES
    like = jax.ShapeDtypeStruct(qa.shape, BF16)
    return pl.pallas_call(
        functools.partial(attn_fwd_body, heads),
        out_shape=(like, like, jax.ShapeDtypeStruct((strips, tok_dev, packed), BF16)),
        in_specs=[SMEM, SMEM] + [ANY] * 4,
        out_specs=(ANY,) * 3,
        scratch_shapes=[pltpu.VMEM(qa.shape, BF16)] * 6 + [
            pltpu.VMEM((strips, tok_dev, packed), BF16),
            pltpu.SMEM((2, image_len.shape[0] + 1), jnp.int32),
            pltpu.VMEM((heads, strips * middle_rows(tok_dev), LANES), F32),
            pltpu.SemaphoreType.DMA((4, PIECES)),
            pltpu.SemaphoreType.DMA((3, PIECES)),
        ],
        compiler_params=pltpu.CompilerParams(vmem_limit_bytes=60 << 20),
        cost_estimate=pl.CostEstimate(flops=8 * 10**9, bytes_accessed=30 * 10**6, transcendentals=8 * 10**6),
        name="attention_forward",
    )(image_len, image_group, qa, ka, va, do)


def attn_bwd_body(
    heads, len_ref, group_ref, qb_hbm, ka_hbm, va_hbm, dob_hbm, u_hbm, r_hbm, q_gain, k_gain,
    d_qkv_hbm, gain_grad, seg, k_turned, dq_turned, dk_acc, dv_acc, dq, dk, dv, qb, ka, va, dob, u_rows, r_rows, d_qkv,
    in_sem, out_sem, sems,
):
    strips, tok_dev = qb.shape[0], qb.shape[1]
    pieces = pieces_of([(qb_hbm, qb), (ka_hbm, ka), (va_hbm, va), (dob_hbm, dob)], in_sem, tok_dev)
    loads = [pltpu.make_async_copy(u_hbm, u_rows, sems.at[0]), pltpu.make_async_copy(r_hbm, r_rows, sems.at[1])]
    zero = jnp.zeros((), BF16)
    big = middle_rows(tok_dev)

    def products(at_q, at_k, q_mask, k_turned_of, win_q=WIN, win_k=WIN):
        every = range(heads)
        qs = [tile(qb, at_q, h, win_q) for h in every]
        d_outs = [jnp.where(q_mask, tile(dob, at_q, h, win_q), zero) for h in every]
        scores = [nt(tile(ka, at_k, h, win_k), qs[h]) for h in every]
        d_weights = [nt(tile(va, at_k, h, win_k), d_outs[h]) for h in every]
        weights = [jnp.exp2(s) for s in scores]
        d_scores = [(weights[h] * d_weights[h]).astype(BF16) for h in every]
        dv_new = [nn(weights[h].astype(BF16), d_outs[h]) for h in every]
        dk_new = [nn(d_scores[h], qs[h]) for h in every]
        dq_new = [nn(k_turned_of(h), d_scores[h]) for h in every]
        return dq_new, dk_new, dv_new

    def turned(h, at_k, mask, win=WIN):
        return jnp.where(mask, tile(ka, at_k, h, win), zero).T[:DH]

    def small(at, low, high):
        mask = row_mask(low, high, strips)
        half = row_mask(low, high, strips, width=DH)
        dq_t, dk_new, dv_new = products(at, at, mask, lambda h: turned(h, at, mask))
        for h in range(heads):
            put_tile(dq, at, h, half, dq_t[h].T, width=DH)
            put_tile(dk, at, h, mask, dk_new[h])
            put_tile(dv, at, h, mask, dv_new[h])

    def middle(at, low, high):
        mask = row_mask(low, high, strips, big)
        for h in range(heads):
            k_turned[h] = turned(h, at, mask, big)

        def q_window(at_q, low_q, high_q, win, first=False):
            mask_q = row_mask(low_q, high_q, strips, win)
            half = row_mask(low_q, high_q, strips, win, DH)
            dq_t, dk_new, dv_new = products(at_q, at, mask_q, lambda h: k_turned[h], win, big)
            for h in range(heads):
                put_tile(dq, at_q, h, half, dq_t[h].T, win, DH)
                dk_acc[h] = dk_new[h] if first else dk_acc[h] + dk_new[h]
                dv_acc[h] = dv_new[h] if first else dv_acc[h] + dv_new[h]

        rest = big % WIN
        offset = big - rest
        if rest:
            q_window(at + offset, low - offset, high - offset, rest, True)
        else:
            dk_acc[...] = jnp.zeros_like(dk_acc)
            dv_acc[...] = jnp.zeros_like(dv_acc)

        def each(i, _):
            q_window(pl.multiple_of(at + i * WIN, ALIGN), low - i * WIN, high - i * WIN, WIN)
            return 0

        lax.fori_loop(0, big // WIN, each, 0)
        for h in range(heads):
            put_tile(dk, at, h, mask, dk_acc[h], big)
            put_tile(dv, at, h, mask, dv_acc[h], big)

    def large(start, end, first, windows):
        rows = strips * WIN

        def clear(i, _):
            for h in range(heads):
                dq_turned[h, i] = jnp.zeros(dq_turned.shape[2:], F32)
            return 0

        lax.fori_loop(0, windows, clear, 0)

        def k_window(k, _):
            at_k, low_k, high_k = window(start, end, first, k, tok_dev)
            mask_k = row_mask(low_k, high_k, strips)
            for h in range(heads):
                k_turned[h, :, :rows] = turned(h, at_k, mask_k)
            dk_acc[:, :rows] = jnp.zeros((heads, rows, LANES), F32)
            dv_acc[:, :rows] = jnp.zeros((heads, rows, LANES), F32)

            def q_window(i, _):
                at_q, low_q, high_q = window(start, end, first, i, tok_dev)
                mask_q = row_mask(low_q, high_q, strips)
                dq_t, dk_new, dv_new = products(at_q, at_k, mask_q, lambda h: k_turned[h, :, :rows])
                for h in range(heads):
                    dq_turned[h, i] += dq_t[h]
                    dk_acc[h, :rows] += dk_new[h]
                    dv_acc[h, :rows] += dv_new[h]
                return 0

            lax.fori_loop(0, windows, q_window, 0)
            for h in range(heads):
                put_tile(dk, at_k, h, mask_k, dk_acc[h, :rows])
                put_tile(dv, at_k, h, mask_k, dv_acc[h, :rows])
            return 0

        lax.fori_loop(0, windows, k_window, 0)

        def q_out(i, _):
            at_q, low_q, high_q = window(start, end, first, i, tok_dev)
            half = row_mask(low_q, high_q, strips, width=DH)
            for h in range(heads):
                put_tile(dq, at_q, h, half, dq_turned[h, i].T, width=DH)
            return 0

        lax.fori_loop(0, windows, q_out, 0)

    for_segments(len_ref, group_ref, seg, strips, tok_dev, pieces, loads, [], small, middle, large)

    rows = strips * WIN
    left = left_half(rows)
    sums = half_sums()
    gains = pair_row(q_gain, k_gain, heads)
    for load in loads:
        load.wait()

    def save(i):
        where = pl.ds(pl.multiple_of(i * WIN, WIN), WIN)
        return pltpu.make_async_copy(d_qkv.at[:, where], d_qkv_hbm.at[:, where], out_sem.at[i])

    def chunk(i, totals):
        at = pl.multiple_of(i * WIN, WIN)
        scaled, new_totals, us = [], [], []
        for h in range(heads):
            cols = slice(h * LANES, (h + 1) * LANES)
            d_q, d_k = tile(dq, at, h), tile(dk, at, h) * (1.0 / LOG2E)
            both = jnp.where(left, d_q * DH ** (-0.5), pltpu.roll(d_k, DH, 1))
            u = tile(u_rows, at, h).astype(F32)
            new_totals.append(totals[h] + jnp.sum(both * u, axis=0, keepdims=True))
            scaled.append(both * gains[:, cols])
            us.append(u)
        stacked = [s.astype(BF16) for s in scaled] + [(scaled[h] * us[h]).astype(BF16) for h in range(heads)]
        means = nn(jnp.concatenate(stacked, axis=0), sums) * (1.0 / DH)
        parts = []
        for h in range(heads):
            mean = means[h * rows : (h + 1) * rows]
            mean_u = means[(heads + h) * rows : (heads + h + 1) * rows]
            parts.append((scaled[h] - mean - us[h] * mean_u) * tile(r_rows, at, h).astype(F32))
        values = [tile(dv, at, h) for h in range(heads)]
        if heads % 2:
            values.append(jnp.zeros_like(values[0]))
        for b in range(len(values) // 2):
            parts.append(jnp.where(left, values[2 * b], pltpu.roll(values[2 * b + 1], DH, 1)))
        for b, part in enumerate(parts):
            d_qkv[:, pl.ds(at, WIN), b * LANES : (b + 1) * LANES] = part.astype(BF16).reshape(strips, WIN, LANES)
        save(i).start()
        return tuple(new_totals)

    totals = lax.fori_loop(0, tok_dev // WIN, chunk, tuple(jnp.zeros((1, LANES), F32) for _ in range(heads)))
    gain_grad[...] = jnp.zeros_like(gain_grad)
    for h in range(heads):
        gain_grad[0:1, h * LANES : (h + 1) * LANES] = totals[h]

    def saved(i, _):
        save(i).wait()
        return 0

    lax.fori_loop(0, tok_dev // WIN, saved, 0)


def attn_bwd(image_len, image_group, qb, ka, va, dob, u, r, q_gain, k_gain):
    strips, tok_dev, width = qb.shape
    heads = width // LANES
    blocks = heads + (heads + 1) // 2
    rows = strips * WIN
    big = strips * middle_rows(tok_dev)
    windows = tok_dev // WIN + 1
    full = pltpu.VMEM((strips, tok_dev, width), F32)
    return pl.pallas_call(
        functools.partial(attn_bwd_body, heads),
        out_shape=(
            jax.ShapeDtypeStruct((strips, tok_dev, blocks * LANES), BF16),
            jax.ShapeDtypeStruct((8, width), F32),
        ),
        in_specs=[SMEM, SMEM] + [ANY] * 6 + [VMEM] * 2,
        out_specs=(ANY, VMEM),
        scratch_shapes=[
            pltpu.SMEM((2, image_len.shape[0] + 1), jnp.int32),
            pltpu.VMEM((heads, DH, big), BF16),
            pltpu.VMEM((heads, windows, DH, rows), F32),
            pltpu.VMEM((heads, big, LANES), F32),
            pltpu.VMEM((heads, big, LANES), F32),
            full, full, full,
        ] + [pltpu.VMEM(qb.shape, BF16)] * 6 + [
            pltpu.VMEM((strips, tok_dev, blocks * LANES), BF16),
            pltpu.SemaphoreType.DMA((4, PIECES)),
            pltpu.SemaphoreType.DMA((tok_dev // WIN,)),
            pltpu.SemaphoreType.DMA((2,)),
        ],
        compiler_params=pltpu.CompilerParams(vmem_limit_bytes=60 << 20),
        cost_estimate=pl.CostEstimate(flops=16 * 10**9, bytes_accessed=30 * 10**6, transcendentals=8 * 10**6),
        name="attention_backward",
    )(image_len, image_group, qb, ka, va, dob, u, r, q_gain, k_gain)


CHUNKS = 8
BACK_CHUNKS = 4


def kind_order(heads):
    return [3 * h + i for h in range(heads) for i in range(2)] + [3 * h + 2 for h in range(heads)]


def remote(src, dst, send, recv, device):
    return pltpu.make_async_remote_copy(
        src_ref=src, dst_ref=dst, send_sem=send, recv_sem=recv, device_id=device, device_id_type=pl.DeviceIdType.MESH
    )


def lo_rows(features):
    return 2 * features * 2 // 3


def front_body(
    heads, n_hi, n_lo, tokens, cot, ln_gain, q_gain, k_gain, mlp_bias, qkv_hbm, attn_hbm, mlp_in_hbm, mlp_out_hbm,
    qa_out, ka_out, va_out, do_out, u_out, r_out, mlp_part_out, dn_part_out, nall_out, call_out,
    *rest,
):
    (rows_out, both, wide, narrow, qkv_rows, attn_pad, mlp_in, mlp_out, g_in, g_out,
     send_sem, recv_sem, save_sem, load_sem) = rest[-14:]
    lo_first, hi_first = rest[:n_lo], rest[n_lo : n_lo + n_hi]
    batch, me = lax.axis_index("batch"), lax.axis_index("tensor")
    sibling = me + 1 - 2 * (me % 2)
    across = (me + 2) % 4
    chip, far_chip = me // 2, 1 - me // 2
    tok_dev = tokens.shape[0]
    step = tok_dev // CHUNKS
    features = tokens.shape[1]
    heads_wide = heads * LANES

    def rows_of(c):
        return pl.ds(pl.multiple_of(c * step, step), step)

    def move(kind, route, c, strip, to):
        part = both.at[kind, strip, rows_of(c)]
        return remote(part, part, send_sem.at[kind, route, c], recv_sem.at[kind, route, c], (batch, to))

    barrier = pltpu.get_barrier_semaphore()
    for other in (sibling, across):
        pl.semaphore_signal(barrier, inc=1, device_id=(batch, other), device_id_type=pl.DeviceIdType.MESH)
    loads = [(mlp_in_hbm, mlp_in), (mlp_out_hbm, mlp_out)]
    loads += [
        (qkv_hbm.at[pl.ds(to * DH, DH)], qkv_rows.at[pl.ds(i * DH, DH)]) for i, to in enumerate(kind_order(heads))
    ]
    loads += [(attn_hbm.at[pl.ds(h * DH, DH)], attn_pad.at[pl.ds(h * LANES, DH)]) for h in range(heads)]
    loads = [pltpu.make_async_copy(a, b, load_sem.at[i]) for i, (a, b) in enumerate(loads)]
    for load in loads:
        load.start()
    both[0, me] = cot[...]
    gain = row_of(ln_gain)
    gains = pair_row(q_gain, k_gain, heads)

    def norm_chunk(c):
        x = tokens[rows_of(c)].astype(F32)
        centred = x - jnp.mean(x, axis=-1, keepdims=True)
        variance = jnp.mean(centred * centred, axis=-1, keepdims=True)
        both[1, me, rows_of(c)] = (centred * lax.rsqrt(variance + epsilon) * gain).astype(BF16)

    norm_chunk(0)
    pl.semaphore_wait(barrier, 2)

    def send_across(c):
        for kind in range(2):
            move(kind, 1, c, me, across).start()

    def first_sends(c, _):
        @pl.when(c < 3)
        def _():
            send_across(c)

        for kind in range(2):
            move(kind, 0, c, me, sibling).start()

        @pl.when(c + 1 < CHUNKS)
        def _():
            norm_chunk(c + 1)

        return 0

    lax.fori_loop(0, CHUNKS, first_sends, 0)

    g_in[...] = jnp.zeros_like(g_in)
    g_out[...] = jnp.zeros_like(g_out)
    rows_out[...] = jnp.zeros_like(rows_out)
    rows_out[1:2, :] = jnp.sum(cot[...].astype(F32), axis=0, keepdims=True)
    filled = 3 * heads * DH
    if filled < qkv_rows.shape[0]:
        qkv_rows[filled:] = jnp.zeros((qkv_rows.shape[0] - filled, features), BF16)
    for h in range(heads):
        attn_pad[h * LANES + DH : (h + 1) * LANES, :] = jnp.zeros((DH, features), BF16)
    for load in loads:
        load.wait()

    sums = half_sums()
    bias = row_of(mlp_bias)

    def chunks_of(c, n):
        return pl.ds(pl.multiple_of(c * step, step), n * step)

    def saves(at_chip, c, n):
        strips, where = pl.ds(2 * at_chip, 2), chunks_of(c, n)
        first = at_chip * CHUNKS + c
        pairs = [(narrow.at[a, strips, where], ref.at[strips, where]) for a, ref in enumerate(
            (qa_out, ka_out, va_out, do_out, u_out, r_out))]
        pairs += [(wide.at[a, strips, where], ref.at[strips, where]) for a, ref in enumerate((mlp_part_out, dn_part_out))]
        pairs += [(both.at[1, strips, where], nall_out.at[strips, where]), (both.at[0, strips, where], call_out.at[strips, where])]
        return [pltpu.make_async_copy(a, b, save_sem.at[i, first]) for i, (a, b) in enumerate(pairs)]

    def wait_sibling(c):
        for kind in range(2):
            move(kind, 0, c, sibling, sibling).wait_recv()

    def pass_on(c):
        for kind in range(2):
            move(kind, 1, c, across, across).wait_recv()
            move(kind, 2, c, across, sibling).start()

    def wait_passed(c):
        for kind in range(2):
            move(kind, 2, c, across + 1 - 2 * (across % 2), sibling).wait_recv()

    def unit(at_chip, c, n, between=None):
        rows = 2 * n * step
        left = left_half(rows)
        strips, where = pl.ds(2 * at_chip, 2), chunks_of(c, n)
        normed = both[1, strips, where].reshape(rows, features)
        d = both[0, strips, where].reshape(rows, features)

        def save(ref, a, h, value):
            ref[a, strips, where, h * LANES : (h + 1) * LANES] = value.astype(BF16).reshape(2, n * step, LANES)

        qkv = nt(normed, qkv_rows[...])

        def block(b):
            return qkv[:, b * LANES : (b + 1) * LANES]

        def stacked_means(parts):
            stacked = jnp.concatenate([p.astype(BF16) for p in parts], axis=0)
            means = nn(stacked, sums) * (1.0 / DH)
            return [means[h * rows : (h + 1) * rows] for h in range(heads)]

        pairs = [block(h) for h in range(heads)]
        means = stacked_means(pairs)
        centred = [pairs[h] - means[h] for h in range(heads)]
        variances = stacked_means([x * x for x in centred])
        hidden = nn(normed, mlp_in[...]) + bias
        d_act = nt(d, mlp_out[...])
        if between:
            between()
        for h in range(heads):
            rstd = lax.rsqrt(variances[h] + epsilon)
            u = centred[h] * rstd
            scaled = u * gains[:, h * LANES : (h + 1) * LANES]
            save(narrow, 0, h, jnp.where(left, scaled * (DH ** (-0.5) * LOG2E), 0.0))
            save(narrow, 1, h, jnp.where(left, pltpu.roll(scaled, DH, 1), 1.0))
            value = block(heads + h // 2)
            save(narrow, 2, h, jnp.where(left, pltpu.roll(value, DH, 1) if h % 2 else value, 1.0))
            save(narrow, 4, h, u)
            save(narrow, 5, h, rstd)
        narrow[3, strips, where] = nt(d, attn_pad[...]).astype(BF16).reshape(2, n * step, heads_wide)
        cdf = 0.5 + 0.5 * lax.erf(hidden * 0.7071067811865476)
        act = (hidden * cdf).astype(BF16)
        slope = cdf + hidden * (0.3989422804014327 * jnp.exp(hidden * hidden * -0.5))
        d_low = (d_act * slope).astype(BF16)
        wide[0, strips, where] = nn(act, mlp_out[...]).astype(BF16).reshape(2, n * step, features)
        d_normed = nt(d_low, mlp_in[...])
        rows_out[2:3, :] += jnp.sum(d_normed * normed.astype(F32), axis=0, keepdims=True)
        wide[1, strips, where] = d_normed.astype(BF16).reshape(2, n * step, features)
        rows_out[0:1, :] += jnp.sum(d_low.astype(F32), axis=0, keepdims=True)
        g_out[...] += tn(act, d)
        g_in[...] += tn(normed, d_low)
        for copy in saves(at_chip, c, n):
            copy.start()

    half, quarter = CHUNKS // 2, CHUNKS // 4
    for c in range(half):
        wait_sibling(c)
    unit(chip, 0, half)

    def middle(i, _):
        send_across(3 + i)

        @pl.when(i < 2)
        def _():
            for c in range(quarter):
                wait_sibling(half + i * quarter + c)

        @pl.when(i == 4)
        def _():
            pass_on(5)

        @pl.when(i >= 2)
        def _():
            for c in range(quarter):
                wait_passed((i - 2) * quarter + c)

        def between():
            @pl.when((i == 1) | (i == 2))
            def _():
                pass_on(2 * i - 2)
                pass_on(2 * i - 1)

            @pl.when(i == 3)
            def _():
                pass_on(4)

        unit(
            jnp.where(i < 2, chip, far_chip), jnp.where(i < 2, half + i * quarter, (i - 2) * quarter), quarter, between
        )
        return 0

    lax.fori_loop(0, 5, middle, 0)

    def last(i, _):
        pass_on(6 + i)
        wait_passed(6 + i)
        unit(far_chip, 6 + i, 1)
        return 0

    lax.fori_loop(0, 2, last, 0)

    hi, lo = batch // n_lo, batch % n_lo
    for o in range(n_hi * n_lo):
        at_hi = (o // n_lo - hi + n_hi) % n_hi
        at_lo = (o % n_lo - lo + n_lo) % n_lo
        for first, part in ((0, lo_first), (lo_rows(features), hi_first)):
            chunk_rows = part[0].shape[1]
            row = first + o * chunk_rows
            source = (g_in, g_out)[row // features]
            row = row % features
            low = source[row : row + chunk_rows, :].astype(BF16)
            slot, place = (at_lo, at_hi) if first == 0 else (at_hi, at_lo)
            for m in range(len(part)):

                @pl.when(slot == m)
                def _():
                    part[m][place] = low

    for at_chip, c, n in (
        [(chip, 0, half), (chip, half, quarter), (chip, half + quarter, quarter)]
        + [(far_chip, i * quarter, quarter) for i in range(3)] + [(far_chip, 6, 1), (far_chip, 7, 1)]
    ):
        for copy in saves(at_chip, c, n):
            copy.wait()

    def sent(c, _):
        for kind in range(2):
            move(kind, 0, c, me, sibling).wait_send()
            move(kind, 1, c, me, across).wait_send()
            move(kind, 2, c, across, sibling).wait_send()
        return 0

    lax.fori_loop(0, CHUNKS, sent, 0)


def front(strips, n_batch, tokens, cot, ln_gain, q_gain, k_gain, mlp_bias, qkv_weight_t, attn_out, mlp_in, mlp_out):
    tok_dev, features = tokens.shape
    heads = q_gain.shape[0] // DH
    width = heads * LANES
    hidden = mlp_in.shape[1]
    blocks = heads + (heads + 1) // 2
    n_hi, n_lo = levels(n_batch)
    like = jax.ShapeDtypeStruct((strips, tok_dev, width), BF16)
    rows = jax.ShapeDtypeStruct((strips, tok_dev, features), BF16)
    return pl.pallas_call(
        functools.partial(front_body, heads, n_hi, n_lo),
        out_shape=(like,) * 6 + (rows,) * 4 + (
            jax.ShapeDtypeStruct((n_hi, lo_rows(features) // n_batch, features), BF16),
        ) * n_lo + (
            jax.ShapeDtypeStruct((n_lo, (2 * features - lo_rows(features)) // n_batch, features), BF16),
        ) * n_hi + (jax.ShapeDtypeStruct((8, features), F32),),
        in_specs=[VMEM] * 6 + [ANY] * 4,
        out_specs=(ANY,) * 10 + (VMEM,) * (n_lo + n_hi + 1),
        scratch_shapes=[
            pltpu.VMEM((2, strips, tok_dev, features), BF16),
            pltpu.VMEM((2, strips, tok_dev, features), BF16),
            pltpu.VMEM((6, strips, tok_dev, width), BF16),
            pltpu.VMEM((blocks * LANES, features), BF16),
            pltpu.VMEM((width, features), BF16),
            pltpu.VMEM(mlp_in.shape, BF16),
            pltpu.VMEM(mlp_out.shape, BF16),
            pltpu.VMEM((features, hidden), F32),
            pltpu.VMEM((hidden, features), F32),
            pltpu.SemaphoreType.DMA((2, 3, CHUNKS)),
            pltpu.SemaphoreType.DMA((2, 3, CHUNKS)),
            pltpu.SemaphoreType.DMA((10, 2 * CHUNKS)),
            pltpu.SemaphoreType.DMA((2 + 4 * heads,)),
        ],
        compiler_params=pltpu.CompilerParams(collective_id=0, has_side_effects=True, vmem_limit_bytes=60 << 20),
        name="gather_and_project",
    )(tokens, cot, ln_gain, q_gain, k_gain, mlp_bias, qkv_weight_t, attn_out, mlp_in, mlp_out)


def back_body(
    heads, n_hi, n_lo, d_qkv_hbm, nall_hbm, dn_part_hbm, ho_hbm, call_hbm, mlp_part_hbm, qkv_weight_t, attn_out, tokens, cot,
    ln_gain, out_bias, own_lo, own_hi, front_rows, gain_rows, output, input_grad, mlp_all_out, joint_all_out, rows_out,
    d_qkv, nall, dn_part, ho, call, mlp_part, weight_t, attn_pad, acc, attn_acc, joint, joint_low, joint_got, joint_sum,
    joint_got_hi, joint_all, mlp_all, near, core_give, core_got, x_give, x_got, vec, vec_lo, vec_hi, vec_pair,
    load_sem, mlp_z_s, mlp_z_r, mlp_y_s, mlp_y_r, joint_s, joint_r, hi_s, hi_r, all_z_s, all_z_r, all_y_s, all_y_r,
    core_s, core_r, x_s, x_r, vec_s, vec_r, save_sem,
):
    batch, me = lax.axis_index("batch"), lax.axis_index("tensor")
    hi, lo = batch // n_lo, batch % n_lo
    sibling = me + 1 - 2 * (me % 2)
    across = (me + 2) % 4
    far_sibling = (sibling + 2) % 4
    tok_dev, features = tokens.shape
    step = tok_dev // BACK_CHUNKS
    chunk_rows, half_cols = joint.shape[2], joint.shape[3]
    every_k, every_m = range(1, n_hi), range(1, n_lo)
    cut = chunk_rows // 2 // 16 * 16
    parts = [pl.ds(0, cut), pl.ds(cut, chunk_rows - cut)]

    sources = (
        (d_qkv_hbm, d_qkv), (nall_hbm, nall), (ho_hbm, ho), (call_hbm, call), (dn_part_hbm, dn_part), (mlp_part_hbm, mlp_part)
    )
    loads = [pltpu.make_async_copy(a, b, load_sem.at[i]) for i, (a, b) in enumerate(sources)]
    for load in loads:
        load.start()

    def hi_peer(k):
        return (hi + k + n_hi) % n_hi

    def lo_peer(m):
        return (lo + m + n_lo) % n_lo

    def to_hi(k):
        return (hi_peer(k) * n_lo + lo, me)

    def to_lo(m):
        return (hi * n_lo + lo_peer(m), me)

    barrier = pltpu.get_barrier_semaphore()
    peers = [to_hi(k) for k in every_k] + [to_lo(m) for m in every_m] + [(batch, sibling), (batch, across)]
    for peer in peers:
        pl.semaphore_signal(barrier, inc=1, device_id=peer, device_id_type=pl.DeviceIdType.MESH)
    mlp_all[hi, lo] = jnp.concatenate([own_lo[...], own_hi[...]], axis=0)
    pl.semaphore_wait(barrier, len(peers))

    def mlp_hop(s, up, origin):
        part = mlp_all.at[origin, lo]
        to = ((hi + (1 if up else -1) + n_hi) % n_hi * n_lo + lo, me)
        return remote(part, part, mlp_z_s.at[up, s], mlp_z_r.at[up, s], to)

    def mlp_send_hop(s, wait=False):
        for up in range(2):
            origin = hi - (s - 1) if up else hi + (s - 1)
            there = (origin >= 0) & (hi + 1 < n_hi) if up else (origin < n_hi) & (hi >= 1)

            @pl.when(there)
            def _():
                hop = mlp_hop(s, up, (origin + n_hi) % n_hi)
                hop.wait_send() if wait else hop.start()

    def mlp_wait_hop(s):
        for up in range(2):
            origin = hi - s if up else hi + s

            @pl.when((origin >= 0) if up else (origin < n_hi))
            def _():
                mlp_hop(s, up, (origin + n_hi) % n_hi).wait_recv()

    def mlp_lo(m, k, back=0):
        part = mlp_all.at[hi_peer(k), lo_peer(back)]
        return remote(part, part, mlp_y_s.at[m, k], mlp_y_r.at[m, k], to_lo(m))

    def mlp_send_lo(s):
        for m in every_m:
            for k, there in ((s, hi + s < n_hi), (n_hi - s, hi >= s)):

                @pl.when(there)
                def _():
                    mlp_lo(m, k).start()

    for m in every_m:
        mlp_lo(m, 0).start()
    mlp_send_hop(1)

    for i, place in enumerate(kind_order(heads)):
        weight_t[i * DH : (i + 1) * DH] = qkv_weight_t[place * DH : (place + 1) * DH]
    filled = qkv_weight_t.shape[0]
    if filled < weight_t.shape[0]:
        weight_t[filled:] = jnp.zeros((weight_t.shape[0] - filled, features), BF16)
    head_width = attn_out.shape[0]
    attn_pad[:head_width] = attn_out[...]
    attn_pad[head_width:] = jnp.zeros((attn_pad.shape[0] - head_width, features), BF16)
    acc[...] = jnp.zeros_like(acc)
    attn_acc[...] = jnp.zeros_like(attn_acc)
    for load in loads[:4]:
        load.wait()

    def add_strip(i, _):
        acc[...] += tn(d_qkv[i], nall[i])
        attn_acc[...] += tn(ho[i], call[i])
        return 0

    lax.fori_loop(0, nall.shape[0], add_strip, 0)
    width = qkv_weight_t.shape[0]
    joint_low[:width] = acc[:width].astype(BF16)
    joint_low[width:] = attn_acc[:head_width].astype(BF16)
    per_half = features // chunk_rows
    for o in range(n_hi * n_lo):
        row = o % per_half * chunk_rows
        col = o // per_half * half_cols
        joint[o % n_lo, o // n_lo] = joint_low[row : row + chunk_rows, col : col + half_cols]

    def joint_lo(p, m, back=0):
        return remote(
            joint.at[lo_peer(m), :, parts[p]], joint_got.at[lo_peer(back), :, parts[p]], joint_s.at[m, p], joint_r.at[m, p], to_lo(m)
        )

    def joint_hi(p, k, back=0):
        return remote(
            joint_sum.at[hi_peer(k), parts[p]], joint_got_hi.at[hi_peer(back), parts[p]], hi_s.at[k, p], hi_r.at[k, p], to_hi(k)
        )

    def joint_sum_lo(p):
        for m in every_m:
            joint_lo(p, m, -m).wait_recv()
        total = joint[lo, :, parts[p]].astype(F32)
        for m in every_m:
            total = total + joint_got[lo_peer(m), :, parts[p]].astype(F32)
        joint_sum[:, parts[p]] = total.astype(BF16)
        for k in every_k:
            joint_hi(p, k).start()

    def all_hi(p, k, back=0):
        part = joint_all.at[lo, hi_peer(back), parts[p]]
        return remote(part, part, all_z_s.at[k, p], all_z_r.at[k, p], to_hi(k))

    def all_lo(p, m, back=0):
        part = joint_all.at[lo_peer(back), :, parts[p]]
        return remote(part, part, all_y_s.at[m, p], all_y_r.at[m, p], to_lo(m))

    def joint_sum_hi(p):
        total = joint_sum[hi, parts[p]].astype(F32)
        for k in every_k:
            joint_hi(p, k, -k).wait_recv()
            total = total + joint_got_hi[hi_peer(-k), parts[p]].astype(F32)
        joint_all[lo, hi, parts[p]] = total.astype(BF16)
        for k in every_k:
            all_hi(p, k).start()

    def joint_pass(p):
        for k in every_k:
            all_hi(p, k, -k).wait_recv()
        for m in every_m:
            all_lo(p, m).start()

    for m in every_m:
        joint_lo(0, m).start()

    ln_row = jnp.sum(acc[...] * weight_t[...].astype(F32), axis=0, keepdims=True)
    gain = row_of(ln_gain)
    vec_lo[lo] = front_rows[...]
    vec_lo[lo, 2:3, :] = (front_rows[2:3, :] + ln_row) / gain
    vec_lo[lo, 3:4, 0 : heads * LANES] = gain_rows[0:1, :]

    def vec_lo_move(m, back=0):
        part = vec_lo.at[lo_peer(back)]
        return remote(part, part, vec_s.at[m], vec_r.at[m], to_lo(m))

    def vec_hi_move(k, back=0):
        part = vec_hi.at[hi_peer(back)]
        return remote(part, part, vec_s.at[n_lo + k], vec_r.at[n_lo + k], to_hi(k))

    def vec_pair_move(i, to):
        return remote(vec.at[i], vec_pair.at[i], vec_s.at[n_lo + n_hi + i], vec_r.at[n_lo + n_hi + i], (batch, to))

    for m in every_m:
        vec_lo_move(m).start()
    mlp_wait_hop(1)
    mlp_send_hop(2)

    def rows_of(c):
        return pl.ds(pl.multiple_of(c * step, step), step)

    def partial_rows(which, strip, c):
        if which == 0:
            return nn(d_qkv[strip, rows_of(c)], weight_t[...]) + dn_part[strip, rows_of(c)].astype(F32)
        return nn(ho[strip, rows_of(c)], attn_pad[...]) + mlp_part[strip, rows_of(c)].astype(F32)

    def core_move(which, side, c):
        where = rows_of(c)
        return remote(
            core_give.at[which, side, where], core_got.at[which, side, where],
            core_s.at[which, side, c], core_r.at[which, side, c], (batch, sibling),
        )

    def x_move(which, c):
        where = rows_of(c)
        return remote(x_give.at[which, where], x_got.at[which, where], x_s.at[which, c], x_r.at[which, c], (batch, across))

    def far(which):
        def give(c, _):
            core_give[which, 0, rows_of(c)] = partial_rows(which, far_sibling, c).astype(BF16)
            core_move(which, 0, c).start()
            return 0

        def send(c, _):
            mine = partial_rows(which, across, c)
            core_move(which, 0, c).wait_recv()
            x_give[which, rows_of(c)] = (mine + core_got[which, 0, rows_of(c)].astype(F32)).astype(BF16)
            x_move(which, c).start()
            return 0

        lax.fori_loop(0, BACK_CHUNKS, give, 0)
        lax.fori_loop(0, BACK_CHUNKS, send, 0)

    def close(which):
        def give(c, _):
            core_give[which, 1, rows_of(c)] = partial_rows(which, sibling, c).astype(BF16)
            core_move(which, 1, c).start()
            return 0

        def keep(c, _):
            mine = partial_rows(which, me, c)
            core_move(which, 1, c).wait_recv()
            near[which, rows_of(c)] = mine + core_got[which, 1, rows_of(c)].astype(F32)
            return 0

        lax.fori_loop(0, BACK_CHUNKS, give, 0)
        lax.fori_loop(0, BACK_CHUNKS, keep, 0)

    for load in loads[4:]:
        load.wait()
    far(0)
    for m in every_m:
        joint_lo(1, m).start()
    far(1)
    joint_sum_lo(0)
    for s in range(2, n_hi - 1):
        mlp_wait_hop(s)
        mlp_send_hop(s + 1)
    close(0)
    joint_sum_lo(1)
    mlp_send_lo(1)
    close(1)

    for m in every_m:
        vec_lo_move(m, -m).wait_recv()
    total = vec_lo[0]
    for i in range(1, n_lo):
        total = total + vec_lo[i]
    vec_hi[hi] = total
    for k in every_k:
        vec_hi_move(k).start()

    joint_sum_hi(0)
    for s in range(2, n_hi - 1):
        mlp_send_lo(s)
    joint_sum_hi(1)
    if n_hi > 2:
        mlp_wait_hop(n_hi - 1)
        mlp_send_lo(n_hi - 1)

    for k in every_k:
        vec_hi_move(k, -k).wait_recv()
    total = vec_hi[0]
    for i in range(1, n_hi):
        total = total + vec_hi[i]
    vec[0] = total
    vec_pair_move(0, sibling).start()

    joint_pass(0)
    vec_pair_move(0, sibling).wait_recv()
    vec[1] = vec[0] + vec_pair[0]
    vec_pair_move(1, across).start()

    def last_rows(c, _):
        x_move(0, c).wait_recv()
        where = rows_of(c)
        d_normed = near[0, where] + x_got[0, where].astype(F32)
        x = tokens[where].astype(F32)
        centred = x - jnp.mean(x, axis=-1, keepdims=True)
        r = lax.rsqrt(jnp.mean(centred * centred, axis=-1, keepdims=True) + epsilon)
        xhat = centred * r
        e = d_normed * gain
        d_x = r * (e - jnp.mean(e, axis=-1, keepdims=True) - xhat * jnp.mean(e * xhat, axis=-1, keepdims=True))
        input_grad[where] = (cot[where].astype(F32) + d_x).astype(BF16)
        return 0

    lax.fori_loop(0, BACK_CHUNKS, last_rows, 0)
    joint_pass(1)
    bias = row_of(out_bias)

    def out_rows(c, _):
        x_move(1, c).wait_recv()
        where = rows_of(c)
        output[where] = (tokens[where].astype(F32) + near[1, where] + x_got[1, where].astype(F32) + bias).astype(BF16)
        return 0

    lax.fori_loop(0, BACK_CHUNKS, out_rows, 0)
    vec_pair_move(1, across).wait_recv()
    rows_out[...] = vec[0]
    rows_out[1:3, :] = vec[1, 1:3, :] + vec_pair[1, 1:3, :]

    for m in every_m:
        for k in range(n_hi):
            mlp_lo(m, k, -m).wait_recv()
    save_mlp = pltpu.make_async_copy(mlp_all, mlp_all_out, save_sem.at[0])
    save_mlp.start()
    for s in range(1, n_hi):
        mlp_send_hop(s, wait=True)
    for m in every_m:
        for k in range(n_hi):
            mlp_lo(m, k).wait_send()
        for p in range(2):
            joint_lo(p, m).wait_send()
        vec_lo_move(m).wait_send()
    for k in every_k:
        for p in range(2):
            joint_hi(p, k).wait_send()
            all_hi(p, k).wait_send()
        vec_hi_move(k).wait_send()
    vec_pair_move(0, sibling).wait_send()
    vec_pair_move(1, across).wait_send()

    def sent(c, _):
        for which in range(2):
            core_move(which, 0, c).wait_send()
            core_move(which, 1, c).wait_send()
            x_move(which, c).wait_send()
        return 0

    lax.fori_loop(0, BACK_CHUNKS, sent, 0)
    for m in every_m:
        for p in range(2):
            all_lo(p, m, -m).wait_recv()
            all_lo(p, m).wait_send()
    save_joint = pltpu.make_async_copy(joint_all, joint_all_out, save_sem.at[1])
    save_joint.start()
    save_mlp.wait()
    save_joint.wait()


def levels(n_batch):
    lo = 2 if n_batch <= 8 else 4
    return n_batch // lo, lo


def back(
    n_batch, d_qkv, nall, dn_part, ho, call, mlp_part, qkv_weight_t, attn_out, tokens, cot, ln_gain, out_bias,
    own_lo, own_hi, front_rows, gain_rows,
):
    n_hi, n_lo = levels(n_batch)
    strips, tok_dev, features = nall.shape
    own = (own_lo.shape[0] + own_hi.shape[0], features)
    wide, packed = d_qkv.shape[2], ho.shape[2]
    heads = attn_out.shape[0] // DH
    chunk = (2 * features // n_batch, features // 2)
    dma = pltpu.SemaphoreType.DMA
    vmem = pltpu.VMEM
    return pl.pallas_call(
        functools.partial(back_body, heads, n_hi, n_lo),
        out_shape=(
            jax.ShapeDtypeStruct(tokens.shape, BF16),
            jax.ShapeDtypeStruct(tokens.shape, BF16),
            jax.ShapeDtypeStruct((n_hi, n_lo) + own, BF16),
            jax.ShapeDtypeStruct((n_lo, n_hi) + chunk, BF16),
            jax.ShapeDtypeStruct((8, features), F32),
        ),
        in_specs=[ANY] * 6 + [VMEM] * 10,
        out_specs=(VMEM, VMEM, ANY, ANY, VMEM),
        scratch_shapes=[
            vmem(d_qkv.shape, BF16), vmem(nall.shape, BF16), vmem(dn_part.shape, BF16),
            vmem(ho.shape, BF16), vmem(call.shape, BF16), vmem(mlp_part.shape, BF16),
            vmem((wide, features), BF16),
            vmem((packed, features), BF16),
            vmem((wide, features), F32),
            vmem((packed, features), F32),
            vmem((n_lo, n_hi) + chunk, BF16),
            vmem((features, features), BF16),
            vmem((n_lo, n_hi) + chunk, BF16),
            vmem((n_hi,) + chunk, BF16),
            vmem((n_hi,) + chunk, BF16),
            vmem((n_lo, n_hi) + chunk, BF16),
            vmem((n_hi, n_lo) + own, BF16),
            vmem((2,) + tokens.shape, F32),
            vmem((2, 2) + tokens.shape, BF16),
            vmem((2, 2) + tokens.shape, BF16),
            vmem((2,) + tokens.shape, BF16),
            vmem((2,) + tokens.shape, BF16),
            vmem((2, 8, features), F32),
            vmem((n_lo, 8, features), F32),
            vmem((n_hi, 8, features), F32),
            vmem((2, 8, features), F32),
            dma((6,)),
            dma((2, n_hi)), dma((2, n_hi)),
            dma((n_lo, n_hi)), dma((n_lo, n_hi)),
            dma((n_lo, 2)), dma((n_lo, 2)),
            dma((n_hi, 2)), dma((n_hi, 2)),
            dma((n_hi, 2)), dma((n_hi, 2)),
            dma((n_lo, 2)), dma((n_lo, 2)),
            dma((2, 2, BACK_CHUNKS)), dma((2, 2, BACK_CHUNKS)),
            dma((2, BACK_CHUNKS)), dma((2, BACK_CHUNKS)),
            dma((n_lo + n_hi + 2,)), dma((n_lo + n_hi + 2,)),
            dma((2,)),
        ],
        compiler_params=pltpu.CompilerParams(collective_id=1, has_side_effects=True, vmem_limit_bytes=60 << 20),
        name="reduce_gradients",
    )(
        d_qkv, nall, dn_part, ho, call, mlp_part, qkv_weight_t, attn_out, tokens, cot, ln_gain, out_bias,
        own_lo, own_hi, front_rows, gain_rows,
    )


def widen_body(
    heads, mlp_hbm, joint_hbm, output_in, input_grad_in, rows,
    output, input_grad, qkv_out, attn_out, mlp_in_out, mlp_out_out, ln_gain, q_gain, k_gain, mlp_bias, out_bias,
    kept, mlp_all, joint_all, joint, qkv_t, attn, mlp, sems,
):
    def copy(i, source, to):
        made = pltpu.make_async_copy(source, to, sems.at[i])
        made.start()
        return made

    load_joint = copy(0, joint_hbm, joint_all)
    load_mlp = copy(1, mlp_hbm, mlp_all)
    load_rows = [copy(2, output_in, kept.at[0]), copy(3, input_grad_in, kept.at[1])]
    features = rows.shape[1]
    mlp_bias[...] = rows[0:1, :].reshape(features)
    out_bias[...] = rows[1:2, :].reshape(features)
    ln_gain[...] = rows[2:3, :].reshape(features)
    for offset, ref in ((0, q_gain), (DH, k_gain)):
        parts = [rows[3:4, h * LANES + offset : h * LANES + offset + DH] for h in range(heads)]
        ref[...] = jnp.concatenate(parts, axis=1).reshape(heads * DH)
    load_joint.wait()
    n_lo, n_hi, chunk_rows, cols = joint_all.shape
    width = qkv_t.shape[0]
    per_half = features // chunk_rows
    for o in range(n_lo * n_hi):
        row = o % per_half * chunk_rows
        joint[o // per_half, row : row + chunk_rows] = joint_all[o % n_lo, o // n_lo]
    pending = []
    for half in range(2):
        at = slice(half * cols, (half + 1) * cols)
        attn[:, at] = joint[half, width:].astype(F32)
        for i, place in enumerate(kind_order(heads)):
            qkv_t[place * DH : (place + 1) * DH, at] = joint[half, i * DH : (i + 1) * DH].astype(F32)
    pending += [copy(4, qkv_t, qkv_out), copy(5, attn, attn_out)]
    load_mlp.wait()
    chunks = mlp_all.shape[0]
    cut = lo_rows(features) // chunks
    rest = mlp_all.shape[1] - cut
    for o in range(features // cut):
        mlp[o * cut : (o + 1) * cut] = mlp_all[o, :cut].astype(F32)
    pending.append(copy(6, mlp.at[pl.ds(0, features)], mlp_in_out))
    for o in range(features // cut, chunks):
        mlp[o * cut : (o + 1) * cut] = mlp_all[o, :cut].astype(F32)
    for o in range(chunks):
        row = lo_rows(features) + o * rest
        mlp[row : row + rest] = mlp_all[o, cut:].astype(F32)
    pending.append(copy(7, mlp.at[pl.ds(features, features)], mlp_out_out))
    for i, (load, to) in enumerate(zip(load_rows, (output, input_grad))):
        load.wait()
        pending.append(copy(8 + i, kept.at[i], to))
    for made in pending:
        made.wait()


def widen(heads, width, mlp_all, joint_all, output, input_grad, rows):
    features = rows.shape[1]
    head_width = heads * DH

    def out(*shape):
        return jax.ShapeDtypeStruct(shape, F32)

    like = jax.ShapeDtypeStruct(output.shape, BF16)
    return pl.pallas_call(
        functools.partial(widen_body, heads),
        out_shape=(
            like, like, out(width, features), out(head_width, features), out(features, features), out(features, features),
            out(features), out(head_width), out(head_width), out(features), out(features),
        ),
        in_specs=[ANY] * 4 + [VMEM],
        out_specs=(ANY,) * 6 + (VMEM,) * 5,
        scratch_shapes=[
            pltpu.VMEM((2,) + output.shape, BF16),
            pltpu.VMEM(mlp_all.shape, BF16),
            pltpu.VMEM(joint_all.shape, BF16),
            pltpu.VMEM((2, features, features // 2), BF16),
            pltpu.VMEM((width, features), F32),
            pltpu.VMEM((head_width, features), F32),
            pltpu.VMEM((2 * features, features), F32),
            pltpu.SemaphoreType.DMA((10,)),
        ],
        compiler_params=pltpu.CompilerParams(vmem_limit_bytes=60 << 20),
        name="widen_gradients",
    )(mlp_all, joint_all, output, input_grad, rows)


def on_device(
    tokens, out_cotangent, ln_gain, qkv_weight, q_gain, k_gain, attn_out,
    mlp_in, mlp_bias, mlp_out, out_bias, image_len, image_group,
):
    tok_dev, features = tokens.shape
    strips = lax.axis_size("tensor")
    n_batch = lax.axis_size("batch")
    n_hi, n_lo = levels(n_batch)
    heads = q_gain.shape[0] // DH
    qkv_cols = qkv_weight.shape[1]

    weight_t = qkv_weight.T
    (qa, ka, va, do, u, r, mlp_part, dn_part, nall, call, *mlp_grad, front_rows) = front(
        strips, n_batch, tokens, out_cotangent, ln_gain, q_gain, k_gain, mlp_bias, weight_t, attn_out, mlp_in, mlp_out
    )

    def along_lo(x, m):
        pairs = [(h * n_lo + i, h * n_lo + (i + m) % n_lo) for h in range(n_hi) for i in range(n_lo)]
        return lax.ppermute(x, "batch", pairs)

    def along_hi(x, k):
        pairs = [(h * n_lo + i, (h + k) % n_hi * n_lo + i) for h in range(n_hi) for i in range(n_lo)]
        return lax.ppermute(x, "batch", pairs)

    def add(first, others):
        total = first.astype(F32)
        for other in others:
            total = total + other.astype(F32)
        return total.astype(BF16)

    lo_first, hi_first = mlp_grad[:n_lo], mlp_grad[n_lo:]
    lo_got = [along_lo(lo_first[m], m) for m in range(1, n_lo)]
    hi_got = [along_hi(hi_first[k], k) for k in range(1, n_hi)]
    qb, dob, ho = attn_fwd(image_len, image_group, qa, ka, va, do)
    lo_sum = [add(lo_first[0][k], [got[k] for got in lo_got]) for k in range(n_hi)]
    hi_sum = [add(hi_first[0][m], [got[m] for got in hi_got]) for m in range(n_lo)]
    qb, lo_sum, hi_sum = lax.optimization_barrier((qb, lo_sum, hi_sum))
    lo_got = [along_hi(lo_sum[k], k) for k in range(1, n_hi)]
    hi_got = [along_lo(hi_sum[m], m) for m in range(1, n_lo)]
    d_qkv, gain_rows = attn_bwd(image_len, image_group, qb, ka, va, dob, u, r, q_gain, k_gain)
    own_lo, own_hi = add(lo_sum[0], lo_got), add(hi_sum[0], hi_got)
    output, input_grad, mlp_all, joint_all, rows = back(
        n_batch, d_qkv, nall, dn_part, ho, call, mlp_part, weight_t, attn_out, tokens, out_cotangent, ln_gain, out_bias,
        own_lo, own_hi, front_rows, gain_rows,
    )
    output, input_grad, qkv_t, attn, mlp_in_grad, mlp_out_grad, ln, q, k, bias, out_bias_grad = widen(
        heads, qkv_cols, mlp_all.reshape((n_batch,) + mlp_all.shape[2:]), joint_all,
        output, input_grad, rows,
    )
    return output, input_grad, ln, qkv_t.T, q, k, attn, mlp_in_grad, bias, mlp_out_grad, out_bias_grad


def solution(mesh):
    rows, cols, first = P(("batch", "tensor"), None), P(None, "tensor"), P("tensor", None)
    return jax.shard_map(
        on_device,
        mesh=mesh,
        in_specs=(rows, rows, P(), cols, P("tensor"), P("tensor"), first, cols, P("tensor"), first, P(), P(), P()),
        out_specs=(rows, rows, P(), cols, P("tensor"), P("tensor"), first, cols, P("tensor"), first, P()),
        check_vma=False,
    )
```

```python
import functools

import jax
import jax.numpy as jnp
from jax import lax
from jax.experimental import pallas as pl
from jax.experimental.pallas import tpu as pltpu
from jax.sharding import PartitionSpec as P

DH = 64
LANES = 128
WIN = 64
ALIGN = 16
LOG2E = 1.4426950408889634
epsilon = 1e-06
F32 = jnp.float32
BF16 = jnp.bfloat16
VMEM = pl.BlockSpec(memory_space=pltpu.VMEM)
SMEM = pl.BlockSpec(memory_space=pltpu.SMEM)
ANY = pl.BlockSpec(memory_space=pl.ANY)


def nn(left, right):
    return lax.dot_general(left, right, (((1,), (0,)), ((), ())), preferred_element_type=F32)


def nt(left, right):
    return lax.dot_general(left, right, (((1,), (1,)), ((), ())), preferred_element_type=F32)


def tn(left, right):
    return lax.dot_general(left, right, (((0,), (0,)), ((), ())), preferred_element_type=F32)


def row_of(vector):
    return vector[...].astype(F32).reshape(1, -1)


def pair_row(q_vector, k_vector, heads):
    q, k = row_of(q_vector), row_of(k_vector)
    parts = []
    for h in range(heads):
        parts += [q[:, h * DH : (h + 1) * DH], k[:, h * DH : (h + 1) * DH]]
    return jnp.concatenate(parts, axis=1)


def half_sums(lanes=LANES):
    row = lax.broadcasted_iota(jnp.int32, (lanes, lanes), 0) // DH
    col = lax.broadcasted_iota(jnp.int32, (lanes, lanes), 1) // DH
    return jnp.where(row == col, 1.0, 0.0).astype(BF16)


def left_half(rows):
    return lax.broadcasted_iota(jnp.int32, (rows, LANES), 1) < DH


def find_segments(len_ref, group_ref, seg_ref, strips, tok_dev):
    group = lax.axis_index("batch")

    def entry(i, carry):
        count, run = carry
        rows = jnp.where(group_ref[i] == group, len_ref[i] // strips, 0)

        @pl.when(rows > 0)
        def _():
            seg_ref[0, count] = run
            seg_ref[1, count] = run + rows

        return count + jnp.where(rows > 0, 1, 0), run + rows

    count, run = lax.fori_loop(0, len_ref.shape[0], entry, (jnp.int32(0), jnp.int32(0)))

    @pl.when(run < tok_dev)
    def _():
        seg_ref[0, count] = run
        seg_ref[1, count] = tok_dev

    return count + jnp.where(run < tok_dev, 1, 0)


def window(start, end, first, i, tok_dev):
    nominal = first + WIN * i
    at = pl.multiple_of(jnp.minimum(nominal, tok_dev - WIN), ALIGN)
    return at, jnp.maximum(start, nominal) - at, jnp.minimum(end, nominal + WIN) - at


def row_mask(low, high, strips, win=WIN, width=LANES):
    j = lax.broadcasted_iota(jnp.int32, (strips, win, width), 1).reshape(strips * win, width)
    return (j >= low) & (j < high)


def low_mask(mask):
    return jnp.where(mask, 1.0, 0.0).astype(BF16) > jnp.asarray(0.5, BF16)


def tile(ref, at, h, win=WIN):
    strips = ref.shape[0]
    return ref[:, pl.ds(at, win), h * LANES : (h + 1) * LANES].reshape(strips * win, LANES)


def put_tile(ref, at, h, mask, value, win=WIN, width=LANES):
    strips = ref.shape[0]
    where = (slice(None), pl.ds(at, win), slice(h * LANES, h * LANES + width))
    old = ref[where].reshape(strips * win, width)
    ref[where] = jnp.where(mask, value.astype(ref.dtype), old).reshape(strips, win, width)


PIECES = 4


def pieces_of(pairs, sem, tok_dev):
    rows = tok_dev // PIECES
    return [
        [
            pltpu.make_async_copy(a.at[:, pl.ds(p * rows, rows)], b.at[:, pl.ds(p * rows, rows)], sem.at[i, p])
            for i, (a, b) in enumerate(pairs)
        ]
        for p in range(PIECES)
    ]


def for_segments(len_ref, group_ref, seg, strips, tok_dev, loads, later, stores, small, middle, large):
    for piece in loads:
        for copy in piece:
            copy.start()
    for copy in later:
        copy.start()
    count = find_segments(len_ref, group_ref, seg, strips, tok_dev)
    big = middle_rows(tok_dev)
    rows = tok_dev // PIECES

    def segment(index, ready):
        start, end = seg[0, index], seg[1, index]
        first = (start // ALIGN) * ALIGN
        windows = (end - first + WIN - 1) // WIN
        fits = (end - first <= big) & (end - start <= big - ALIGN)
        reach = jnp.where(windows == 1, first + WIN, jnp.where(fits, first + big, first + windows * WIN))
        needed = jnp.minimum((reach + rows - 1) // rows, PIECES)
        for p in range(PIECES):

            @pl.when((p >= ready) & (p < needed))
            def _():
                for copy in loads[p]:
                    copy.wait()

        @pl.when(windows == 1)
        def _():
            small(*window(start, end, first, 0, tok_dev))

        @pl.when((windows > 1) & fits)
        def _():
            at = pl.multiple_of(jnp.minimum(first, tok_dev - big), ALIGN)
            middle(at, start - at, end - at)

        @pl.when(jnp.logical_not(fits))
        def _():
            large(start, end, first, windows)

        for p, piece in enumerate(stores):

            @pl.when((start < (p + 1) * rows) & ((p + 1) * rows <= end))
            def _():
                for copy in piece:
                    copy.start()

        return jnp.maximum(ready, needed)

    lax.fori_loop(0, count, segment, jnp.int32(0))


def edge_tile(ref, at, h, low):
    strips = ref.shape[0]
    cols = slice(h * LANES, (h + 1) * LANES)
    last = middle_rows(ref.shape[1]) - ALIGN
    body = ref[:, pl.ds(at + last - WIN + ALIGN, WIN - ALIGN), cols]
    late = low_mask(row_mask(low, ALIGN, strips, ALIGN))
    edge = jnp.where(late, tile(ref, at, h, ALIGN), tile(ref, at + last, h, ALIGN))
    return jnp.concatenate([body, edge.reshape(strips, ALIGN, LANES)], axis=1).reshape(strips * WIN, LANES)


def edge_mask(low, high, strips, tok_dev):
    last = middle_rows(tok_dev) - ALIGN
    j = lax.broadcasted_iota(jnp.int32, (strips, WIN, LANES), 1).reshape(strips * WIN, LANES)
    edge = j - (WIN - ALIGN)
    body = j + (last - WIN + ALIGN)
    inner = (edge < 0) & (body >= low) & (body < high)
    return inner | ((edge >= 0) & ((edge >= low) | (edge < high - last)))


def middle_rows(tok_dev):
    return min(tok_dev, tok_dev // 2 + ALIGN)


def attn_fwd_body(
    heads, len_ref, group_ref, qa_hbm, ka_hbm, va_hbm, do_hbm, qb_hbm, dob_hbm, ho_hbm,
    qa, ka, va, do, qb, dob, ho, seg, acc, in_sem, out_sem,
):
    strips, tok_dev = qa.shape[0], qa.shape[1]
    loads = pieces_of([(qa_hbm, qa), (ka_hbm, ka), (va_hbm, va), (do_hbm, do)], in_sem, tok_dev)
    stores = pieces_of([(qb, qb_hbm), (dob, dob_hbm), (ho, ho_hbm)], out_sem, tok_dev)
    zero = jnp.zeros((), BF16)
    big = middle_rows(tok_dev)

    def finish(at, low, high, totals, win=WIN):
        rows = strips * win
        mask = low_mask(row_mask(low, high, strips, win))
        lane = lax.broadcasted_iota(jnp.int32, (rows, LANES), 1)
        left = lane < DH
        first, second = low_mask(lane == DH), low_mask(lane == DH + 1)
        outs = []
        for h in range(heads):
            total = totals[h]
            log_sum = jnp.log2(jnp.where(left, pltpu.roll(total, DH, 1), total))
            out = jnp.where(left, total * jnp.exp2(-log_sum), 0.0)
            d_out = tile(do, at, h, win)
            delta = jnp.sum(out * d_out.astype(F32), axis=-1, keepdims=True)
            delta = jnp.broadcast_to(delta, (rows, LANES))
            log_hi, delta_hi = log_sum.astype(BF16), delta.astype(BF16)
            log_low = (log_hi.astype(F32) - log_sum).astype(BF16)
            delta_low = (delta_hi.astype(F32) - delta).astype(BF16)
            q = jnp.where(first, -log_hi, jnp.where(second, log_low, tile(qa, at, h, win)))
            d_out = jnp.where(first, -delta_hi, jnp.where(second, delta_low, d_out))
            put_tile(qb, at, h, mask, q, win)
            put_tile(dob, at, h, mask, d_out, win)
            outs.append(out)
        if heads % 2:
            outs.append(jnp.zeros_like(outs[0]))
        for b in range(len(outs) // 2):
            put_tile(ho, at, b, mask, jnp.where(left, outs[2 * b], pltpu.roll(outs[2 * b + 1], DH, 1)), win)

    def products(at_q, keys, values, k_mask, win_q=WIN):
        scores = [nt(tile(qa, at_q, h, win_q), keys(h)) for h in range(heads)]
        weights = [jnp.exp2(s).astype(BF16) for s in scores]
        k_mask = low_mask(k_mask)
        return [nn(weights[h], jnp.where(k_mask, values(h), zero)) for h in range(heads)]

    def plain(at_q, at_k, k_mask, win_q=WIN):
        return products(at_q, lambda h: tile(ka, at_k, h), lambda h: tile(va, at_k, h), k_mask, win_q)

    def small(at, low, high):
        finish(at, low, high, plain(at, at, row_mask(low, high, strips)))

    def middle(at, low, high):
        edges = products(
            at, lambda h: edge_tile(ka, at, h, low), lambda h: edge_tile(va, at, h, low),
            edge_mask(low, high, strips, tok_dev), big,
        )
        for h in range(heads):
            acc[h] = edges[h]

        def k_window(k, _):
            offset = ALIGN + k * WIN
            new = plain(pl.multiple_of(at, ALIGN), pl.multiple_of(at + offset, ALIGN), row_mask(low - offset, high - offset, strips), big)
            for h in range(heads):
                acc[h] = acc[h] + new[h]
            return 0

        lax.fori_loop(0, big // WIN - 1, k_window, 0)
        rest = big % WIN
        base = at + big - rest

        def total(h, offset, win):
            return acc[h].reshape(strips, big, LANES)[:, offset : offset + win].reshape(strips * win, LANES)

        for w in range(big // WIN):
            offset = w * WIN
            finish(
                pl.multiple_of(at + offset, ALIGN), low - offset, high - offset, [total(h, offset, WIN) for h in range(heads)]
            )
        if rest:
            offset = big - rest
            finish(base, low - offset, high - offset, [total(h, offset, rest) for h in range(heads)], rest)

    def large(start, end, first, windows):
        def q_window(i, _):
            at_q, low_q, high_q = window(start, end, first, i, tok_dev)
            rows = strips * WIN
            acc[:, :rows] = jnp.zeros((heads, rows, LANES), F32)

            def k_window(k, _):
                at_k, low_k, high_k = window(start, end, first, k, tok_dev)
                for h, new in enumerate(plain(at_q, at_k, row_mask(low_k, high_k, strips))):
                    acc[h, :rows] += new
                return 0

            lax.fori_loop(0, windows, k_window, 0)
            finish(at_q, low_q, high_q, [acc[h, :rows] for h in range(heads)])
            return 0

        lax.fori_loop(0, windows, q_window, 0)

    for_segments(len_ref, group_ref, seg, strips, tok_dev, loads, [], stores, small, middle, large)
    for piece in stores:
        for copy in piece:
            copy.wait()


def attn_fwd(image_len, image_group, qa, ka, va, do):
    strips, tok_dev, width = qa.shape
    heads = width // LANES
    packed = (heads + 1) // 2 * LANES
    like = jax.ShapeDtypeStruct(qa.shape, BF16)
    return pl.pallas_call(
        functools.partial(attn_fwd_body, heads),
        out_shape=(like, like, jax.ShapeDtypeStruct((strips, tok_dev, packed), BF16)),
        in_specs=[SMEM, SMEM] + [ANY] * 4,
        out_specs=(ANY,) * 3,
        scratch_shapes=[pltpu.VMEM(qa.shape, BF16)] * 6 + [
            pltpu.VMEM((strips, tok_dev, packed), BF16),
            pltpu.SMEM((2, image_len.shape[0] + 1), jnp.int32),
            pltpu.VMEM((heads, strips * middle_rows(tok_dev), LANES), F32),
            pltpu.SemaphoreType.DMA((4, PIECES)),
            pltpu.SemaphoreType.DMA((3, PIECES)),
        ],
        compiler_params=pltpu.CompilerParams(vmem_limit_bytes=60 << 20),
        cost_estimate=pl.CostEstimate(flops=8 * 10**9, bytes_accessed=30 * 10**6, transcendentals=8 * 10**6),
        name="attention_forward",
    )(image_len, image_group, qa, ka, va, do)


def attn_bwd_body(
    heads, len_ref, group_ref, qb_hbm, ka_hbm, va_hbm, dob_hbm, u_hbm, r_hbm, q_gain, k_gain,
    d_qkv_hbm, gain_grad, seg, k_turned, dq_turned, dk_acc, dv_acc, dq, dk, dv, qb, ka, va, dob, u_rows, r_rows, d_qkv,
    in_sem, out_sem, sems,
):
    strips, tok_dev = qb.shape[0], qb.shape[1]
    pieces = pieces_of([(qb_hbm, qb), (ka_hbm, ka), (va_hbm, va), (dob_hbm, dob)], in_sem, tok_dev)
    loads = [pltpu.make_async_copy(u_hbm, u_rows, sems.at[0]), pltpu.make_async_copy(r_hbm, r_rows, sems.at[1])]
    zero = jnp.zeros((), BF16)
    big = middle_rows(tok_dev)

    def products(queries, d_rows, at_k, q_mask, k_turned_of, win_k=WIN):
        every = range(heads)
        qs = [queries(h) for h in every]
        q_mask = low_mask(q_mask)
        d_outs = [jnp.where(q_mask, d_rows(h), zero) for h in every]
        scores = [nt(tile(ka, at_k, h, win_k), qs[h]) for h in every]
        d_weights = [nt(tile(va, at_k, h, win_k), d_outs[h]) for h in every]
        weights = [jnp.exp2(s) for s in scores]
        d_scores = [(weights[h] * d_weights[h]).astype(BF16) for h in every]
        dv_new = [nn(weights[h].astype(BF16), d_outs[h]) for h in every]
        dk_new = [nn(d_scores[h], qs[h]) for h in every]
        dq_new = [nn(k_turned_of(h), d_scores[h]) for h in every]
        return dq_new, dk_new, dv_new

    def plain(at_q, at_k, q_mask, k_turned_of, win_k=WIN):
        return products(lambda h: tile(qb, at_q, h), lambda h: tile(dob, at_q, h), at_k, q_mask, k_turned_of, win_k)

    def turned(h, at_k, mask, win=WIN):
        return jnp.where(low_mask(mask), tile(ka, at_k, h, win), zero).T[:DH]

    def small(at, low, high):
        mask = row_mask(low, high, strips)
        half = row_mask(low, high, strips, width=DH)
        dq_t, dk_new, dv_new = plain(at, at, mask, lambda h: turned(h, at, mask))
        for h in range(heads):
            put_tile(dq, at, h, half, dq_t[h].T, width=DH)
            put_tile(dk, at, h, mask, dk_new[h])
            put_tile(dv, at, h, mask, dv_new[h])

    def middle(at, low, high):
        mask = row_mask(low, high, strips, big)
        for h in range(heads):
            k_turned[h] = turned(h, at, mask, big)

        dq_t, dk_new, dv_new = products(
            lambda h: edge_tile(qb, at, h, low), lambda h: edge_tile(dob, at, h, low), at,
            edge_mask(low, high, strips, tok_dev), lambda h: k_turned[h], big,
        )
        last = big - ALIGN
        body = last - WIN + ALIGN
        body_mask = row_mask(low - body, high - body, strips, WIN - ALIGN, DH)
        first_mask = row_mask(low, ALIGN, strips, ALIGN, DH)
        last_mask = row_mask(0, high - last, strips, ALIGN, DH)
        for h in range(heads):
            dk_acc[h], dv_acc[h] = dk_new[h], dv_new[h]
            rows_new = dq_t[h].T.reshape(strips, WIN, DH)
            edge = rows_new[:, WIN - ALIGN :].reshape(strips * ALIGN, DH)
            inner = rows_new[:, : WIN - ALIGN].reshape(strips * (WIN - ALIGN), DH)
            put_tile(dq, at + body, h, body_mask, inner, WIN - ALIGN, DH)
            put_tile(dq, at, h, first_mask, edge, ALIGN, DH)
            put_tile(dq, at + last, h, last_mask, edge, ALIGN, DH)

        def each(i, _):
            offset = ALIGN + i * WIN
            at_q = pl.multiple_of(at + offset, ALIGN)
            mask_q = row_mask(low - offset, high - offset, strips)
            half = row_mask(low - offset, high - offset, strips, width=DH)
            dq_t, dk_new, dv_new = plain(at_q, pl.multiple_of(at, ALIGN), mask_q, lambda h: k_turned[h], big)
            for h in range(heads):
                put_tile(dq, at_q, h, half, dq_t[h].T, width=DH)
                dk_acc[h] = dk_acc[h] + dk_new[h]
                dv_acc[h] = dv_acc[h] + dv_new[h]
            return 0

        lax.fori_loop(0, big // WIN - 1, each, 0)
        for h in range(heads):
            put_tile(dk, at, h, mask, dk_acc[h], big)
            put_tile(dv, at, h, mask, dv_acc[h], big)

    def large(start, end, first, windows):
        rows = strips * WIN

        def clear(i, _):
            for h in range(heads):
                dq_turned[h, i] = jnp.zeros(dq_turned.shape[2:], F32)
            return 0

        lax.fori_loop(0, windows, clear, 0)

        def k_window(k, _):
            at_k, low_k, high_k = window(start, end, first, k, tok_dev)
            mask_k = row_mask(low_k, high_k, strips)
            for h in range(heads):
                k_turned[h, :, :rows] = turned(h, at_k, mask_k)
            dk_acc[:, :rows] = jnp.zeros((heads, rows, LANES), F32)
            dv_acc[:, :rows] = jnp.zeros((heads, rows, LANES), F32)

            def q_window(i, _):
                at_q, low_q, high_q = window(start, end, first, i, tok_dev)
                mask_q = row_mask(low_q, high_q, strips)
                dq_t, dk_new, dv_new = plain(at_q, at_k, mask_q, lambda h: k_turned[h, :, :rows])
                for h in range(heads):
                    dq_turned[h, i] += dq_t[h]
                    dk_acc[h, :rows] += dk_new[h]
                    dv_acc[h, :rows] += dv_new[h]
                return 0

            lax.fori_loop(0, windows, q_window, 0)
            for h in range(heads):
                put_tile(dk, at_k, h, mask_k, dk_acc[h, :rows])
                put_tile(dv, at_k, h, mask_k, dv_acc[h, :rows])
            return 0

        lax.fori_loop(0, windows, k_window, 0)

        def q_out(i, _):
            at_q, low_q, high_q = window(start, end, first, i, tok_dev)
            half = row_mask(low_q, high_q, strips, width=DH)
            for h in range(heads):
                put_tile(dq, at_q, h, half, dq_turned[h, i].T, width=DH)
            return 0

        lax.fori_loop(0, windows, q_out, 0)

    for_segments(len_ref, group_ref, seg, strips, tok_dev, pieces, loads, [], small, middle, large)

    rows = strips * WIN
    left = left_half(rows)
    sums = half_sums(2 * LANES)
    gains = pair_row(q_gain, k_gain, heads)
    for load in loads:
        load.wait()

    def save(i):
        where = pl.ds(pl.multiple_of(i * WIN, WIN), WIN)
        return pltpu.make_async_copy(d_qkv.at[:, where], d_qkv_hbm.at[:, where], out_sem.at[i])

    def chunk(i, totals):
        at = pl.multiple_of(i * WIN, WIN)
        scaled, new_totals, us = [], [], []
        for h in range(heads):
            cols = slice(h * LANES, (h + 1) * LANES)
            d_q, d_k = tile(dq, at, h), tile(dk, at, h) * (1.0 / LOG2E)
            both = jnp.where(left, d_q * DH ** (-0.5), pltpu.roll(d_k, DH, 1))
            u = tile(u_rows, at, h).astype(F32)
            new_totals.append(totals[h] + jnp.sum(both * u, axis=0, keepdims=True))
            scaled.append(both * gains[:, cols])
            us.append(u)
        pairs = [jnp.concatenate([scaled[h].astype(BF16), (scaled[h] * us[h]).astype(BF16)], axis=1) for h in range(heads)]
        means = nn(jnp.concatenate(pairs, axis=0), sums) * (1.0 / DH)
        parts = []
        for h in range(heads):
            mean = means[h * rows : (h + 1) * rows, :LANES]
            mean_u = means[h * rows : (h + 1) * rows, LANES:]
            parts.append((scaled[h] - mean - us[h] * mean_u) * tile(r_rows, at, h).astype(F32))
        values = [tile(dv, at, h) for h in range(heads)]
        if heads % 2:
            values.append(jnp.zeros_like(values[0]))
        for b in range(len(values) // 2):
            parts.append(jnp.where(left, values[2 * b], pltpu.roll(values[2 * b + 1], DH, 1)))
        for b, part in enumerate(parts):
            d_qkv[:, pl.ds(at, WIN), b * LANES : (b + 1) * LANES] = part.astype(BF16).reshape(strips, WIN, LANES)
        save(i).start()
        return tuple(new_totals)

    totals = lax.fori_loop(0, tok_dev // WIN, chunk, tuple(jnp.zeros((1, LANES), F32) for _ in range(heads)))
    gain_grad[...] = jnp.zeros_like(gain_grad)
    for h in range(heads):
        gain_grad[0:1, h * LANES : (h + 1) * LANES] = totals[h]

    def saved(i, _):
        save(i).wait()
        return 0

    lax.fori_loop(0, tok_dev // WIN, saved, 0)


def attn_bwd(image_len, image_group, qb, ka, va, dob, u, r, q_gain, k_gain):
    strips, tok_dev, width = qb.shape
    heads = width // LANES
    blocks = heads + (heads + 1) // 2
    rows = strips * WIN
    big = strips * middle_rows(tok_dev)
    windows = tok_dev // WIN + 1
    full = pltpu.VMEM((strips, tok_dev, width), F32)
    return pl.pallas_call(
        functools.partial(attn_bwd_body, heads),
        out_shape=(
            jax.ShapeDtypeStruct((strips, tok_dev, blocks * LANES), BF16),
            jax.ShapeDtypeStruct((8, width), F32),
        ),
        in_specs=[SMEM, SMEM] + [ANY] * 6 + [VMEM] * 2,
        out_specs=(ANY, VMEM),
        scratch_shapes=[
            pltpu.SMEM((2, image_len.shape[0] + 1), jnp.int32),
            pltpu.VMEM((heads, DH, big), BF16),
            pltpu.VMEM((heads, windows, DH, rows), F32),
            pltpu.VMEM((heads, big, LANES), F32),
            pltpu.VMEM((heads, big, LANES), F32),
            full, full, full,
        ] + [pltpu.VMEM(qb.shape, BF16)] * 6 + [
            pltpu.VMEM((strips, tok_dev, blocks * LANES), BF16),
            pltpu.SemaphoreType.DMA((4, PIECES)),
            pltpu.SemaphoreType.DMA((tok_dev // WIN,)),
            pltpu.SemaphoreType.DMA((2,)),
        ],
        compiler_params=pltpu.CompilerParams(vmem_limit_bytes=60 << 20),
        cost_estimate=pl.CostEstimate(flops=16 * 10**9, bytes_accessed=30 * 10**6, transcendentals=8 * 10**6),
        name="attention_backward",
    )(image_len, image_group, qb, ka, va, dob, u, r, q_gain, k_gain)


CHUNKS = 8
BACK_CHUNKS = 4


def kind_order(heads):
    return [3 * h + i for h in range(heads) for i in range(2)] + [3 * h + 2 for h in range(heads)]


def remote(src, dst, send, recv, device):
    return pltpu.make_async_remote_copy(
        src_ref=src, dst_ref=dst, send_sem=send, recv_sem=recv, device_id=device, device_id_type=pl.DeviceIdType.MESH
    )


def lo_rows(features):
    return 2 * features * 2 // 3


def front_body(
    heads, n_hi, n_lo, tokens_hbm, cot_hbm, ln_gain, q_gain, k_gain, mlp_bias, qkv_hbm, attn_hbm, mlp_in_hbm, mlp_out_hbm,
    qa_out, ka_out, va_out, do_out, u_out, r_out, mlp_part_out, dn_part_out, nall_out, call_out,
    *rest,
):
    (rows_out, both, wide, narrow, qkv_rows, attn_pad, mlp_in, mlp_out, g_in, g_out,
     tokens, low, send_sem, recv_sem, save_sem, load_sem, row_sem) = rest[-17:]
    lo_first, hi_first = rest[:n_lo], rest[n_lo : n_lo + n_hi]
    batch, me = lax.axis_index("batch"), lax.axis_index("tensor")
    sibling = me + 1 - 2 * (me % 2)
    across = (me + 2) % 4
    chip, far_chip = me // 2, 1 - me // 2
    tok_dev = tokens_hbm.shape[0]
    step = tok_dev // CHUNKS
    features = tokens_hbm.shape[1]
    heads_wide = heads * LANES

    def rows_of(c):
        return pl.ds(pl.multiple_of(c * step, step), step)

    def move(kind, route, c, strip, to):
        part = both.at[kind, strip, rows_of(c)]
        return remote(part, part, send_sem.at[kind, route, c], recv_sem.at[kind, route, c], (batch, to))

    load_cot = pltpu.make_async_copy(cot_hbm, both.at[0, me], row_sem.at[0])
    load_tokens = pltpu.make_async_copy(tokens_hbm, tokens, row_sem.at[1])
    load_cot.start()
    load_tokens.start()
    barrier = pltpu.get_barrier_semaphore()
    for other in (sibling, across):
        pl.semaphore_signal(barrier, inc=1, device_id=(batch, other), device_id_type=pl.DeviceIdType.MESH)
    loads = [(mlp_in_hbm, mlp_in), (mlp_out_hbm, mlp_out)]
    loads += [
        (qkv_hbm.at[pl.ds(to * DH, DH)], qkv_rows.at[pl.ds(i * DH, DH)]) for i, to in enumerate(kind_order(heads))
    ]
    loads += [(attn_hbm.at[pl.ds(h * DH, DH)], attn_pad.at[pl.ds(h * LANES, DH)]) for h in range(heads)]
    loads = [pltpu.make_async_copy(a, b, load_sem.at[i]) for i, (a, b) in enumerate(loads)]
    for load in loads:
        load.start()
    gain = row_of(ln_gain)
    gains = pair_row(q_gain, k_gain, heads)

    def norm_chunk(c):
        x = tokens[rows_of(c)].astype(F32)
        centred = x - jnp.mean(x, axis=-1, keepdims=True)
        variance = jnp.mean(centred * centred, axis=-1, keepdims=True)
        both[1, me, rows_of(c)] = (centred * lax.rsqrt(variance + epsilon) * gain).astype(BF16)

    def send_across(c):
        for kind in range(2):
            move(kind, 1, c, me, across).start()

    load_cot.wait()
    pl.semaphore_wait(barrier, 2)
    early = 3
    for c in range(early):
        move(0, 1, c, me, across).start()
    load_tokens.wait()

    def first_sends(c, _):
        norm_chunk(c)

        @pl.when(c < early)
        def _():
            move(1, 1, c, me, across).start()

        for kind in range(2):
            move(kind, 0, c, me, sibling).start()

        return 0

    lax.fori_loop(0, CHUNKS, first_sends, 0)

    g_in[...] = jnp.zeros_like(g_in)
    g_out[...] = jnp.zeros_like(g_out)
    rows_out[...] = jnp.zeros_like(rows_out)
    rows_out[1:2, :] = jnp.sum(both[0, me].astype(F32), axis=0, keepdims=True)
    filled = 3 * heads * DH
    if filled < qkv_rows.shape[0]:
        qkv_rows[filled:] = jnp.zeros((qkv_rows.shape[0] - filled, features), BF16)
    for h in range(heads):
        attn_pad[h * LANES + DH : (h + 1) * LANES, :] = jnp.zeros((DH, features), BF16)
    for load in loads:
        load.wait()

    sums = half_sums()
    bias = row_of(mlp_bias)

    def chunks_of(c, n):
        return pl.ds(pl.multiple_of(c * step, step), n * step)

    def saves(at_chip, c, n):
        strips, where = pl.ds(2 * at_chip, 2), chunks_of(c, n)
        first = at_chip * CHUNKS + c
        pairs = [(narrow.at[a, strips, where], ref.at[strips, where]) for a, ref in enumerate(
            (qa_out, ka_out, va_out, do_out, u_out, r_out))]
        pairs += [(wide.at[a, strips, where], ref.at[strips, where]) for a, ref in enumerate((mlp_part_out, dn_part_out))]
        pairs += [(both.at[1, strips, where], nall_out.at[strips, where]), (both.at[0, strips, where], call_out.at[strips, where])]
        return [pltpu.make_async_copy(a, b, save_sem.at[i, first]) for i, (a, b) in enumerate(pairs)]

    def wait_sibling(c):
        for kind in range(2):
            move(kind, 0, c, sibling, sibling).wait_recv()

    def pass_on(c):
        for kind in range(2):
            move(kind, 1, c, across, across).wait_recv()
            move(kind, 2, c, across, sibling).start()

    def wait_passed(c):
        for kind in range(2):
            move(kind, 2, c, across + 1 - 2 * (across % 2), sibling).wait_recv()

    def unit(at_chip, c, n, between=None):
        rows = 2 * n * step
        left = left_half(rows)
        strips, where = pl.ds(2 * at_chip, 2), chunks_of(c, n)
        normed = both[1, strips, where].reshape(rows, features)
        d = both[0, strips, where].reshape(rows, features)

        def save(ref, a, h, value):
            ref[a, strips, where, h * LANES : (h + 1) * LANES] = value.astype(BF16).reshape(2, n * step, LANES)

        qkv = nt(normed, qkv_rows[...])

        def block(b):
            return qkv[:, b * LANES : (b + 1) * LANES]

        def stacked_means(parts):
            stacked = jnp.concatenate([p.astype(BF16) for p in parts], axis=0)
            means = nn(stacked, sums) * (1.0 / DH)
            return [means[h * rows : (h + 1) * rows] for h in range(heads)]

        pairs = [block(h) for h in range(heads)]
        means = stacked_means(pairs)
        centred = [pairs[h] - means[h] for h in range(heads)]
        variances = stacked_means([x * x for x in centred])
        hidden = nn(normed, mlp_in[...]) + bias
        d_act = nt(d, mlp_out[...])
        if between:
            between()
        for h in range(heads):
            rstd = lax.rsqrt(variances[h] + epsilon)
            u = centred[h] * rstd
            scaled = u * gains[:, h * LANES : (h + 1) * LANES]
            save(narrow, 0, h, jnp.where(left, scaled * (DH ** (-0.5) * LOG2E), 0.0))
            save(narrow, 1, h, jnp.where(left, pltpu.roll(scaled, DH, 1), 1.0))
            value = block(heads + h // 2)
            save(narrow, 2, h, jnp.where(left, pltpu.roll(value, DH, 1) if h % 2 else value, 1.0))
            save(narrow, 4, h, u)
            save(narrow, 5, h, rstd)
        narrow[3, strips, where] = nt(d, attn_pad[...]).astype(BF16).reshape(2, n * step, heads_wide)
        cdf = 0.5 + 0.5 * lax.erf(hidden * 0.7071067811865476)
        act = (hidden * cdf).astype(BF16)
        slope = cdf + hidden * (0.3989422804014327 * jnp.exp(hidden * hidden * -0.5))
        d_low = (d_act * slope).astype(BF16)
        wide[0, strips, where] = nn(act, mlp_out[...]).astype(BF16).reshape(2, n * step, features)
        d_normed = nt(d_low, mlp_in[...])
        rows_out[2:3, :] += jnp.sum(d_normed * normed.astype(F32), axis=0, keepdims=True)
        wide[1, strips, where] = d_normed.astype(BF16).reshape(2, n * step, features)
        rows_out[0:1, :] += jnp.sum(d_low.astype(F32), axis=0, keepdims=True)
        g_out[...] += tn(act, d)
        g_in[...] += tn(normed, d_low)
        for copy in saves(at_chip, c, n):
            copy.start()

    half, quarter = CHUNKS // 2, CHUNKS // 4
    for c in range(half):
        wait_sibling(c)
    unit(chip, 0, half)

    def middle(i, _):
        send_across(3 + i)

        @pl.when(i < 2)
        def _():
            for c in range(quarter):
                wait_sibling(half + i * quarter + c)

        @pl.when(i == 4)
        def _():
            pass_on(5)

        @pl.when(i >= 2)
        def _():
            for c in range(quarter):
                wait_passed((i - 2) * quarter + c)

        def between():
            @pl.when((i == 1) | (i == 2))
            def _():
                pass_on(2 * i - 2)
                pass_on(2 * i - 1)

            @pl.when(i == 3)
            def _():
                pass_on(4)

        unit(
            jnp.where(i < 2, chip, far_chip), jnp.where(i < 2, half + i * quarter, (i - 2) * quarter), quarter, between
        )
        return 0

    lax.fori_loop(0, 5, middle, 0)

    def last(i, _):
        pass_on(6 + i)
        wait_passed(6 + i)
        unit(far_chip, 6 + i, 1)
        return 0

    lax.fori_loop(0, 2, last, 0)

    hi, lo = batch // n_lo, batch % n_lo
    def grad_saves():
        made = []
        for o in range(n_hi * n_lo):
            at_hi = (o // n_lo - hi + n_hi) % n_hi
            at_lo = (o % n_lo - lo + n_lo) % n_lo
            for first, part in ((0, lo_first), (lo_rows(features), hi_first)):
                count = part[0].shape[1]
                rows = low.at[pl.ds(first + o * count, count)]
                slot, place = (at_lo, at_hi) if first == 0 else (at_hi, at_lo)
                for m in range(len(part)):
                    made.append((slot == m, pltpu.make_async_copy(rows, part[m].at[place], save_sem.at[10, (first > 0) * n_hi * n_lo + o])))
        return made

    low[:features] = g_in[...].astype(BF16)
    low[features:] = g_out[...].astype(BF16)
    for chosen, copy in grad_saves():

        @pl.when(chosen)
        def _():
            copy.start()

    for chosen, copy in grad_saves():

        @pl.when(chosen)
        def _():
            copy.wait()

    for at_chip, c, n in (
        [(chip, 0, half), (chip, half, quarter), (chip, half + quarter, quarter)]
        + [(far_chip, i * quarter, quarter) for i in range(3)] + [(far_chip, 6, 1), (far_chip, 7, 1)]
    ):
        for copy in saves(at_chip, c, n):
            copy.wait()

    def sent(c, _):
        for kind in range(2):
            move(kind, 0, c, me, sibling).wait_send()
            move(kind, 1, c, me, across).wait_send()
            move(kind, 2, c, across, sibling).wait_send()
        return 0

    lax.fori_loop(0, CHUNKS, sent, 0)


def front(strips, n_batch, tokens, cot, ln_gain, q_gain, k_gain, mlp_bias, qkv_weight_t, attn_out, mlp_in, mlp_out):
    tok_dev, features = tokens.shape
    heads = q_gain.shape[0] // DH
    width = heads * LANES
    hidden = mlp_in.shape[1]
    blocks = heads + (heads + 1) // 2
    n_hi, n_lo = levels(n_batch)
    like = jax.ShapeDtypeStruct((strips, tok_dev, width), BF16)
    rows = jax.ShapeDtypeStruct((strips, tok_dev, features), BF16)
    return pl.pallas_call(
        functools.partial(front_body, heads, n_hi, n_lo),
        out_shape=(like,) * 6 + (rows,) * 4 + (
            jax.ShapeDtypeStruct((n_hi, lo_rows(features) // n_batch, features), BF16),
        ) * n_lo + (
            jax.ShapeDtypeStruct((n_lo, (2 * features - lo_rows(features)) // n_batch, features), BF16),
        ) * n_hi + (jax.ShapeDtypeStruct((8, features), F32),),
        in_specs=[ANY] * 2 + [VMEM] * 4 + [ANY] * 4,
        out_specs=(ANY,) * (10 + n_lo + n_hi) + (VMEM,),
        scratch_shapes=[
            pltpu.VMEM((2, strips, tok_dev, features), BF16),
            pltpu.VMEM((2, strips, tok_dev, features), BF16),
            pltpu.VMEM((6, strips, tok_dev, width), BF16),
            pltpu.VMEM((blocks * LANES, features), BF16),
            pltpu.VMEM((width, features), BF16),
            pltpu.VMEM(mlp_in.shape, BF16),
            pltpu.VMEM(mlp_out.shape, BF16),
            pltpu.VMEM((features, hidden), F32),
            pltpu.VMEM((hidden, features), F32),
            pltpu.VMEM(tokens.shape, BF16),
            pltpu.VMEM((features + hidden, features), BF16),
            pltpu.SemaphoreType.DMA((2, 3, CHUNKS)),
            pltpu.SemaphoreType.DMA((2, 3, CHUNKS)),
            pltpu.SemaphoreType.DMA((11, max(2 * CHUNKS, 2 * n_batch))),
            pltpu.SemaphoreType.DMA((2 + 4 * heads,)),
            pltpu.SemaphoreType.DMA((2,)),
        ],
        compiler_params=pltpu.CompilerParams(collective_id=0, has_side_effects=True, vmem_limit_bytes=60 << 20),
        name="gather_and_project",
    )(tokens, cot, ln_gain, q_gain, k_gain, mlp_bias, qkv_weight_t, attn_out, mlp_in, mlp_out)


def back_body(
    heads, n_hi, n_lo, d_qkv_hbm, nall_hbm, dn_part_hbm, ho_hbm, call_hbm, mlp_part_hbm, qkv_weight_t, attn_out, tokens, cot,
    ln_gain, out_bias, own_lo, own_hi, front_rows, gain_rows, output, input_grad, mlp_all_out, joint_all_out, rows_out,
    d_qkv, nall, dn_part, ho, call, mlp_part, weight_t, attn_pad, acc, attn_acc, joint, joint_low, joint_got, joint_sum,
    joint_got_hi, joint_all, mlp_all, near, core_give, core_got, x_give, x_got, vec, vec_lo, vec_hi, vec_pair,
    load_sem, mlp_z_s, mlp_z_r, mlp_y_s, mlp_y_r, joint_s, joint_r, hi_s, hi_r, all_z_s, all_z_r, all_y_s, all_y_r,
    core_s, core_r, x_s, x_r, vec_s, vec_r, save_sem,
):
    batch, me = lax.axis_index("batch"), lax.axis_index("tensor")
    hi, lo = batch // n_lo, batch % n_lo
    sibling = me + 1 - 2 * (me % 2)
    across = (me + 2) % 4
    far_sibling = (sibling + 2) % 4
    tok_dev, features = tokens.shape
    step = tok_dev // BACK_CHUNKS
    chunk_rows, half_cols = joint.shape[2], joint.shape[3]
    every_k, every_m = range(1, n_hi), range(1, n_lo)
    cut = chunk_rows // 2 // 16 * 16
    parts = [pl.ds(0, cut), pl.ds(cut, chunk_rows - cut)]

    strips = call.shape[0]
    by_strip = ((ho_hbm, ho), (call_hbm, call), (d_qkv_hbm, d_qkv), (nall_hbm, nall))

    def strip_loads(i):
        return [pltpu.make_async_copy(a.at[i], b.at[i], load_sem.at[n, i]) for n, (a, b) in enumerate(by_strip)]

    def rest_loads():
        pairs = ((dn_part_hbm, dn_part), (mlp_part_hbm, mlp_part))
        return [pltpu.make_async_copy(a, b, load_sem.at[len(by_strip) + n, 0]) for n, (a, b) in enumerate(pairs)]

    for i in range(strips):
        for load in strip_loads(i):
            load.start()
    for load in rest_loads():
        load.start()

    def hi_peer(k):
        return (hi + k + n_hi) % n_hi

    def lo_peer(m):
        return (lo + m + n_lo) % n_lo

    def to_hi(k):
        return (hi_peer(k) * n_lo + lo, me)

    def to_lo(m):
        return (hi * n_lo + lo_peer(m), me)

    barrier = pltpu.get_barrier_semaphore()
    peers = [to_hi(k) for k in every_k] + [to_lo(m) for m in every_m] + [(batch, sibling), (batch, across)]
    for peer in peers:
        pl.semaphore_signal(barrier, inc=1, device_id=peer, device_id_type=pl.DeviceIdType.MESH)
    mlp_all[hi, lo] = jnp.concatenate([own_lo[...], own_hi[...]], axis=0)
    pl.semaphore_wait(barrier, len(peers))

    def mlp_hop(s, up, origin):
        part = mlp_all.at[origin, lo]
        to = ((hi + (1 if up else -1) + n_hi) % n_hi * n_lo + lo, me)
        return remote(part, part, mlp_z_s.at[up, s], mlp_z_r.at[up, s], to)

    def mlp_send_hop(s, wait=False):
        for up in range(2):
            origin = hi - (s - 1) if up else hi + (s - 1)
            there = (origin >= 0) & (hi + 1 < n_hi) if up else (origin < n_hi) & (hi >= 1)

            @pl.when(there)
            def _():
                hop = mlp_hop(s, up, (origin + n_hi) % n_hi)
                hop.wait_send() if wait else hop.start()

    def mlp_wait_hop(s):
        for up in range(2):
            origin = hi - s if up else hi + s

            @pl.when((origin >= 0) if up else (origin < n_hi))
            def _():
                mlp_hop(s, up, (origin + n_hi) % n_hi).wait_recv()

    def mlp_lo(m, k, back=0):
        part = mlp_all.at[hi_peer(k), lo_peer(back)]
        return remote(part, part, mlp_y_s.at[m, k], mlp_y_r.at[m, k], to_lo(m))

    def mlp_send_lo(s):
        for m in every_m:
            for k, there in ((s, hi + s < n_hi), (n_hi - s, hi >= s)):

                @pl.when(there)
                def _():
                    mlp_lo(m, k).start()

    for m in every_m:
        mlp_lo(m, 0).start()
    mlp_send_hop(1)

    for i, place in enumerate(kind_order(heads)):
        weight_t[i * DH : (i + 1) * DH] = qkv_weight_t[place * DH : (place + 1) * DH]
    filled = qkv_weight_t.shape[0]
    if filled < weight_t.shape[0]:
        weight_t[filled:] = jnp.zeros((weight_t.shape[0] - filled, features), BF16)
    head_width = attn_out.shape[0]
    attn_pad[:head_width] = attn_out[...]
    attn_pad[head_width:] = jnp.zeros((attn_pad.shape[0] - head_width, features), BF16)
    acc[...] = jnp.zeros_like(acc)
    attn_acc[...] = jnp.zeros_like(attn_acc)

    def add_strip(i, _):
        for load in strip_loads(i):
            load.wait()
        acc[...] += tn(d_qkv[i], nall[i])
        attn_acc[...] += tn(ho[i], call[i])
        return 0

    lax.fori_loop(0, nall.shape[0], add_strip, 0)
    width = qkv_weight_t.shape[0]
    joint_low[:width] = acc[:width].astype(BF16)
    joint_low[width:] = attn_acc[:head_width].astype(BF16)
    per_half = features // chunk_rows
    for o in range(n_hi * n_lo):
        row = o % per_half * chunk_rows
        col = o // per_half * half_cols
        joint[o % n_lo, o // n_lo] = joint_low[row : row + chunk_rows, col : col + half_cols]

    def joint_lo(p, m, back=0):
        return remote(
            joint.at[lo_peer(m), :, parts[p]], joint_got.at[lo_peer(back), :, parts[p]], joint_s.at[m, p], joint_r.at[m, p], to_lo(m)
        )

    def joint_hi(p, k, back=0):
        return remote(
            joint_sum.at[hi_peer(k), parts[p]], joint_got_hi.at[hi_peer(back), parts[p]], hi_s.at[k, p], hi_r.at[k, p], to_hi(k)
        )

    def joint_sum_lo(p):
        for m in every_m:
            joint_lo(p, m, -m).wait_recv()
        total = joint[lo, :, parts[p]].astype(F32)
        for m in every_m:
            total = total + joint_got[lo_peer(m), :, parts[p]].astype(F32)
        joint_sum[:, parts[p]] = total.astype(BF16)
        for k in every_k:
            joint_hi(p, k).start()

    def all_hi(p, k, back=0):
        part = joint_all.at[lo, hi_peer(back), parts[p]]
        return remote(part, part, all_z_s.at[k, p], all_z_r.at[k, p], to_hi(k))

    def all_lo(p, m, back=0):
        part = joint_all.at[lo_peer(back), :, parts[p]]
        return remote(part, part, all_y_s.at[m, p], all_y_r.at[m, p], to_lo(m))

    def joint_sum_hi(p):
        total = joint_sum[hi, parts[p]].astype(F32)
        for k in every_k:
            joint_hi(p, k, -k).wait_recv()
            total = total + joint_got_hi[hi_peer(-k), parts[p]].astype(F32)
        joint_all[lo, hi, parts[p]] = total.astype(BF16)
        for k in every_k:
            all_hi(p, k).start()

    def joint_pass(p):
        for k in every_k:
            all_hi(p, k, -k).wait_recv()
        for m in every_m:
            all_lo(p, m).start()

    for m in every_m:
        joint_lo(0, m).start()

    ln_row = jnp.sum(acc[...] * weight_t[...].astype(F32), axis=0, keepdims=True)
    gain = row_of(ln_gain)
    vec_lo[lo] = front_rows[...]
    vec_lo[lo, 2:3, :] = (front_rows[2:3, :] + ln_row) / gain
    vec_lo[lo, 3:4, 0 : heads * LANES] = gain_rows[0:1, :]

    def vec_lo_move(m, back=0):
        part = vec_lo.at[lo_peer(back)]
        return remote(part, part, vec_s.at[m], vec_r.at[m], to_lo(m))

    def vec_hi_move(k, back=0):
        part = vec_hi.at[hi_peer(back)]
        return remote(part, part, vec_s.at[n_lo + k], vec_r.at[n_lo + k], to_hi(k))

    def vec_pair_move(i, to):
        return remote(vec.at[i], vec_pair.at[i], vec_s.at[n_lo + n_hi + i], vec_r.at[n_lo + n_hi + i], (batch, to))

    for m in every_m:
        vec_lo_move(m).start()
    mlp_wait_hop(1)
    mlp_send_hop(2)

    def rows_of(c):
        return pl.ds(pl.multiple_of(c * step, step), step)

    def partial_rows(which, strip, c):
        if which == 0:
            return nn(d_qkv[strip, rows_of(c)], weight_t[...]) + dn_part[strip, rows_of(c)].astype(F32)
        return nn(ho[strip, rows_of(c)], attn_pad[...]) + mlp_part[strip, rows_of(c)].astype(F32)

    def core_move(which, side, c):
        where = rows_of(c)
        return remote(
            core_give.at[which, side, where], core_got.at[which, side, where],
            core_s.at[which, side, c], core_r.at[which, side, c], (batch, sibling),
        )

    def x_move(which, c):
        where = rows_of(c)
        return remote(x_give.at[which, where], x_got.at[which, where], x_s.at[which, c], x_r.at[which, c], (batch, across))

    def far(which):
        def give(c, _):
            core_give[which, 0, rows_of(c)] = partial_rows(which, far_sibling, c).astype(BF16)
            core_move(which, 0, c).start()
            return 0

        def send(c, _):
            mine = partial_rows(which, across, c)
            core_move(which, 0, c).wait_recv()
            x_give[which, rows_of(c)] = (mine + core_got[which, 0, rows_of(c)].astype(F32)).astype(BF16)
            x_move(which, c).start()
            return 0

        lax.fori_loop(0, BACK_CHUNKS, give, 0)
        lax.fori_loop(0, BACK_CHUNKS, send, 0)

    def close(which):
        def give(c, _):
            core_give[which, 1, rows_of(c)] = partial_rows(which, sibling, c).astype(BF16)
            core_move(which, 1, c).start()
            return 0

        def keep(c, _):
            mine = partial_rows(which, me, c)
            core_move(which, 1, c).wait_recv()
            near[which, rows_of(c)] = mine + core_got[which, 1, rows_of(c)].astype(F32)
            return 0

        lax.fori_loop(0, BACK_CHUNKS, give, 0)
        lax.fori_loop(0, BACK_CHUNKS, keep, 0)

    for load in rest_loads():
        load.wait()
    far(0)
    for m in every_m:
        joint_lo(1, m).start()
    far(1)
    joint_sum_lo(0)
    for s in range(2, n_hi - 1):
        mlp_wait_hop(s)
        mlp_send_hop(s + 1)
    close(0)
    joint_sum_lo(1)
    mlp_send_lo(1)
    close(1)

    for m in every_m:
        vec_lo_move(m, -m).wait_recv()
    total = vec_lo[0]
    for i in range(1, n_lo):
        total = total + vec_lo[i]
    vec_hi[hi] = total
    for k in every_k:
        vec_hi_move(k).start()

    joint_sum_hi(0)
    for s in range(2, n_hi - 1):
        mlp_send_lo(s)
    joint_sum_hi(1)
    if n_hi > 2:
        mlp_wait_hop(n_hi - 1)
        mlp_send_lo(n_hi - 1)

    for k in every_k:
        vec_hi_move(k, -k).wait_recv()
    total = vec_hi[0]
    for i in range(1, n_hi):
        total = total + vec_hi[i]
    vec[0] = total
    vec_pair_move(0, sibling).start()

    joint_pass(0)
    vec_pair_move(0, sibling).wait_recv()
    vec[1] = vec[0] + vec_pair[0]
    vec_pair_move(1, across).start()

    def last_rows(c, _):
        x_move(0, c).wait_recv()
        where = rows_of(c)
        d_normed = near[0, where] + x_got[0, where].astype(F32)
        x = tokens[where].astype(F32)
        centred = x - jnp.mean(x, axis=-1, keepdims=True)
        r = lax.rsqrt(jnp.mean(centred * centred, axis=-1, keepdims=True) + epsilon)
        xhat = centred * r
        e = d_normed * gain
        d_x = r * (e - jnp.mean(e, axis=-1, keepdims=True) - xhat * jnp.mean(e * xhat, axis=-1, keepdims=True))
        input_grad[where] = (cot[where].astype(F32) + d_x).astype(BF16)
        return 0

    lax.fori_loop(0, BACK_CHUNKS, last_rows, 0)
    joint_pass(1)
    bias = row_of(out_bias)

    def out_rows(c, _):
        x_move(1, c).wait_recv()
        where = rows_of(c)
        output[where] = (tokens[where].astype(F32) + near[1, where] + x_got[1, where].astype(F32) + bias).astype(BF16)
        return 0

    lax.fori_loop(0, BACK_CHUNKS, out_rows, 0)
    vec_pair_move(1, across).wait_recv()
    rows_out[...] = vec[0]
    rows_out[1:3, :] = vec[1, 1:3, :] + vec_pair[1, 1:3, :]

    for m in every_m:
        for k in range(n_hi):
            mlp_lo(m, k, -m).wait_recv()
    save_mlp = pltpu.make_async_copy(mlp_all, mlp_all_out, save_sem.at[0])
    save_mlp.start()
    for s in range(1, n_hi):
        mlp_send_hop(s, wait=True)
    for m in every_m:
        for k in range(n_hi):
            mlp_lo(m, k).wait_send()
        for p in range(2):
            joint_lo(p, m).wait_send()
        vec_lo_move(m).wait_send()
    for k in every_k:
        for p in range(2):
            joint_hi(p, k).wait_send()
            all_hi(p, k).wait_send()
        vec_hi_move(k).wait_send()
    vec_pair_move(0, sibling).wait_send()
    vec_pair_move(1, across).wait_send()

    def sent(c, _):
        for which in range(2):
            core_move(which, 0, c).wait_send()
            core_move(which, 1, c).wait_send()
            x_move(which, c).wait_send()
        return 0

    lax.fori_loop(0, BACK_CHUNKS, sent, 0)
    for m in every_m:
        for p in range(2):
            all_lo(p, m, -m).wait_recv()
            all_lo(p, m).wait_send()
    save_joint = pltpu.make_async_copy(joint_all, joint_all_out, save_sem.at[1])
    save_joint.start()
    save_mlp.wait()
    save_joint.wait()


def levels(n_batch):
    lo = 2 if n_batch <= 8 else 4
    return n_batch // lo, lo


def back(
    n_batch, d_qkv, nall, dn_part, ho, call, mlp_part, qkv_weight_t, attn_out, tokens, cot, ln_gain, out_bias,
    own_lo, own_hi, front_rows, gain_rows,
):
    n_hi, n_lo = levels(n_batch)
    strips, tok_dev, features = nall.shape
    own = (own_lo.shape[0] + own_hi.shape[0], features)
    wide, packed = d_qkv.shape[2], ho.shape[2]
    heads = attn_out.shape[0] // DH
    chunk = (2 * features // n_batch, features // 2)
    dma = pltpu.SemaphoreType.DMA
    vmem = pltpu.VMEM
    return pl.pallas_call(
        functools.partial(back_body, heads, n_hi, n_lo),
        out_shape=(
            jax.ShapeDtypeStruct(tokens.shape, BF16),
            jax.ShapeDtypeStruct(tokens.shape, BF16),
            jax.ShapeDtypeStruct((n_hi, n_lo) + own, BF16),
            jax.ShapeDtypeStruct((n_lo, n_hi) + chunk, BF16),
            jax.ShapeDtypeStruct((8, features), F32),
        ),
        in_specs=[ANY] * 6 + [VMEM] * 10,
        out_specs=(VMEM, VMEM, ANY, ANY, VMEM),
        scratch_shapes=[
            vmem(d_qkv.shape, BF16), vmem(nall.shape, BF16), vmem(dn_part.shape, BF16),
            vmem(ho.shape, BF16), vmem(call.shape, BF16), vmem(mlp_part.shape, BF16),
            vmem((wide, features), BF16),
            vmem((packed, features), BF16),
            vmem((wide, features), F32),
            vmem((packed, features), F32),
            vmem((n_lo, n_hi) + chunk, BF16),
            vmem((features, features), BF16),
            vmem((n_lo, n_hi) + chunk, BF16),
            vmem((n_hi,) + chunk, BF16),
            vmem((n_hi,) + chunk, BF16),
            vmem((n_lo, n_hi) + chunk, BF16),
            vmem((n_hi, n_lo) + own, BF16),
            vmem((2,) + tokens.shape, F32),
            vmem((2, 2) + tokens.shape, BF16),
            vmem((2, 2) + tokens.shape, BF16),
            vmem((2,) + tokens.shape, BF16),
            vmem((2,) + tokens.shape, BF16),
            vmem((2, 8, features), F32),
            vmem((n_lo, 8, features), F32),
            vmem((n_hi, 8, features), F32),
            vmem((2, 8, features), F32),
            dma((6, strips)),
            dma((2, n_hi)), dma((2, n_hi)),
            dma((n_lo, n_hi)), dma((n_lo, n_hi)),
            dma((n_lo, 2)), dma((n_lo, 2)),
            dma((n_hi, 2)), dma((n_hi, 2)),
            dma((n_hi, 2)), dma((n_hi, 2)),
            dma((n_lo, 2)), dma((n_lo, 2)),
            dma((2, 2, BACK_CHUNKS)), dma((2, 2, BACK_CHUNKS)),
            dma((2, BACK_CHUNKS)), dma((2, BACK_CHUNKS)),
            dma((n_lo + n_hi + 2,)), dma((n_lo + n_hi + 2,)),
            dma((2,)),
        ],
        compiler_params=pltpu.CompilerParams(collective_id=1, has_side_effects=True, vmem_limit_bytes=60 << 20),
        name="reduce_gradients",
    )(
        d_qkv, nall, dn_part, ho, call, mlp_part, qkv_weight_t, attn_out, tokens, cot, ln_gain, out_bias,
        own_lo, own_hi, front_rows, gain_rows,
    )


def widen_body(
    heads, mlp_hbm, joint_hbm, output_in, input_grad_in, rows,
    output, input_grad, qkv_out, attn_out, mlp_in_out, mlp_out_out, ln_gain, q_gain, k_gain, mlp_bias, out_bias,
    kept, mlp_all, joint_all, joint, qkv_t, attn, mlp, sems,
):
    def copy(i, source, to):
        made = pltpu.make_async_copy(source, to, sems.at[i])
        made.start()
        return made

    load_joint = copy(0, joint_hbm, joint_all)
    load_mlp = copy(1, mlp_hbm, mlp_all)
    load_rows = [copy(2, output_in, kept.at[0]), copy(3, input_grad_in, kept.at[1])]
    features = rows.shape[1]
    mlp_bias[...] = rows[0:1, :].reshape(features)
    out_bias[...] = rows[1:2, :].reshape(features)
    ln_gain[...] = rows[2:3, :].reshape(features)
    for offset, ref in ((0, q_gain), (DH, k_gain)):
        parts = [rows[3:4, h * LANES + offset : h * LANES + offset + DH] for h in range(heads)]
        ref[...] = jnp.concatenate(parts, axis=1).reshape(heads * DH)
    load_joint.wait()
    n_lo, n_hi, chunk_rows, cols = joint_all.shape
    width = qkv_t.shape[0]
    per_half = features // chunk_rows
    for o in range(n_lo * n_hi):
        row = o % per_half * chunk_rows
        joint[o // per_half, row : row + chunk_rows] = joint_all[o % n_lo, o // n_lo]
    pending = []
    for half in range(2):
        at = slice(half * cols, (half + 1) * cols)
        attn[:, at] = joint[half, width:].astype(F32)
        for i, place in enumerate(kind_order(heads)):
            qkv_t[place * DH : (place + 1) * DH, at] = joint[half, i * DH : (i + 1) * DH].astype(F32)
    pending += [copy(4, qkv_t, qkv_out), copy(5, attn, attn_out)]
    load_mlp.wait()
    chunks = mlp_all.shape[0]
    cut = lo_rows(features) // chunks
    rest = mlp_all.shape[1] - cut
    for o in range(features // cut):
        mlp[o * cut : (o + 1) * cut] = mlp_all[o, :cut].astype(F32)
    pending.append(copy(6, mlp.at[pl.ds(0, features)], mlp_in_out))
    for o in range(features // cut, chunks):
        mlp[o * cut : (o + 1) * cut] = mlp_all[o, :cut].astype(F32)
    for o in range(chunks):
        row = lo_rows(features) + o * rest
        mlp[row : row + rest] = mlp_all[o, cut:].astype(F32)
    pending.append(copy(7, mlp.at[pl.ds(features, features)], mlp_out_out))
    for i, (load, to) in enumerate(zip(load_rows, (output, input_grad))):
        load.wait()
        pending.append(copy(8 + i, kept.at[i], to))
    for made in pending:
        made.wait()


def widen(heads, width, mlp_all, joint_all, output, input_grad, rows):
    features = rows.shape[1]
    head_width = heads * DH

    def out(*shape):
        return jax.ShapeDtypeStruct(shape, F32)

    like = jax.ShapeDtypeStruct(output.shape, BF16)
    return pl.pallas_call(
        functools.partial(widen_body, heads),
        out_shape=(
            like, like, out(width, features), out(head_width, features), out(features, features), out(features, features),
            out(features), out(head_width), out(head_width), out(features), out(features),
        ),
        in_specs=[ANY] * 4 + [VMEM],
        out_specs=(ANY,) * 6 + (VMEM,) * 5,
        scratch_shapes=[
            pltpu.VMEM((2,) + output.shape, BF16),
            pltpu.VMEM(mlp_all.shape, BF16),
            pltpu.VMEM(joint_all.shape, BF16),
            pltpu.VMEM((2, features, features // 2), BF16),
            pltpu.VMEM((width, features), F32),
            pltpu.VMEM((head_width, features), F32),
            pltpu.VMEM((2 * features, features), F32),
            pltpu.SemaphoreType.DMA((10,)),
        ],
        compiler_params=pltpu.CompilerParams(vmem_limit_bytes=60 << 20),
        name="widen_gradients",
    )(mlp_all, joint_all, output, input_grad, rows)


def on_device(
    tokens, out_cotangent, ln_gain, qkv_weight, q_gain, k_gain, attn_out,
    mlp_in, mlp_bias, mlp_out, out_bias, image_len, image_group,
):
    tok_dev, features = tokens.shape
    strips = lax.axis_size("tensor")
    n_batch = lax.axis_size("batch")
    n_hi, n_lo = levels(n_batch)
    heads = q_gain.shape[0] // DH
    qkv_cols = qkv_weight.shape[1]

    weight_t = qkv_weight.T
    (qa, ka, va, do, u, r, mlp_part, dn_part, nall, call, *mlp_grad, front_rows) = front(
        strips, n_batch, tokens, out_cotangent, ln_gain, q_gain, k_gain, mlp_bias, weight_t, attn_out, mlp_in, mlp_out
    )

    def along_lo(x, m):
        pairs = [(h * n_lo + i, h * n_lo + (i + m) % n_lo) for h in range(n_hi) for i in range(n_lo)]
        return lax.ppermute(x, "batch", pairs)

    def along_hi(x, k):
        pairs = [(h * n_lo + i, (h + k) % n_hi * n_lo + i) for h in range(n_hi) for i in range(n_lo)]
        return lax.ppermute(x, "batch", pairs)

    def add(first, others):
        total = first.astype(F32)
        for other in others:
            total = total + other.astype(F32)
        return total.astype(BF16)

    lo_first, hi_first = mlp_grad[:n_lo], mlp_grad[n_lo:]
    lo_got = [along_lo(lo_first[m], m) for m in range(1, n_lo)]
    hi_got = [along_hi(hi_first[k], k) for k in range(1, n_hi)]
    qb, dob, ho = attn_fwd(image_len, image_group, qa, ka, va, do)
    lo_sum = [add(lo_first[0][k], [got[k] for got in lo_got]) for k in range(n_hi)]
    hi_sum = [add(hi_first[0][m], [got[m] for got in hi_got]) for m in range(n_lo)]
    qb, lo_sum, hi_sum = lax.optimization_barrier((qb, lo_sum, hi_sum))
    lo_got = [along_hi(lo_sum[k], k) for k in range(1, n_hi)]
    hi_got = [along_lo(hi_sum[m], m) for m in range(1, n_lo)]
    d_qkv, gain_rows = attn_bwd(image_len, image_group, qb, ka, va, dob, u, r, q_gain, k_gain)
    own_lo, own_hi = add(lo_sum[0], lo_got), add(hi_sum[0], hi_got)
    output, input_grad, mlp_all, joint_all, rows = back(
        n_batch, d_qkv, nall, dn_part, ho, call, mlp_part, weight_t, attn_out, tokens, out_cotangent, ln_gain, out_bias,
        own_lo, own_hi, front_rows, gain_rows,
    )
    output, input_grad, qkv_t, attn, mlp_in_grad, mlp_out_grad, ln, q, k, bias, out_bias_grad = widen(
        heads, qkv_cols, mlp_all.reshape((n_batch,) + mlp_all.shape[2:]), joint_all,
        output, input_grad, rows,
    )
    return output, input_grad, ln, qkv_t.T, q, k, attn, mlp_in_grad, bias, mlp_out_grad, out_bias_grad


def solution(mesh):
    rows, cols, first = P(("batch", "tensor"), None), P(None, "tensor"), P("tensor", None)
    return jax.shard_map(
        on_device,
        mesh=mesh,
        in_specs=(rows, rows, P(), cols, P("tensor"), P("tensor"), first, cols, P("tensor"), first, P(), P(), P()),
        out_specs=(rows, rows, P(), cols, P("tensor"), P("tensor"), first, cols, P("tensor"), first, P()),
        check_vma=False,
    )
```

```python
import functools

import jax
import jax.numpy as jnp
from jax import lax
from jax.experimental import pallas as pl
from jax.experimental.pallas import tpu as pltpu
from jax.sharding import PartitionSpec as P

DH = 64
LANES = 128
WIN = 64
ALIGN = 16
LOG2E = 1.4426950408889634
epsilon = 1e-06
F32 = jnp.float32
BF16 = jnp.bfloat16
VMEM = pl.BlockSpec(memory_space=pltpu.VMEM)
SMEM = pl.BlockSpec(memory_space=pltpu.SMEM)
ANY = pl.BlockSpec(memory_space=pl.ANY)


def nn(left, right):
    return lax.dot_general(left, right, (((1,), (0,)), ((), ())), preferred_element_type=F32)


def nt(left, right):
    return lax.dot_general(left, right, (((1,), (1,)), ((), ())), preferred_element_type=F32)


def tn(left, right):
    return lax.dot_general(left, right, (((0,), (0,)), ((), ())), preferred_element_type=F32)


def row_of(vector):
    return vector[...].astype(F32).reshape(1, -1)


def pair_row(q_vector, k_vector, heads):
    q, k = row_of(q_vector), row_of(k_vector)
    parts = []
    for h in range(heads):
        parts += [q[:, h * DH : (h + 1) * DH], k[:, h * DH : (h + 1) * DH]]
    return jnp.concatenate(parts, axis=1)


def half_sums(lanes=LANES):
    row = lax.broadcasted_iota(jnp.int32, (lanes, lanes), 0) // DH
    col = lax.broadcasted_iota(jnp.int32, (lanes, lanes), 1) // DH
    return jnp.where(row == col, 1.0, 0.0).astype(BF16)


def left_half(rows):
    return lax.broadcasted_iota(jnp.int32, (rows, LANES), 1) < DH


def find_segments(len_ref, group_ref, seg_ref, strips, tok_dev):
    group = lax.axis_index("batch")

    def entry(i, carry):
        count, run = carry
        rows = jnp.where(group_ref[i] == group, len_ref[i] // strips, 0)

        @pl.when(rows > 0)
        def _():
            seg_ref[0, count] = run
            seg_ref[1, count] = run + rows

        return count + jnp.where(rows > 0, 1, 0), run + rows

    count, run = lax.fori_loop(0, len_ref.shape[0], entry, (jnp.int32(0), jnp.int32(0)))

    @pl.when(run < tok_dev)
    def _():
        seg_ref[0, count] = run
        seg_ref[1, count] = tok_dev

    return count + jnp.where(run < tok_dev, 1, 0)


def window(start, end, first, i, tok_dev):
    nominal = first + WIN * i
    at = pl.multiple_of(jnp.minimum(nominal, tok_dev - WIN), ALIGN)
    return at, jnp.maximum(start, nominal) - at, jnp.minimum(end, nominal + WIN) - at


def row_mask(low, high, strips, win=WIN, width=LANES):
    j = lax.broadcasted_iota(jnp.int32, (strips, win, width), 1).reshape(strips * win, width)
    return (j >= low) & (j < high)


def low_mask(mask):
    return jnp.where(mask, 1.0, 0.0).astype(BF16) > jnp.asarray(0.5, BF16)


def tile(ref, at, h, win=WIN):
    strips = ref.shape[0]
    return ref[:, pl.ds(at, win), h * LANES : (h + 1) * LANES].reshape(strips * win, LANES)


def put_tile(ref, at, h, mask, value, win=WIN, width=LANES):
    strips = ref.shape[0]
    where = (slice(None), pl.ds(at, win), slice(h * LANES, h * LANES + width))
    old = ref[where].reshape(strips * win, width)
    ref[where] = jnp.where(mask, value.astype(ref.dtype), old).reshape(strips, win, width)


PIECES = 4


def pieces_of(pairs, sem, tok_dev):
    rows = tok_dev // PIECES
    return [
        [
            pltpu.make_async_copy(a.at[:, pl.ds(p * rows, rows)], b.at[:, pl.ds(p * rows, rows)], sem.at[i, p])
            for i, (a, b) in enumerate(pairs)
        ]
        for p in range(PIECES)
    ]


def for_segments(len_ref, group_ref, seg, strips, tok_dev, loads, later, stores, small, middle, large):
    for piece in loads:
        for copy in piece:
            copy.start()
    for copy in later:
        copy.start()
    count = find_segments(len_ref, group_ref, seg, strips, tok_dev)
    big = middle_rows(tok_dev)
    rows = tok_dev // PIECES

    def segment(index, ready):
        start, end = seg[0, index], seg[1, index]
        first = (start // ALIGN) * ALIGN
        windows = (end - first + WIN - 1) // WIN
        fits = (end - first <= big) & (end - start <= big - ALIGN)
        reach = jnp.where(windows == 1, first + WIN, jnp.where(fits, first + big, first + windows * WIN))
        needed = jnp.minimum((reach + rows - 1) // rows, PIECES)
        for p in range(PIECES):

            @pl.when((p >= ready) & (p < needed))
            def _():
                for copy in loads[p]:
                    copy.wait()

        @pl.when(windows == 1)
        def _():
            small(*window(start, end, first, 0, tok_dev))

        @pl.when((windows > 1) & fits)
        def _():
            at = pl.multiple_of(jnp.minimum(first, tok_dev - big), ALIGN)
            middle(at, start - at, end - at)

        @pl.when(jnp.logical_not(fits))
        def _():
            large(start, end, first, windows)

        for p, piece in enumerate(stores):

            @pl.when((start < (p + 1) * rows) & ((p + 1) * rows <= end))
            def _():
                for copy in piece:
                    copy.start()

        return jnp.maximum(ready, needed)

    lax.fori_loop(0, count, segment, jnp.int32(0))


def edge_tile(ref, at, h, low):
    strips = ref.shape[0]
    cols = slice(h * LANES, (h + 1) * LANES)
    last = middle_rows(ref.shape[1]) - ALIGN
    body = ref[:, pl.ds(at + last - WIN + ALIGN, WIN - ALIGN), cols]
    late = low_mask(row_mask(low, ALIGN, strips, ALIGN))
    edge = jnp.where(late, tile(ref, at, h, ALIGN), tile(ref, at + last, h, ALIGN))
    return jnp.concatenate([body, edge.reshape(strips, ALIGN, LANES)], axis=1).reshape(strips * WIN, LANES)


def edge_mask(low, high, strips, tok_dev):
    last = middle_rows(tok_dev) - ALIGN
    j = lax.broadcasted_iota(jnp.int32, (strips, WIN, LANES), 1).reshape(strips * WIN, LANES)
    edge = j - (WIN - ALIGN)
    body = j + (last - WIN + ALIGN)
    inner = (edge < 0) & (body >= low) & (body < high)
    return inner | ((edge >= 0) & ((edge >= low) | (edge < high - last)))


def middle_rows(tok_dev):
    return min(tok_dev, tok_dev // 2 + ALIGN)


def attn_fwd_body(
    heads, len_ref, group_ref, qa_hbm, ka_hbm, va_hbm, do_hbm, qb_hbm, dob_hbm, ho_hbm,
    qa, ka, va, do, qb, dob, ho, seg, acc, in_sem, out_sem,
):
    strips, tok_dev = qa.shape[0], qa.shape[1]
    loads = pieces_of([(qa_hbm, qa), (ka_hbm, ka), (va_hbm, va), (do_hbm, do)], in_sem, tok_dev)
    stores = pieces_of([(qb, qb_hbm), (dob, dob_hbm), (ho, ho_hbm)], out_sem, tok_dev)
    zero = jnp.zeros((), BF16)
    big = middle_rows(tok_dev)

    def finish(at, low, high, totals, win=WIN):
        rows = strips * win
        mask = low_mask(row_mask(low, high, strips, win))
        lane = lax.broadcasted_iota(jnp.int32, (rows, LANES), 1)
        left = lane < DH
        first, second = low_mask(lane == DH), low_mask(lane == DH + 1)
        outs = []
        for h in range(heads):
            total = totals[h]
            log_sum = jnp.log2(jnp.where(left, pltpu.roll(total, DH, 1), total))
            out = jnp.where(left, total * jnp.exp2(-log_sum), 0.0)
            d_out = tile(do, at, h, win)
            delta = jnp.sum(out * d_out.astype(F32), axis=-1, keepdims=True)
            delta = jnp.broadcast_to(delta, (rows, LANES))
            log_hi, delta_hi = log_sum.astype(BF16), delta.astype(BF16)
            log_low = (log_hi.astype(F32) - log_sum).astype(BF16)
            delta_low = (delta_hi.astype(F32) - delta).astype(BF16)
            q = jnp.where(first, -log_hi, jnp.where(second, log_low, tile(qa, at, h, win)))
            d_out = jnp.where(first, -delta_hi, jnp.where(second, delta_low, d_out))
            put_tile(qb, at, h, mask, q, win)
            put_tile(dob, at, h, mask, d_out, win)
            outs.append(out)
        if heads % 2:
            outs.append(jnp.zeros_like(outs[0]))
        for b in range(len(outs) // 2):
            put_tile(ho, at, b, mask, jnp.where(left, outs[2 * b], pltpu.roll(outs[2 * b + 1], DH, 1)), win)

    def products(at_q, keys, values, k_mask, win_q=WIN):
        scores = [nt(tile(qa, at_q, h, win_q), keys(h)) for h in range(heads)]
        weights = [jnp.exp2(s).astype(BF16) for s in scores]
        k_mask = low_mask(k_mask)
        return [nn(weights[h], jnp.where(k_mask, values(h), zero)) for h in range(heads)]

    def plain(at_q, at_k, k_mask, win_q=WIN):
        return products(at_q, lambda h: tile(ka, at_k, h), lambda h: tile(va, at_k, h), k_mask, win_q)

    def small(at, low, high):
        finish(at, low, high, plain(at, at, row_mask(low, high, strips)))

    def middle(at, low, high):
        edges = products(
            at, lambda h: edge_tile(ka, at, h, low), lambda h: edge_tile(va, at, h, low),
            edge_mask(low, high, strips, tok_dev), big,
        )
        for h in range(heads):
            acc[h] = edges[h]

        def k_window(k, _):
            offset = ALIGN + k * WIN
            new = plain(pl.multiple_of(at, ALIGN), pl.multiple_of(at + offset, ALIGN), row_mask(low - offset, high - offset, strips), big)
            for h in range(heads):
                acc[h] = acc[h] + new[h]
            return 0

        lax.fori_loop(0, big // WIN - 1, k_window, 0)
        rest = big % WIN
        base = at + big - rest

        def total(h, offset, win):
            return acc[h].reshape(strips, big, LANES)[:, offset : offset + win].reshape(strips * win, LANES)

        for w in range(big // WIN):
            offset = w * WIN
            finish(
                pl.multiple_of(at + offset, ALIGN), low - offset, high - offset, [total(h, offset, WIN) for h in range(heads)]
            )
        if rest:
            offset = big - rest
            finish(base, low - offset, high - offset, [total(h, offset, rest) for h in range(heads)], rest)

    def large(start, end, first, windows):
        def q_window(i, _):
            at_q, low_q, high_q = window(start, end, first, i, tok_dev)
            rows = strips * WIN
            acc[:, :rows] = jnp.zeros((heads, rows, LANES), F32)

            def k_window(k, _):
                at_k, low_k, high_k = window(start, end, first, k, tok_dev)
                for h, new in enumerate(plain(at_q, at_k, row_mask(low_k, high_k, strips))):
                    acc[h, :rows] += new
                return 0

            lax.fori_loop(0, windows, k_window, 0)
            finish(at_q, low_q, high_q, [acc[h, :rows] for h in range(heads)])
            return 0

        lax.fori_loop(0, windows, q_window, 0)

    for_segments(len_ref, group_ref, seg, strips, tok_dev, loads, [], stores, small, middle, large)
    for piece in stores:
        for copy in piece:
            copy.wait()


def attn_fwd(image_len, image_group, qa, ka, va, do):
    strips, tok_dev, width = qa.shape
    heads = width // LANES
    packed = (heads + 1) // 2 * LANES
    like = jax.ShapeDtypeStruct(qa.shape, BF16)
    return pl.pallas_call(
        functools.partial(attn_fwd_body, heads),
        out_shape=(like, like, jax.ShapeDtypeStruct((strips, tok_dev, packed), BF16)),
        in_specs=[SMEM, SMEM] + [ANY] * 4,
        out_specs=(ANY,) * 3,
        scratch_shapes=[pltpu.VMEM(qa.shape, BF16)] * 6 + [
            pltpu.VMEM((strips, tok_dev, packed), BF16),
            pltpu.SMEM((2, image_len.shape[0] + 1), jnp.int32),
            pltpu.VMEM((heads, strips * middle_rows(tok_dev), LANES), F32),
            pltpu.SemaphoreType.DMA((4, PIECES)),
            pltpu.SemaphoreType.DMA((3, PIECES)),
        ],
        compiler_params=pltpu.CompilerParams(vmem_limit_bytes=60 << 20),
        cost_estimate=pl.CostEstimate(flops=8 * 10**9, bytes_accessed=30 * 10**6, transcendentals=8 * 10**6),
        name="attention_forward",
    )(image_len, image_group, qa, ka, va, do)


def attn_bwd_body(
    heads, len_ref, group_ref, qb_hbm, ka_hbm, va_hbm, dob_hbm, u_hbm, r_hbm, q_gain, k_gain,
    d_qkv_hbm, gain_grad, seg, k_turned, dq_turned, dk_acc, dv_acc, dq, dk, dv, qb, ka, va, dob, u_rows, r_rows, d_qkv,
    in_sem, out_sem, sems,
):
    strips, tok_dev = qb.shape[0], qb.shape[1]
    pieces = pieces_of([(qb_hbm, qb), (ka_hbm, ka), (va_hbm, va), (dob_hbm, dob)], in_sem, tok_dev)
    loads = [pltpu.make_async_copy(u_hbm, u_rows, sems.at[0]), pltpu.make_async_copy(r_hbm, r_rows, sems.at[1])]
    zero = jnp.zeros((), BF16)
    big = middle_rows(tok_dev)

    def products(queries, d_rows, at_k, q_mask, k_turned_of, win_k=WIN):
        every = range(heads)
        qs = [queries(h) for h in every]
        q_mask = low_mask(q_mask)
        d_outs = [jnp.where(q_mask, d_rows(h), zero) for h in every]
        scores = [nt(tile(ka, at_k, h, win_k), qs[h]) for h in every]
        d_weights = [nt(tile(va, at_k, h, win_k), d_outs[h]) for h in every]
        weights = [jnp.exp2(s) for s in scores]
        d_scores = [(weights[h] * d_weights[h]).astype(BF16) for h in every]
        dv_new = [nn(weights[h].astype(BF16), d_outs[h]) for h in every]
        dk_new = [nn(d_scores[h], qs[h]) for h in every]
        dq_new = [nn(k_turned_of(h), d_scores[h]) for h in every]
        return dq_new, dk_new, dv_new

    def plain(at_q, at_k, q_mask, k_turned_of, win_k=WIN):
        return products(lambda h: tile(qb, at_q, h), lambda h: tile(dob, at_q, h), at_k, q_mask, k_turned_of, win_k)

    def turned(h, at_k, mask, win=WIN):
        return jnp.where(low_mask(mask), tile(ka, at_k, h, win), zero).T[:DH]

    def small(at, low, high):
        mask = row_mask(low, high, strips)
        half = row_mask(low, high, strips, width=DH)
        dq_t, dk_new, dv_new = plain(at, at, mask, lambda h: turned(h, at, mask))
        for h in range(heads):
            put_tile(dq, at, h, half, dq_t[h].T, width=DH)
            put_tile(dk, at, h, mask, dk_new[h])
            put_tile(dv, at, h, mask, dv_new[h])

    def middle(at, low, high):
        mask = row_mask(low, high, strips, big)
        for h in range(heads):
            k_turned[h] = turned(h, at, mask, big)

        dq_t, dk_new, dv_new = products(
            lambda h: edge_tile(qb, at, h, low), lambda h: edge_tile(dob, at, h, low), at,
            edge_mask(low, high, strips, tok_dev), lambda h: k_turned[h], big,
        )
        last = big - ALIGN
        body = last - WIN + ALIGN
        body_mask = row_mask(low - body, high - body, strips, WIN - ALIGN, DH)
        first_mask = row_mask(low, ALIGN, strips, ALIGN, DH)
        last_mask = row_mask(0, high - last, strips, ALIGN, DH)
        for h in range(heads):
            dk_acc[h], dv_acc[h] = dk_new[h], dv_new[h]
            rows_new = dq_t[h].T.reshape(strips, WIN, DH)
            edge = rows_new[:, WIN - ALIGN :].reshape(strips * ALIGN, DH)
            inner = rows_new[:, : WIN - ALIGN].reshape(strips * (WIN - ALIGN), DH)
            put_tile(dq, at + body, h, body_mask, inner, WIN - ALIGN, DH)
            put_tile(dq, at, h, first_mask, edge, ALIGN, DH)
            put_tile(dq, at + last, h, last_mask, edge, ALIGN, DH)

        def each(i, _):
            offset = ALIGN + i * WIN
            at_q = pl.multiple_of(at + offset, ALIGN)
            mask_q = row_mask(low - offset, high - offset, strips)
            half = row_mask(low - offset, high - offset, strips, width=DH)
            dq_t, dk_new, dv_new = plain(at_q, pl.multiple_of(at, ALIGN), mask_q, lambda h: k_turned[h], big)
            for h in range(heads):
                put_tile(dq, at_q, h, half, dq_t[h].T, width=DH)
                dk_acc[h] = dk_acc[h] + dk_new[h]
                dv_acc[h] = dv_acc[h] + dv_new[h]
            return 0

        lax.fori_loop(0, big // WIN - 1, each, 0)
        for h in range(heads):
            put_tile(dk, at, h, mask, dk_acc[h], big)
            put_tile(dv, at, h, mask, dv_acc[h], big)

    def large(start, end, first, windows):
        rows = strips * WIN

        def clear(i, _):
            for h in range(heads):
                dq_turned[h, i] = jnp.zeros(dq_turned.shape[2:], F32)
            return 0

        lax.fori_loop(0, windows, clear, 0)

        def k_window(k, _):
            at_k, low_k, high_k = window(start, end, first, k, tok_dev)
            mask_k = row_mask(low_k, high_k, strips)
            for h in range(heads):
                k_turned[h, :, :rows] = turned(h, at_k, mask_k)
            dk_acc[:, :rows] = jnp.zeros((heads, rows, LANES), F32)
            dv_acc[:, :rows] = jnp.zeros((heads, rows, LANES), F32)

            def q_window(i, _):
                at_q, low_q, high_q = window(start, end, first, i, tok_dev)
                mask_q = row_mask(low_q, high_q, strips)
                dq_t, dk_new, dv_new = plain(at_q, at_k, mask_q, lambda h: k_turned[h, :, :rows])
                for h in range(heads):
                    dq_turned[h, i] += dq_t[h]
                    dk_acc[h, :rows] += dk_new[h]
                    dv_acc[h, :rows] += dv_new[h]
                return 0

            lax.fori_loop(0, windows, q_window, 0)
            for h in range(heads):
                put_tile(dk, at_k, h, mask_k, dk_acc[h, :rows])
                put_tile(dv, at_k, h, mask_k, dv_acc[h, :rows])
            return 0

        lax.fori_loop(0, windows, k_window, 0)

        def q_out(i, _):
            at_q, low_q, high_q = window(start, end, first, i, tok_dev)
            half = row_mask(low_q, high_q, strips, width=DH)
            for h in range(heads):
                put_tile(dq, at_q, h, half, dq_turned[h, i].T, width=DH)
            return 0

        lax.fori_loop(0, windows, q_out, 0)

    for_segments(len_ref, group_ref, seg, strips, tok_dev, pieces, loads, [], small, middle, large)

    rows = strips * WIN
    left = left_half(rows)
    sums = half_sums(2 * LANES)
    gains = pair_row(q_gain, k_gain, heads)
    for load in loads:
        load.wait()

    def save(i):
        where = pl.ds(pl.multiple_of(i * WIN, WIN), WIN)
        return pltpu.make_async_copy(d_qkv.at[:, where], d_qkv_hbm.at[:, where], out_sem.at[i])

    def chunk(i, totals):
        at = pl.multiple_of(i * WIN, WIN)
        scaled, new_totals, us = [], [], []
        for h in range(heads):
            cols = slice(h * LANES, (h + 1) * LANES)
            d_q, d_k = tile(dq, at, h), tile(dk, at, h) * (1.0 / LOG2E)
            both = jnp.where(left, d_q * DH ** (-0.5), pltpu.roll(d_k, DH, 1))
            u = tile(u_rows, at, h).astype(F32)
            new_totals.append(totals[h] + jnp.sum(both * u, axis=0, keepdims=True))
            scaled.append(both * gains[:, cols])
            us.append(u)
        pairs = [jnp.concatenate([scaled[h].astype(BF16), (scaled[h] * us[h]).astype(BF16)], axis=1) for h in range(heads)]
        means = nn(jnp.concatenate(pairs, axis=0), sums) * (1.0 / DH)
        parts = []
        for h in range(heads):
            mean = means[h * rows : (h + 1) * rows, :LANES]
            mean_u = means[h * rows : (h + 1) * rows, LANES:]
            parts.append((scaled[h] - mean - us[h] * mean_u) * tile(r_rows, at, h).astype(F32))
        values = [tile(dv, at, h) for h in range(heads)]
        if heads % 2:
            values.append(jnp.zeros_like(values[0]))
        for b in range(len(values) // 2):
            parts.append(jnp.where(left, values[2 * b], pltpu.roll(values[2 * b + 1], DH, 1)))
        for b, part in enumerate(parts):
            d_qkv[:, pl.ds(at, WIN), b * LANES : (b + 1) * LANES] = part.astype(BF16).reshape(strips, WIN, LANES)
        save(i).start()
        return tuple(new_totals)

    totals = lax.fori_loop(0, tok_dev // WIN, chunk, tuple(jnp.zeros((1, LANES), F32) for _ in range(heads)))
    gain_grad[...] = jnp.zeros_like(gain_grad)
    for h in range(heads):
        gain_grad[0:1, h * LANES : (h + 1) * LANES] = totals[h]

    def saved(i, _):
        save(i).wait()
        return 0

    lax.fori_loop(0, tok_dev // WIN, saved, 0)


def attn_bwd(image_len, image_group, qb, ka, va, dob, u, r, q_gain, k_gain):
    strips, tok_dev, width = qb.shape
    heads = width // LANES
    blocks = heads + (heads + 1) // 2
    rows = strips * WIN
    big = strips * middle_rows(tok_dev)
    windows = tok_dev // WIN + 1
    full = pltpu.VMEM((strips, tok_dev, width), F32)
    return pl.pallas_call(
        functools.partial(attn_bwd_body, heads),
        out_shape=(
            jax.ShapeDtypeStruct((strips, tok_dev, blocks * LANES), BF16),
            jax.ShapeDtypeStruct((8, width), F32),
        ),
        in_specs=[SMEM, SMEM] + [ANY] * 6 + [VMEM] * 2,
        out_specs=(ANY, VMEM),
        scratch_shapes=[
            pltpu.SMEM((2, image_len.shape[0] + 1), jnp.int32),
            pltpu.VMEM((heads, DH, big), BF16),
            pltpu.VMEM((heads, windows, DH, rows), F32),
            pltpu.VMEM((heads, big, LANES), F32),
            pltpu.VMEM((heads, big, LANES), F32),
            full, full, full,
        ] + [pltpu.VMEM(qb.shape, BF16)] * 6 + [
            pltpu.VMEM((strips, tok_dev, blocks * LANES), BF16),
            pltpu.SemaphoreType.DMA((4, PIECES)),
            pltpu.SemaphoreType.DMA((tok_dev // WIN,)),
            pltpu.SemaphoreType.DMA((2,)),
        ],
        compiler_params=pltpu.CompilerParams(vmem_limit_bytes=60 << 20),
        cost_estimate=pl.CostEstimate(flops=16 * 10**9, bytes_accessed=30 * 10**6, transcendentals=8 * 10**6),
        name="attention_backward",
    )(image_len, image_group, qb, ka, va, dob, u, r, q_gain, k_gain)


CHUNKS = 8
BACK_CHUNKS = 4


def kind_order(heads):
    return [3 * h + i for h in range(heads) for i in range(2)] + [3 * h + 2 for h in range(heads)]


def remote(src, dst, send, recv, device):
    return pltpu.make_async_remote_copy(
        src_ref=src, dst_ref=dst, send_sem=send, recv_sem=recv, device_id=device, device_id_type=pl.DeviceIdType.MESH
    )


def lo_rows(features):
    return 2 * features * 2 // 3


def front_body(
    heads, n_hi, n_lo, tokens_hbm, cot_hbm, ln_gain, q_gain, k_gain, mlp_bias, qkv_hbm, attn_hbm, mlp_in_hbm, mlp_out_hbm,
    qa_out, ka_out, va_out, do_out, u_out, r_out, mlp_part_out, dn_part_out, nall_out, call_out,
    *rest,
):
    (rows_out, both, wide, narrow, qkv_rows, attn_pad, mlp_in, mlp_out, g_in, g_out,
     tokens, low, send_sem, recv_sem, save_sem, load_sem, row_sem) = rest[-17:]
    lo_first, hi_first = rest[:n_lo], rest[n_lo : n_lo + n_hi]
    batch, me = lax.axis_index("batch"), lax.axis_index("tensor")
    sibling = me + 1 - 2 * (me % 2)
    across = (me + 2) % 4
    chip, far_chip = me // 2, 1 - me // 2
    tok_dev = tokens_hbm.shape[0]
    step = tok_dev // CHUNKS
    features = tokens_hbm.shape[1]
    heads_wide = heads * LANES

    def rows_of(c):
        return pl.ds(pl.multiple_of(c * step, step), step)

    def move(kind, route, c, strip, to):
        part = both.at[kind, strip, rows_of(c)]
        return remote(part, part, send_sem.at[kind, route, c], recv_sem.at[kind, route, c], (batch, to))

    load_cot = pltpu.make_async_copy(cot_hbm, both.at[0, me], row_sem.at[0])
    load_tokens = pltpu.make_async_copy(tokens_hbm, tokens, row_sem.at[1])
    load_cot.start()
    load_tokens.start()
    barrier = pltpu.get_barrier_semaphore()
    for other in (sibling, across):
        pl.semaphore_signal(barrier, inc=1, device_id=(batch, other), device_id_type=pl.DeviceIdType.MESH)
    loads = [(mlp_in_hbm, mlp_in), (mlp_out_hbm, mlp_out)]
    loads += [
        (qkv_hbm.at[pl.ds(to * DH, DH)], qkv_rows.at[pl.ds(i * DH, DH)]) for i, to in enumerate(kind_order(heads))
    ]
    loads += [(attn_hbm.at[pl.ds(h * DH, DH)], attn_pad.at[pl.ds(h * LANES, DH)]) for h in range(heads)]
    loads = [pltpu.make_async_copy(a, b, load_sem.at[i]) for i, (a, b) in enumerate(loads)]
    for load in loads:
        load.start()
    gain = row_of(ln_gain)
    gains = pair_row(q_gain, k_gain, heads)

    def norm_chunk(c):
        x = tokens[rows_of(c)].astype(F32)
        centred = x - jnp.mean(x, axis=-1, keepdims=True)
        variance = jnp.mean(centred * centred, axis=-1, keepdims=True)
        both[1, me, rows_of(c)] = (centred * lax.rsqrt(variance + epsilon) * gain).astype(BF16)

    def send_across(c):
        for kind in range(2):
            move(kind, 1, c, me, across).start()

    load_cot.wait()
    pl.semaphore_wait(barrier, 2)
    early = 3
    for c in range(early):
        move(0, 1, c, me, across).start()
    load_tokens.wait()

    def first_sends(c, _):
        norm_chunk(c)

        @pl.when(c < early)
        def _():
            move(1, 1, c, me, across).start()

        for kind in range(2):
            move(kind, 0, c, me, sibling).start()

        return 0

    lax.fori_loop(0, CHUNKS, first_sends, 0)

    g_in[...] = jnp.zeros_like(g_in)
    g_out[...] = jnp.zeros_like(g_out)
    rows_out[...] = jnp.zeros_like(rows_out)
    rows_out[1:2, :] = jnp.sum(both[0, me].astype(F32), axis=0, keepdims=True)
    filled = 3 * heads * DH
    if filled < qkv_rows.shape[0]:
        qkv_rows[filled:] = jnp.zeros((qkv_rows.shape[0] - filled, features), BF16)
    for h in range(heads):
        attn_pad[h * LANES + DH : (h + 1) * LANES, :] = jnp.zeros((DH, features), BF16)
    for load in loads:
        load.wait()

    sums = half_sums()
    bias = row_of(mlp_bias)

    def chunks_of(c, n):
        return pl.ds(pl.multiple_of(c * step, step), n * step)

    def saves(at_chip, c, n):
        strips, where = pl.ds(2 * at_chip, 2), chunks_of(c, n)
        first = at_chip * CHUNKS + c
        pairs = [(narrow.at[a, strips, where], ref.at[strips, where]) for a, ref in enumerate(
            (qa_out, ka_out, va_out, do_out, u_out, r_out))]
        pairs += [(wide.at[a, strips, where], ref.at[strips, where]) for a, ref in enumerate((mlp_part_out, dn_part_out))]
        pairs += [(both.at[1, strips, where], nall_out.at[strips, where]), (both.at[0, strips, where], call_out.at[strips, where])]
        return [pltpu.make_async_copy(a, b, save_sem.at[i, first]) for i, (a, b) in enumerate(pairs)]

    def wait_sibling(c):
        for kind in range(2):
            move(kind, 0, c, sibling, sibling).wait_recv()

    def pass_on(c):
        for kind in range(2):
            move(kind, 1, c, across, across).wait_recv()
            move(kind, 2, c, across, sibling).start()

    def wait_passed(c):
        for kind in range(2):
            move(kind, 2, c, across + 1 - 2 * (across % 2), sibling).wait_recv()

    def unit(at_chip, c, n, between=None):
        rows = 2 * n * step
        left = left_half(rows)
        strips, where = pl.ds(2 * at_chip, 2), chunks_of(c, n)
        normed = both[1, strips, where].reshape(rows, features)
        d = both[0, strips, where].reshape(rows, features)

        def save(ref, a, h, value):
            ref[a, strips, where, h * LANES : (h + 1) * LANES] = value.astype(BF16).reshape(2, n * step, LANES)

        qkv = nt(normed, qkv_rows[...])

        def block(b):
            return qkv[:, b * LANES : (b + 1) * LANES]

        def stacked_means(parts):
            stacked = jnp.concatenate([p.astype(BF16) for p in parts], axis=0)
            means = nn(stacked, sums) * (1.0 / DH)
            return [means[h * rows : (h + 1) * rows] for h in range(heads)]

        pairs = [block(h) for h in range(heads)]
        means = stacked_means(pairs)
        centred = [pairs[h] - means[h] for h in range(heads)]
        variances = stacked_means([x * x for x in centred])
        hidden = nn(normed, mlp_in[...]) + bias
        d_act = nt(d, mlp_out[...])
        if between:
            between()
        for h in range(heads):
            rstd = lax.rsqrt(variances[h] + epsilon)
            u = centred[h] * rstd
            scaled = u * gains[:, h * LANES : (h + 1) * LANES]
            save(narrow, 0, h, jnp.where(left, scaled * (DH ** (-0.5) * LOG2E), 0.0))
            save(narrow, 1, h, jnp.where(left, pltpu.roll(scaled, DH, 1), 1.0))
            value = block(heads + h // 2)
            save(narrow, 2, h, jnp.where(left, pltpu.roll(value, DH, 1) if h % 2 else value, 1.0))
            save(narrow, 4, h, u)
            save(narrow, 5, h, rstd)
        narrow[3, strips, where] = nt(d, attn_pad[...]).astype(BF16).reshape(2, n * step, heads_wide)
        cdf = 0.5 + 0.5 * lax.erf(hidden * 0.7071067811865476)
        act = (hidden * cdf).astype(BF16)
        slope = cdf + hidden * (0.3989422804014327 * jnp.exp(hidden * hidden * -0.5))
        d_low = (d_act * slope).astype(BF16)
        wide[0, strips, where] = nn(act, mlp_out[...]).astype(BF16).reshape(2, n * step, features)
        d_normed = nt(d_low, mlp_in[...])
        rows_out[2:3, :] += jnp.sum(d_normed * normed.astype(F32), axis=0, keepdims=True)
        wide[1, strips, where] = d_normed.astype(BF16).reshape(2, n * step, features)
        rows_out[0:1, :] += jnp.sum(d_low.astype(F32), axis=0, keepdims=True)
        g_out[...] += tn(act, d)
        g_in[...] += tn(normed, d_low)
        for copy in saves(at_chip, c, n):
            copy.start()

    half, quarter = CHUNKS // 2, CHUNKS // 4
    for c in range(half):
        wait_sibling(c)
    unit(chip, 0, half)

    def middle(i, _):
        send_across(3 + i)

        @pl.when(i < 2)
        def _():
            for c in range(quarter):
                wait_sibling(half + i * quarter + c)

        @pl.when(i == 4)
        def _():
            pass_on(5)

        @pl.when(i >= 2)
        def _():
            for c in range(quarter):
                wait_passed((i - 2) * quarter + c)

        def between():
            @pl.when((i == 1) | (i == 2))
            def _():
                pass_on(2 * i - 2)
                pass_on(2 * i - 1)

            @pl.when(i == 3)
            def _():
                pass_on(4)

        unit(
            jnp.where(i < 2, chip, far_chip), jnp.where(i < 2, half + i * quarter, (i - 2) * quarter), quarter, between
        )
        return 0

    lax.fori_loop(0, 5, middle, 0)

    def last(i, _):
        pass_on(6 + i)
        wait_passed(6 + i)
        unit(far_chip, 6 + i, 1)
        return 0

    lax.fori_loop(0, 2, last, 0)

    hi, lo = batch // n_lo, batch % n_lo
    def grad_saves():
        made = []
        for o in range(n_hi * n_lo):
            at_hi = (o // n_lo - hi + n_hi) % n_hi
            at_lo = (o % n_lo - lo + n_lo) % n_lo
            for first, part in ((0, lo_first), (lo_rows(features), hi_first)):
                count = part[0].shape[1]
                rows = low.at[pl.ds(first + o * count, count)]
                slot, place = (at_lo, at_hi) if first == 0 else (at_hi, at_lo)
                for m in range(len(part)):
                    made.append((slot == m, pltpu.make_async_copy(rows, part[m].at[place], save_sem.at[10, (first > 0) * n_hi * n_lo + o])))
        return made

    low[:features] = g_in[...].astype(BF16)
    low[features:] = g_out[...].astype(BF16)
    for chosen, copy in grad_saves():

        @pl.when(chosen)
        def _():
            copy.start()

    for chosen, copy in grad_saves():

        @pl.when(chosen)
        def _():
            copy.wait()

    for at_chip, c, n in (
        [(chip, 0, half), (chip, half, quarter), (chip, half + quarter, quarter)]
        + [(far_chip, i * quarter, quarter) for i in range(3)] + [(far_chip, 6, 1), (far_chip, 7, 1)]
    ):
        for copy in saves(at_chip, c, n):
            copy.wait()

    def sent(c, _):
        for kind in range(2):
            move(kind, 0, c, me, sibling).wait_send()
            move(kind, 1, c, me, across).wait_send()
            move(kind, 2, c, across, sibling).wait_send()
        return 0

    lax.fori_loop(0, CHUNKS, sent, 0)


def front(strips, n_batch, tokens, cot, ln_gain, q_gain, k_gain, mlp_bias, qkv_weight_t, attn_out, mlp_in, mlp_out):
    tok_dev, features = tokens.shape
    heads = q_gain.shape[0] // DH
    width = heads * LANES
    hidden = mlp_in.shape[1]
    blocks = heads + (heads + 1) // 2
    n_hi, n_lo = levels(n_batch)
    like = jax.ShapeDtypeStruct((strips, tok_dev, width), BF16)
    rows = jax.ShapeDtypeStruct((strips, tok_dev, features), BF16)
    return pl.pallas_call(
        functools.partial(front_body, heads, n_hi, n_lo),
        out_shape=(like,) * 6 + (rows,) * 4 + (
            jax.ShapeDtypeStruct((n_hi, lo_rows(features) // n_batch, features), BF16),
        ) * n_lo + (
            jax.ShapeDtypeStruct((n_lo, (2 * features - lo_rows(features)) // n_batch, features), BF16),
        ) * n_hi + (jax.ShapeDtypeStruct((8, features), F32),),
        in_specs=[ANY] * 2 + [VMEM] * 4 + [ANY] * 4,
        out_specs=(ANY,) * (10 + n_lo + n_hi) + (VMEM,),
        scratch_shapes=[
            pltpu.VMEM((2, strips, tok_dev, features), BF16),
            pltpu.VMEM((2, strips, tok_dev, features), BF16),
            pltpu.VMEM((6, strips, tok_dev, width), BF16),
            pltpu.VMEM((blocks * LANES, features), BF16),
            pltpu.VMEM((width, features), BF16),
            pltpu.VMEM(mlp_in.shape, BF16),
            pltpu.VMEM(mlp_out.shape, BF16),
            pltpu.VMEM((features, hidden), F32),
            pltpu.VMEM((hidden, features), F32),
            pltpu.VMEM(tokens.shape, BF16),
            pltpu.VMEM((features + hidden, features), BF16),
            pltpu.SemaphoreType.DMA((2, 3, CHUNKS)),
            pltpu.SemaphoreType.DMA((2, 3, CHUNKS)),
            pltpu.SemaphoreType.DMA((11, max(2 * CHUNKS, 2 * n_batch))),
            pltpu.SemaphoreType.DMA((2 + 4 * heads,)),
            pltpu.SemaphoreType.DMA((2,)),
        ],
        compiler_params=pltpu.CompilerParams(collective_id=0, has_side_effects=True, vmem_limit_bytes=60 << 20),
        name="gather_and_project",
    )(tokens, cot, ln_gain, q_gain, k_gain, mlp_bias, qkv_weight_t, attn_out, mlp_in, mlp_out)


def back_body(
    heads, n_hi, n_lo, d_qkv_hbm, nall_hbm, dn_part_hbm, ho_hbm, call_hbm, mlp_part_hbm, qkv_weight_t, attn_out, tokens, cot,
    ln_gain, out_bias, own_lo, own_hi, front_rows, gain_rows, output, input_grad, mlp_all_out, joint_all_out, rows_out,
    d_qkv, nall, dn_part, ho, call, mlp_part, weight_t, attn_pad, acc, attn_acc, joint, joint_low, joint_got, joint_sum,
    joint_got_hi, joint_all, mlp_all, near, core_give, core_got, x_give, x_got, vec, vec_lo, vec_hi, vec_pair,
    load_sem, mlp_z_s, mlp_z_r, mlp_y_s, mlp_y_r, joint_s, joint_r, hi_s, hi_r, all_z_s, all_z_r, all_y_s, all_y_r,
    core_s, core_r, x_s, x_r, vec_s, vec_r, save_sem,
):
    batch, me = lax.axis_index("batch"), lax.axis_index("tensor")
    hi, lo = batch // n_lo, batch % n_lo
    sibling = me + 1 - 2 * (me % 2)
    across = (me + 2) % 4
    far_sibling = (sibling + 2) % 4
    tok_dev, features = tokens.shape
    step = tok_dev // BACK_CHUNKS
    chunk_rows, half_cols = joint.shape[2], joint.shape[3]
    every_k, every_m = range(1, n_hi), range(1, n_lo)
    cut = chunk_rows // 2 // 16 * 16
    parts = [pl.ds(0, cut), pl.ds(cut, chunk_rows - cut)]

    strips = call.shape[0]
    by_strip = ((ho_hbm, ho), (call_hbm, call), (d_qkv_hbm, d_qkv), (nall_hbm, nall))

    def strip_loads(i):
        return [pltpu.make_async_copy(a.at[i], b.at[i], load_sem.at[n, i]) for n, (a, b) in enumerate(by_strip)]

    def rest_loads():
        pairs = ((dn_part_hbm, dn_part), (mlp_part_hbm, mlp_part))
        return [pltpu.make_async_copy(a, b, load_sem.at[len(by_strip) + n, 0]) for n, (a, b) in enumerate(pairs)]

    for i in range(strips):
        for load in strip_loads(i):
            load.start()
    for load in rest_loads():
        load.start()

    def hi_peer(k):
        return (hi + k + n_hi) % n_hi

    def lo_peer(m):
        return (lo + m + n_lo) % n_lo

    def to_hi(k):
        return (hi_peer(k) * n_lo + lo, me)

    def to_lo(m):
        return (hi * n_lo + lo_peer(m), me)

    barrier = pltpu.get_barrier_semaphore()
    peers = [to_hi(k) for k in every_k] + [to_lo(m) for m in every_m] + [(batch, sibling), (batch, across)]
    for peer in peers:
        pl.semaphore_signal(barrier, inc=1, device_id=peer, device_id_type=pl.DeviceIdType.MESH)
    mlp_all[hi, lo] = jnp.concatenate([own_lo[...], own_hi[...]], axis=0)
    pl.semaphore_wait(barrier, len(peers))

    def mlp_hop(s, up, origin):
        part = mlp_all.at[origin, lo]
        to = ((hi + (1 if up else -1) + n_hi) % n_hi * n_lo + lo, me)
        return remote(part, part, mlp_z_s.at[up, s], mlp_z_r.at[up, s], to)

    def mlp_send_hop(s, wait=False):
        for up in range(2):
            origin = hi - (s - 1) if up else hi + (s - 1)
            there = (origin >= 0) & (hi + 1 < n_hi) if up else (origin < n_hi) & (hi >= 1)

            @pl.when(there)
            def _():
                hop = mlp_hop(s, up, (origin + n_hi) % n_hi)
                hop.wait_send() if wait else hop.start()

    def mlp_wait_hop(s):
        for up in range(2):
            origin = hi - s if up else hi + s

            @pl.when((origin >= 0) if up else (origin < n_hi))
            def _():
                mlp_hop(s, up, (origin + n_hi) % n_hi).wait_recv()

    def mlp_lo(m, k, back=0):
        part = mlp_all.at[hi_peer(k), lo_peer(back)]
        return remote(part, part, mlp_y_s.at[m, k], mlp_y_r.at[m, k], to_lo(m))

    def mlp_send_lo(s):
        for m in every_m:
            for k, there in ((s, hi + s < n_hi), (n_hi - s, hi >= s)):

                @pl.when(there)
                def _():
                    mlp_lo(m, k).start()

    for m in every_m:
        mlp_lo(m, 0).start()
    mlp_send_hop(1)

    for i, place in enumerate(kind_order(heads)):
        weight_t[i * DH : (i + 1) * DH] = qkv_weight_t[place * DH : (place + 1) * DH]
    filled = qkv_weight_t.shape[0]
    if filled < weight_t.shape[0]:
        weight_t[filled:] = jnp.zeros((weight_t.shape[0] - filled, features), BF16)
    head_width = attn_out.shape[0]
    attn_pad[:head_width] = attn_out[...]
    attn_pad[head_width:] = jnp.zeros((attn_pad.shape[0] - head_width, features), BF16)
    def rows_of_pair(ref, i):
        return ref[2 * i : 2 * i + 2].reshape(2 * ref.shape[1], ref.shape[2])

    for i in range(strips // 2):
        for load in strip_loads(2 * i) + strip_loads(2 * i + 1):
            load.wait()
        new = tn(rows_of_pair(d_qkv, i), rows_of_pair(nall, i))
        acc[...] = acc[...] + new if i else new
        new = tn(rows_of_pair(ho, i), rows_of_pair(call, i))
        attn_acc[...] = attn_acc[...] + new if i else new

    width = qkv_weight_t.shape[0]
    joint_low[:width] = acc[:width].astype(BF16)
    joint_low[width:] = attn_acc[:head_width].astype(BF16)
    per_half = features // chunk_rows
    for o in range(n_hi * n_lo):
        row = o % per_half * chunk_rows
        col = o // per_half * half_cols
        joint[o % n_lo, o // n_lo] = joint_low[row : row + chunk_rows, col : col + half_cols]

    def joint_lo(p, m, back=0):
        return remote(
            joint.at[lo_peer(m), :, parts[p]], joint_got.at[lo_peer(back), :, parts[p]], joint_s.at[m, p], joint_r.at[m, p], to_lo(m)
        )

    def joint_hi(p, k, back=0):
        return remote(
            joint_sum.at[hi_peer(k), parts[p]], joint_got_hi.at[hi_peer(back), parts[p]], hi_s.at[k, p], hi_r.at[k, p], to_hi(k)
        )

    def joint_sum_lo(p):
        for m in every_m:
            joint_lo(p, m, -m).wait_recv()
        total = joint[lo, :, parts[p]].astype(F32)
        for m in every_m:
            total = total + joint_got[lo_peer(m), :, parts[p]].astype(F32)
        joint_sum[:, parts[p]] = total.astype(BF16)
        for k in every_k:
            joint_hi(p, k).start()

    def all_hi(p, k, back=0):
        part = joint_all.at[lo, hi_peer(back), parts[p]]
        return remote(part, part, all_z_s.at[k, p], all_z_r.at[k, p], to_hi(k))

    def all_lo(p, m, back=0):
        part = joint_all.at[lo_peer(back), :, parts[p]]
        return remote(part, part, all_y_s.at[m, p], all_y_r.at[m, p], to_lo(m))

    def joint_sum_hi(p):
        total = joint_sum[hi, parts[p]].astype(F32)
        for k in every_k:
            joint_hi(p, k, -k).wait_recv()
            total = total + joint_got_hi[hi_peer(-k), parts[p]].astype(F32)
        joint_all[lo, hi, parts[p]] = total.astype(BF16)
        for k in every_k:
            all_hi(p, k).start()

    def joint_pass(p):
        for k in every_k:
            all_hi(p, k, -k).wait_recv()
        for m in every_m:
            all_lo(p, m).start()

    for m in every_m:
        joint_lo(0, m).start()

    ln_row = jnp.sum(acc[...] * weight_t[...].astype(F32), axis=0, keepdims=True)
    gain = row_of(ln_gain)
    vec_lo[lo] = front_rows[...]
    vec_lo[lo, 2:3, :] = (front_rows[2:3, :] + ln_row) / gain
    vec_lo[lo, 3:4, 0 : heads * LANES] = gain_rows[0:1, :]

    def vec_lo_move(m, back=0):
        part = vec_lo.at[lo_peer(back)]
        return remote(part, part, vec_s.at[m], vec_r.at[m], to_lo(m))

    def vec_hi_move(k, back=0):
        part = vec_hi.at[hi_peer(back)]
        return remote(part, part, vec_s.at[n_lo + k], vec_r.at[n_lo + k], to_hi(k))

    def vec_pair_move(i, to):
        return remote(vec.at[i], vec_pair.at[i], vec_s.at[n_lo + n_hi + i], vec_r.at[n_lo + n_hi + i], (batch, to))

    for m in every_m:
        vec_lo_move(m).start()
    mlp_wait_hop(1)
    mlp_send_hop(2)

    def rows_of(c):
        return pl.ds(pl.multiple_of(c * step, step), step)

    def partial_rows(which, strip, c):
        if which == 0:
            return nn(d_qkv[strip, rows_of(c)], weight_t[...]) + dn_part[strip, rows_of(c)].astype(F32)
        return nn(ho[strip, rows_of(c)], attn_pad[...]) + mlp_part[strip, rows_of(c)].astype(F32)

    def core_move(which, side, c):
        where = rows_of(c)
        return remote(
            core_give.at[which, side, where], core_got.at[which, side, where],
            core_s.at[which, side, c], core_r.at[which, side, c], (batch, sibling),
        )

    def x_move(which, c):
        where = rows_of(c)
        return remote(x_give.at[which, where], x_got.at[which, where], x_s.at[which, c], x_r.at[which, c], (batch, across))

    def far(which):
        def give(c, _):
            core_give[which, 0, rows_of(c)] = partial_rows(which, far_sibling, c).astype(BF16)
            core_move(which, 0, c).start()
            return 0

        def send(c, _):
            mine = partial_rows(which, across, c)
            core_move(which, 0, c).wait_recv()
            x_give[which, rows_of(c)] = (mine + core_got[which, 0, rows_of(c)].astype(F32)).astype(BF16)
            x_move(which, c).start()
            return 0

        lax.fori_loop(0, BACK_CHUNKS, give, 0)
        lax.fori_loop(0, BACK_CHUNKS, send, 0)

    def close(which):
        def give(c, _):
            core_give[which, 1, rows_of(c)] = partial_rows(which, sibling, c).astype(BF16)
            core_move(which, 1, c).start()
            return 0

        def keep(c, _):
            mine = partial_rows(which, me, c)
            core_move(which, 1, c).wait_recv()
            near[which, rows_of(c)] = mine + core_got[which, 1, rows_of(c)].astype(F32)
            return 0

        lax.fori_loop(0, BACK_CHUNKS, give, 0)
        lax.fori_loop(0, BACK_CHUNKS, keep, 0)

    for load in rest_loads():
        load.wait()
    far(0)
    for m in every_m:
        joint_lo(1, m).start()
    far(1)
    mlp_send_lo(1)
    joint_sum_lo(0)
    for s in range(2, n_hi - 1):
        mlp_wait_hop(s)
        mlp_send_hop(s + 1)
    close(0)
    joint_sum_lo(1)
    close(1)

    for m in every_m:
        vec_lo_move(m, -m).wait_recv()
    total = vec_lo[0]
    for i in range(1, n_lo):
        total = total + vec_lo[i]
    vec_hi[hi] = total
    for k in every_k:
        vec_hi_move(k).start()

    for s in range(2, n_hi - 1):
        mlp_send_lo(s)
    joint_sum_hi(0)
    if n_hi > 2:
        mlp_wait_hop(n_hi - 1)
        mlp_send_lo(n_hi - 1)
    joint_sum_hi(1)

    for k in every_k:
        vec_hi_move(k, -k).wait_recv()
    total = vec_hi[0]
    for i in range(1, n_hi):
        total = total + vec_hi[i]
    vec[0] = total
    vec_pair_move(0, sibling).start()

    joint_pass(0)
    vec_pair_move(0, sibling).wait_recv()
    vec[1] = vec[0] + vec_pair[0]
    vec_pair_move(1, across).start()

    def last_rows(c, _):
        x_move(0, c).wait_recv()
        where = rows_of(c)
        d_normed = near[0, where] + x_got[0, where].astype(F32)
        x = tokens[where].astype(F32)
        centred = x - jnp.mean(x, axis=-1, keepdims=True)
        r = lax.rsqrt(jnp.mean(centred * centred, axis=-1, keepdims=True) + epsilon)
        xhat = centred * r
        e = d_normed * gain
        d_x = r * (e - jnp.mean(e, axis=-1, keepdims=True) - xhat * jnp.mean(e * xhat, axis=-1, keepdims=True))
        input_grad[where] = (cot[where].astype(F32) + d_x).astype(BF16)
        return 0

    lax.fori_loop(0, BACK_CHUNKS, last_rows, 0)
    joint_pass(1)
    bias = row_of(out_bias)

    def out_rows(c, _):
        x_move(1, c).wait_recv()
        where = rows_of(c)
        output[where] = (tokens[where].astype(F32) + near[1, where] + x_got[1, where].astype(F32) + bias).astype(BF16)
        return 0

    lax.fori_loop(0, BACK_CHUNKS, out_rows, 0)
    vec_pair_move(1, across).wait_recv()
    rows_out[...] = vec[0]
    rows_out[1:3, :] = vec[1, 1:3, :] + vec_pair[1, 1:3, :]

    for m in every_m:
        for k in range(n_hi):
            mlp_lo(m, k, -m).wait_recv()
    save_mlp = pltpu.make_async_copy(mlp_all, mlp_all_out, save_sem.at[0])
    save_mlp.start()
    for s in range(1, n_hi):
        mlp_send_hop(s, wait=True)
    for m in every_m:
        for k in range(n_hi):
            mlp_lo(m, k).wait_send()
        for p in range(2):
            joint_lo(p, m).wait_send()
        vec_lo_move(m).wait_send()
    for k in every_k:
        for p in range(2):
            joint_hi(p, k).wait_send()
            all_hi(p, k).wait_send()
        vec_hi_move(k).wait_send()
    vec_pair_move(0, sibling).wait_send()
    vec_pair_move(1, across).wait_send()

    def sent(c, _):
        for which in range(2):
            core_move(which, 0, c).wait_send()
            core_move(which, 1, c).wait_send()
            x_move(which, c).wait_send()
        return 0

    lax.fori_loop(0, BACK_CHUNKS, sent, 0)
    for m in every_m:
        for p in range(2):
            all_lo(p, m, -m).wait_recv()
            all_lo(p, m).wait_send()
    save_joint = pltpu.make_async_copy(joint_all, joint_all_out, save_sem.at[1])
    save_joint.start()
    save_mlp.wait()
    save_joint.wait()


def levels(n_batch):
    lo = 2 if n_batch <= 8 else 4
    return n_batch // lo, lo


def back(
    n_batch, d_qkv, nall, dn_part, ho, call, mlp_part, qkv_weight_t, attn_out, tokens, cot, ln_gain, out_bias,
    own_lo, own_hi, front_rows, gain_rows,
):
    n_hi, n_lo = levels(n_batch)
    strips, tok_dev, features = nall.shape
    own = (own_lo.shape[0] + own_hi.shape[0], features)
    wide, packed = d_qkv.shape[2], ho.shape[2]
    heads = attn_out.shape[0] // DH
    chunk = (2 * features // n_batch, features // 2)
    dma = pltpu.SemaphoreType.DMA
    vmem = pltpu.VMEM
    return pl.pallas_call(
        functools.partial(back_body, heads, n_hi, n_lo),
        out_shape=(
            jax.ShapeDtypeStruct(tokens.shape, BF16),
            jax.ShapeDtypeStruct(tokens.shape, BF16),
            jax.ShapeDtypeStruct((n_hi, n_lo) + own, BF16),
            jax.ShapeDtypeStruct((n_lo, n_hi) + chunk, BF16),
            jax.ShapeDtypeStruct((8, features), F32),
        ),
        in_specs=[ANY] * 6 + [VMEM] * 10,
        out_specs=(VMEM, VMEM, ANY, ANY, VMEM),
        scratch_shapes=[
            vmem(d_qkv.shape, BF16), vmem(nall.shape, BF16), vmem(dn_part.shape, BF16),
            vmem(ho.shape, BF16), vmem(call.shape, BF16), vmem(mlp_part.shape, BF16),
            vmem((wide, features), BF16),
            vmem((packed, features), BF16),
            vmem((wide, features), F32),
            vmem((packed, features), F32),
            vmem((n_lo, n_hi) + chunk, BF16),
            vmem((features, features), BF16),
            vmem((n_lo, n_hi) + chunk, BF16),
            vmem((n_hi,) + chunk, BF16),
            vmem((n_hi,) + chunk, BF16),
            vmem((n_lo, n_hi) + chunk, BF16),
            vmem((n_hi, n_lo) + own, BF16),
            vmem((2,) + tokens.shape, F32),
            vmem((2, 2) + tokens.shape, BF16),
            vmem((2, 2) + tokens.shape, BF16),
            vmem((2,) + tokens.shape, BF16),
            vmem((2,) + tokens.shape, BF16),
            vmem((2, 8, features), F32),
            vmem((n_lo, 8, features), F32),
            vmem((n_hi, 8, features), F32),
            vmem((2, 8, features), F32),
            dma((6, strips)),
            dma((2, n_hi)), dma((2, n_hi)),
            dma((n_lo, n_hi)), dma((n_lo, n_hi)),
            dma((n_lo, 2)), dma((n_lo, 2)),
            dma((n_hi, 2)), dma((n_hi, 2)),
            dma((n_hi, 2)), dma((n_hi, 2)),
            dma((n_lo, 2)), dma((n_lo, 2)),
            dma((2, 2, BACK_CHUNKS)), dma((2, 2, BACK_CHUNKS)),
            dma((2, BACK_CHUNKS)), dma((2, BACK_CHUNKS)),
            dma((n_lo + n_hi + 2,)), dma((n_lo + n_hi + 2,)),
            dma((2,)),
        ],
        compiler_params=pltpu.CompilerParams(collective_id=1, has_side_effects=True, vmem_limit_bytes=60 << 20),
        name="reduce_gradients",
    )(
        d_qkv, nall, dn_part, ho, call, mlp_part, qkv_weight_t, attn_out, tokens, cot, ln_gain, out_bias,
        own_lo, own_hi, front_rows, gain_rows,
    )


def widen_body(
    heads, mlp_hbm, joint_hbm, output_in, input_grad_in, rows,
    output, input_grad, qkv_out, attn_out, mlp_in_out, mlp_out_out, ln_gain, q_gain, k_gain, mlp_bias, out_bias,
    kept, mlp_all, joint_all, joint, qkv_t, attn, mlp, sems,
):
    def copy(i, source, to):
        made = pltpu.make_async_copy(source, to, sems.at[i])
        made.start()
        return made

    load_joint = copy(0, joint_hbm, joint_all)
    load_mlp = copy(1, mlp_hbm, mlp_all)
    load_rows = [copy(2, output_in, kept.at[0]), copy(3, input_grad_in, kept.at[1])]
    features = rows.shape[1]
    mlp_bias[...] = rows[0:1, :].reshape(features)
    out_bias[...] = rows[1:2, :].reshape(features)
    ln_gain[...] = rows[2:3, :].reshape(features)
    for offset, ref in ((0, q_gain), (DH, k_gain)):
        parts = [rows[3:4, h * LANES + offset : h * LANES + offset + DH] for h in range(heads)]
        ref[...] = jnp.concatenate(parts, axis=1).reshape(heads * DH)
    load_joint.wait()
    n_lo, n_hi, chunk_rows, cols = joint_all.shape
    width = qkv_t.shape[0]
    per_half = features // chunk_rows
    for o in range(n_lo * n_hi):
        row = o % per_half * chunk_rows
        joint[o // per_half, row : row + chunk_rows] = joint_all[o % n_lo, o // n_lo]
    pending = []
    for half in range(2):
        at = slice(half * cols, (half + 1) * cols)
        attn[:, at] = joint[half, width:].astype(F32)
        for i, place in enumerate(kind_order(heads)):
            qkv_t[place * DH : (place + 1) * DH, at] = joint[half, i * DH : (i + 1) * DH].astype(F32)
    pending += [copy(4, qkv_t, qkv_out), copy(5, attn, attn_out)]
    load_mlp.wait()
    chunks = mlp_all.shape[0]
    cut = lo_rows(features) // chunks
    rest = mlp_all.shape[1] - cut
    for o in range(features // cut):
        mlp[o * cut : (o + 1) * cut] = mlp_all[o, :cut].astype(F32)
    pending.append(copy(6, mlp.at[pl.ds(0, features)], mlp_in_out))
    for o in range(features // cut, chunks):
        mlp[o * cut : (o + 1) * cut] = mlp_all[o, :cut].astype(F32)
    for o in range(chunks):
        row = lo_rows(features) + o * rest
        mlp[row : row + rest] = mlp_all[o, cut:].astype(F32)
    pending.append(copy(7, mlp.at[pl.ds(features, features)], mlp_out_out))
    for i, (load, to) in enumerate(zip(load_rows, (output, input_grad))):
        load.wait()
        pending.append(copy(8 + i, kept.at[i], to))
    for made in pending:
        made.wait()


def widen(heads, width, mlp_all, joint_all, output, input_grad, rows):
    features = rows.shape[1]
    head_width = heads * DH

    def out(*shape):
        return jax.ShapeDtypeStruct(shape, F32)

    like = jax.ShapeDtypeStruct(output.shape, BF16)
    return pl.pallas_call(
        functools.partial(widen_body, heads),
        out_shape=(
            like, like, out(width, features), out(head_width, features), out(features, features), out(features, features),
            out(features), out(head_width), out(head_width), out(features), out(features),
        ),
        in_specs=[ANY] * 4 + [VMEM],
        out_specs=(ANY,) * 6 + (VMEM,) * 5,
        scratch_shapes=[
            pltpu.VMEM((2,) + output.shape, BF16),
            pltpu.VMEM(mlp_all.shape, BF16),
            pltpu.VMEM(joint_all.shape, BF16),
            pltpu.VMEM((2, features, features // 2), BF16),
            pltpu.VMEM((width, features), F32),
            pltpu.VMEM((head_width, features), F32),
            pltpu.VMEM((2 * features, features), F32),
            pltpu.SemaphoreType.DMA((10,)),
        ],
        compiler_params=pltpu.CompilerParams(vmem_limit_bytes=60 << 20),
        name="widen_gradients",
    )(mlp_all, joint_all, output, input_grad, rows)


def on_device(
    tokens, out_cotangent, ln_gain, qkv_weight, q_gain, k_gain, attn_out,
    mlp_in, mlp_bias, mlp_out, out_bias, image_len, image_group,
):
    tok_dev, features = tokens.shape
    strips = lax.axis_size("tensor")
    n_batch = lax.axis_size("batch")
    n_hi, n_lo = levels(n_batch)
    heads = q_gain.shape[0] // DH
    qkv_cols = qkv_weight.shape[1]

    weight_t = qkv_weight.T
    (qa, ka, va, do, u, r, mlp_part, dn_part, nall, call, *mlp_grad, front_rows) = front(
        strips, n_batch, tokens, out_cotangent, ln_gain, q_gain, k_gain, mlp_bias, weight_t, attn_out, mlp_in, mlp_out
    )

    def along_lo(x, m):
        pairs = [(h * n_lo + i, h * n_lo + (i + m) % n_lo) for h in range(n_hi) for i in range(n_lo)]
        return lax.ppermute(x, "batch", pairs)

    def along_hi(x, k):
        pairs = [(h * n_lo + i, (h + k) % n_hi * n_lo + i) for h in range(n_hi) for i in range(n_lo)]
        return lax.ppermute(x, "batch", pairs)

    def add(first, others):
        total = first.astype(F32)
        for other in others:
            total = total + other.astype(F32)
        return total.astype(BF16)

    lo_first, hi_first = mlp_grad[:n_lo], mlp_grad[n_lo:]
    lo_got = [along_lo(lo_first[m], m) for m in range(1, n_lo)]
    hi_got = [along_hi(hi_first[k], k) for k in range(1, n_hi)]
    qb, dob, ho = attn_fwd(image_len, image_group, qa, ka, va, do)
    lo_sum = [add(lo_first[0][k], [got[k] for got in lo_got]) for k in range(n_hi)]
    hi_sum = [add(hi_first[0][m], [got[m] for got in hi_got]) for m in range(n_lo)]
    qb, lo_sum, hi_sum = lax.optimization_barrier((qb, lo_sum, hi_sum))
    lo_got = [along_hi(lo_sum[k], k) for k in range(1, n_hi)]
    hi_got = [along_lo(hi_sum[m], m) for m in range(1, n_lo)]
    d_qkv, gain_rows = attn_bwd(image_len, image_group, qb, ka, va, dob, u, r, q_gain, k_gain)
    own_lo, own_hi = add(lo_sum[0], lo_got), add(hi_sum[0], hi_got)
    output, input_grad, mlp_all, joint_all, rows = back(
        n_batch, d_qkv, nall, dn_part, ho, call, mlp_part, weight_t, attn_out, tokens, out_cotangent, ln_gain, out_bias,
        own_lo, own_hi, front_rows, gain_rows,
    )
    output, input_grad, qkv_t, attn, mlp_in_grad, mlp_out_grad, ln, q, k, bias, out_bias_grad = widen(
        heads, qkv_cols, mlp_all.reshape((n_batch,) + mlp_all.shape[2:]), joint_all,
        output, input_grad, rows,
    )
    return output, input_grad, ln, qkv_t.T, q, k, attn, mlp_in_grad, bias, mlp_out_grad, out_bias_grad


def solution(mesh):
    rows, cols, first = P(("batch", "tensor"), None), P(None, "tensor"), P("tensor", None)
    return jax.shard_map(
        on_device,
        mesh=mesh,
        in_specs=(rows, rows, P(), cols, P("tensor"), P("tensor"), first, cols, P("tensor"), first, P(), P(), P()),
        out_specs=(rows, rows, P(), cols, P("tensor"), P("tensor"), first, cols, P("tensor"), first, P()),
        check_vma=False,
    )
```

```python
import functools

import jax
import jax.numpy as jnp
from jax import lax
from jax.experimental import pallas as pl
from jax.experimental.pallas import tpu as pltpu
from jax.sharding import PartitionSpec as P

DH = 64
LANES = 128
WIN = 64
ALIGN = 16
LOG2E = 1.4426950408889634
epsilon = 1e-06
F32 = jnp.float32
BF16 = jnp.bfloat16
VMEM = pl.BlockSpec(memory_space=pltpu.VMEM)
SMEM = pl.BlockSpec(memory_space=pltpu.SMEM)
ANY = pl.BlockSpec(memory_space=pl.ANY)


def nn(left, right):
    return lax.dot_general(left, right, (((1,), (0,)), ((), ())), preferred_element_type=F32)


def nt(left, right):
    return lax.dot_general(left, right, (((1,), (1,)), ((), ())), preferred_element_type=F32)


def tn(left, right):
    return lax.dot_general(left, right, (((0,), (0,)), ((), ())), preferred_element_type=F32)


def row_of(vector):
    return vector[...].astype(F32).reshape(1, -1)


def pair_row(q_vector, k_vector, heads):
    q, k = row_of(q_vector), row_of(k_vector)
    parts = []
    for h in range(heads):
        parts += [q[:, h * DH : (h + 1) * DH], k[:, h * DH : (h + 1) * DH]]
    return jnp.concatenate(parts, axis=1)


def half_sums(lanes=LANES):
    row = lax.broadcasted_iota(jnp.int32, (lanes, lanes), 0) // DH
    col = lax.broadcasted_iota(jnp.int32, (lanes, lanes), 1) // DH
    return jnp.where(row == col, 1.0, 0.0).astype(BF16)


def left_half(rows):
    return lax.broadcasted_iota(jnp.int32, (rows, LANES), 1) < DH


def find_segments(len_ref, group_ref, seg_ref, strips, tok_dev):
    group = lax.axis_index("batch")

    def entry(i, carry):
        count, run = carry
        rows = jnp.where(group_ref[i] == group, len_ref[i] // strips, 0)

        @pl.when(rows > 0)
        def _():
            seg_ref[0, count] = run
            seg_ref[1, count] = run + rows

        return count + jnp.where(rows > 0, 1, 0), run + rows

    count, run = lax.fori_loop(0, len_ref.shape[0], entry, (jnp.int32(0), jnp.int32(0)))

    @pl.when(run < tok_dev)
    def _():
        seg_ref[0, count] = run
        seg_ref[1, count] = tok_dev

    return count + jnp.where(run < tok_dev, 1, 0)


def window(start, end, first, i, tok_dev):
    nominal = first + WIN * i
    at = pl.multiple_of(jnp.minimum(nominal, tok_dev - WIN), ALIGN)
    return at, jnp.maximum(start, nominal) - at, jnp.minimum(end, nominal + WIN) - at


def row_mask(low, high, strips, win=WIN, width=LANES):
    j = lax.broadcasted_iota(jnp.int32, (strips, win, width), 1).reshape(strips * win, width)
    return (j >= low) & (j < high)


def low_mask(mask):
    return jnp.where(mask, 1.0, 0.0).astype(BF16) > jnp.asarray(0.5, BF16)


def tile(ref, at, h, win=WIN):
    strips = ref.shape[0]
    return ref[:, pl.ds(at, win), h * LANES : (h + 1) * LANES].reshape(strips * win, LANES)


def put_tile(ref, at, h, mask, value, win=WIN, width=LANES):
    strips = ref.shape[0]
    where = (slice(None), pl.ds(at, win), slice(h * LANES, h * LANES + width))
    old = ref[where].reshape(strips * win, width)
    ref[where] = jnp.where(mask, value.astype(ref.dtype), old).reshape(strips, win, width)


PIECES = 4


def pieces_of(pairs, sem, tok_dev):
    rows = tok_dev // PIECES
    return [
        [
            pltpu.make_async_copy(a.at[:, pl.ds(p * rows, rows)], b.at[:, pl.ds(p * rows, rows)], sem.at[i, p])
            for i, (a, b) in enumerate(pairs)
        ]
        for p in range(PIECES)
    ]


def for_segments(len_ref, group_ref, seg, strips, tok_dev, loads, later, stores, small, middle, large):
    for piece in loads:
        for copy in piece:
            copy.start()
    for copy in later:
        copy.start()
    count = find_segments(len_ref, group_ref, seg, strips, tok_dev)
    big = middle_rows(tok_dev)
    rows = tok_dev // PIECES

    def segment(index, ready):
        start, end = seg[0, index], seg[1, index]
        first = (start // ALIGN) * ALIGN
        windows = (end - first + WIN - 1) // WIN
        fits = (end - first <= big) & (end - start <= big - ALIGN)
        reach = jnp.where(windows == 1, first + WIN, jnp.where(fits, first + big, first + windows * WIN))
        needed = jnp.minimum((reach + rows - 1) // rows, PIECES)
        for p in range(PIECES):

            @pl.when((p >= ready) & (p < needed))
            def _():
                for copy in loads[p]:
                    copy.wait()

        @pl.when(windows == 1)
        def _():
            small(*window(start, end, first, 0, tok_dev))

        @pl.when((windows > 1) & fits)
        def _():
            at = pl.multiple_of(jnp.minimum(first, tok_dev - big), ALIGN)
            middle(at, start - at, end - at)

        @pl.when(jnp.logical_not(fits))
        def _():
            large(start, end, first, windows)

        for p, piece in enumerate(stores):

            @pl.when((start < (p + 1) * rows) & ((p + 1) * rows <= end))
            def _():
                for copy in piece:
                    copy.start()

        return jnp.maximum(ready, needed)

    lax.fori_loop(0, count, segment, jnp.int32(0))


def edge_tile(ref, at, h, low):
    strips = ref.shape[0]
    cols = slice(h * LANES, (h + 1) * LANES)
    last = middle_rows(ref.shape[1]) - ALIGN
    body = ref[:, pl.ds(at + last - WIN + ALIGN, WIN - ALIGN), cols]
    late = low_mask(row_mask(low, ALIGN, strips, ALIGN))
    edge = jnp.where(late, tile(ref, at, h, ALIGN), tile(ref, at + last, h, ALIGN))
    return jnp.concatenate([body, edge.reshape(strips, ALIGN, LANES)], axis=1).reshape(strips * WIN, LANES)


def edge_mask(low, high, strips, tok_dev):
    last = middle_rows(tok_dev) - ALIGN
    j = lax.broadcasted_iota(jnp.int32, (strips, WIN, LANES), 1).reshape(strips * WIN, LANES)
    edge = j - (WIN - ALIGN)
    body = j + (last - WIN + ALIGN)
    inner = (edge < 0) & (body >= low) & (body < high)
    return inner | ((edge >= 0) & ((edge >= low) | (edge < high - last)))


def middle_rows(tok_dev):
    return min(tok_dev, tok_dev // 2 + ALIGN)


def attn_fwd_body(
    heads, len_ref, group_ref, qa_hbm, ka_hbm, va_hbm, do_hbm, qb_hbm, dob_hbm, ho_hbm,
    qa, ka, va, do, qb, dob, ho, seg, acc, in_sem, out_sem,
):
    strips, tok_dev = qa.shape[0], qa.shape[1]
    loads = pieces_of([(qa_hbm, qa), (ka_hbm, ka), (va_hbm, va), (do_hbm, do)], in_sem, tok_dev)
    stores = pieces_of([(qb, qb_hbm), (dob, dob_hbm), (ho, ho_hbm)], out_sem, tok_dev)
    zero = jnp.zeros((), BF16)
    big = middle_rows(tok_dev)

    def finish(at, low, high, totals, win=WIN):
        rows = strips * win
        mask = low_mask(row_mask(low, high, strips, win))
        lane = lax.broadcasted_iota(jnp.int32, (rows, LANES), 1)
        left = lane < DH
        first, second = low_mask(lane == DH), low_mask(lane == DH + 1)
        outs = []
        for h in range(heads):
            total = totals[h]
            log_sum = jnp.log2(jnp.where(left, pltpu.roll(total, DH, 1), total))
            out = jnp.where(left, total * jnp.exp2(-log_sum), 0.0)
            d_out = tile(do, at, h, win)
            delta = jnp.sum(out * d_out.astype(F32), axis=-1, keepdims=True)
            delta = jnp.broadcast_to(delta, (rows, LANES))
            log_hi, delta_hi = log_sum.astype(BF16), delta.astype(BF16)
            log_low = (log_hi.astype(F32) - log_sum).astype(BF16)
            delta_low = (delta_hi.astype(F32) - delta).astype(BF16)
            q = jnp.where(first, -log_hi, jnp.where(second, log_low, tile(qa, at, h, win)))
            d_out = jnp.where(first, -delta_hi, jnp.where(second, delta_low, d_out))
            put_tile(qb, at, h, mask, q, win)
            put_tile(dob, at, h, mask, d_out, win)
            outs.append(out)
        if heads % 2:
            outs.append(jnp.zeros_like(outs[0]))
        for b in range(len(outs) // 2):
            put_tile(ho, at, b, mask, jnp.where(left, outs[2 * b], pltpu.roll(outs[2 * b + 1], DH, 1)), win)

    def products(at_q, keys, values, k_mask, win_q=WIN):
        scores = [nt(tile(qa, at_q, h, win_q), keys(h)) for h in range(heads)]
        weights = [jnp.exp2(s).astype(BF16) for s in scores]
        k_mask = low_mask(k_mask)
        return [nn(weights[h], jnp.where(k_mask, values(h), zero)) for h in range(heads)]

    def plain(at_q, at_k, k_mask, win_q=WIN):
        return products(at_q, lambda h: tile(ka, at_k, h), lambda h: tile(va, at_k, h), k_mask, win_q)

    def small(at, low, high):
        finish(at, low, high, plain(at, at, row_mask(low, high, strips)))

    def middle(at, low, high):
        edges = products(
            at, lambda h: edge_tile(ka, at, h, low), lambda h: edge_tile(va, at, h, low),
            edge_mask(low, high, strips, tok_dev), big,
        )
        for h in range(heads):
            acc[h] = edges[h]

        def k_window(k, _):
            offset = ALIGN + k * WIN
            new = plain(pl.multiple_of(at, ALIGN), pl.multiple_of(at + offset, ALIGN), row_mask(low - offset, high - offset, strips), big)
            for h in range(heads):
                acc[h] = acc[h] + new[h]
            return 0

        lax.fori_loop(0, big // WIN - 1, k_window, 0)
        rest = big % WIN
        base = at + big - rest

        def total(h, offset, win):
            return acc[h].reshape(strips, big, LANES)[:, offset : offset + win].reshape(strips * win, LANES)

        for w in range(big // WIN):
            offset = w * WIN
            finish(
                pl.multiple_of(at + offset, ALIGN), low - offset, high - offset, [total(h, offset, WIN) for h in range(heads)]
            )
        if rest:
            offset = big - rest
            finish(base, low - offset, high - offset, [total(h, offset, rest) for h in range(heads)], rest)

    def large(start, end, first, windows):
        def q_window(i, _):
            at_q, low_q, high_q = window(start, end, first, i, tok_dev)
            rows = strips * WIN
            acc[:, :rows] = jnp.zeros((heads, rows, LANES), F32)

            def k_window(k, _):
                at_k, low_k, high_k = window(start, end, first, k, tok_dev)
                for h, new in enumerate(plain(at_q, at_k, row_mask(low_k, high_k, strips))):
                    acc[h, :rows] += new
                return 0

            lax.fori_loop(0, windows, k_window, 0)
            finish(at_q, low_q, high_q, [acc[h, :rows] for h in range(heads)])
            return 0

        lax.fori_loop(0, windows, q_window, 0)

    for_segments(len_ref, group_ref, seg, strips, tok_dev, loads, [], stores, small, middle, large)
    for piece in stores:
        for copy in piece:
            copy.wait()


def attn_fwd(image_len, image_group, qa, ka, va, do):
    strips, tok_dev, width = qa.shape
    heads = width // LANES
    packed = (heads + 1) // 2 * LANES
    like = jax.ShapeDtypeStruct(qa.shape, BF16)
    return pl.pallas_call(
        functools.partial(attn_fwd_body, heads),
        out_shape=(like, like, jax.ShapeDtypeStruct((strips, tok_dev, packed), BF16)),
        in_specs=[SMEM, SMEM] + [ANY] * 4,
        out_specs=(ANY,) * 3,
        scratch_shapes=[pltpu.VMEM(qa.shape, BF16)] * 6 + [
            pltpu.VMEM((strips, tok_dev, packed), BF16),
            pltpu.SMEM((2, image_len.shape[0] + 1), jnp.int32),
            pltpu.VMEM((heads, strips * middle_rows(tok_dev), LANES), F32),
            pltpu.SemaphoreType.DMA((4, PIECES)),
            pltpu.SemaphoreType.DMA((3, PIECES)),
        ],
        compiler_params=pltpu.CompilerParams(vmem_limit_bytes=60 << 20),
        cost_estimate=pl.CostEstimate(flops=8 * 10**9, bytes_accessed=30 * 10**6, transcendentals=8 * 10**6),
        name="attention_forward",
    )(image_len, image_group, qa, ka, va, do)


def attn_bwd_body(
    heads, len_ref, group_ref, qb_hbm, ka_hbm, va_hbm, dob_hbm, u_hbm, r_hbm, q_gain, k_gain,
    d_qkv_hbm, gain_grad, seg, k_turned, dq_turned, dk_acc, dv_acc, dq, dk, dv, qb, ka, va, dob, u_rows, r_rows, d_qkv,
    in_sem, out_sem, sems,
):
    strips, tok_dev = qb.shape[0], qb.shape[1]
    pieces = pieces_of([(qb_hbm, qb), (ka_hbm, ka), (va_hbm, va), (dob_hbm, dob)], in_sem, tok_dev)
    loads = [pltpu.make_async_copy(u_hbm, u_rows, sems.at[0]), pltpu.make_async_copy(r_hbm, r_rows, sems.at[1])]
    zero = jnp.zeros((), BF16)
    big = middle_rows(tok_dev)

    def products(queries, d_rows, at_k, q_mask, k_turned_of, win_k=WIN):
        every = range(heads)
        qs = [queries(h) for h in every]
        q_mask = low_mask(q_mask)
        d_outs = [jnp.where(q_mask, d_rows(h), zero) for h in every]
        scores = [nt(tile(ka, at_k, h, win_k), qs[h]) for h in every]
        d_weights = [nt(tile(va, at_k, h, win_k), d_outs[h]) for h in every]
        weights = [jnp.exp2(s) for s in scores]
        d_scores = [(weights[h] * d_weights[h]).astype(BF16) for h in every]
        dv_new = [nn(weights[h].astype(BF16), d_outs[h]) for h in every]
        dk_new = [nn(d_scores[h], qs[h]) for h in every]
        dq_new = [nn(k_turned_of(h), d_scores[h]) for h in every]
        return dq_new, dk_new, dv_new

    def plain(at_q, at_k, q_mask, k_turned_of, win_k=WIN):
        return products(lambda h: tile(qb, at_q, h), lambda h: tile(dob, at_q, h), at_k, q_mask, k_turned_of, win_k)

    def turned(h, at_k, mask, win=WIN):
        return jnp.where(low_mask(mask), tile(ka, at_k, h, win), zero).T[:DH]

    def small(at, low, high):
        mask = row_mask(low, high, strips)
        half = row_mask(low, high, strips, width=DH)
        dq_t, dk_new, dv_new = plain(at, at, mask, lambda h: turned(h, at, mask))
        for h in range(heads):
            put_tile(dq, at, h, half, dq_t[h].T, width=DH)
            put_tile(dk, at, h, mask, dk_new[h])
            put_tile(dv, at, h, mask, dv_new[h])

    def middle(at, low, high):
        mask = row_mask(low, high, strips, big)
        for h in range(heads):
            k_turned[h] = turned(h, at, mask, big)

        dq_t, dk_new, dv_new = products(
            lambda h: edge_tile(qb, at, h, low), lambda h: edge_tile(dob, at, h, low), at,
            edge_mask(low, high, strips, tok_dev), lambda h: k_turned[h], big,
        )
        last = big - ALIGN
        body = last - WIN + ALIGN
        body_mask = row_mask(low - body, high - body, strips, WIN - ALIGN, DH)
        first_mask = row_mask(low, ALIGN, strips, ALIGN, DH)
        last_mask = row_mask(0, high - last, strips, ALIGN, DH)
        for h in range(heads):
            dk_acc[h], dv_acc[h] = dk_new[h], dv_new[h]
            rows_new = dq_t[h].T.reshape(strips, WIN, DH)
            edge = rows_new[:, WIN - ALIGN :].reshape(strips * ALIGN, DH)
            inner = rows_new[:, : WIN - ALIGN].reshape(strips * (WIN - ALIGN), DH)
            put_tile(dq, at + body, h, body_mask, inner, WIN - ALIGN, DH)
            put_tile(dq, at, h, first_mask, edge, ALIGN, DH)
            put_tile(dq, at + last, h, last_mask, edge, ALIGN, DH)

        def each(i, _):
            offset = ALIGN + i * WIN
            at_q = pl.multiple_of(at + offset, ALIGN)
            mask_q = row_mask(low - offset, high - offset, strips)
            half = row_mask(low - offset, high - offset, strips, width=DH)
            dq_t, dk_new, dv_new = plain(at_q, pl.multiple_of(at, ALIGN), mask_q, lambda h: k_turned[h], big)
            for h in range(heads):
                put_tile(dq, at_q, h, half, dq_t[h].T, width=DH)
                dk_acc[h] = dk_acc[h] + dk_new[h]
                dv_acc[h] = dv_acc[h] + dv_new[h]
            return 0

        lax.fori_loop(0, big // WIN - 1, each, 0)
        for h in range(heads):
            put_tile(dk, at, h, mask, dk_acc[h], big)
            put_tile(dv, at, h, mask, dv_acc[h], big)

    def large(start, end, first, windows):
        rows = strips * WIN

        def clear(i, _):
            for h in range(heads):
                dq_turned[h, i] = jnp.zeros(dq_turned.shape[2:], F32)
            return 0

        lax.fori_loop(0, windows, clear, 0)

        def k_window(k, _):
            at_k, low_k, high_k = window(start, end, first, k, tok_dev)
            mask_k = row_mask(low_k, high_k, strips)
            for h in range(heads):
                k_turned[h, :, :rows] = turned(h, at_k, mask_k)
            dk_acc[:, :rows] = jnp.zeros((heads, rows, LANES), F32)
            dv_acc[:, :rows] = jnp.zeros((heads, rows, LANES), F32)

            def q_window(i, _):
                at_q, low_q, high_q = window(start, end, first, i, tok_dev)
                mask_q = row_mask(low_q, high_q, strips)
                dq_t, dk_new, dv_new = plain(at_q, at_k, mask_q, lambda h: k_turned[h, :, :rows])
                for h in range(heads):
                    dq_turned[h, i] += dq_t[h]
                    dk_acc[h, :rows] += dk_new[h]
                    dv_acc[h, :rows] += dv_new[h]
                return 0

            lax.fori_loop(0, windows, q_window, 0)
            for h in range(heads):
                put_tile(dk, at_k, h, mask_k, dk_acc[h, :rows])
                put_tile(dv, at_k, h, mask_k, dv_acc[h, :rows])
            return 0

        lax.fori_loop(0, windows, k_window, 0)

        def q_out(i, _):
            at_q, low_q, high_q = window(start, end, first, i, tok_dev)
            half = row_mask(low_q, high_q, strips, width=DH)
            for h in range(heads):
                put_tile(dq, at_q, h, half, dq_turned[h, i].T, width=DH)
            return 0

        lax.fori_loop(0, windows, q_out, 0)

    for_segments(len_ref, group_ref, seg, strips, tok_dev, pieces, loads, [], small, middle, large)

    rows = strips * WIN
    left = left_half(rows)
    sums = half_sums(2 * LANES)
    gains = pair_row(q_gain, k_gain, heads)
    for load in loads:
        load.wait()

    def save(i):
        where = pl.ds(pl.multiple_of(i * WIN, WIN), WIN)
        return pltpu.make_async_copy(d_qkv.at[:, where], d_qkv_hbm.at[:, where], out_sem.at[i])

    def chunk(i, totals):
        at = pl.multiple_of(i * WIN, WIN)
        scaled, new_totals, us = [], [], []
        for h in range(heads):
            cols = slice(h * LANES, (h + 1) * LANES)
            d_q, d_k = tile(dq, at, h), tile(dk, at, h) * (1.0 / LOG2E)
            both = jnp.where(left, d_q * DH ** (-0.5), pltpu.roll(d_k, DH, 1))
            u = tile(u_rows, at, h).astype(F32)
            new_totals.append(totals[h] + jnp.sum(both * u, axis=0, keepdims=True))
            scaled.append(both * gains[:, cols])
            us.append(u)
        pairs = [jnp.concatenate([scaled[h].astype(BF16), (scaled[h] * us[h]).astype(BF16)], axis=1) for h in range(heads)]
        means = nn(jnp.concatenate(pairs, axis=0), sums) * (1.0 / DH)
        parts = []
        for h in range(heads):
            mean = means[h * rows : (h + 1) * rows, :LANES]
            mean_u = means[h * rows : (h + 1) * rows, LANES:]
            parts.append((scaled[h] - mean - us[h] * mean_u) * tile(r_rows, at, h).astype(F32))
        values = [tile(dv, at, h) for h in range(heads)]
        if heads % 2:
            values.append(jnp.zeros_like(values[0]))
        for b in range(len(values) // 2):
            parts.append(jnp.where(left, values[2 * b], pltpu.roll(values[2 * b + 1], DH, 1)))
        for b, part in enumerate(parts):
            d_qkv[:, pl.ds(at, WIN), b * LANES : (b + 1) * LANES] = part.astype(BF16).reshape(strips, WIN, LANES)
        save(i).start()
        return tuple(new_totals)

    totals = lax.fori_loop(0, tok_dev // WIN, chunk, tuple(jnp.zeros((1, LANES), F32) for _ in range(heads)))
    gain_grad[...] = jnp.zeros_like(gain_grad)
    for h in range(heads):
        gain_grad[0:1, h * LANES : (h + 1) * LANES] = totals[h]

    def saved(i, _):
        save(i).wait()
        return 0

    lax.fori_loop(0, tok_dev // WIN, saved, 0)


def attn_bwd(image_len, image_group, qb, ka, va, dob, u, r, q_gain, k_gain):
    strips, tok_dev, width = qb.shape
    heads = width // LANES
    blocks = heads + (heads + 1) // 2
    rows = strips * WIN
    big = strips * middle_rows(tok_dev)
    windows = tok_dev // WIN + 1
    full = pltpu.VMEM((strips, tok_dev, width), F32)
    return pl.pallas_call(
        functools.partial(attn_bwd_body, heads),
        out_shape=(
            jax.ShapeDtypeStruct((strips, tok_dev, blocks * LANES), BF16),
            jax.ShapeDtypeStruct((8, width), F32),
        ),
        in_specs=[SMEM, SMEM] + [ANY] * 6 + [VMEM] * 2,
        out_specs=(ANY, VMEM),
        scratch_shapes=[
            pltpu.SMEM((2, image_len.shape[0] + 1), jnp.int32),
            pltpu.VMEM((heads, DH, big), BF16),
            pltpu.VMEM((heads, windows, DH, rows), F32),
            pltpu.VMEM((heads, big, LANES), F32),
            pltpu.VMEM((heads, big, LANES), F32),
            full, full, full,
        ] + [pltpu.VMEM(qb.shape, BF16)] * 6 + [
            pltpu.VMEM((strips, tok_dev, blocks * LANES), BF16),
            pltpu.SemaphoreType.DMA((4, PIECES)),
            pltpu.SemaphoreType.DMA((tok_dev // WIN,)),
            pltpu.SemaphoreType.DMA((2,)),
        ],
        compiler_params=pltpu.CompilerParams(vmem_limit_bytes=60 << 20),
        cost_estimate=pl.CostEstimate(flops=16 * 10**9, bytes_accessed=30 * 10**6, transcendentals=8 * 10**6),
        name="attention_backward",
    )(image_len, image_group, qb, ka, va, dob, u, r, q_gain, k_gain)


CHUNKS = 8
BACK_CHUNKS = 4


def kind_order(heads):
    return [3 * h + i for h in range(heads) for i in range(2)] + [3 * h + 2 for h in range(heads)]


def remote(src, dst, send, recv, device):
    return pltpu.make_async_remote_copy(
        src_ref=src, dst_ref=dst, send_sem=send, recv_sem=recv, device_id=device, device_id_type=pl.DeviceIdType.MESH
    )


def lo_rows(features):
    return 2 * features * 2 // 3


def front_body(
    heads, n_hi, n_lo, tokens_hbm, cot_hbm, ln_gain, q_gain, k_gain, mlp_bias, qkv_hbm, attn_hbm, mlp_in_hbm, mlp_out_hbm,
    qa_out, ka_out, va_out, do_out, u_out, r_out, mlp_part_out, dn_part_out, nall_out, call_out,
    *rest,
):
    (rows_out, both, wide, narrow, qkv_rows, attn_pad, mlp_in, mlp_out, g_in, g_out,
     tokens, low, send_sem, recv_sem, save_sem, load_sem, row_sem) = rest[-17:]
    lo_first, hi_first = rest[:n_lo], rest[n_lo : n_lo + n_hi]
    batch, me = lax.axis_index("batch"), lax.axis_index("tensor")
    sibling = me + 1 - 2 * (me % 2)
    across = (me + 2) % 4
    chip, far_chip = me // 2, 1 - me // 2
    tok_dev = tokens_hbm.shape[0]
    step = tok_dev // CHUNKS
    features = tokens_hbm.shape[1]
    heads_wide = heads * LANES

    def rows_of(c):
        return pl.ds(pl.multiple_of(c * step, step), step)

    def move(kind, route, c, strip, to):
        part = both.at[kind, strip, rows_of(c)]
        return remote(part, part, send_sem.at[kind, route, c], recv_sem.at[kind, route, c], (batch, to))

    load_cot = pltpu.make_async_copy(cot_hbm, both.at[0, me], row_sem.at[0])
    load_tokens = pltpu.make_async_copy(tokens_hbm, tokens, row_sem.at[1])
    load_cot.start()
    load_tokens.start()
    barrier = pltpu.get_barrier_semaphore()
    for other in (sibling, across):
        pl.semaphore_signal(barrier, inc=1, device_id=(batch, other), device_id_type=pl.DeviceIdType.MESH)
    loads = [(mlp_in_hbm, mlp_in), (mlp_out_hbm, mlp_out)]
    loads += [
        (qkv_hbm.at[pl.ds(to * DH, DH)], qkv_rows.at[pl.ds(i * DH, DH)]) for i, to in enumerate(kind_order(heads))
    ]
    loads += [(attn_hbm.at[pl.ds(h * DH, DH)], attn_pad.at[pl.ds(h * LANES, DH)]) for h in range(heads)]
    loads = [pltpu.make_async_copy(a, b, load_sem.at[i]) for i, (a, b) in enumerate(loads)]
    for load in loads:
        load.start()
    gain = row_of(ln_gain)
    gains = pair_row(q_gain, k_gain, heads)

    def norm_chunk(c):
        x = tokens[rows_of(c)].astype(F32)
        centred = x - jnp.mean(x, axis=-1, keepdims=True)
        variance = jnp.mean(centred * centred, axis=-1, keepdims=True)
        both[1, me, rows_of(c)] = (centred * lax.rsqrt(variance + epsilon) * gain).astype(BF16)

    def send_across(c):
        for kind in range(2):
            move(kind, 1, c, me, across).start()

    load_cot.wait()
    pl.semaphore_wait(barrier, 2)
    early = 3
    for c in range(early):
        move(0, 1, c, me, across).start()
    load_tokens.wait()

    def first_sends(c, _):
        norm_chunk(c)

        @pl.when(c < early)
        def _():
            move(1, 1, c, me, across).start()

        for kind in range(2):
            move(kind, 0, c, me, sibling).start()

        return 0

    lax.fori_loop(0, CHUNKS, first_sends, 0)

    g_in[...] = jnp.zeros_like(g_in)
    g_out[...] = jnp.zeros_like(g_out)
    rows_out[...] = jnp.zeros_like(rows_out)
    rows_out[1:2, :] = jnp.sum(both[0, me].astype(F32), axis=0, keepdims=True)
    filled = 3 * heads * DH
    if filled < qkv_rows.shape[0]:
        qkv_rows[filled:] = jnp.zeros((qkv_rows.shape[0] - filled, features), BF16)
    for h in range(heads):
        attn_pad[h * LANES + DH : (h + 1) * LANES, :] = jnp.zeros((DH, features), BF16)
    for load in loads:
        load.wait()

    sums = half_sums()
    bias = row_of(mlp_bias)

    def chunks_of(c, n):
        return pl.ds(pl.multiple_of(c * step, step), n * step)

    def saves(at_chip, c, n):
        strips, where = pl.ds(2 * at_chip, 2), chunks_of(c, n)
        first = at_chip * CHUNKS + c
        pairs = [(narrow.at[a, strips, where], ref.at[strips, where]) for a, ref in enumerate(
            (qa_out, ka_out, va_out, do_out, u_out, r_out))]
        pairs += [(wide.at[a, strips, where], ref.at[strips, where]) for a, ref in enumerate((mlp_part_out, dn_part_out))]
        pairs += [(both.at[1, strips, where], nall_out.at[strips, where]), (both.at[0, strips, where], call_out.at[strips, where])]
        return [pltpu.make_async_copy(a, b, save_sem.at[i, first]) for i, (a, b) in enumerate(pairs)]

    def wait_sibling(c):
        for kind in range(2):
            move(kind, 0, c, sibling, sibling).wait_recv()

    def pass_on(c):
        for kind in range(2):
            move(kind, 1, c, across, across).wait_recv()
            move(kind, 2, c, across, sibling).start()

    def wait_passed(c):
        for kind in range(2):
            move(kind, 2, c, across + 1 - 2 * (across % 2), sibling).wait_recv()

    def unit(at_chip, c, n, between=None):
        rows = 2 * n * step
        left = left_half(rows)
        strips, where = pl.ds(2 * at_chip, 2), chunks_of(c, n)
        normed = both[1, strips, where].reshape(rows, features)
        d = both[0, strips, where].reshape(rows, features)

        def save(ref, a, h, value):
            ref[a, strips, where, h * LANES : (h + 1) * LANES] = value.astype(BF16).reshape(2, n * step, LANES)

        qkv = nt(normed, qkv_rows[...])

        def block(b):
            return qkv[:, b * LANES : (b + 1) * LANES]

        def stacked_means(parts):
            stacked = jnp.concatenate([p.astype(BF16) for p in parts], axis=0)
            means = nn(stacked, sums) * (1.0 / DH)
            return [means[h * rows : (h + 1) * rows] for h in range(heads)]

        pairs = [block(h) for h in range(heads)]
        means = stacked_means(pairs)
        centred = [pairs[h] - means[h] for h in range(heads)]
        variances = stacked_means([x * x for x in centred])
        hidden = nn(normed, mlp_in[...]) + bias
        d_act = nt(d, mlp_out[...])
        if between:
            between()
        for h in range(heads):
            rstd = lax.rsqrt(variances[h] + epsilon)
            u = centred[h] * rstd
            scaled = u * gains[:, h * LANES : (h + 1) * LANES]
            save(narrow, 0, h, jnp.where(left, scaled * (DH ** (-0.5) * LOG2E), 0.0))
            save(narrow, 1, h, jnp.where(left, pltpu.roll(scaled, DH, 1), 1.0))
            value = block(heads + h // 2)
            save(narrow, 2, h, jnp.where(left, pltpu.roll(value, DH, 1) if h % 2 else value, 1.0))
            save(narrow, 4, h, u)
            save(narrow, 5, h, rstd)
        narrow[3, strips, where] = nt(d, attn_pad[...]).astype(BF16).reshape(2, n * step, heads_wide)
        cdf = 0.5 + 0.5 * lax.erf(hidden * 0.7071067811865476)
        act = (hidden * cdf).astype(BF16)
        slope = cdf + hidden * (0.3989422804014327 * jnp.exp(hidden * hidden * -0.5))
        d_low = (d_act * slope).astype(BF16)
        wide[0, strips, where] = nn(act, mlp_out[...]).astype(BF16).reshape(2, n * step, features)
        d_normed = nt(d_low, mlp_in[...])
        rows_out[2:3, :] += jnp.sum(d_normed * normed.astype(F32), axis=0, keepdims=True)
        wide[1, strips, where] = d_normed.astype(BF16).reshape(2, n * step, features)
        rows_out[0:1, :] += jnp.sum(d_low.astype(F32), axis=0, keepdims=True)
        g_out[...] += tn(act, d)
        g_in[...] += tn(normed, d_low)
        for copy in saves(at_chip, c, n):
            copy.start()

    half, quarter = CHUNKS // 2, CHUNKS // 4
    for c in range(half):
        wait_sibling(c)
    unit(chip, 0, half)

    def middle(i, _):
        send_across(3 + i)

        @pl.when(i < 2)
        def _():
            for c in range(quarter):
                wait_sibling(half + i * quarter + c)

        @pl.when(i == 4)
        def _():
            pass_on(5)

        @pl.when(i >= 2)
        def _():
            for c in range(quarter):
                wait_passed((i - 2) * quarter + c)

        def between():
            @pl.when((i == 1) | (i == 2))
            def _():
                pass_on(2 * i - 2)
                pass_on(2 * i - 1)

            @pl.when(i == 3)
            def _():
                pass_on(4)

        unit(
            jnp.where(i < 2, chip, far_chip), jnp.where(i < 2, half + i * quarter, (i - 2) * quarter), quarter, between
        )
        return 0

    lax.fori_loop(0, 5, middle, 0)

    def last(i, _):
        pass_on(6 + i)
        wait_passed(6 + i)
        unit(far_chip, 6 + i, 1)
        return 0

    lax.fori_loop(0, 2, last, 0)

    hi, lo = batch // n_lo, batch % n_lo
    def grad_saves():
        made = []
        for o in range(n_hi * n_lo):
            at_hi = (o // n_lo - hi + n_hi) % n_hi
            at_lo = (o % n_lo - lo + n_lo) % n_lo
            for first, part in ((0, lo_first), (lo_rows(features), hi_first)):
                count = part[0].shape[1]
                rows = low.at[pl.ds(first + o * count, count)]
                slot, place = (at_lo, at_hi) if first == 0 else (at_hi, at_lo)
                for m in range(len(part)):
                    made.append((slot == m, pltpu.make_async_copy(rows, part[m].at[place], save_sem.at[10, (first > 0) * n_hi * n_lo + o])))
        return made

    low[:features] = g_in[...].astype(BF16)
    low[features:] = g_out[...].astype(BF16)
    for chosen, copy in grad_saves():

        @pl.when(chosen)
        def _():
            copy.start()

    for chosen, copy in grad_saves():

        @pl.when(chosen)
        def _():
            copy.wait()

    for at_chip, c, n in (
        [(chip, 0, half), (chip, half, quarter), (chip, half + quarter, quarter)]
        + [(far_chip, i * quarter, quarter) for i in range(3)] + [(far_chip, 6, 1), (far_chip, 7, 1)]
    ):
        for copy in saves(at_chip, c, n):
            copy.wait()

    def sent(c, _):
        for kind in range(2):
            move(kind, 0, c, me, sibling).wait_send()
            move(kind, 1, c, me, across).wait_send()
            move(kind, 2, c, across, sibling).wait_send()
        return 0

    lax.fori_loop(0, CHUNKS, sent, 0)


def front(strips, n_batch, tokens, cot, ln_gain, q_gain, k_gain, mlp_bias, qkv_weight_t, attn_out, mlp_in, mlp_out):
    tok_dev, features = tokens.shape
    heads = q_gain.shape[0] // DH
    width = heads * LANES
    hidden = mlp_in.shape[1]
    blocks = heads + (heads + 1) // 2
    n_hi, n_lo = levels(n_batch)
    like = jax.ShapeDtypeStruct((strips, tok_dev, width), BF16)
    rows = jax.ShapeDtypeStruct((strips, tok_dev, features), BF16)
    return pl.pallas_call(
        functools.partial(front_body, heads, n_hi, n_lo),
        out_shape=(like,) * 6 + (rows,) * 4 + (
            jax.ShapeDtypeStruct((n_hi, lo_rows(features) // n_batch, features), BF16),
        ) * n_lo + (
            jax.ShapeDtypeStruct((n_lo, (2 * features - lo_rows(features)) // n_batch, features), BF16),
        ) * n_hi + (jax.ShapeDtypeStruct((8, features), F32),),
        in_specs=[ANY] * 2 + [VMEM] * 4 + [ANY] * 4,
        out_specs=(ANY,) * (10 + n_lo + n_hi) + (VMEM,),
        scratch_shapes=[
            pltpu.VMEM((2, strips, tok_dev, features), BF16),
            pltpu.VMEM((2, strips, tok_dev, features), BF16),
            pltpu.VMEM((6, strips, tok_dev, width), BF16),
            pltpu.VMEM((blocks * LANES, features), BF16),
            pltpu.VMEM((width, features), BF16),
            pltpu.VMEM(mlp_in.shape, BF16),
            pltpu.VMEM(mlp_out.shape, BF16),
            pltpu.VMEM((features, hidden), F32),
            pltpu.VMEM((hidden, features), F32),
            pltpu.VMEM(tokens.shape, BF16),
            pltpu.VMEM((features + hidden, features), BF16),
            pltpu.SemaphoreType.DMA((2, 3, CHUNKS)),
            pltpu.SemaphoreType.DMA((2, 3, CHUNKS)),
            pltpu.SemaphoreType.DMA((11, max(2 * CHUNKS, 2 * n_batch))),
            pltpu.SemaphoreType.DMA((2 + 4 * heads,)),
            pltpu.SemaphoreType.DMA((2,)),
        ],
        compiler_params=pltpu.CompilerParams(collective_id=0, has_side_effects=True, vmem_limit_bytes=60 << 20),
        name="gather_and_project",
    )(tokens, cot, ln_gain, q_gain, k_gain, mlp_bias, qkv_weight_t, attn_out, mlp_in, mlp_out)


def back_body(
    heads, n_hi, n_lo, d_qkv_hbm, nall_hbm, dn_part_hbm, ho_hbm, call_hbm, mlp_part_hbm, qkv_weight_t, attn_out, tokens, cot,
    ln_gain, out_bias, own_lo, own_hi, front_rows, gain_rows, output, input_grad, mlp_all_out, joint_all_out, rows_out,
    d_qkv, nall, dn_part, ho, call, mlp_part, weight_t, attn_pad, acc, attn_acc, joint, joint_low, joint_got, joint_sum,
    joint_got_hi, joint_all, mlp_all, near, core_give, core_got, x_give, x_got, vec, vec_lo, vec_hi, vec_pair,
    load_sem, mlp_z_s, mlp_z_r, mlp_y_s, mlp_y_r, joint_s, joint_r, hi_s, hi_r, all_z_s, all_z_r, all_y_s, all_y_r,
    core_s, core_r, x_s, x_r, vec_s, vec_r, save_sem,
):
    batch, me = lax.axis_index("batch"), lax.axis_index("tensor")
    hi, lo = batch // n_lo, batch % n_lo
    sibling = me + 1 - 2 * (me % 2)
    across = (me + 2) % 4
    far_sibling = (sibling + 2) % 4
    tok_dev, features = tokens.shape
    step = tok_dev // BACK_CHUNKS
    chunk_rows, half_cols = joint.shape[2], joint.shape[3]
    every_k, every_m = range(1, n_hi), range(1, n_lo)
    cut = chunk_rows // 2 // 16 * 16
    parts = [pl.ds(0, cut), pl.ds(cut, chunk_rows - cut)]

    strips = call.shape[0]
    by_strip = ((ho_hbm, ho), (call_hbm, call), (d_qkv_hbm, d_qkv), (nall_hbm, nall))

    def strip_loads(i):
        return [pltpu.make_async_copy(a.at[i], b.at[i], load_sem.at[n, i]) for n, (a, b) in enumerate(by_strip)]

    def rest_loads():
        pairs = ((dn_part_hbm, dn_part), (mlp_part_hbm, mlp_part))
        return [pltpu.make_async_copy(a, b, load_sem.at[len(by_strip) + n, 0]) for n, (a, b) in enumerate(pairs)]

    for i in range(strips):
        for load in strip_loads(i):
            load.start()
    for load in rest_loads():
        load.start()

    def hi_peer(k):
        return (hi + k + n_hi) % n_hi

    def lo_peer(m):
        return (lo + m + n_lo) % n_lo

    def to_hi(k):
        return (hi_peer(k) * n_lo + lo, me)

    def to_lo(m):
        return (hi * n_lo + lo_peer(m), me)

    barrier = pltpu.get_barrier_semaphore()
    peers = [to_hi(k) for k in every_k] + [to_lo(m) for m in every_m] + [(batch, sibling), (batch, across)]
    for peer in peers:
        pl.semaphore_signal(barrier, inc=1, device_id=peer, device_id_type=pl.DeviceIdType.MESH)
    mlp_all[hi, lo] = jnp.concatenate([own_lo[...], own_hi[...]], axis=0)
    pl.semaphore_wait(barrier, len(peers))

    def mlp_hop(s, up, origin):
        part = mlp_all.at[origin, lo]
        to = ((hi + (1 if up else -1) + n_hi) % n_hi * n_lo + lo, me)
        return remote(part, part, mlp_z_s.at[up, s], mlp_z_r.at[up, s], to)

    def mlp_send_hop(s, wait=False):
        for up in range(2):
            origin = hi - (s - 1) if up else hi + (s - 1)
            there = (origin >= 0) & (hi + 1 < n_hi) if up else (origin < n_hi) & (hi >= 1)

            @pl.when(there)
            def _():
                hop = mlp_hop(s, up, (origin + n_hi) % n_hi)
                hop.wait_send() if wait else hop.start()

    def mlp_wait_hop(s):
        for up in range(2):
            origin = hi - s if up else hi + s

            @pl.when((origin >= 0) if up else (origin < n_hi))
            def _():
                mlp_hop(s, up, (origin + n_hi) % n_hi).wait_recv()

    def mlp_lo(m, k, back=0):
        part = mlp_all.at[hi_peer(k), lo_peer(back)]
        return remote(part, part, mlp_y_s.at[m, k], mlp_y_r.at[m, k], to_lo(m))

    def mlp_send_lo(s):
        for m in every_m:
            for k, there in ((s, hi + s < n_hi), (n_hi - s, hi >= s)):

                @pl.when(there)
                def _():
                    mlp_lo(m, k).start()

    for m in every_m:
        mlp_lo(m, 0).start()
    mlp_send_hop(1)

    for i, place in enumerate(kind_order(heads)):
        weight_t[i * DH : (i + 1) * DH] = qkv_weight_t[place * DH : (place + 1) * DH]
    filled = qkv_weight_t.shape[0]
    if filled < weight_t.shape[0]:
        weight_t[filled:] = jnp.zeros((weight_t.shape[0] - filled, features), BF16)
    head_width = attn_out.shape[0]
    attn_pad[:head_width] = attn_out[...]
    attn_pad[head_width:] = jnp.zeros((attn_pad.shape[0] - head_width, features), BF16)
    def rows_of_pair(ref, i):
        return ref[2 * i : 2 * i + 2].reshape(2 * ref.shape[1], ref.shape[2])

    for i in range(strips // 2):
        for load in strip_loads(2 * i) + strip_loads(2 * i + 1):
            load.wait()
        new = tn(rows_of_pair(d_qkv, i), rows_of_pair(nall, i))
        acc[...] = acc[...] + new if i else new
        new = tn(rows_of_pair(ho, i), rows_of_pair(call, i))
        attn_acc[...] = attn_acc[...] + new if i else new

    width = qkv_weight_t.shape[0]
    joint_low[:width] = acc[:width].astype(BF16)
    joint_low[width:] = attn_acc[:head_width].astype(BF16)
    per_half = features // chunk_rows
    for o in range(n_hi * n_lo):
        row = o % per_half * chunk_rows
        col = o // per_half * half_cols
        joint[o % n_lo, o // n_lo] = joint_low[row : row + chunk_rows, col : col + half_cols]

    def joint_lo(p, m, back=0):
        return remote(
            joint.at[lo_peer(m), :, parts[p]], joint_got.at[lo_peer(back), :, parts[p]], joint_s.at[m, p], joint_r.at[m, p], to_lo(m)
        )

    def joint_hi(p, k, back=0):
        return remote(
            joint_sum.at[hi_peer(k), parts[p]], joint_got_hi.at[hi_peer(back), parts[p]], hi_s.at[k, p], hi_r.at[k, p], to_hi(k)
        )

    def joint_sum_lo(p):
        for m in every_m:
            joint_lo(p, m, -m).wait_recv()
        total = joint[lo, :, parts[p]].astype(F32)
        for m in every_m:
            total = total + joint_got[lo_peer(m), :, parts[p]].astype(F32)
        joint_sum[:, parts[p]] = total.astype(BF16)
        for k in every_k:
            joint_hi(p, k).start()

    def all_hi(p, k, back=0):
        part = joint_all.at[lo, hi_peer(back), parts[p]]
        return remote(part, part, all_z_s.at[k, p], all_z_r.at[k, p], to_hi(k))

    def all_lo(p, m, back=0):
        part = joint_all.at[lo_peer(back), :, parts[p]]
        return remote(part, part, all_y_s.at[m, p], all_y_r.at[m, p], to_lo(m))

    def joint_sum_hi(p):
        total = joint_sum[hi, parts[p]].astype(F32)
        for k in every_k:
            joint_hi(p, k, -k).wait_recv()
            total = total + joint_got_hi[hi_peer(-k), parts[p]].astype(F32)
        joint_all[lo, hi, parts[p]] = total.astype(BF16)
        for k in every_k:
            all_hi(p, k).start()

    def joint_pass(p):
        for k in every_k:
            all_hi(p, k, -k).wait_recv()
        for m in every_m:
            all_lo(p, m).start()

    for m in every_m:
        joint_lo(0, m).start()

    ln_row = jnp.sum(acc[...] * weight_t[...].astype(F32), axis=0, keepdims=True)
    gain = row_of(ln_gain)
    vec_lo[lo] = front_rows[...]
    vec_lo[lo, 2:3, :] = (front_rows[2:3, :] + ln_row) / gain
    vec_lo[lo, 3:4, 0 : heads * LANES] = gain_rows[0:1, :]

    def vec_lo_move(m, back=0):
        part = vec_lo.at[lo_peer(back)]
        return remote(part, part, vec_s.at[m], vec_r.at[m], to_lo(m))

    def vec_hi_move(k, back=0):
        part = vec_hi.at[hi_peer(back)]
        return remote(part, part, vec_s.at[n_lo + k], vec_r.at[n_lo + k], to_hi(k))

    def vec_pair_move(i, to):
        return remote(vec.at[i], vec_pair.at[i], vec_s.at[n_lo + n_hi + i], vec_r.at[n_lo + n_hi + i], (batch, to))

    for m in every_m:
        vec_lo_move(m).start()
    mlp_wait_hop(1)
    mlp_send_hop(2)

    def rows_of(c):
        return pl.ds(pl.multiple_of(c * step, step), step)

    def partial_rows(which, strip, c):
        if which == 0:
            return nn(d_qkv[strip, rows_of(c)], weight_t[...]) + dn_part[strip, rows_of(c)].astype(F32)
        return nn(ho[strip, rows_of(c)], attn_pad[...]) + mlp_part[strip, rows_of(c)].astype(F32)

    def core_move(which, side, c):
        where = rows_of(c)
        return remote(
            core_give.at[which, side, where], core_got.at[which, side, where],
            core_s.at[which, side, c], core_r.at[which, side, c], (batch, sibling),
        )

    def x_move(which, c):
        where = rows_of(c)
        return remote(x_give.at[which, where], x_got.at[which, where], x_s.at[which, c], x_r.at[which, c], (batch, across))

    def far(which):
        def give(c, _):
            core_give[which, 0, rows_of(c)] = partial_rows(which, far_sibling, c).astype(BF16)
            core_move(which, 0, c).start()
            return 0

        def send(c, _):
            mine = partial_rows(which, across, c)
            core_move(which, 0, c).wait_recv()
            x_give[which, rows_of(c)] = (mine + core_got[which, 0, rows_of(c)].astype(F32)).astype(BF16)
            x_move(which, c).start()
            return 0

        lax.fori_loop(0, BACK_CHUNKS, give, 0)
        lax.fori_loop(0, BACK_CHUNKS, send, 0)

    def close(which):
        def give(c, _):
            core_give[which, 1, rows_of(c)] = partial_rows(which, sibling, c).astype(BF16)
            core_move(which, 1, c).start()
            return 0

        def keep(c, _):
            mine = partial_rows(which, me, c)
            core_move(which, 1, c).wait_recv()
            near[which, rows_of(c)] = mine + core_got[which, 1, rows_of(c)].astype(F32)
            return 0

        lax.fori_loop(0, BACK_CHUNKS, give, 0)
        lax.fori_loop(0, BACK_CHUNKS, keep, 0)

    for load in rest_loads():
        load.wait()
    far(0)
    for m in every_m:
        joint_lo(1, m).start()
    far(1)
    mlp_send_lo(1)
    joint_sum_lo(0)
    for s in range(2, n_hi - 1):
        mlp_wait_hop(s)
        mlp_send_hop(s + 1)
    close(0)
    joint_sum_lo(1)
    close(1)

    for m in every_m:
        vec_lo_move(m, -m).wait_recv()
    total = vec_lo[0]
    for i in range(1, n_lo):
        total = total + vec_lo[i]
    vec_hi[hi] = total
    for k in every_k:
        vec_hi_move(k).start()

    for s in range(2, n_hi - 1):
        mlp_send_lo(s)
    joint_sum_hi(0)
    if n_hi > 2:
        mlp_wait_hop(n_hi - 1)
        mlp_send_lo(n_hi - 1)
    joint_sum_hi(1)

    for k in every_k:
        vec_hi_move(k, -k).wait_recv()
    total = vec_hi[0]
    for i in range(1, n_hi):
        total = total + vec_hi[i]
    vec[0] = total
    vec_pair_move(0, sibling).start()

    joint_pass(0)
    vec_pair_move(0, sibling).wait_recv()
    vec[1] = vec[0] + vec_pair[0]
    vec_pair_move(1, across).start()

    joint_pass(1)

    def last_rows(c, _):
        x_move(0, c).wait_recv()
        where = rows_of(c)
        d_normed = near[0, where] + x_got[0, where].astype(F32)
        x = tokens[where].astype(F32)
        centred = x - jnp.mean(x, axis=-1, keepdims=True)
        r = lax.rsqrt(jnp.mean(centred * centred, axis=-1, keepdims=True) + epsilon)
        xhat = centred * r
        e = d_normed * gain
        d_x = r * (e - jnp.mean(e, axis=-1, keepdims=True) - xhat * jnp.mean(e * xhat, axis=-1, keepdims=True))
        input_grad[where] = (cot[where].astype(F32) + d_x).astype(BF16)
        return 0

    lax.fori_loop(0, BACK_CHUNKS, last_rows, 0)
    bias = row_of(out_bias)

    def out_rows(c, _):
        x_move(1, c).wait_recv()
        where = rows_of(c)
        output[where] = (tokens[where].astype(F32) + near[1, where] + x_got[1, where].astype(F32) + bias).astype(BF16)
        return 0

    lax.fori_loop(0, BACK_CHUNKS, out_rows, 0)
    vec_pair_move(1, across).wait_recv()
    rows_out[...] = vec[0]
    rows_out[1:3, :] = vec[1, 1:3, :] + vec_pair[1, 1:3, :]

    for m in every_m:
        for k in range(n_hi):
            mlp_lo(m, k, -m).wait_recv()
    save_mlp = pltpu.make_async_copy(mlp_all, mlp_all_out, save_sem.at[0])
    save_mlp.start()
    for s in range(1, n_hi):
        mlp_send_hop(s, wait=True)
    for m in every_m:
        for k in range(n_hi):
            mlp_lo(m, k).wait_send()
        for p in range(2):
            joint_lo(p, m).wait_send()
        vec_lo_move(m).wait_send()
    for k in every_k:
        for p in range(2):
            joint_hi(p, k).wait_send()
            all_hi(p, k).wait_send()
        vec_hi_move(k).wait_send()
    vec_pair_move(0, sibling).wait_send()
    vec_pair_move(1, across).wait_send()

    def sent(c, _):
        for which in range(2):
            core_move(which, 0, c).wait_send()
            core_move(which, 1, c).wait_send()
            x_move(which, c).wait_send()
        return 0

    lax.fori_loop(0, BACK_CHUNKS, sent, 0)
    for m in every_m:
        for p in range(2):
            all_lo(p, m, -m).wait_recv()
            all_lo(p, m).wait_send()
    save_joint = pltpu.make_async_copy(joint_all, joint_all_out, save_sem.at[1])
    save_joint.start()
    save_mlp.wait()
    save_joint.wait()


def levels(n_batch):
    lo = 2 if n_batch <= 8 else 4
    return n_batch // lo, lo


def back(
    n_batch, d_qkv, nall, dn_part, ho, call, mlp_part, qkv_weight_t, attn_out, tokens, cot, ln_gain, out_bias,
    own_lo, own_hi, front_rows, gain_rows,
):
    n_hi, n_lo = levels(n_batch)
    strips, tok_dev, features = nall.shape
    own = (own_lo.shape[0] + own_hi.shape[0], features)
    wide, packed = d_qkv.shape[2], ho.shape[2]
    heads = attn_out.shape[0] // DH
    chunk = (2 * features // n_batch, features // 2)
    dma = pltpu.SemaphoreType.DMA
    vmem = pltpu.VMEM
    return pl.pallas_call(
        functools.partial(back_body, heads, n_hi, n_lo),
        out_shape=(
            jax.ShapeDtypeStruct(tokens.shape, BF16),
            jax.ShapeDtypeStruct(tokens.shape, BF16),
            jax.ShapeDtypeStruct((n_hi, n_lo) + own, BF16),
            jax.ShapeDtypeStruct((n_lo, n_hi) + chunk, BF16),
            jax.ShapeDtypeStruct((8, features), F32),
        ),
        in_specs=[ANY] * 6 + [VMEM] * 10,
        out_specs=(VMEM, VMEM, ANY, ANY, VMEM),
        scratch_shapes=[
            vmem(d_qkv.shape, BF16), vmem(nall.shape, BF16), vmem(dn_part.shape, BF16),
            vmem(ho.shape, BF16), vmem(call.shape, BF16), vmem(mlp_part.shape, BF16),
            vmem((wide, features), BF16),
            vmem((packed, features), BF16),
            vmem((wide, features), F32),
            vmem((packed, features), F32),
            vmem((n_lo, n_hi) + chunk, BF16),
            vmem((features, features), BF16),
            vmem((n_lo, n_hi) + chunk, BF16),
            vmem((n_hi,) + chunk, BF16),
            vmem((n_hi,) + chunk, BF16),
            vmem((n_lo, n_hi) + chunk, BF16),
            vmem((n_hi, n_lo) + own, BF16),
            vmem((2,) + tokens.shape, F32),
            vmem((2, 2) + tokens.shape, BF16),
            vmem((2, 2) + tokens.shape, BF16),
            vmem((2,) + tokens.shape, BF16),
            vmem((2,) + tokens.shape, BF16),
            vmem((2, 8, features), F32),
            vmem((n_lo, 8, features), F32),
            vmem((n_hi, 8, features), F32),
            vmem((2, 8, features), F32),
            dma((6, strips)),
            dma((2, n_hi)), dma((2, n_hi)),
            dma((n_lo, n_hi)), dma((n_lo, n_hi)),
            dma((n_lo, 2)), dma((n_lo, 2)),
            dma((n_hi, 2)), dma((n_hi, 2)),
            dma((n_hi, 2)), dma((n_hi, 2)),
            dma((n_lo, 2)), dma((n_lo, 2)),
            dma((2, 2, BACK_CHUNKS)), dma((2, 2, BACK_CHUNKS)),
            dma((2, BACK_CHUNKS)), dma((2, BACK_CHUNKS)),
            dma((n_lo + n_hi + 2,)), dma((n_lo + n_hi + 2,)),
            dma((2,)),
        ],
        compiler_params=pltpu.CompilerParams(collective_id=1, has_side_effects=True, vmem_limit_bytes=60 << 20),
        name="reduce_gradients",
    )(
        d_qkv, nall, dn_part, ho, call, mlp_part, qkv_weight_t, attn_out, tokens, cot, ln_gain, out_bias,
        own_lo, own_hi, front_rows, gain_rows,
    )


def widen_body(
    heads, mlp_hbm, joint_hbm, output_in, input_grad_in, rows,
    output, input_grad, qkv_out, attn_out, mlp_in_out, mlp_out_out, ln_gain, q_gain, k_gain, mlp_bias, out_bias,
    kept, mlp_all, joint_all, joint, qkv_t, attn, mlp, sems,
):
    def copy(i, source, to):
        made = pltpu.make_async_copy(source, to, sems.at[i])
        made.start()
        return made

    chunks = mlp_all.shape[0]
    load_mlp = [copy(10 + o, mlp_hbm.at[o], mlp_all.at[o]) for o in range(chunks)]
    load_joint = copy(0, joint_hbm, joint_all)
    load_rows = [copy(2, output_in, kept.at[0]), copy(3, input_grad_in, kept.at[1])]
    features = rows.shape[1]
    mlp_bias[...] = rows[0:1, :].reshape(features)
    out_bias[...] = rows[1:2, :].reshape(features)
    ln_gain[...] = rows[2:3, :].reshape(features)
    for offset, ref in ((0, q_gain), (DH, k_gain)):
        parts = [rows[3:4, h * LANES + offset : h * LANES + offset + DH] for h in range(heads)]
        ref[...] = jnp.concatenate(parts, axis=1).reshape(heads * DH)
    cut = lo_rows(features) // chunks
    rest = mlp_all.shape[1] - cut
    pending = []

    def store(sem, row, count):
        to = mlp_in_out if row < features else mlp_out_out
        pending.append(copy(sem, mlp.at[pl.ds(row, count)], to.at[pl.ds(row % features, count)]))

    for o in range(chunks):
        load_mlp[o].wait()
        row = lo_rows(features) + o * rest
        mlp[o * cut : (o + 1) * cut] = mlp_all[o, :cut].astype(F32)
        mlp[row : row + rest] = mlp_all[o, cut:].astype(F32)
        store(10 + chunks + o, o * cut, cut)
        store(10 + 2 * chunks + o, row, rest)
    load_joint.wait()
    n_lo, n_hi, chunk_rows, cols = joint_all.shape
    width = qkv_t.shape[0]
    per_half = features // chunk_rows
    for o in range(n_lo * n_hi):
        row = o % per_half * chunk_rows
        joint[o // per_half, row : row + chunk_rows] = joint_all[o % n_lo, o // n_lo]
    for half in range(2):
        at = slice(half * cols, (half + 1) * cols)
        attn[:, at] = joint[half, width:].astype(F32)
        for i, place in enumerate(kind_order(heads)):
            qkv_t[place * DH : (place + 1) * DH, at] = joint[half, i * DH : (i + 1) * DH].astype(F32)
    pending += [copy(4, qkv_t, qkv_out), copy(5, attn, attn_out)]
    for i, (load, to) in enumerate(zip(load_rows, (output, input_grad))):
        load.wait()
        pending.append(copy(8 + i, kept.at[i], to))
    for made in pending:
        made.wait()


def widen(heads, width, mlp_all, joint_all, output, input_grad, rows):
    features = rows.shape[1]
    head_width = heads * DH

    def out(*shape):
        return jax.ShapeDtypeStruct(shape, F32)

    like = jax.ShapeDtypeStruct(output.shape, BF16)
    return pl.pallas_call(
        functools.partial(widen_body, heads),
        out_shape=(
            like, like, out(width, features), out(head_width, features), out(features, features), out(features, features),
            out(features), out(head_width), out(head_width), out(features), out(features),
        ),
        in_specs=[ANY] * 4 + [VMEM],
        out_specs=(ANY,) * 6 + (VMEM,) * 5,
        scratch_shapes=[
            pltpu.VMEM((2,) + output.shape, BF16),
            pltpu.VMEM(mlp_all.shape, BF16),
            pltpu.VMEM(joint_all.shape, BF16),
            pltpu.VMEM((2, features, features // 2), BF16),
            pltpu.VMEM((width, features), F32),
            pltpu.VMEM((head_width, features), F32),
            pltpu.VMEM((2 * features, features), F32),
            pltpu.SemaphoreType.DMA((10 + 3 * mlp_all.shape[0],)),
        ],
        compiler_params=pltpu.CompilerParams(vmem_limit_bytes=60 << 20),
        name="widen_gradients",
    )(mlp_all, joint_all, output, input_grad, rows)


def on_device(
    tokens, out_cotangent, ln_gain, qkv_weight, q_gain, k_gain, attn_out,
    mlp_in, mlp_bias, mlp_out, out_bias, image_len, image_group,
):
    tok_dev, features = tokens.shape
    strips = lax.axis_size("tensor")
    n_batch = lax.axis_size("batch")
    n_hi, n_lo = levels(n_batch)
    heads = q_gain.shape[0] // DH
    qkv_cols = qkv_weight.shape[1]

    weight_t = qkv_weight.T
    (qa, ka, va, do, u, r, mlp_part, dn_part, nall, call, *mlp_grad, front_rows) = front(
        strips, n_batch, tokens, out_cotangent, ln_gain, q_gain, k_gain, mlp_bias, weight_t, attn_out, mlp_in, mlp_out
    )

    def along_lo(x, m):
        pairs = [(h * n_lo + i, h * n_lo + (i + m) % n_lo) for h in range(n_hi) for i in range(n_lo)]
        return lax.ppermute(x, "batch", pairs)

    def along_hi(x, k):
        pairs = [(h * n_lo + i, (h + k) % n_hi * n_lo + i) for h in range(n_hi) for i in range(n_lo)]
        return lax.ppermute(x, "batch", pairs)

    def add(first, others):
        total = first.astype(F32)
        for other in others:
            total = total + other.astype(F32)
        return total.astype(BF16)

    lo_first, hi_first = mlp_grad[:n_lo], mlp_grad[n_lo:]
    lo_got = [along_lo(lo_first[m], m) for m in range(1, n_lo)]
    hi_got = [along_hi(hi_first[k], k) for k in range(1, n_hi)]
    qb, dob, ho = attn_fwd(image_len, image_group, qa, ka, va, do)
    lo_sum = [add(lo_first[0][k], [got[k] for got in lo_got]) for k in range(n_hi)]
    hi_sum = [add(hi_first[0][m], [got[m] for got in hi_got]) for m in range(n_lo)]
    qb, lo_sum, hi_sum = lax.optimization_barrier((qb, lo_sum, hi_sum))
    lo_got = [along_hi(lo_sum[k], k) for k in range(1, n_hi)]
    hi_got = [along_lo(hi_sum[m], m) for m in range(1, n_lo)]
    d_qkv, gain_rows = attn_bwd(image_len, image_group, qb, ka, va, dob, u, r, q_gain, k_gain)
    own_lo, own_hi = add(lo_sum[0], lo_got), add(hi_sum[0], hi_got)
    output, input_grad, mlp_all, joint_all, rows = back(
        n_batch, d_qkv, nall, dn_part, ho, call, mlp_part, weight_t, attn_out, tokens, out_cotangent, ln_gain, out_bias,
        own_lo, own_hi, front_rows, gain_rows,
    )
    output, input_grad, qkv_t, attn, mlp_in_grad, mlp_out_grad, ln, q, k, bias, out_bias_grad = widen(
        heads, qkv_cols, mlp_all.reshape((n_batch,) + mlp_all.shape[2:]), joint_all,
        output, input_grad, rows,
    )
    return output, input_grad, ln, qkv_t.T, q, k, attn, mlp_in_grad, bias, mlp_out_grad, out_bias_grad


def solution(mesh):
    rows, cols, first = P(("batch", "tensor"), None), P(None, "tensor"), P("tensor", None)
    return jax.shard_map(
        on_device,
        mesh=mesh,
        in_specs=(rows, rows, P(), cols, P("tensor"), P("tensor"), first, cols, P("tensor"), first, P(), P(), P()),
        out_specs=(rows, rows, P(), cols, P("tensor"), P("tensor"), first, cols, P("tensor"), first, P()),
        check_vma=False,
    )
```

```python
import functools

import jax
import jax.numpy as jnp
from jax import lax
from jax.experimental import pallas as pl
from jax.experimental.pallas import tpu as pltpu
from jax.sharding import PartitionSpec as P

DH = 64
LANES = 128
WIN = 64
ALIGN = 16
LOG2E = 1.4426950408889634
epsilon = 1e-06
F32 = jnp.float32
BF16 = jnp.bfloat16
VMEM = pl.BlockSpec(memory_space=pltpu.VMEM)
SMEM = pl.BlockSpec(memory_space=pltpu.SMEM)
ANY = pl.BlockSpec(memory_space=pl.ANY)


def nn(left, right):
    return lax.dot_general(left, right, (((1,), (0,)), ((), ())), preferred_element_type=F32)


def nt(left, right):
    return lax.dot_general(left, right, (((1,), (1,)), ((), ())), preferred_element_type=F32)


def tn(left, right):
    return lax.dot_general(left, right, (((0,), (0,)), ((), ())), preferred_element_type=F32)


def row_of(vector):
    return vector[...].astype(F32).reshape(1, -1)


def pair_row(q_vector, k_vector, heads):
    q, k = row_of(q_vector), row_of(k_vector)
    parts = []
    for h in range(heads):
        parts += [q[:, h * DH : (h + 1) * DH], k[:, h * DH : (h + 1) * DH]]
    return jnp.concatenate(parts, axis=1)


def half_sums(lanes=LANES):
    row = lax.broadcasted_iota(jnp.int32, (lanes, lanes), 0) // DH
    col = lax.broadcasted_iota(jnp.int32, (lanes, lanes), 1) // DH
    return jnp.where(row == col, 1.0, 0.0).astype(BF16)


def left_half(rows):
    return lax.broadcasted_iota(jnp.int32, (rows, LANES), 1) < DH


def find_segments(len_ref, group_ref, seg_ref, strips, tok_dev):
    group = lax.axis_index("batch")

    def entry(i, carry):
        count, run = carry
        rows = jnp.where(group_ref[i] == group, len_ref[i] // strips, 0)

        @pl.when(rows > 0)
        def _():
            seg_ref[0, count] = run
            seg_ref[1, count] = run + rows

        return count + jnp.where(rows > 0, 1, 0), run + rows

    count, run = lax.fori_loop(0, len_ref.shape[0], entry, (jnp.int32(0), jnp.int32(0)))

    @pl.when(run < tok_dev)
    def _():
        seg_ref[0, count] = run
        seg_ref[1, count] = tok_dev

    return count + jnp.where(run < tok_dev, 1, 0)


def window(start, end, first, i, tok_dev):
    nominal = first + WIN * i
    at = pl.multiple_of(jnp.minimum(nominal, tok_dev - WIN), ALIGN)
    return at, jnp.maximum(start, nominal) - at, jnp.minimum(end, nominal + WIN) - at


def row_mask(low, high, strips, win=WIN, width=LANES):
    j = lax.broadcasted_iota(jnp.int32, (strips, win, width), 1).reshape(strips * win, width)
    return (j >= low) & (j < high)


def low_mask(mask):
    return jnp.where(mask, 1.0, 0.0).astype(BF16) > jnp.asarray(0.5, BF16)


def tile(ref, at, h, win=WIN):
    strips = ref.shape[0]
    return ref[:, pl.ds(at, win), h * LANES : (h + 1) * LANES].reshape(strips * win, LANES)


def put_tile(ref, at, h, mask, value, win=WIN, width=LANES):
    strips = ref.shape[0]
    where = (slice(None), pl.ds(at, win), slice(h * LANES, h * LANES + width))
    old = ref[where].reshape(strips * win, width)
    ref[where] = jnp.where(mask, value.astype(ref.dtype), old).reshape(strips, win, width)


PIECES = 4


def pieces_of(pairs, sem, tok_dev):
    rows = tok_dev // PIECES
    return [
        [
            pltpu.make_async_copy(a.at[:, pl.ds(p * rows, rows)], b.at[:, pl.ds(p * rows, rows)], sem.at[i, p])
            for i, (a, b) in enumerate(pairs)
        ]
        for p in range(PIECES)
    ]


def for_segments(len_ref, group_ref, seg, strips, tok_dev, loads, later, stores, small, middle, large):
    for piece in loads:
        for copy in piece:
            copy.start()
    for copy in later:
        copy.start()
    count = find_segments(len_ref, group_ref, seg, strips, tok_dev)
    big = middle_rows(tok_dev)
    rows = tok_dev // PIECES

    def segment(index, ready):
        start, end = seg[0, index], seg[1, index]
        first = (start // ALIGN) * ALIGN
        windows = (end - first + WIN - 1) // WIN
        fits = (end - first <= big) & (end - start <= big - ALIGN)
        reach = jnp.where(windows == 1, first + WIN, jnp.where(fits, first + big, first + windows * WIN))
        needed = jnp.minimum((reach + rows - 1) // rows, PIECES)
        for p in range(PIECES):

            @pl.when((p >= ready) & (p < needed))
            def _():
                for copy in loads[p]:
                    copy.wait()

        @pl.when(windows == 1)
        def _():
            small(*window(start, end, first, 0, tok_dev))

        @pl.when((windows > 1) & fits)
        def _():
            at = pl.multiple_of(jnp.minimum(first, tok_dev - big), ALIGN)
            middle(at, start - at, end - at)

        @pl.when(jnp.logical_not(fits))
        def _():
            large(start, end, first, windows)

        for p, piece in enumerate(stores):

            @pl.when((start < (p + 1) * rows) & ((p + 1) * rows <= end))
            def _():
                for copy in piece:
                    copy.start()

        return jnp.maximum(ready, needed)

    lax.fori_loop(0, count, segment, jnp.int32(0))


def edge_tile(ref, at, h, low):
    strips = ref.shape[0]
    cols = slice(h * LANES, (h + 1) * LANES)
    last = middle_rows(ref.shape[1]) - ALIGN
    body = ref[:, pl.ds(at + last - WIN + ALIGN, WIN - ALIGN), cols]
    late = low_mask(row_mask(low, ALIGN, strips, ALIGN))
    edge = jnp.where(late, tile(ref, at, h, ALIGN), tile(ref, at + last, h, ALIGN))
    return jnp.concatenate([body, edge.reshape(strips, ALIGN, LANES)], axis=1).reshape(strips * WIN, LANES)


def edge_mask(low, high, strips, tok_dev):
    last = middle_rows(tok_dev) - ALIGN
    j = lax.broadcasted_iota(jnp.int32, (strips, WIN, LANES), 1).reshape(strips * WIN, LANES)
    edge = j - (WIN - ALIGN)
    body = j + (last - WIN + ALIGN)
    inner = (edge < 0) & (body >= low) & (body < high)
    return inner | ((edge >= 0) & ((edge >= low) | (edge < high - last)))


def middle_rows(tok_dev):
    return min(tok_dev, tok_dev // 2 + ALIGN)


def attn_fwd_body(
    heads, len_ref, group_ref, qa_hbm, ka_hbm, va_hbm, do_hbm, qb_hbm, dob_hbm, ho_hbm,
    qa, ka, va, do, qb, dob, ho, seg, acc, in_sem, out_sem,
):
    strips, tok_dev = qa.shape[0], qa.shape[1]
    loads = pieces_of([(qa_hbm, qa), (ka_hbm, ka), (va_hbm, va), (do_hbm, do)], in_sem, tok_dev)
    stores = pieces_of([(qb, qb_hbm), (dob, dob_hbm), (ho, ho_hbm)], out_sem, tok_dev)
    zero = jnp.zeros((), BF16)
    big = middle_rows(tok_dev)

    def finish(at, low, high, totals, win=WIN):
        rows = strips * win
        mask = low_mask(row_mask(low, high, strips, win))
        lane = lax.broadcasted_iota(jnp.int32, (rows, LANES), 1)
        left = lane < DH
        first, second = low_mask(lane == DH), low_mask(lane == DH + 1)
        outs = []
        for h in range(heads):
            total = totals[h]
            log_sum = jnp.log2(jnp.where(left, pltpu.roll(total, DH, 1), total))
            out = jnp.where(left, total * jnp.exp2(-log_sum), 0.0)
            d_out = tile(do, at, h, win)
            delta = jnp.sum(out * d_out.astype(F32), axis=-1, keepdims=True)
            delta = jnp.broadcast_to(delta, (rows, LANES))
            log_hi, delta_hi = log_sum.astype(BF16), delta.astype(BF16)
            log_low = (log_hi.astype(F32) - log_sum).astype(BF16)
            delta_low = (delta_hi.astype(F32) - delta).astype(BF16)
            q = jnp.where(first, -log_hi, jnp.where(second, log_low, tile(qa, at, h, win)))
            d_out = jnp.where(first, -delta_hi, jnp.where(second, delta_low, d_out))
            put_tile(qb, at, h, mask, q, win)
            put_tile(dob, at, h, mask, d_out, win)
            outs.append(out)
        if heads % 2:
            outs.append(jnp.zeros_like(outs[0]))
        for b in range(len(outs) // 2):
            put_tile(ho, at, b, mask, jnp.where(left, outs[2 * b], pltpu.roll(outs[2 * b + 1], DH, 1)), win)

    def products(at_q, keys, values, k_mask, win_q=WIN):
        scores = [nt(tile(qa, at_q, h, win_q), keys(h)) for h in range(heads)]
        weights = [jnp.exp2(s).astype(BF16) for s in scores]
        k_mask = low_mask(k_mask)
        return [nn(weights[h], jnp.where(k_mask, values(h), zero)) for h in range(heads)]

    def plain(at_q, at_k, k_mask, win_q=WIN):
        return products(at_q, lambda h: tile(ka, at_k, h), lambda h: tile(va, at_k, h), k_mask, win_q)

    def small(at, low, high):
        finish(at, low, high, plain(at, at, row_mask(low, high, strips)))

    def middle(at, low, high):
        edges = products(
            at, lambda h: edge_tile(ka, at, h, low), lambda h: edge_tile(va, at, h, low),
            edge_mask(low, high, strips, tok_dev), big,
        )
        for h in range(heads):
            acc[h] = edges[h]

        def k_window(k, _):
            offset = ALIGN + k * WIN
            new = plain(pl.multiple_of(at, ALIGN), pl.multiple_of(at + offset, ALIGN), row_mask(low - offset, high - offset, strips), big)
            for h in range(heads):
                acc[h] = acc[h] + new[h]
            return 0

        lax.fori_loop(0, big // WIN - 1, k_window, 0)
        rest = big % WIN
        base = at + big - rest

        def total(h, offset, win):
            return acc[h].reshape(strips, big, LANES)[:, offset : offset + win].reshape(strips * win, LANES)

        for w in range(big // WIN):
            offset = w * WIN
            finish(
                pl.multiple_of(at + offset, ALIGN), low - offset, high - offset, [total(h, offset, WIN) for h in range(heads)]
            )
        if rest:
            offset = big - rest
            finish(base, low - offset, high - offset, [total(h, offset, rest) for h in range(heads)], rest)

    def large(start, end, first, windows):
        def q_window(i, _):
            at_q, low_q, high_q = window(start, end, first, i, tok_dev)
            rows = strips * WIN
            acc[:, :rows] = jnp.zeros((heads, rows, LANES), F32)

            def k_window(k, _):
                at_k, low_k, high_k = window(start, end, first, k, tok_dev)
                for h, new in enumerate(plain(at_q, at_k, row_mask(low_k, high_k, strips))):
                    acc[h, :rows] += new
                return 0

            lax.fori_loop(0, windows, k_window, 0)
            finish(at_q, low_q, high_q, [acc[h, :rows] for h in range(heads)])
            return 0

        lax.fori_loop(0, windows, q_window, 0)

    for_segments(len_ref, group_ref, seg, strips, tok_dev, loads, [], stores, small, middle, large)
    for piece in stores:
        for copy in piece:
            copy.wait()


def attn_fwd(image_len, image_group, qa, ka, va, do):
    strips, tok_dev, width = qa.shape
    heads = width // LANES
    packed = (heads + 1) // 2 * LANES
    like = jax.ShapeDtypeStruct(qa.shape, BF16)
    return pl.pallas_call(
        functools.partial(attn_fwd_body, heads),
        out_shape=(like, like, jax.ShapeDtypeStruct((strips, tok_dev, packed), BF16)),
        in_specs=[SMEM, SMEM] + [ANY] * 4,
        out_specs=(ANY,) * 3,
        scratch_shapes=[pltpu.VMEM(qa.shape, BF16)] * 6 + [
            pltpu.VMEM((strips, tok_dev, packed), BF16),
            pltpu.SMEM((2, image_len.shape[0] + 1), jnp.int32),
            pltpu.VMEM((heads, strips * middle_rows(tok_dev), LANES), F32),
            pltpu.SemaphoreType.DMA((4, PIECES)),
            pltpu.SemaphoreType.DMA((3, PIECES)),
        ],
        compiler_params=pltpu.CompilerParams(vmem_limit_bytes=60 << 20),
        cost_estimate=pl.CostEstimate(flops=8 * 10**9, bytes_accessed=30 * 10**6, transcendentals=8 * 10**6),
        name="attention_forward",
    )(image_len, image_group, qa, ka, va, do)


def attn_bwd_body(
    heads, len_ref, group_ref, qb_hbm, ka_hbm, va_hbm, dob_hbm, u_hbm, r_hbm, q_gain, k_gain,
    d_qkv_hbm, gain_grad, seg, k_turned, dq_turned, dk_acc, dv_acc, dq, dk, dv, qb, ka, va, dob, u_rows, r_rows, d_qkv,
    in_sem, out_sem, sems,
):
    strips, tok_dev = qb.shape[0], qb.shape[1]
    pieces = pieces_of([(qb_hbm, qb), (ka_hbm, ka), (va_hbm, va), (dob_hbm, dob)], in_sem, tok_dev)
    loads = [pltpu.make_async_copy(u_hbm, u_rows, sems.at[0]), pltpu.make_async_copy(r_hbm, r_rows, sems.at[1])]
    zero = jnp.zeros((), BF16)
    big = middle_rows(tok_dev)

    def products(queries, d_rows, at_k, q_mask, k_turned_of, win_k=WIN):
        every = range(heads)
        qs = [queries(h) for h in every]
        q_mask = low_mask(q_mask)
        d_outs = [jnp.where(q_mask, d_rows(h), zero) for h in every]
        scores = [nt(tile(ka, at_k, h, win_k), qs[h]) for h in every]
        d_weights = [nt(tile(va, at_k, h, win_k), d_outs[h]) for h in every]
        weights = [jnp.exp2(s) for s in scores]
        d_scores = [(weights[h] * d_weights[h]).astype(BF16) for h in every]
        dv_new = [nn(weights[h].astype(BF16), d_outs[h]) for h in every]
        dk_new = [nn(d_scores[h], qs[h]) for h in every]
        dq_new = [nn(k_turned_of(h), d_scores[h]) for h in every]
        return dq_new, dk_new, dv_new

    def plain(at_q, at_k, q_mask, k_turned_of, win_k=WIN):
        return products(lambda h: tile(qb, at_q, h), lambda h: tile(dob, at_q, h), at_k, q_mask, k_turned_of, win_k)

    def turned(h, at_k, mask, win=WIN):
        return jnp.where(low_mask(mask), tile(ka, at_k, h, win), zero).T[:DH]

    def small(at, low, high):
        mask = row_mask(low, high, strips)
        half = row_mask(low, high, strips, width=DH)
        dq_t, dk_new, dv_new = plain(at, at, mask, lambda h: turned(h, at, mask))
        for h in range(heads):
            put_tile(dq, at, h, half, dq_t[h].T, width=DH)
            put_tile(dk, at, h, mask, dk_new[h])
            put_tile(dv, at, h, mask, dv_new[h])

    def middle(at, low, high):
        mask = row_mask(low, high, strips, big)
        for h in range(heads):
            k_turned[h] = turned(h, at, mask, big)

        dq_t, dk_new, dv_new = products(
            lambda h: edge_tile(qb, at, h, low), lambda h: edge_tile(dob, at, h, low), at,
            edge_mask(low, high, strips, tok_dev), lambda h: k_turned[h], big,
        )
        last = big - ALIGN
        body = last - WIN + ALIGN
        body_mask = row_mask(low - body, high - body, strips, WIN - ALIGN, DH)
        first_mask = row_mask(low, ALIGN, strips, ALIGN, DH)
        last_mask = row_mask(0, high - last, strips, ALIGN, DH)
        for h in range(heads):
            dk_acc[h], dv_acc[h] = dk_new[h], dv_new[h]
            rows_new = dq_t[h].T.reshape(strips, WIN, DH)
            edge = rows_new[:, WIN - ALIGN :].reshape(strips * ALIGN, DH)
            inner = rows_new[:, : WIN - ALIGN].reshape(strips * (WIN - ALIGN), DH)
            put_tile(dq, at + body, h, body_mask, inner, WIN - ALIGN, DH)
            put_tile(dq, at, h, first_mask, edge, ALIGN, DH)
            put_tile(dq, at + last, h, last_mask, edge, ALIGN, DH)

        def each(i, _):
            offset = ALIGN + i * WIN
            at_q = pl.multiple_of(at + offset, ALIGN)
            mask_q = row_mask(low - offset, high - offset, strips)
            half = row_mask(low - offset, high - offset, strips, width=DH)
            dq_t, dk_new, dv_new = plain(at_q, pl.multiple_of(at, ALIGN), mask_q, lambda h: k_turned[h], big)
            for h in range(heads):
                put_tile(dq, at_q, h, half, dq_t[h].T, width=DH)
                dk_acc[h] = dk_acc[h] + dk_new[h]
                dv_acc[h] = dv_acc[h] + dv_new[h]
            return 0

        lax.fori_loop(0, big // WIN - 1, each, 0)
        for h in range(heads):
            put_tile(dk, at, h, mask, dk_acc[h], big)
            put_tile(dv, at, h, mask, dv_acc[h], big)

    def large(start, end, first, windows):
        rows = strips * WIN

        def clear(i, _):
            for h in range(heads):
                dq_turned[h, i] = jnp.zeros(dq_turned.shape[2:], F32)
            return 0

        lax.fori_loop(0, windows, clear, 0)

        def k_window(k, _):
            at_k, low_k, high_k = window(start, end, first, k, tok_dev)
            mask_k = row_mask(low_k, high_k, strips)
            for h in range(heads):
                k_turned[h, :, :rows] = turned(h, at_k, mask_k)
            dk_acc[:, :rows] = jnp.zeros((heads, rows, LANES), F32)
            dv_acc[:, :rows] = jnp.zeros((heads, rows, LANES), F32)

            def q_window(i, _):
                at_q, low_q, high_q = window(start, end, first, i, tok_dev)
                mask_q = row_mask(low_q, high_q, strips)
                dq_t, dk_new, dv_new = plain(at_q, at_k, mask_q, lambda h: k_turned[h, :, :rows])
                for h in range(heads):
                    dq_turned[h, i] += dq_t[h]
                    dk_acc[h, :rows] += dk_new[h]
                    dv_acc[h, :rows] += dv_new[h]
                return 0

            lax.fori_loop(0, windows, q_window, 0)
            for h in range(heads):
                put_tile(dk, at_k, h, mask_k, dk_acc[h, :rows])
                put_tile(dv, at_k, h, mask_k, dv_acc[h, :rows])
            return 0

        lax.fori_loop(0, windows, k_window, 0)

        def q_out(i, _):
            at_q, low_q, high_q = window(start, end, first, i, tok_dev)
            half = row_mask(low_q, high_q, strips, width=DH)
            for h in range(heads):
                put_tile(dq, at_q, h, half, dq_turned[h, i].T, width=DH)
            return 0

        lax.fori_loop(0, windows, q_out, 0)

    for_segments(len_ref, group_ref, seg, strips, tok_dev, pieces, loads, [], small, middle, large)

    rows = strips * WIN
    left = left_half(rows)
    sums = half_sums(2 * LANES)
    gains = pair_row(q_gain, k_gain, heads)
    for load in loads:
        load.wait()

    def save(i):
        where = pl.ds(pl.multiple_of(i * WIN, WIN), WIN)
        return pltpu.make_async_copy(d_qkv.at[:, where], d_qkv_hbm.at[:, where], out_sem.at[i])

    def chunk(i, totals):
        at = pl.multiple_of(i * WIN, WIN)
        scaled, new_totals, us = [], [], []
        for h in range(heads):
            cols = slice(h * LANES, (h + 1) * LANES)
            d_q, d_k = tile(dq, at, h), tile(dk, at, h) * (1.0 / LOG2E)
            both = jnp.where(left, d_q * DH ** (-0.5), pltpu.roll(d_k, DH, 1))
            u = tile(u_rows, at, h).astype(F32)
            new_totals.append(totals[h] + jnp.sum(both * u, axis=0, keepdims=True))
            scaled.append(both * gains[:, cols])
            us.append(u)
        pairs = [jnp.concatenate([scaled[h].astype(BF16), (scaled[h] * us[h]).astype(BF16)], axis=1) for h in range(heads)]
        means = nn(jnp.concatenate(pairs, axis=0), sums) * (1.0 / DH)
        parts = []
        for h in range(heads):
            mean = means[h * rows : (h + 1) * rows, :LANES]
            mean_u = means[h * rows : (h + 1) * rows, LANES:]
            parts.append((scaled[h] - mean - us[h] * mean_u) * tile(r_rows, at, h).astype(F32))
        values = [tile(dv, at, h) for h in range(heads)]
        if heads % 2:
            values.append(jnp.zeros_like(values[0]))
        for b in range(len(values) // 2):
            parts.append(jnp.where(left, values[2 * b], pltpu.roll(values[2 * b + 1], DH, 1)))
        for b, part in enumerate(parts):
            d_qkv[:, pl.ds(at, WIN), b * LANES : (b + 1) * LANES] = part.astype(BF16).reshape(strips, WIN, LANES)
        save(i).start()
        return tuple(new_totals)

    totals = lax.fori_loop(0, tok_dev // WIN, chunk, tuple(jnp.zeros((1, LANES), F32) for _ in range(heads)))
    gain_grad[...] = jnp.zeros_like(gain_grad)
    for h in range(heads):
        gain_grad[0:1, h * LANES : (h + 1) * LANES] = totals[h]

    def saved(i, _):
        save(i).wait()
        return 0

    lax.fori_loop(0, tok_dev // WIN, saved, 0)


def attn_bwd(image_len, image_group, qb, ka, va, dob, u, r, q_gain, k_gain):
    strips, tok_dev, width = qb.shape
    heads = width // LANES
    blocks = heads + (heads + 1) // 2
    rows = strips * WIN
    big = strips * middle_rows(tok_dev)
    windows = tok_dev // WIN + 1
    full = pltpu.VMEM((strips, tok_dev, width), F32)
    return pl.pallas_call(
        functools.partial(attn_bwd_body, heads),
        out_shape=(
            jax.ShapeDtypeStruct((strips, tok_dev, blocks * LANES), BF16),
            jax.ShapeDtypeStruct((8, width), F32),
        ),
        in_specs=[SMEM, SMEM] + [ANY] * 6 + [VMEM] * 2,
        out_specs=(ANY, VMEM),
        scratch_shapes=[
            pltpu.SMEM((2, image_len.shape[0] + 1), jnp.int32),
            pltpu.VMEM((heads, DH, big), BF16),
            pltpu.VMEM((heads, windows, DH, rows), F32),
            pltpu.VMEM((heads, big, LANES), F32),
            pltpu.VMEM((heads, big, LANES), F32),
            full, full, full,
        ] + [pltpu.VMEM(qb.shape, BF16)] * 6 + [
            pltpu.VMEM((strips, tok_dev, blocks * LANES), BF16),
            pltpu.SemaphoreType.DMA((4, PIECES)),
            pltpu.SemaphoreType.DMA((tok_dev // WIN,)),
            pltpu.SemaphoreType.DMA((2,)),
        ],
        compiler_params=pltpu.CompilerParams(vmem_limit_bytes=60 << 20),
        cost_estimate=pl.CostEstimate(flops=16 * 10**9, bytes_accessed=30 * 10**6, transcendentals=8 * 10**6),
        name="attention_backward",
    )(image_len, image_group, qb, ka, va, dob, u, r, q_gain, k_gain)


CHUNKS = 8
BACK_CHUNKS = 4


def kind_order(heads):
    return [3 * h + i for h in range(heads) for i in range(2)] + [3 * h + 2 for h in range(heads)]


def remote(src, dst, send, recv, device):
    return pltpu.make_async_remote_copy(
        src_ref=src, dst_ref=dst, send_sem=send, recv_sem=recv, device_id=device, device_id_type=pl.DeviceIdType.MESH
    )


def lo_rows(features):
    return 2 * features * 2 // 3


def front_body(
    heads, n_hi, n_lo, tokens_hbm, cot_hbm, ln_gain, q_gain, k_gain, mlp_bias, qkv_hbm, attn_hbm, mlp_in_hbm, mlp_out_hbm,
    qa_out, ka_out, va_out, do_out, u_out, r_out, mlp_part_out, dn_part_out, nall_out, call_out,
    *rest,
):
    (rows_out, both, wide, narrow, qkv_rows, attn_pad, mlp_in, mlp_out, g_in, g_out,
     tokens, low, send_sem, recv_sem, save_sem, load_sem, row_sem) = rest[-17:]
    lo_first, hi_first = rest[:n_lo], rest[n_lo : n_lo + n_hi]
    batch, me = lax.axis_index("batch"), lax.axis_index("tensor")
    sibling = me + 1 - 2 * (me % 2)
    across = (me + 2) % 4
    chip, far_chip = me // 2, 1 - me // 2
    tok_dev = tokens_hbm.shape[0]
    step = tok_dev // CHUNKS
    features = tokens_hbm.shape[1]
    heads_wide = heads * LANES

    def rows_of(c):
        return pl.ds(pl.multiple_of(c * step, step), step)

    def move(kind, route, c, strip, to):
        part = both.at[kind, strip, rows_of(c)]
        return remote(part, part, send_sem.at[kind, route, c], recv_sem.at[kind, route, c], (batch, to))

    load_cot = pltpu.make_async_copy(cot_hbm, both.at[0, me], row_sem.at[0])
    load_tokens = pltpu.make_async_copy(tokens_hbm, tokens, row_sem.at[1])
    load_cot.start()
    load_tokens.start()
    barrier = pltpu.get_barrier_semaphore()
    for other in (sibling, across):
        pl.semaphore_signal(barrier, inc=1, device_id=(batch, other), device_id_type=pl.DeviceIdType.MESH)
    loads = [(mlp_in_hbm, mlp_in), (mlp_out_hbm, mlp_out)]
    loads += [
        (qkv_hbm.at[pl.ds(to * DH, DH)], qkv_rows.at[pl.ds(i * DH, DH)]) for i, to in enumerate(kind_order(heads))
    ]
    loads += [(attn_hbm.at[pl.ds(h * DH, DH)], attn_pad.at[pl.ds(h * LANES, DH)]) for h in range(heads)]
    loads = [pltpu.make_async_copy(a, b, load_sem.at[i]) for i, (a, b) in enumerate(loads)]
    for load in loads:
        load.start()
    gain = row_of(ln_gain)
    gains = pair_row(q_gain, k_gain, heads)

    def norm_chunk(c):
        x = tokens[rows_of(c)].astype(F32)
        centred = x - jnp.mean(x, axis=-1, keepdims=True)
        variance = jnp.mean(centred * centred, axis=-1, keepdims=True)
        both[1, me, rows_of(c)] = (centred * lax.rsqrt(variance + epsilon) * gain).astype(BF16)

    def send_across(c):
        for kind in range(2):
            move(kind, 1, c, me, across).start()

    load_cot.wait()
    pl.semaphore_wait(barrier, 2)
    early = 3
    for c in range(early):
        move(0, 1, c, me, across).start()
    load_tokens.wait()

    def first_sends(c, _):
        norm_chunk(c)

        @pl.when(c < early)
        def _():
            move(1, 1, c, me, across).start()

        for kind in range(2):
            move(kind, 0, c, me, sibling).start()

        return 0

    lax.fori_loop(0, CHUNKS, first_sends, 0)

    g_in[...] = jnp.zeros_like(g_in)
    g_out[...] = jnp.zeros_like(g_out)
    rows_out[...] = jnp.zeros_like(rows_out)
    rows_out[1:2, :] = jnp.sum(both[0, me].astype(F32), axis=0, keepdims=True)
    filled = 3 * heads * DH
    if filled < qkv_rows.shape[0]:
        qkv_rows[filled:] = jnp.zeros((qkv_rows.shape[0] - filled, features), BF16)
    for h in range(heads):
        attn_pad[h * LANES + DH : (h + 1) * LANES, :] = jnp.zeros((DH, features), BF16)
    for load in loads:
        load.wait()

    sums = half_sums()
    bias = row_of(mlp_bias)

    def chunks_of(c, n):
        return pl.ds(pl.multiple_of(c * step, step), n * step)

    def saves(at_chip, c, n):
        strips, where = pl.ds(2 * at_chip, 2), chunks_of(c, n)
        first = at_chip * CHUNKS + c
        pairs = [(narrow.at[a, strips, where], ref.at[strips, where]) for a, ref in enumerate(
            (qa_out, ka_out, va_out, do_out, u_out, r_out))]
        pairs += [(wide.at[a, strips, where], ref.at[strips, where]) for a, ref in enumerate((mlp_part_out, dn_part_out))]
        pairs += [(both.at[1, strips, where], nall_out.at[strips, where]), (both.at[0, strips, where], call_out.at[strips, where])]
        return [pltpu.make_async_copy(a, b, save_sem.at[i, first]) for i, (a, b) in enumerate(pairs)]

    def wait_sibling(c):
        for kind in range(2):
            move(kind, 0, c, sibling, sibling).wait_recv()

    def pass_on(c):
        for kind in range(2):
            move(kind, 1, c, across, across).wait_recv()
            move(kind, 2, c, across, sibling).start()

    def wait_passed(c):
        for kind in range(2):
            move(kind, 2, c, across + 1 - 2 * (across % 2), sibling).wait_recv()

    def unit(at_chip, c, n, between=None):
        rows = 2 * n * step
        left = left_half(rows)
        strips, where = pl.ds(2 * at_chip, 2), chunks_of(c, n)
        normed = both[1, strips, where].reshape(rows, features)
        d = both[0, strips, where].reshape(rows, features)

        def save(ref, a, h, value):
            ref[a, strips, where, h * LANES : (h + 1) * LANES] = value.astype(BF16).reshape(2, n * step, LANES)

        qkv = nt(normed, qkv_rows[...])

        def block(b):
            return qkv[:, b * LANES : (b + 1) * LANES]

        def stacked_means(parts):
            stacked = jnp.concatenate([p.astype(BF16) for p in parts], axis=0)
            means = nn(stacked, sums) * (1.0 / DH)
            return [means[h * rows : (h + 1) * rows] for h in range(heads)]

        pairs = [block(h) for h in range(heads)]
        means = stacked_means(pairs)
        centred = [pairs[h] - means[h] for h in range(heads)]
        variances = stacked_means([x * x for x in centred])
        hidden = nn(normed, mlp_in[...]) + bias
        d_act = nt(d, mlp_out[...])
        if between:
            between()
        for h in range(heads):
            rstd = lax.rsqrt(variances[h] + epsilon)
            u = centred[h] * rstd
            scaled = u * gains[:, h * LANES : (h + 1) * LANES]
            save(narrow, 0, h, jnp.where(left, scaled * (DH ** (-0.5) * LOG2E), 0.0))
            save(narrow, 1, h, jnp.where(left, pltpu.roll(scaled, DH, 1), 1.0))
            value = block(heads + h // 2)
            save(narrow, 2, h, jnp.where(left, pltpu.roll(value, DH, 1) if h % 2 else value, 1.0))
            save(narrow, 4, h, u)
            save(narrow, 5, h, rstd)
        narrow[3, strips, where] = nt(d, attn_pad[...]).astype(BF16).reshape(2, n * step, heads_wide)
        cdf = 0.5 + 0.5 * lax.erf(hidden * 0.7071067811865476)
        act = (hidden * cdf).astype(BF16)
        slope = cdf + hidden * (0.3989422804014327 * jnp.exp(hidden * hidden * -0.5))
        d_low = (d_act * slope).astype(BF16)
        wide[0, strips, where] = nn(act, mlp_out[...]).astype(BF16).reshape(2, n * step, features)
        d_normed = nt(d_low, mlp_in[...])
        rows_out[2:3, :] += jnp.sum(d_normed * normed.astype(F32), axis=0, keepdims=True)
        wide[1, strips, where] = d_normed.astype(BF16).reshape(2, n * step, features)
        rows_out[0:1, :] += jnp.sum(d_low.astype(F32), axis=0, keepdims=True)
        g_out[...] += tn(act, d)
        g_in[...] += tn(normed, d_low)
        for copy in saves(at_chip, c, n):
            copy.start()

    half, quarter = CHUNKS // 2, CHUNKS // 4
    for c in range(half):
        wait_sibling(c)
    unit(chip, 0, half)

    def middle(i, _):
        send_across(3 + i)

        @pl.when(i < 2)
        def _():
            for c in range(quarter):
                wait_sibling(half + i * quarter + c)

        @pl.when(i == 4)
        def _():
            pass_on(5)

        @pl.when(i >= 2)
        def _():
            for c in range(quarter):
                wait_passed((i - 2) * quarter + c)

        def between():
            @pl.when((i == 1) | (i == 2))
            def _():
                pass_on(2 * i - 2)
                pass_on(2 * i - 1)

            @pl.when(i == 3)
            def _():
                pass_on(4)

        unit(
            jnp.where(i < 2, chip, far_chip), jnp.where(i < 2, half + i * quarter, (i - 2) * quarter), quarter, between
        )
        return 0

    lax.fori_loop(0, 5, middle, 0)

    def last(i, _):
        pass_on(6 + i)
        wait_passed(6 + i)
        unit(far_chip, 6 + i, 1)
        return 0

    lax.fori_loop(0, 2, last, 0)

    hi, lo = batch // n_lo, batch % n_lo
    def grad_saves():
        made = []
        for o in range(n_hi * n_lo):
            at_hi = (o // n_lo - hi + n_hi) % n_hi
            at_lo = (o % n_lo - lo + n_lo) % n_lo
            for first, part in ((0, lo_first), (lo_rows(features), hi_first)):
                count = part[0].shape[1]
                rows = low.at[pl.ds(first + o * count, count)]
                slot, place = (at_lo, at_hi) if first == 0 else (at_hi, at_lo)
                for m in range(len(part)):
                    made.append((slot == m, pltpu.make_async_copy(rows, part[m].at[place], save_sem.at[10, (first > 0) * n_hi * n_lo + o])))
        return made

    low[:features] = g_in[...].astype(BF16)
    low[features:] = g_out[...].astype(BF16)
    for chosen, copy in grad_saves():

        @pl.when(chosen)
        def _():
            copy.start()

    for chosen, copy in grad_saves():

        @pl.when(chosen)
        def _():
            copy.wait()

    for at_chip, c, n in (
        [(chip, 0, half), (chip, half, quarter), (chip, half + quarter, quarter)]
        + [(far_chip, i * quarter, quarter) for i in range(3)] + [(far_chip, 6, 1), (far_chip, 7, 1)]
    ):
        for copy in saves(at_chip, c, n):
            copy.wait()

    def sent(c, _):
        for kind in range(2):
            move(kind, 0, c, me, sibling).wait_send()
            move(kind, 1, c, me, across).wait_send()
            move(kind, 2, c, across, sibling).wait_send()
        return 0

    lax.fori_loop(0, CHUNKS, sent, 0)


def front(strips, n_batch, tokens, cot, ln_gain, q_gain, k_gain, mlp_bias, qkv_weight_t, attn_out, mlp_in, mlp_out):
    tok_dev, features = tokens.shape
    heads = q_gain.shape[0] // DH
    width = heads * LANES
    hidden = mlp_in.shape[1]
    blocks = heads + (heads + 1) // 2
    n_hi, n_lo = levels(n_batch)
    like = jax.ShapeDtypeStruct((strips, tok_dev, width), BF16)
    rows = jax.ShapeDtypeStruct((strips, tok_dev, features), BF16)
    return pl.pallas_call(
        functools.partial(front_body, heads, n_hi, n_lo),
        out_shape=(like,) * 6 + (rows,) * 4 + (
            jax.ShapeDtypeStruct((n_hi, lo_rows(features) // n_batch, features), BF16),
        ) * n_lo + (
            jax.ShapeDtypeStruct((n_lo, (2 * features - lo_rows(features)) // n_batch, features), BF16),
        ) * n_hi + (jax.ShapeDtypeStruct((8, features), F32),),
        in_specs=[ANY] * 2 + [VMEM] * 4 + [ANY] * 4,
        out_specs=(ANY,) * (10 + n_lo + n_hi) + (VMEM,),
        scratch_shapes=[
            pltpu.VMEM((2, strips, tok_dev, features), BF16),
            pltpu.VMEM((2, strips, tok_dev, features), BF16),
            pltpu.VMEM((6, strips, tok_dev, width), BF16),
            pltpu.VMEM((blocks * LANES, features), BF16),
            pltpu.VMEM((width, features), BF16),
            pltpu.VMEM(mlp_in.shape, BF16),
            pltpu.VMEM(mlp_out.shape, BF16),
            pltpu.VMEM((features, hidden), F32),
            pltpu.VMEM((hidden, features), F32),
            pltpu.VMEM(tokens.shape, BF16),
            pltpu.VMEM((features + hidden, features), BF16),
            pltpu.SemaphoreType.DMA((2, 3, CHUNKS)),
            pltpu.SemaphoreType.DMA((2, 3, CHUNKS)),
            pltpu.SemaphoreType.DMA((11, max(2 * CHUNKS, 2 * n_batch))),
            pltpu.SemaphoreType.DMA((2 + 4 * heads,)),
            pltpu.SemaphoreType.DMA((2,)),
        ],
        compiler_params=pltpu.CompilerParams(collective_id=0, has_side_effects=True, vmem_limit_bytes=60 << 20),
        name="gather_and_project",
    )(tokens, cot, ln_gain, q_gain, k_gain, mlp_bias, qkv_weight_t, attn_out, mlp_in, mlp_out)


def back_body(
    heads, n_hi, n_lo, d_qkv_hbm, nall_hbm, dn_part_hbm, ho_hbm, call_hbm, mlp_part_hbm, qkv_weight_t, attn_out, tokens, cot,
    ln_gain, out_bias, own_lo, own_hi, front_rows, gain_rows, output, input_grad, mlp_all_out, joint_all_out, rows_out,
    d_qkv, nall, dn_part, ho, call, mlp_part, weight_t, attn_pad, acc, attn_acc, joint, joint_low, joint_got, joint_sum,
    joint_got_hi, joint_all, mlp_all, near, core_give, core_got, x_give, x_got, vec, vec_lo, vec_hi, vec_pair,
    load_sem, mlp_z_s, mlp_z_r, mlp_y_s, mlp_y_r, joint_s, joint_r, hi_s, hi_r, all_z_s, all_z_r, all_y_s, all_y_r,
    core_s, core_r, x_s, x_r, vec_s, vec_r, save_sem,
):
    batch, me = lax.axis_index("batch"), lax.axis_index("tensor")
    hi, lo = batch // n_lo, batch % n_lo
    sibling = me + 1 - 2 * (me % 2)
    across = (me + 2) % 4
    far_sibling = (sibling + 2) % 4
    tok_dev, features = tokens.shape
    step = tok_dev // BACK_CHUNKS
    chunk_rows, half_cols = joint.shape[2], joint.shape[3]
    every_k, every_m = range(1, n_hi), range(1, n_lo)
    cut = chunk_rows // 2 // 16 * 16
    parts = [pl.ds(0, cut), pl.ds(cut, chunk_rows - cut)]

    strips = call.shape[0]
    by_strip = ((ho_hbm, ho), (call_hbm, call), (d_qkv_hbm, d_qkv), (nall_hbm, nall))

    def strip_loads(i):
        return [pltpu.make_async_copy(a.at[i], b.at[i], load_sem.at[n, i]) for n, (a, b) in enumerate(by_strip)]

    def rest_loads():
        pairs = ((dn_part_hbm, dn_part), (mlp_part_hbm, mlp_part))
        return [pltpu.make_async_copy(a, b, load_sem.at[len(by_strip) + n, 0]) for n, (a, b) in enumerate(pairs)]

    for i in range(strips):
        for load in strip_loads(i):
            load.start()
    for load in rest_loads():
        load.start()

    def hi_peer(k):
        return (hi + k + n_hi) % n_hi

    def lo_peer(m):
        return (lo + m + n_lo) % n_lo

    def to_hi(k):
        return (hi_peer(k) * n_lo + lo, me)

    def to_lo(m):
        return (hi * n_lo + lo_peer(m), me)

    barrier = pltpu.get_barrier_semaphore()
    peers = [to_hi(k) for k in every_k] + [to_lo(m) for m in every_m] + [(batch, sibling), (batch, across)]
    for peer in peers:
        pl.semaphore_signal(barrier, inc=1, device_id=peer, device_id_type=pl.DeviceIdType.MESH)
    mlp_all[hi, lo] = jnp.concatenate([own_lo[...], own_hi[...]], axis=0)
    pl.semaphore_wait(barrier, len(peers))

    def mlp_hop(s, up, origin):
        part = mlp_all.at[origin, lo]
        to = ((hi + (1 if up else -1) + n_hi) % n_hi * n_lo + lo, me)
        return remote(part, part, mlp_z_s.at[up, s], mlp_z_r.at[up, s], to)

    def mlp_send_hop(s, wait=False):
        for up in range(2):
            origin = hi - (s - 1) if up else hi + (s - 1)
            there = (origin >= 0) & (hi + 1 < n_hi) if up else (origin < n_hi) & (hi >= 1)

            @pl.when(there)
            def _():
                hop = mlp_hop(s, up, (origin + n_hi) % n_hi)
                hop.wait_send() if wait else hop.start()

    def mlp_wait_hop(s):
        for up in range(2):
            origin = hi - s if up else hi + s

            @pl.when((origin >= 0) if up else (origin < n_hi))
            def _():
                mlp_hop(s, up, (origin + n_hi) % n_hi).wait_recv()

    def mlp_lo(m, k, back=0):
        part = mlp_all.at[hi_peer(k), lo_peer(back)]
        return remote(part, part, mlp_y_s.at[m, k], mlp_y_r.at[m, k], to_lo(m))

    def mlp_send_lo(s):
        for m in every_m:
            for k, there in ((s, hi + s < n_hi), (n_hi - s, hi >= s)):

                @pl.when(there)
                def _():
                    mlp_lo(m, k).start()

    for m in every_m:
        mlp_lo(m, 0).start()
    mlp_send_hop(1)

    for i, place in enumerate(kind_order(heads)):
        weight_t[i * DH : (i + 1) * DH] = qkv_weight_t[place * DH : (place + 1) * DH]
    filled = qkv_weight_t.shape[0]
    if filled < weight_t.shape[0]:
        weight_t[filled:] = jnp.zeros((weight_t.shape[0] - filled, features), BF16)
    head_width = attn_out.shape[0]
    attn_pad[:head_width] = attn_out[...]
    attn_pad[head_width:] = jnp.zeros((attn_pad.shape[0] - head_width, features), BF16)
    def rows_of_pair(ref, i):
        return ref[2 * i : 2 * i + 2].reshape(2 * ref.shape[1], ref.shape[2])

    for i in range(strips // 2):
        for load in strip_loads(2 * i) + strip_loads(2 * i + 1):
            load.wait()
        new = tn(rows_of_pair(d_qkv, i), rows_of_pair(nall, i))
        acc[...] = acc[...] + new if i else new
        new = tn(rows_of_pair(ho, i), rows_of_pair(call, i))
        attn_acc[...] = attn_acc[...] + new if i else new

    width = qkv_weight_t.shape[0]
    joint_low[:width] = acc[:width].astype(BF16)
    joint_low[width:] = attn_acc[:head_width].astype(BF16)
    per_half = features // chunk_rows
    for o in range(n_hi * n_lo):
        row = o % per_half * chunk_rows
        col = o // per_half * half_cols
        joint[o % n_lo, o // n_lo] = joint_low[row : row + chunk_rows, col : col + half_cols]

    def joint_lo(p, m, back=0):
        return remote(
            joint.at[lo_peer(m), :, parts[p]], joint_got.at[lo_peer(back), :, parts[p]], joint_s.at[m, p], joint_r.at[m, p], to_lo(m)
        )

    def joint_hi(p, k, back=0):
        return remote(
            joint_sum.at[hi_peer(k), parts[p]], joint_got_hi.at[hi_peer(back), parts[p]], hi_s.at[k, p], hi_r.at[k, p], to_hi(k)
        )

    def joint_sum_lo(p):
        for m in every_m:
            joint_lo(p, m, -m).wait_recv()
        total = joint[lo, :, parts[p]].astype(F32)
        for m in every_m:
            total = total + joint_got[lo_peer(m), :, parts[p]].astype(F32)
        joint_sum[:, parts[p]] = total.astype(BF16)
        for k in every_k:
            joint_hi(p, k).start()

    def all_hi(p, k, back=0):
        part = joint_all.at[lo, hi_peer(back), parts[p]]
        return remote(part, part, all_z_s.at[k, p], all_z_r.at[k, p], to_hi(k))

    def all_lo(p, m, back=0):
        part = joint_all.at[lo_peer(back), :, parts[p]]
        return remote(part, part, all_y_s.at[m, p], all_y_r.at[m, p], to_lo(m))

    def joint_sum_hi(p):
        total = joint_sum[hi, parts[p]].astype(F32)
        for k in every_k:
            joint_hi(p, k, -k).wait_recv()
            total = total + joint_got_hi[hi_peer(-k), parts[p]].astype(F32)
        joint_all[lo, hi, parts[p]] = total.astype(BF16)
        for k in every_k:
            all_hi(p, k).start()

    def joint_pass(p):
        for k in every_k:
            all_hi(p, k, -k).wait_recv()
        for m in every_m:
            all_lo(p, m).start()

    for m in every_m:
        joint_lo(0, m).start()

    ln_row = jnp.sum(acc[...] * weight_t[...].astype(F32), axis=0, keepdims=True)
    gain = row_of(ln_gain)
    vec_lo[lo] = front_rows[...]
    vec_lo[lo, 2:3, :] = (front_rows[2:3, :] + ln_row) / gain
    vec_lo[lo, 3:4, 0 : heads * LANES] = gain_rows[0:1, :]

    def vec_lo_move(m, back=0):
        part = vec_lo.at[lo_peer(back)]
        return remote(part, part, vec_s.at[m], vec_r.at[m], to_lo(m))

    def vec_hi_move(k, back=0):
        part = vec_hi.at[hi_peer(back)]
        return remote(part, part, vec_s.at[n_lo + k], vec_r.at[n_lo + k], to_hi(k))

    def vec_pair_move(i, to):
        return remote(vec.at[i], vec_pair.at[i], vec_s.at[n_lo + n_hi + i], vec_r.at[n_lo + n_hi + i], (batch, to))

    for m in every_m:
        vec_lo_move(m).start()
    mlp_wait_hop(1)
    mlp_send_hop(2)

    def rows_of(c):
        return pl.ds(pl.multiple_of(c * step, step), step)

    def partial_rows(which, strip, c):
        if which == 0:
            return nn(d_qkv[strip, rows_of(c)], weight_t[...]) + dn_part[strip, rows_of(c)].astype(F32)
        return nn(ho[strip, rows_of(c)], attn_pad[...]) + mlp_part[strip, rows_of(c)].astype(F32)

    def core_move(which, side, c):
        where = rows_of(c)
        return remote(
            core_give.at[which, side, where], core_got.at[which, side, where],
            core_s.at[which, side, c], core_r.at[which, side, c], (batch, sibling),
        )

    def x_move(which, c):
        where = rows_of(c)
        return remote(x_give.at[which, where], x_got.at[which, where], x_s.at[which, c], x_r.at[which, c], (batch, across))

    def far(which):
        def give(c, _):
            core_give[which, 0, rows_of(c)] = partial_rows(which, far_sibling, c).astype(BF16)
            core_move(which, 0, c).start()
            return 0

        def send(c, _):
            mine = partial_rows(which, across, c)
            core_move(which, 0, c).wait_recv()
            x_give[which, rows_of(c)] = (mine + core_got[which, 0, rows_of(c)].astype(F32)).astype(BF16)
            x_move(which, c).start()
            return 0

        lax.fori_loop(0, BACK_CHUNKS, give, 0)
        lax.fori_loop(0, BACK_CHUNKS, send, 0)

    def close(which):
        def give(c, _):
            core_give[which, 1, rows_of(c)] = partial_rows(which, sibling, c).astype(BF16)
            core_move(which, 1, c).start()
            return 0

        def keep(c, _):
            mine = partial_rows(which, me, c)
            core_move(which, 1, c).wait_recv()
            near[which, rows_of(c)] = mine + core_got[which, 1, rows_of(c)].astype(F32)
            return 0

        lax.fori_loop(0, BACK_CHUNKS, give, 0)
        lax.fori_loop(0, BACK_CHUNKS, keep, 0)

    for load in rest_loads():
        load.wait()
    far(0)
    for m in every_m:
        joint_lo(1, m).start()
    far(1)
    mlp_send_lo(1)
    joint_sum_lo(0)
    for s in range(2, n_hi - 1):
        mlp_wait_hop(s)
        mlp_send_hop(s + 1)
    close(0)
    joint_sum_lo(1)
    close(1)

    for m in every_m:
        vec_lo_move(m, -m).wait_recv()
    total = vec_lo[0]
    for i in range(1, n_lo):
        total = total + vec_lo[i]
    vec_hi[hi] = total
    for k in every_k:
        vec_hi_move(k).start()

    for s in range(2, n_hi - 1):
        mlp_send_lo(s)
    joint_sum_hi(0)
    if n_hi > 2:
        mlp_wait_hop(n_hi - 1)
        mlp_send_lo(n_hi - 1)
    joint_sum_hi(1)

    for k in every_k:
        vec_hi_move(k, -k).wait_recv()
    total = vec_hi[0]
    for i in range(1, n_hi):
        total = total + vec_hi[i]
    vec[0] = total
    vec_pair_move(0, sibling).start()

    joint_pass(0)
    vec_pair_move(0, sibling).wait_recv()
    vec[1] = vec[0] + vec_pair[0]
    vec_pair_move(1, across).start()

    joint_pass(1)

    def last_rows(c, _):
        x_move(0, c).wait_recv()
        where = rows_of(c)
        d_normed = near[0, where] + x_got[0, where].astype(F32)
        x = tokens[where].astype(F32)
        centred = x - jnp.mean(x, axis=-1, keepdims=True)
        r = lax.rsqrt(jnp.mean(centred * centred, axis=-1, keepdims=True) + epsilon)
        xhat = centred * r
        e = d_normed * gain
        d_x = r * (e - jnp.mean(e, axis=-1, keepdims=True) - xhat * jnp.mean(e * xhat, axis=-1, keepdims=True))
        input_grad[where] = (cot[where].astype(F32) + d_x).astype(BF16)
        return 0

    lax.fori_loop(0, BACK_CHUNKS, last_rows, 0)
    bias = row_of(out_bias)

    def out_rows(c, _):
        x_move(1, c).wait_recv()
        where = rows_of(c)
        output[where] = (tokens[where].astype(F32) + near[1, where] + x_got[1, where].astype(F32) + bias).astype(BF16)
        return 0

    lax.fori_loop(0, BACK_CHUNKS, out_rows, 0)
    vec_pair_move(1, across).wait_recv()
    rows_out[...] = vec[0]
    rows_out[1:3, :] = vec[1, 1:3, :] + vec_pair[1, 1:3, :]

    for m in every_m:
        for k in range(n_hi):
            mlp_lo(m, k, -m).wait_recv()
    save_mlp = pltpu.make_async_copy(mlp_all, mlp_all_out, save_sem.at[0])
    save_mlp.start()
    for s in range(1, n_hi):
        mlp_send_hop(s, wait=True)
    for m in every_m:
        for k in range(n_hi):
            mlp_lo(m, k).wait_send()
        for p in range(2):
            joint_lo(p, m).wait_send()
        vec_lo_move(m).wait_send()
    for k in every_k:
        for p in range(2):
            joint_hi(p, k).wait_send()
            all_hi(p, k).wait_send()
        vec_hi_move(k).wait_send()
    vec_pair_move(0, sibling).wait_send()
    vec_pair_move(1, across).wait_send()

    def sent(c, _):
        for which in range(2):
            core_move(which, 0, c).wait_send()
            core_move(which, 1, c).wait_send()
            x_move(which, c).wait_send()
        return 0

    lax.fori_loop(0, BACK_CHUNKS, sent, 0)
    for m in every_m:
        for p in range(2):
            all_lo(p, m, -m).wait_recv()
            all_lo(p, m).wait_send()
    save_joint = pltpu.make_async_copy(joint_all, joint_all_out, save_sem.at[1])
    save_joint.start()
    save_mlp.wait()
    save_joint.wait()


def levels(n_batch):
    lo = 2 if n_batch <= 8 else 4
    return n_batch // lo, lo


def back(
    n_batch, d_qkv, nall, dn_part, ho, call, mlp_part, qkv_weight_t, attn_out, tokens, cot, ln_gain, out_bias,
    own_lo, own_hi, front_rows, gain_rows,
):
    n_hi, n_lo = levels(n_batch)
    strips, tok_dev, features = nall.shape
    own = (own_lo.shape[0] + own_hi.shape[0], features)
    wide, packed = d_qkv.shape[2], ho.shape[2]
    heads = attn_out.shape[0] // DH
    chunk = (2 * features // n_batch, features // 2)
    dma = pltpu.SemaphoreType.DMA
    vmem = pltpu.VMEM
    return pl.pallas_call(
        functools.partial(back_body, heads, n_hi, n_lo),
        out_shape=(
            jax.ShapeDtypeStruct(tokens.shape, BF16),
            jax.ShapeDtypeStruct(tokens.shape, BF16),
            jax.ShapeDtypeStruct((n_hi, n_lo) + own, BF16),
            jax.ShapeDtypeStruct((n_lo, n_hi) + chunk, BF16),
            jax.ShapeDtypeStruct((8, features), F32),
        ),
        in_specs=[ANY] * 6 + [VMEM] * 10,
        out_specs=(VMEM, VMEM, ANY, ANY, VMEM),
        scratch_shapes=[
            vmem(d_qkv.shape, BF16), vmem(nall.shape, BF16), vmem(dn_part.shape, BF16),
            vmem(ho.shape, BF16), vmem(call.shape, BF16), vmem(mlp_part.shape, BF16),
            vmem((wide, features), BF16),
            vmem((packed, features), BF16),
            vmem((wide, features), F32),
            vmem((packed, features), F32),
            vmem((n_lo, n_hi) + chunk, BF16),
            vmem((features, features), BF16),
            vmem((n_lo, n_hi) + chunk, BF16),
            vmem((n_hi,) + chunk, BF16),
            vmem((n_hi,) + chunk, BF16),
            vmem((n_lo, n_hi) + chunk, BF16),
            vmem((n_hi, n_lo) + own, BF16),
            vmem((2,) + tokens.shape, F32),
            vmem((2, 2) + tokens.shape, BF16),
            vmem((2, 2) + tokens.shape, BF16),
            vmem((2,) + tokens.shape, BF16),
            vmem((2,) + tokens.shape, BF16),
            vmem((2, 8, features), F32),
            vmem((n_lo, 8, features), F32),
            vmem((n_hi, 8, features), F32),
            vmem((2, 8, features), F32),
            dma((6, strips)),
            dma((2, n_hi)), dma((2, n_hi)),
            dma((n_lo, n_hi)), dma((n_lo, n_hi)),
            dma((n_lo, 2)), dma((n_lo, 2)),
            dma((n_hi, 2)), dma((n_hi, 2)),
            dma((n_hi, 2)), dma((n_hi, 2)),
            dma((n_lo, 2)), dma((n_lo, 2)),
            dma((2, 2, BACK_CHUNKS)), dma((2, 2, BACK_CHUNKS)),
            dma((2, BACK_CHUNKS)), dma((2, BACK_CHUNKS)),
            dma((n_lo + n_hi + 2,)), dma((n_lo + n_hi + 2,)),
            dma((2,)),
        ],
        compiler_params=pltpu.CompilerParams(collective_id=1, has_side_effects=True, vmem_limit_bytes=60 << 20),
        name="reduce_gradients",
    )(
        d_qkv, nall, dn_part, ho, call, mlp_part, qkv_weight_t, attn_out, tokens, cot, ln_gain, out_bias,
        own_lo, own_hi, front_rows, gain_rows,
    )


def widen_body(
    heads, mlp_hbm, joint_hbm, output_in, input_grad_in, rows,
    output, input_grad, qkv_out, attn_out, mlp_in_out, mlp_out_out, ln_gain, q_gain, k_gain, mlp_bias, out_bias,
    kept, mlp_all, joint_all, joint, qkv_t, attn, mlp, sems,
):
    def copy(i, source, to):
        made = pltpu.make_async_copy(source, to, sems.at[i])
        made.start()
        return made

    chunks = mlp_all.shape[0]
    load_mlp = [copy(10 + o, mlp_hbm.at[o], mlp_all.at[o]) for o in range(chunks)]
    load_joint = copy(0, joint_hbm, joint_all)
    load_rows = [copy(2, output_in, kept.at[0]), copy(3, input_grad_in, kept.at[1])]
    features = rows.shape[1]
    mlp_bias[...] = rows[0:1, :].reshape(features)
    out_bias[...] = rows[1:2, :].reshape(features)
    ln_gain[...] = rows[2:3, :].reshape(features)
    for offset, ref in ((0, q_gain), (DH, k_gain)):
        parts = [rows[3:4, h * LANES + offset : h * LANES + offset + DH] for h in range(heads)]
        ref[...] = jnp.concatenate(parts, axis=1).reshape(heads * DH)
    cut = lo_rows(features) // chunks
    rest = mlp_all.shape[1] - cut
    pending = []

    def store(sem, row, count):
        to = mlp_in_out if row < features else mlp_out_out
        pending.append(copy(sem, mlp.at[pl.ds(row, count)], to.at[pl.ds(row % features, count)]))

    for o in range(chunks):
        load_mlp[o].wait()
        row = lo_rows(features) + o * rest
        mlp[o * cut : (o + 1) * cut] = mlp_all[o, :cut].astype(F32)
        mlp[row : row + rest] = mlp_all[o, cut:].astype(F32)
        store(10 + chunks + o, o * cut, cut)
        store(10 + 2 * chunks + o, row, rest)
    load_joint.wait()
    n_lo, n_hi, chunk_rows, cols = joint_all.shape
    width = qkv_t.shape[0]
    per_half = features // chunk_rows
    for o in range(n_lo * n_hi):
        row = o % per_half * chunk_rows
        joint[o // per_half, row : row + chunk_rows] = joint_all[o % n_lo, o // n_lo]
    for i, place in enumerate(kind_order(heads)):
        for half in range(2):
            at = slice(half * cols, (half + 1) * cols)
            qkv_t[place * DH : (place + 1) * DH, at] = joint[half, i * DH : (i + 1) * DH].astype(F32)
        rows_at = pl.ds(place * DH, DH)
        pending.append(copy(10 + 3 * chunks + i, qkv_t.at[rows_at], qkv_out.at[rows_at]))
    for half in range(2):
        attn[:, half * cols : (half + 1) * cols] = joint[half, width:].astype(F32)
    pending.append(copy(5, attn, attn_out))
    for i, (load, to) in enumerate(zip(load_rows, (output, input_grad))):
        load.wait()
        pending.append(copy(8 + i, kept.at[i], to))
    for made in pending:
        made.wait()


def widen(heads, width, mlp_all, joint_all, output, input_grad, rows):
    features = rows.shape[1]
    head_width = heads * DH

    def out(*shape):
        return jax.ShapeDtypeStruct(shape, F32)

    like = jax.ShapeDtypeStruct(output.shape, BF16)
    return pl.pallas_call(
        functools.partial(widen_body, heads),
        out_shape=(
            like, like, out(width, features), out(head_width, features), out(features, features), out(features, features),
            out(features), out(head_width), out(head_width), out(features), out(features),
        ),
        in_specs=[ANY] * 4 + [VMEM],
        out_specs=(ANY,) * 6 + (VMEM,) * 5,
        scratch_shapes=[
            pltpu.VMEM((2,) + output.shape, BF16),
            pltpu.VMEM(mlp_all.shape, BF16),
            pltpu.VMEM(joint_all.shape, BF16),
            pltpu.VMEM((2, features, features // 2), BF16),
            pltpu.VMEM((width, features), F32),
            pltpu.VMEM((head_width, features), F32),
            pltpu.VMEM((2 * features, features), F32),
            pltpu.SemaphoreType.DMA((10 + 3 * mlp_all.shape[0] + 3 * heads,)),
        ],
        compiler_params=pltpu.CompilerParams(vmem_limit_bytes=60 << 20),
        name="widen_gradients",
    )(mlp_all, joint_all, output, input_grad, rows)


def on_device(
    tokens, out_cotangent, ln_gain, qkv_weight, q_gain, k_gain, attn_out,
    mlp_in, mlp_bias, mlp_out, out_bias, image_len, image_group,
):
    tok_dev, features = tokens.shape
    strips = lax.axis_size("tensor")
    n_batch = lax.axis_size("batch")
    n_hi, n_lo = levels(n_batch)
    heads = q_gain.shape[0] // DH
    qkv_cols = qkv_weight.shape[1]

    weight_t = qkv_weight.T
    (qa, ka, va, do, u, r, mlp_part, dn_part, nall, call, *mlp_grad, front_rows) = front(
        strips, n_batch, tokens, out_cotangent, ln_gain, q_gain, k_gain, mlp_bias, weight_t, attn_out, mlp_in, mlp_out
    )

    def along_lo(x, m):
        pairs = [(h * n_lo + i, h * n_lo + (i + m) % n_lo) for h in range(n_hi) for i in range(n_lo)]
        return lax.ppermute(x, "batch", pairs)

    def along_hi(x, k):
        pairs = [(h * n_lo + i, (h + k) % n_hi * n_lo + i) for h in range(n_hi) for i in range(n_lo)]
        return lax.ppermute(x, "batch", pairs)

    def add(first, others):
        total = first.astype(F32)
        for other in others:
            total = total + other.astype(F32)
        return total.astype(BF16)

    lo_first, hi_first = mlp_grad[:n_lo], mlp_grad[n_lo:]
    lo_got = [along_lo(lo_first[m], m) for m in range(1, n_lo)]
    hi_got = [along_hi(hi_first[k], k) for k in range(1, n_hi)]
    qb, dob, ho = attn_fwd(image_len, image_group, qa, ka, va, do)
    lo_sum = [add(lo_first[0][k], [got[k] for got in lo_got]) for k in range(n_hi)]
    hi_sum = [add(hi_first[0][m], [got[m] for got in hi_got]) for m in range(n_lo)]
    qb, lo_sum, hi_sum = lax.optimization_barrier((qb, lo_sum, hi_sum))
    lo_got = [along_hi(lo_sum[k], k) for k in range(1, n_hi)]
    hi_got = [along_lo(hi_sum[m], m) for m in range(1, n_lo)]
    d_qkv, gain_rows = attn_bwd(image_len, image_group, qb, ka, va, dob, u, r, q_gain, k_gain)
    own_lo, own_hi = add(lo_sum[0], lo_got), add(hi_sum[0], hi_got)
    output, input_grad, mlp_all, joint_all, rows = back(
        n_batch, d_qkv, nall, dn_part, ho, call, mlp_part, weight_t, attn_out, tokens, out_cotangent, ln_gain, out_bias,
        own_lo, own_hi, front_rows, gain_rows,
    )
    output, input_grad, qkv_t, attn, mlp_in_grad, mlp_out_grad, ln, q, k, bias, out_bias_grad = widen(
        heads, qkv_cols, mlp_all.reshape((n_batch,) + mlp_all.shape[2:]), joint_all,
        output, input_grad, rows,
    )
    return output, input_grad, ln, qkv_t.T, q, k, attn, mlp_in_grad, bias, mlp_out_grad, out_bias_grad


def solution(mesh):
    rows, cols, first = P(("batch", "tensor"), None), P(None, "tensor"), P("tensor", None)
    return jax.shard_map(
        on_device,
        mesh=mesh,
        in_specs=(rows, rows, P(), cols, P("tensor"), P("tensor"), first, cols, P("tensor"), first, P(), P(), P()),
        out_specs=(rows, rows, P(), cols, P("tensor"), P("tensor"), first, cols, P("tensor"), first, P()),
        check_vma=False,
    )
```
